32 devices in a mesh: blk: 16 (over z, y, core), uly: 2 (over x).
Axes of the slice: x: 2, y: 2, z: 4, core: 2. Of those that a mesh axis runs over, the one named last changes fastest.
Arguments:
- hidden: bfloat16 [2, 2048, 1024], P('uly', 'blk'), may hold values from -6 to 6
- skip_in: bfloat16 [2, 2048, 1024], P('uly', 'blk'), may hold values from -6 to 6
- time_embed: bfloat16 [2, 1, 1024], P('uly'), may hold values from -6 to 6
- lengths: int32 [2, 1], replicated, may hold values from 0 to 2048, as said below
- cotangent: bfloat16 [2, 2048, 1024], P('uly', 'blk'), may hold values from -6 to 6
- w_skip: bfloat16 [2048, 1024], P(('blk', 'uly')), may hold values from -0.125 to 0.125
- b_skip: bfloat16 [1024], P(('blk', 'uly')), may hold values from -3 to 3
- w_mod: bfloat16 [1024, 4096], P(('blk', 'uly')), may hold values from -0.0625 to 0.0625
- w_qkv: bfloat16 [1024, 3072], P(('blk', 'uly')), may hold values from -0.1875 to 0.1875
- w_out: bfloat16 [1024, 1024], P(('blk', 'uly')), may hold values from -0.1875 to 0.1875
- w_up: bfloat16 [1024, 4096], P(('blk', 'uly')), may hold values from -0.1875 to 0.1875
- b_up: bfloat16 [4096], P(('blk', 'uly')), may hold values from -3 to 3
- w_down: bfloat16 [4096, 1024], P(('blk', 'uly')), may hold values from -0.09375 to 0.09375
- b_down: bfloat16 [1024], P(('blk', 'uly')), may hold values from -3 to 3
Outputs:
- output: bfloat16 [2, 2048, 1024], P('uly', 'blk')
- hidden_grad: bfloat16 [2, 2048, 1024], P('uly', 'blk')
- skip_grad: bfloat16 [2, 2048, 1024], P('uly', 'blk')
- time_grad: float32 [2, 1, 1024], P('uly')
- w_skip_grad: float32 [2048, 1024], P(('blk', 'uly'))
- b_skip_grad: float32 [1024], P(('blk', 'uly'))
- w_mod_grad: float32 [1024, 4096], P(('blk', 'uly'))
- w_qkv_grad: float32 [1024, 3072], P(('blk', 'uly'))
- w_out_grad: float32 [1024, 1024], P(('blk', 'uly'))
- w_up_grad: float32 [1024, 4096], P(('blk', 'uly'))
- b_up_grad: float32 [4096], P(('blk', 'uly'))
- w_down_grad: float32 [4096, 1024], P(('blk', 'uly'))
- b_down_grad: float32 [1024], P(('blk', 'uly'))
The draws below stay inside these ranges and needn't reach their ends.
Inputs may be any that keep to these rules, and one draw needn't show every extreme that they name: Each row's lengths are its utterances in frame order; their sum is at most 2048, and the frames after it are padding. In one row, drawn from the seed, a single utterance fills all 2048 frames and the row's other entries are 0; in the other rows each entry is between 1024 and 2048.
All inputs are finite; a program needn't handle non-finite values.
Results may differ from the reference program's by a relative error of at most 0.013.
Values may be sent and summed in bfloat16 or wider, within the bound.
A program may use at most 256 MiB of HBM per device.

```python
import jax
import jax.numpy as jnp
from jax import lax

D = 1024
HEADS = 16
HEAD_DIM = 64
FF = 4096
ROWS = 2
PACK = 2048
UTT_LEN = 2048
SEGS = 1


def draw_lengths(key, part):
    key = jax.random.fold_in(key, 11)
    first_key, second_key = jax.random.split(key)
    drawn = jax.random.randint(first_key, (ROWS, SEGS), UTT_LEN // 2, UTT_LEN + 1)
    chosen = jax.random.randint(second_key, (), 0, ROWS)
    whole_row = jnp.where(jnp.arange(SEGS) == 0, PACK, 0)
    picked = jnp.arange(ROWS)[:, None] == chosen
    return jnp.where(picked, whole_row[None, :], drawn).astype(jnp.int32)


def block_levels(stream_key, shape, cuts, smallest, high):
    level = 1.0
    for position, blocks in cuts:
        steps = jax.random.uniform(jax.random.fold_in(jax.random.fold_in(stream_key, 6), position), (blocks,), jnp.float32, smallest / len(cuts), high / len(cuts))
        level = level * jnp.repeat(jnp.exp(steps), shape[position] // blocks).reshape((-1,) + (1,) * (len(shape) - 1 - position))
    return level


def scatter_about(rng, shape, scale, bound, cuts=(), kind=jnp.bfloat16):
    level = block_levels(rng, shape, cuts, -0.22, 0.18) if cuts else 1.0
    entries = jax.random.normal(rng, shape, jnp.float32) * scale * level
    return jnp.minimum(jnp.maximum(entries, -bound), bound).astype(kind)


def setup_inputs(seed: int = 0) -> dict:
    key_list = jax.random.split(jax.random.key(seed), 15)
    return {
        "hidden": scatter_about(key_list[0], (ROWS, PACK, D), 1.0, 6.0, ((0, 2), (1, 16))),
        "skip_in": scatter_about(key_list[1], (ROWS, PACK, D), 1.0, 6.0, ((0, 2), (1, 16))),
        "time_embed": scatter_about(key_list[2], (ROWS, SEGS, D), 1.0, 6.0, ((0, 2),)),
        "lengths": draw_lengths(jax.random.fold_in(key_list[14], 71), 0),
        "cotangent": scatter_about(key_list[4], (ROWS, PACK, D), 1.0, 6.0, ((0, 2), (1, 16))),
        "w_skip": scatter_about(key_list[5], (2 * D, D), (2 * D) ** -0.5, 0.125, ((0, 32),)),
        "b_skip": scatter_about(key_list[6], (D,), 0.5, 3.0, ((0, 32),)),
        "w_mod": scatter_about(key_list[7], (D, 4 * D), (8 * D) ** -0.5, 0.0625, ((0, 32),)),
        "w_qkv": scatter_about(key_list[8], (D, 3 * D), D ** -0.5, 0.1875, ((0, 32),)),
        "w_out": scatter_about(key_list[9], (D, D), D ** -0.5, 0.1875, ((0, 32),)),
        "w_up": scatter_about(key_list[10], (D, FF), D ** -0.5, 0.1875, ((0, 32),)),
        "b_up": scatter_about(key_list[11], (FF,), 0.5, 3.0, ((0, 32),)),
        "w_down": scatter_about(key_list[12], (FF, D), FF ** -0.5, 0.09375, ((0, 32),)),
        "b_down": scatter_about(key_list[13], (D,), 0.5, 3.0, ((0, 32),)),
    }


@jax.custom_vjp
def low(v):
    return lax.optimization_barrier(v.astype(jnp.bfloat16)).astype(jnp.float32)

@jax.custom_vjp
def low_back(v):
    return v

def low_keep(v):
    return (low(v), None)

def low_pass(kept, grad):
    return (grad,)

def back_keep(v):
    return (v, None)

def back_low(kept, grad):
    return (low(grad),)
low.defvjp(low_keep, low_pass)
low_back.defvjp(back_keep, back_low)
exact_mode = lax.Precision.HIGHEST
epsilon = 1e-05

def segment_info(len_row, positions):
    slots = len_row.shape[0]
    ends = jnp.cumsum(len_row).astype(jnp.int32)
    starts = (ends - len_row).astype(jnp.int32)
    total = ends[-1]
    seg_ids = lax.optimization_barrier(jnp.sum((positions[:, None] >= ends[None, :]).astype(jnp.int32), axis=1)).astype(jnp.int32)
    onehot = seg_ids[:, None] == jnp.arange(slots, dtype=jnp.int32)[None, :]
    begin = lax.optimization_barrier(jnp.sum(jnp.where(onehot, starts[None, :], 0), axis=1)).astype(jnp.int32)
    begin = begin + jnp.where(seg_ids == slots, total, 0).astype(jnp.int32)
    return (seg_ids, (positions - begin).astype(jnp.int32), seg_ids < slots)

def rotary(values, offsets):
    half = values.shape[-1] // 2
    freq = 10000.0 ** (-jnp.arange(half, dtype=jnp.float32) / half)
    angle = offsets.astype(jnp.float32)[:, None] * freq[None, :]
    cosine = jnp.cos(angle)[:, None, :]
    sine = jnp.sin(angle)[:, None, :]
    first = values[..., :half]
    second = values[..., half:]
    return jnp.concatenate([first * cosine - second * sine, second * cosine + first * sine], -1)

def modulate(values, scale, shift):
    center = values - lax.optimization_barrier(jnp.mean(values, -1, keepdims=True))
    spread = lax.optimization_barrier(jnp.mean(center * center, -1, keepdims=True))
    return center * lax.rsqrt(spread + epsilon) * (1.0 + scale) + shift

def attend_row(query, keys, values, seg_ids):
    count = query.shape[0]
    width = min(512, count)
    blocks = count // width
    scaling = HEAD_DIM ** (-0.5)

    def attend_block(member):
        query_block, seg_block = member
        score = low_back(jnp.einsum('qhd,khd->hqk', query_block, keys, precision=exact_mode) * scaling)
        mask = (seg_block[:, None] == seg_ids[None, :])[None]
        masked = jnp.where(mask, score, -1e+30)
        peak = lax.optimization_barrier(jnp.max(masked, -1, keepdims=True))
        weights = jnp.where(mask, jnp.exp(masked - peak), 0.0)
        weights = low(weights / lax.optimization_barrier(jnp.sum(weights, -1, keepdims=True)))
        return jnp.einsum('hqk,khd->qhd', weights, values, precision=exact_mode)
    result = lax.map(jax.checkpoint(attend_block), (query.reshape(blocks, width, HEADS, HEAD_DIM), seg_ids.reshape(blocks, width)))
    return result.reshape(count, HEADS, HEAD_DIM)

def forward(hidden, skip_in, time_embed, w_skip, b_skip, w_mod, w_qkv, w_out, w_up, b_up, w_down, b_down, seg_ids, offsets, valid):
    row_count = hidden.shape[0]
    frames = hidden.shape[1]
    joined = jnp.concatenate([hidden, skip_in], -1)
    base = low_back(jnp.einsum('rnc,cd->rnd', joined, w_skip, precision=exact_mode) + b_skip)
    mods = jnp.einsum('rsd,de->rse', time_embed, w_mod, precision=exact_mode)
    padded = jnp.concatenate([mods, jnp.zeros((row_count, 1, mods.shape[2]), jnp.float32)], 1)
    frame_mod = jax.vmap(lambda table, picks: table[picks])(padded, seg_ids)
    a_scale, a_shift, f_scale, f_shift = jnp.split(frame_mod, 4, -1)
    normed = low(modulate(base, a_scale, a_shift))
    projected = low_back(jnp.einsum('rnd,de->rne', normed, w_qkv, precision=exact_mode))
    parts = projected.reshape(row_count, frames, 3, HEADS, HEAD_DIM)
    query = low(low_back(jax.vmap(rotary)(parts[:, :, 0], offsets)))
    keys = low(low_back(jax.vmap(rotary)(parts[:, :, 1], offsets)))
    values = low(low_back(parts[:, :, 2]))
    attended = lax.map(lambda member: attend_row(*member), (query, keys, values, seg_ids))
    mixed = low(low_back(attended * valid.astype(jnp.float32)[:, :, None, None]))
    branch = low_back(jnp.einsum('rnd,de->rne', mixed.reshape(row_count, frames, D), w_out, precision=exact_mode))
    middle = base + branch
    normed2 = low(modulate(middle, f_scale, f_shift))
    inner = low_back(jnp.einsum('rnd,df->rnf', normed2, w_up, precision=exact_mode) + b_up)
    act = low(jax.nn.gelu(inner, approximate=False))
    return middle + jnp.einsum('rnf,fd->rnd', act, w_down, precision=exact_mode) + b_down

def reference(hidden, skip_in, time_embed, lengths, cotangent, w_skip, b_skip, w_mod, w_qkv, w_out, w_up, b_up, w_down, b_down):
    positions = jnp.arange(PACK, dtype=jnp.int32)
    seg_ids, offsets, valid = jax.vmap(lambda len_row: segment_info(len_row, positions))(lengths)
    inputs = tuple((member.astype(jnp.float32) for member in (hidden, skip_in, time_embed, w_skip, b_skip, w_mod, w_qkv, w_out, w_up, b_up, w_down, b_down)))

    def run(*members):
        return forward(*members, seg_ids, offsets, valid)
    result, pullback = jax.vjp(run, *inputs)
    grads = pullback(cotangent.astype(jnp.float32))
    output = result.astype(jnp.bfloat16)
    hidden_grad = grads[0].astype(jnp.bfloat16)
    skip_grad = grads[1].astype(jnp.bfloat16)
    return (output, hidden_grad, skip_grad, grads[2], grads[3], grads[4], grads[5], grads[6], grads[7], grads[8], grads[9], grads[10], grads[11])
```

```python
import functools
import math

import jax
import jax.numpy as jnp
from jax import lax
from jax.experimental import pallas as pl
from jax.experimental.pallas import tpu as pltpu
from jax.sharding import PartitionSpec as P

HEADS = 16
HEAD_DIM = 64


exact_mode = lax.Precision.HIGHEST
epsilon = 1e-05


def passed_along(x, axis, by):
    devices = lax.axis_size(axis)
    return lax.ppermute(x, axis, [(i, (i + by) % devices) for i in range(devices)])


def segment_info(len_row, positions):
    slots = len_row.shape[0]
    ends = jnp.cumsum(len_row)
    starts = ends - len_row
    total = ends[-1]
    seg_ids = jnp.sum((positions[:, None] >= ends[None, :]).astype(jnp.int32), axis=1)
    onehot = seg_ids[:, None] == jnp.arange(slots, dtype=jnp.int32)[None, :]
    begin = jnp.sum(jnp.where(onehot, starts[None, :], 0), axis=1)
    begin = begin + jnp.where(seg_ids == slots, total, 0)
    return (seg_ids, positions - begin, seg_ids < slots)


def rotary(values, offsets):
    half = values.shape[-1] // 2
    freq = 10000.0 ** (-jnp.arange(half, dtype=jnp.float32) / half)
    angle = offsets.astype(jnp.float32)[:, None] * freq[None, :]
    cosine = jnp.cos(angle)[:, None, :]
    sine = jnp.sin(angle)[:, None, :]
    first = values[..., :half]
    second = values[..., half:]
    return jnp.concatenate([first * cosine - second * sine, second * cosine + first * sine], -1)


def modulate(values, scale, shift):
    center = values - jnp.mean(values, -1, keepdims=True)
    spread = jnp.mean(center * center, -1, keepdims=True)
    return center * lax.rsqrt(spread + epsilon) * (1.0 + scale) + shift


def contract_rows(left, right):
    return lax.dot_general(
        left, right, (((0,), (0,)), ((), ())), preferred_element_type=jnp.float32
    )


def contract_cols(left, right):
    return lax.dot_general(
        left, right, (((1,), (1,)), ((), ())), preferred_element_type=jnp.float32
    )


def gelu_exact(values):
    return jax.nn.gelu(values, approximate=False)


def per_device(
    hidden,
    skip_in,
    time_embed,
    lengths,
    cotangent,
    w_skip,
    b_skip,
    w_mod,
    w_qkv,
    w_out,
    w_up,
    b_up,
    w_down,
    b_down,
):
    gathered = (
        lax.all_gather(w_skip, ("blk", "uly"), axis=0, tiled=True),
        lax.all_gather(b_skip, ("blk", "uly"), axis=0, tiled=True),
        lax.all_gather(w_mod, ("blk", "uly"), axis=0, tiled=True),
        lax.all_gather(w_qkv, ("blk", "uly"), axis=0, tiled=True),
        lax.all_gather(w_out, ("blk", "uly"), axis=0, tiled=True),
        lax.all_gather(w_up, ("blk", "uly"), axis=0, tiled=True),
        lax.all_gather(b_up, ("blk", "uly"), axis=0, tiled=True),
        lax.all_gather(w_down, ("blk", "uly"), axis=0, tiled=True),
        lax.all_gather(b_down, ("blk", "uly"), axis=0, tiled=True),
    )
    (
        skip_full,
        bskip_full,
        mod_full,
        qkv_full,
        out_full,
        up_full,
        bup_full,
        down_full,
        bdown_full,
    ) = gathered
    group_count = lax.axis_size("uly")
    cycle_size = lax.axis_size("blk")
    frame_count = hidden.shape[1]
    row_count = lengths.shape[0]
    slot_count = lengths.shape[1]
    local_heads = HEADS // group_count
    span = local_heads * HEAD_DIM
    scaling = HEAD_DIM ** (-0.5)
    block_index = lax.axis_index("blk")
    row_index = lax.axis_index("uly")
    frame_pos = block_index * frame_count + jnp.arange(frame_count, dtype=jnp.int32)
    all_seg, all_offsets, all_valid = jax.vmap(lambda len_row: segment_info(len_row, frame_pos))(
        lengths
    )
    own_seg = lax.dynamic_index_in_dim(all_seg, row_index, 0, keepdims=False)
    own_offsets = lax.dynamic_index_in_dim(all_offsets, row_index, 0, keepdims=False)
    joined = jnp.concatenate([hidden[0], skip_in[0]], 1)
    base = jnp.dot(joined, skip_full, preferred_element_type=jnp.float32) + bskip_full.astype(
        jnp.float32
    )
    time_row = time_embed[0]
    mods = jnp.dot(time_row, mod_full, preferred_element_type=jnp.float32)
    selector = (own_seg[:, None] == jnp.arange(slot_count, dtype=jnp.int32)[None, :]).astype(
        jnp.float32
    )
    frame_mod = jnp.dot(selector, mods, precision=exact_mode)
    a_scale, a_shift, f_scale, f_shift = jnp.split(frame_mod, 4, 1)
    normed_full, norm_back = jax.vjp(modulate, base, a_scale, a_shift)
    normed = normed_full.astype(jnp.bfloat16)
    projected = jnp.dot(normed, qkv_full, preferred_element_type=jnp.float32).reshape(
        frame_count, 3, HEADS, HEAD_DIM
    )

    def place(parts):
        return jnp.stack(
            [rotary(parts[:, 0], own_offsets), rotary(parts[:, 1], own_offsets), parts[:, 2]], 1
        )

    turned, unturn = jax.vjp(place, projected)
    sending = turned.astype(jnp.bfloat16).reshape(1, frame_count, 3, group_count, span)
    head_data = lax.all_to_all(sending, "uly", split_axis=3, concat_axis=0, tiled=True)
    query = head_data[:, :, 0, 0].reshape(row_count, frame_count, local_heads, HEAD_DIM)
    kv_pairs = head_data[:, :, 1:, 0]

    def key_segments(start, count):
        key_pos = start + jnp.arange(count, dtype=jnp.int32)
        return jax.vmap(lambda len_row: segment_info(len_row, key_pos)[0])(lengths)

    start_state = (
        jnp.full((row_count, local_heads, frame_count), -1e30, jnp.float32),
        jnp.zeros((row_count, local_heads, frame_count), jnp.float32),
        jnp.zeros((row_count, frame_count, local_heads, HEAD_DIM), jnp.float32),
    )
    piece = lax.all_gather(kv_pairs, "blk", axis=1, tiled=True)
    total = piece.shape[1]
    step = math.gcd(total, max(frame_count, 1024))

    def sub_step(step_index, state):
        run_max, run_total, run_acc = state
        offset = step_index * step
        section = lax.dynamic_slice_in_dim(piece, offset, step, 1)
        key_seg = key_segments(offset, step)
        key_part = section[:, :, 0].reshape(row_count, step, local_heads, HEAD_DIM)
        value_part = section[:, :, 1].reshape(row_count, step, local_heads, HEAD_DIM)
        mask = all_seg[:, None, :, None] == key_seg[:, None, None, :]
        score = (
            jnp.einsum("rqhd,rkhd->rhqk", query, key_part, preferred_element_type=jnp.float32)
            * scaling
        )
        masked = jnp.where(mask, score, -1e30)
        fresh = jnp.maximum(run_max, jnp.max(masked, -1))
        weights = jnp.where(mask, jnp.exp(masked - fresh[..., None]), 0.0)
        decay = jnp.exp(run_max - fresh)
        run_total = run_total * decay + jnp.sum(weights, -1)
        run_acc = run_acc * jnp.swapaxes(decay, 1, 2)[..., None] + jnp.einsum(
            "rhqk,rkhd->rqhd",
            weights.astype(jnp.bfloat16),
            value_part,
            preferred_element_type=jnp.float32,
        )
        return (fresh, run_total, run_acc)

    run_max, run_total, run_acc = lax.fori_loop(0, total // step, sub_step, start_state)
    attended = run_acc / jnp.swapaxes(run_total, 1, 2)[..., None]
    log_total = run_max + jnp.log(run_total)
    valid_half = all_valid.astype(jnp.bfloat16)[:, :, None, None]
    leaving = (attended * all_valid.astype(jnp.float32)[:, :, None, None]).astype(jnp.bfloat16)
    leaving = leaving.reshape(row_count, frame_count, 1, span)
    mixed = lax.all_to_all(leaving, "uly", split_axis=0, concat_axis=2, tiled=True).reshape(
        frame_count, HEADS * HEAD_DIM
    )
    branch = jnp.dot(mixed, out_full, preferred_element_type=jnp.float32)
    middle = base + branch
    normed2_full, norm2_back = jax.vjp(modulate, middle, f_scale, f_shift)
    normed2 = normed2_full.astype(jnp.bfloat16)
    inner = jnp.dot(normed2, up_full, preferred_element_type=jnp.float32) + bup_full.astype(
        jnp.float32
    )
    act_full, act_back = jax.vjp(gelu_exact, inner)
    act = act_full.astype(jnp.bfloat16)
    result = (
        middle
        + jnp.dot(act, down_full, preferred_element_type=jnp.float32)
        + bdown_full.astype(jnp.float32)
    )
    output = result.astype(jnp.bfloat16)[None]
    again = (
        lax.all_gather(w_skip, ("blk", "uly"), axis=0, tiled=True),
        lax.all_gather(w_mod, ("blk", "uly"), axis=0, tiled=True),
        lax.all_gather(w_qkv, ("blk", "uly"), axis=0, tiled=True),
        lax.all_gather(w_out, ("blk", "uly"), axis=0, tiled=True),
        lax.all_gather(w_up, ("blk", "uly"), axis=0, tiled=True),
        lax.all_gather(w_down, ("blk", "uly"), axis=0, tiled=True),
    )
    skip_back, mod_back, qkv_back, out_back, up_back, down_back = again
    upstream = cotangent[0]
    upstream_full = upstream.astype(jnp.float32)
    grad_down = contract_rows(act, upstream)
    grad_bdown = jnp.sum(upstream_full, 0)
    grad_act = contract_cols(upstream, down_back)
    grad_inner = act_back(grad_act)[0].astype(jnp.bfloat16)
    grad_up = contract_rows(normed2, grad_inner)
    grad_bup = jnp.sum(grad_inner.astype(jnp.float32), 0)
    grad_normed2 = contract_cols(grad_inner, up_back)
    grad_mid_norm, grad_fscale, grad_fshift = norm2_back(grad_normed2)
    grad_middle = upstream_full + grad_mid_norm
    grad_branch = grad_middle.astype(jnp.bfloat16)
    grad_out = contract_rows(mixed, grad_branch)
    grad_mixed = (
        contract_cols(grad_branch, out_back)
        .astype(jnp.bfloat16)
        .reshape(1, frame_count, group_count, span)
    )
    returning = lax.all_to_all(grad_mixed, "uly", split_axis=2, concat_axis=0, tiled=True)
    grad_attn = returning.reshape(row_count, frame_count, local_heads, HEAD_DIM) * valid_half
    delta_rows = jnp.swapaxes(jnp.sum(grad_attn.astype(jnp.float32) * attended, -1), 1, 2)

    def contribution(held_pairs, key_start):
        count = held_pairs.shape[1]
        key_seg = key_segments(key_start, count)
        key_part = held_pairs[:, :, 0].reshape(row_count, count, local_heads, HEAD_DIM)
        value_part = held_pairs[:, :, 1].reshape(row_count, count, local_heads, HEAD_DIM)
        mask = all_seg[:, None, :, None] == key_seg[:, None, None, :]
        score = (
            jnp.einsum("rqhd,rkhd->rhqk", query, key_part, preferred_element_type=jnp.float32)
            * scaling
        )
        weights = jnp.exp(jnp.where(mask, score - log_total[..., None], -1e30))
        grad_weights = jnp.einsum(
            "rqhd,rkhd->rhqk", grad_attn, value_part, preferred_element_type=jnp.float32
        )
        grad_score = (weights * (grad_weights - delta_rows[..., None])).astype(jnp.bfloat16)
        more_query = (
            jnp.einsum("rhqk,rkhd->rqhd", grad_score, key_part, preferred_element_type=jnp.float32)
            * scaling
        )
        more_key = (
            jnp.einsum("rhqk,rqhd->rkhd", grad_score, query, preferred_element_type=jnp.float32)
            * scaling
        )
        more_value = jnp.einsum(
            "rhqk,rqhd->rkhd",
            weights.astype(jnp.bfloat16),
            grad_attn,
            preferred_element_type=jnp.float32,
        )
        more_pairs = jnp.stack(
            [more_key.reshape(row_count, count, span), more_value.reshape(row_count, count, span)],
            2,
        )
        return (more_query, more_pairs)

    def pass_grads(held_grads):
        return passed_along(held_grads.astype(jnp.bfloat16), "blk", 1).astype(held_grads.dtype)

    def cycle_step(turn, state):
        held_pairs, held_grads, query_grad = state
        more_query, more_pairs = contribution(
            held_pairs, (block_index - turn) % cycle_size * frame_count
        )
        held_pairs = passed_along(held_pairs, "blk", 1)
        held_grads = pass_grads(held_grads + more_pairs)
        return (held_pairs, held_grads, query_grad + more_query)

    cycle_start = (
        kv_pairs,
        jnp.zeros((row_count, frame_count, 2, span), jnp.float32),
        jnp.zeros((row_count, frame_count, local_heads, HEAD_DIM), jnp.float32),
    )
    held_pairs, held_grads, query_grad = lax.fori_loop(0, cycle_size - 1, cycle_step, cycle_start)
    last_query, last_pairs = contribution(
        held_pairs, (block_index - (cycle_size - 1)) % cycle_size * frame_count
    )
    pair_grads = pass_grads(held_grads + last_pairs)
    query_grad = query_grad + last_query
    head_grads = jnp.concatenate(
        [
            query_grad.astype(jnp.bfloat16).reshape(row_count, frame_count, 1, span),
            pair_grads.astype(jnp.bfloat16),
        ],
        2,
    ).reshape(row_count, frame_count, 3, 1, span)
    frames_grad = lax.all_to_all(head_grads, "uly", split_axis=0, concat_axis=3, tiled=True)
    frames_grad = frames_grad.reshape(frame_count, 3, HEADS, HEAD_DIM).astype(jnp.float32)
    grad_projected = (
        unturn(frames_grad)[0].astype(jnp.bfloat16).reshape(frame_count, 3 * HEADS * HEAD_DIM)
    )
    grad_qkv = contract_rows(normed, grad_projected)
    grad_normed = contract_cols(grad_projected, qkv_back)
    grad_base_norm, grad_ascale, grad_ashift = norm_back(grad_normed)
    grad_base = (grad_middle + grad_base_norm).astype(jnp.bfloat16)
    grad_skip_w = contract_rows(joined, grad_base)
    grad_bskip = jnp.sum(grad_base.astype(jnp.float32), 0)
    grad_joined = contract_cols(grad_base, skip_back).astype(jnp.bfloat16)
    model_width = hidden.shape[2]
    hidden_grad = grad_joined[:, :model_width][None]
    skip_grad = grad_joined[:, model_width:][None]
    frame_mod_grad = jnp.concatenate([grad_ascale, grad_ashift, grad_fscale, grad_fshift], 1)
    slot_grad = lax.dot_general(
        selector, frame_mod_grad, (((0,), (0,)), ((), ())), precision=exact_mode
    )
    grad_mod = lax.dot_general(
        time_row.astype(jnp.float32), slot_grad, (((0,), (0,)), ((), ())), precision=exact_mode
    )
    slot_total = lax.psum(slot_grad, "blk")
    time_grad = lax.dot_general(
        slot_total, mod_back.astype(jnp.float32), (((1,), (1,)), ((), ())), precision=exact_mode
    )[None]
    owned = (
        lax.psum_scatter(grad_skip_w, ("blk", "uly"), scatter_dimension=0, tiled=True),
        lax.psum_scatter(grad_bskip, ("blk", "uly"), scatter_dimension=0, tiled=True),
        lax.psum_scatter(grad_mod, ("blk", "uly"), scatter_dimension=0, tiled=True),
        lax.psum_scatter(grad_qkv, ("blk", "uly"), scatter_dimension=0, tiled=True),
        lax.psum_scatter(grad_out, ("blk", "uly"), scatter_dimension=0, tiled=True),
        lax.psum_scatter(grad_up, ("blk", "uly"), scatter_dimension=0, tiled=True),
        lax.psum_scatter(grad_bup, ("blk", "uly"), scatter_dimension=0, tiled=True),
        lax.psum_scatter(grad_down, ("blk", "uly"), scatter_dimension=0, tiled=True),
        lax.psum_scatter(grad_bdown, ("blk", "uly"), scatter_dimension=0, tiled=True),
    )
    return (
        output,
        hidden_grad,
        skip_grad,
        time_grad,
        owned[0],
        owned[1],
        owned[2],
        owned[3],
        owned[4],
        owned[5],
        owned[6],
        owned[7],
        owned[8],
    )


MESH = pl.DeviceIdType.MESH


class Place:
    def __init__(self, depth):
        self.depth = depth
        self.b = lax.axis_index("blk")
        self.x = lax.axis_index("uly")
        self.z = self.b // 4
        self.y = (self.b // 2) % 2
        self.c = self.b % 2
        self.to_x = (self.b, 1 - self.x)
        self.to_y = (self.b + 2 - 4 * self.y, self.x)
        self.to_core = (self.b + 1 - 2 * self.c, self.x)
        self.to_up = (self.b + 4, self.x)
        self.to_down = (self.b - 4, self.x)

    def shard(self, z, y, c, x):
        return ((z * 2 + y) * 2 + c) * 2 + x

    def greet(self):
        barrier = pltpu.get_barrier_semaphore()
        for to in (self.to_x, self.to_y, self.to_core):
            pl.semaphore_signal(barrier, inc=1, device_id=to, device_id_type=MESH)

        @pl.when(self.z < self.depth - 1)
        def _():
            pl.semaphore_signal(barrier, inc=1, device_id=self.to_up, device_id_type=MESH)

        @pl.when(self.z > 0)
        def _():
            pl.semaphore_signal(barrier, inc=1, device_id=self.to_down, device_id_type=MESH)

        top = self.depth - 1
        pl.semaphore_wait(barrier, 3 + (self.z + top - 1) // top + (2 * top - 1 - self.z) // top)


def remote(src, dst, send, recv, to):
    return pltpu.make_async_remote_copy(
        src_ref=src, dst_ref=dst, send_sem=send, recv_sem=recv, device_id=to, device_id_type=MESH
    )


class Gather:
    SENDS = 64
    RECVS = 48

    def __init__(self, place, src, dst, rows, lo, hi, split, plane_first, sends, recvs):
        self.p, self.src, self.dst, self.rows = place, src, dst, rows
        self.lo, self.hi, self.split, self.plane_first = lo, hi, split, plane_first
        self.sends, self.recvs = sends, recvs
        self.pending = []

    def part(self, z, y, c, x, half=None):
        base = self.p.shard(z, y, c, x) * self.rows
        rows = self.rows
        if half is not None:
            rows = rows // 2
            base = base + half * rows
        return self.dst.at[pl.ds(pl.multiple_of(base, rows), rows), pl.ds(self.lo, self.hi - self.lo)]

    def mine(self):
        return self.src.at[:, pl.ds(self.lo, self.hi - self.lo)]

    def go(self, when, src, dst, send, recv, to):
        def start():
            remote(src, dst, self.sends.at[send], self.recvs.at[recv], to).start()

        def finish():
            remote(src, dst, self.sends.at[send], self.recvs.at[recv], to).wait_send()

        if when is None:
            start()
            self.pending.append(finish)
        else:
            pl.when(when)(start)
            self.pending.append(lambda: pl.when(when)(finish))

    def got(self, dst, recv):
        remote(dst, dst, self.sends.at[0], self.recvs.at[recv], self.p.to_x).wait_recv()

    def share(self, when, src, z, y, x):
        slot = z * 4 + y * 2 + x
        self.go(when, src, self.part(z, y, self.p.c, x), slot, slot, self.p.to_core)

    def steps(self):
        return self.plane_steps() if self.plane_first else self.line_steps()

    def line_steps(self):
        p = self.p
        top = p.depth - 1

        def hand_on(when, src, z):
            whole = self.part(z, p.y, p.c, p.x)
            self.go(when, src, whole, 24 + z, 20 + z, p.to_x)
            self.go(when, src, whole, 28 + z, 24 + z, p.to_y)
            self.share(when, src, z, p.y, p.x)

        def own():
            src = self.mine()
            whole = self.part(p.z, p.y, p.c, p.x)
            self.go(p.z < top, src, whole, 16 + p.z, 16 + p.z, p.to_up)
            self.go(p.z > 0, src, whole, 20 + p.z, 16 + p.z, p.to_down)
            hand_on(None, src, p.z)

        def line(d):
            for side in (-1, 1):
                z = p.z + side * d
                here = (z >= 0) & (z <= top)
                whole = self.part(z, p.y, p.c, p.x)
                pl.when(here)(lambda: self.got(whole, 16 + z))
                if side < 0:
                    self.go(here & (p.z < top), whole, whole, 16 + z, 16 + z, p.to_up)
                else:
                    self.go(here & (p.z > 0), whole, whole, 20 + z, 16 + z, p.to_down)
                hand_on(here, whole, z)

        def origins(d):
            return [(None, p.z)] if d == 0 else [
                ((p.z + s * d >= 0) & (p.z + s * d <= top), p.z + s * d) for s in (-1, 1)
            ]

        def cond(when, f):
            f() if when is None else pl.when(when)(f)

        def cross(d):
            for when, z in origins(d):
                from_x = self.part(z, p.y, p.c, 1 - p.x)
                cond(when, lambda: self.got(from_x, 20 + z))
                self.share(when, from_x, z, p.y, 1 - p.x)
                if self.split:
                    part = self.part(z, p.y, p.c, 1 - p.x, 0)
                else:
                    part = from_x
                self.go(when, part, part, 32 + z, 28 + z, p.to_y)
                from_y = self.part(z, 1 - p.y, p.c, p.x)
                cond(when, lambda: self.got(from_y, 24 + z))
                self.share(when, from_y, z, 1 - p.y, p.x)
                if self.split:
                    part = self.part(z, 1 - p.y, p.c, p.x, 1)
                    self.go(when, part, part, 36 + z, 32 + z, p.to_x)

        def corner(d):
            for when, z in origins(d):
                whole = self.part(z, 1 - p.y, p.c, 1 - p.x)
                if self.split:
                    for half in (0, 1):
                        part = self.part(z, 1 - p.y, p.c, 1 - p.x, half)
                        cond(when, lambda: self.got(part, 28 + 4 * half + z))
                else:
                    cond(when, lambda: self.got(whole, 28 + z))
                self.share(when, whole, z, 1 - p.y, 1 - p.x)

        out = [(0, own)]
        for d in range(p.depth):
            if d:
                out.append((d, functools.partial(line, d)))
            out.append((d + 1, functools.partial(cross, d)))
            out.append((d + 2, functools.partial(corner, d)))
        return out

    def plane_steps(self):
        p = self.p
        top = p.depth - 1

        def along(when, src, z, y, x, up, down):
            slot = 20 + z * 4 + y * 2 + x
            whole = self.part(z, y, p.c, x)
            if up:
                w = p.z < top
                self.go(w if when is None else w & when, src, whole, slot, slot, p.to_up)
            if down:
                w = p.z > 0
                self.go(w if when is None else w & when, src, whole, slot + 16, slot, p.to_down)

        def own():
            src = self.mine()
            whole = self.part(p.z, p.y, p.c, p.x)
            self.go(None, src, whole, 16, 16, p.to_x)
            self.go(None, src, whole, 17, 17, p.to_y)
            along(None, src, p.z, p.y, p.x, True, True)
            self.share(None, src, p.z, p.y, p.x)

        def cross():
            from_x = self.part(p.z, p.y, p.c, 1 - p.x)
            self.got(from_x, 16)
            part = self.part(p.z, p.y, p.c, 1 - p.x, 0) if self.split else from_x
            self.go(None, part, part, 18, 18, p.to_y)
            along(None, from_x, p.z, p.y, 1 - p.x, True, True)
            self.share(None, from_x, p.z, p.y, 1 - p.x)
            from_y = self.part(p.z, 1 - p.y, p.c, p.x)
            self.got(from_y, 17)
            if self.split:
                part = self.part(p.z, 1 - p.y, p.c, p.x, 1)
                self.go(None, part, part, 19, 19, p.to_x)
            along(None, from_y, p.z, 1 - p.y, p.x, True, True)
            self.share(None, from_y, p.z, 1 - p.y, p.x)

        def corner():
            whole = self.part(p.z, 1 - p.y, p.c, 1 - p.x)
            if self.split:
                for half in (0, 1):
                    self.got(self.part(p.z, 1 - p.y, p.c, 1 - p.x, half), 18 + half)
            else:
                self.got(whole, 18)
            along(None, whole, p.z, 1 - p.y, 1 - p.x, True, True)
            self.share(None, whole, p.z, 1 - p.y, 1 - p.x)

        def line(d, k):
            y = p.y if k in (0, 1) else 1 - p.y
            x = p.x if k in (0, 2) else 1 - p.x
            for side in (-1, 1):
                z = p.z + side * d
                here = (z >= 0) & (z <= top)
                whole = self.part(z, y, p.c, x)
                pl.when(here)(lambda: self.got(whole, 20 + z * 4 + y * 2 + x))
                along(here, whole, z, y, x, side < 0, side > 0)
                self.share(here, whole, z, y, x)

        out = [(0, own), (1, cross), (2, corner)]
        for d in range(1, p.depth):
            for k in range(4):
                out.append((d + 0.1 + min(k, 2) * 0.9, functools.partial(line, d, k)))
        return out

    def finish(self):
        p = self.p
        for z in range(p.depth):
            for y in range(2):
                for x in range(2):
                    self.got(self.part(z, y, 1 - p.c, x), z * 4 + y * 2 + x)
        for wait in self.pending:
            wait()


def gather_sems(n):
    return [pltpu.SemaphoreType.DMA((n, Gather.SENDS)), pltpu.SemaphoreType.DMA((n, Gather.RECVS))]


class Reduce:
    def __init__(self, place, xt, g, turned, rows, lo, hi, line_first, out, full, outgo, income, sends, recvs):
        self.p, self.xt, self.g, self.turned, self.rows = place, xt, g, turned, rows
        self.lo, self.width, self.line_first, self.out = lo, hi - lo, line_first, out
        self.full, self.outgo, self.income = full, outgo, income
        self.sends, self.recvs = sends, recvs
        self.chunk = math.gcd(self.width, 512)
        self.order = [0, place.depth - 1] + list(range(1, place.depth - 1))
        self.pending = []

    @staticmethod
    def scratch(rows, width, depth, line_first):
        full = (4 if line_first else 3 * depth) * rows
        outgo = (4 * depth + 3) if line_first else 4 * depth
        income = (4 * (depth + 1) + 3) if line_first else 4 * depth + 1
        return [
            pltpu.VMEM((full, width), jnp.float32),
            pltpu.VMEM((outgo * rows, width), jnp.bfloat16),
            pltpu.VMEM((income * rows, width), jnp.bfloat16),
            pltpu.SemaphoreType.DMA((32,)),
            pltpu.SemaphoreType.DMA((32,)),
        ]

    def piece(self, ref, slot, half=None, count=1):
        rows = self.rows * count
        base = slot * self.rows
        if half is not None:
            rows = rows // 2
            base = base + half * rows
        return ref.at[pl.ds(pl.multiple_of(base, 16), rows)]

    def go(self, when, src, dst, send, recv, to):
        def start():
            remote(src, dst, self.sends.at[send], self.recvs.at[recv], to).start()

        def finish():
            remote(src, dst, self.sends.at[send], self.recvs.at[recv], to).wait_send()

        if when is None:
            start()
            self.pending.append(finish)
        else:
            pl.when(when)(start)
            self.pending.append(lambda: pl.when(when)(finish))

    def got(self, when, dst, recv):
        def wait():
            remote(dst, dst, self.sends.at[0], self.recvs.at[recv], self.p.to_x).wait_recv()

        wait() if when is None else pl.when(when)(wait)

    def columns(self, body):
        @pl.loop(0, self.width // self.chunk)
        def _(j):
            start = pl.multiple_of(j * self.chunk, self.chunk)
            body(pl.ds(start, self.chunk), pl.ds(pl.multiple_of(self.lo + start, 128), self.chunk))

    def product(self, owners, cols):
        x = jnp.concatenate(
            [self.xt[pl.ds(pl.multiple_of(o * self.rows, self.rows), self.rows), :] for o in owners], 0
        )
        if self.turned:
            return lax.dot_general(
                x, self.g[cols, :], (((1,), (1,)), ((), ())), preferred_element_type=jnp.float32
            )
        return jnp.dot(x, self.g[:, cols], preferred_element_type=jnp.float32)

    def steps(self):
        return self.line_steps() if self.line_first else self.plane_steps()

    def line_slots(self, count, base):
        p, top = self.p, self.p.depth - 1

        def zero(slot):
            ref = self.piece(self.income, slot, None, count)
            ref[...] = jnp.zeros(ref.shape, ref.dtype)

        for z in range(p.depth):
            pl.when((p.z == 0) if z == top else (p.z == 0) | (p.z == top))(
                functools.partial(zero, base + count * z)
            )
        pl.when(p.z == top)(functools.partial(zero, base + count * p.depth))

    def line_wait(self, z, count, base, number):
        p, top = self.p, self.p.depth - 1
        here = ((p.z < z) & (p.z > 0)) | ((p.z > z) & (p.z < top))
        self.got(here, self.piece(self.income, base + count * z, None, count), number + z)

    def line_go(self, z, src, count, base, number):
        p = self.p
        dst = self.piece(self.income, base + count * z, None, count)
        last = self.piece(self.income, base + count * p.depth, None, count)
        if z > 0:
            self.go(p.z < z, src, dst, number + z, number + z, p.to_up)
        if z < p.depth - 1:
            self.go(p.z > z + 1, src, dst, number + z, number + z, p.to_down)
            self.go(p.z == z + 1, src, last, number + z, number + p.depth, p.to_down)

    def line_end(self, count, base, number):
        p, top = self.p, self.p.depth - 1
        for z in range(p.depth):
            if z > 0:
                self.got(p.z == z, self.piece(self.income, base + count * z, None, count), number + z)
        self.got(p.z < top, self.piece(self.income, base + count * p.depth, None, count), number + p.depth)

    def plane_steps(self):
        p, n, r = self.p, self.p.depth, self.rows
        sides = ((1 - p.x, 1 - p.y), (1 - p.x, p.y), (p.x, 1 - p.y), (p.x, p.y))

        def owners(k):
            x, y = sides[k]
            return [p.shard(z, y, p.c, x) for z in range(n)]

        def far():
            self.line_slots(1, 3 * n)

            def body(here, cols):
                self.outgo[pl.ds(0, n * r), here] = self.product(owners(0), cols).astype(jnp.bfloat16)

            self.columns(body)
            for z in self.order:
                self.go(None, self.piece(self.outgo, z, 0), self.piece(self.income, z, 0), z, z, p.to_y)
                self.go(None, self.piece(self.outgo, z, 1), self.piece(self.income, z, 1), n + z, n + z, p.to_x)

        def near():
            def body(here, cols):
                for k in range(3):
                    self.full[pl.ds(k * n * r, n * r), here] = self.product(owners(k + 1), cols)

            self.columns(body)

        def cross(z):
            self.got(None, self.piece(self.income, z, 0), z)
            self.got(None, self.piece(self.income, z, 1), n + z)
            h = r // 2

            def body(here, cols):
                for k in range(2):
                    base = (k * n + z) * r
                    to = ((k + 1) * n + z) * r
                    far_half = pl.ds(z * r + k * h, h)
                    mine = self.full[pl.ds(base + k * h, h), here]
                    self.outgo[pl.ds(to + k * h, h), here] = (
                        mine + self.income[far_half, here].astype(jnp.float32)
                    ).astype(jnp.bfloat16)
                    self.outgo[pl.ds(to + (1 - k) * h, h), here] = self.full[
                        pl.ds(base + (1 - k) * h, h), here
                    ].astype(jnp.bfloat16)

            self.columns(body)
            for k, to in ((1, p.to_x), (2, p.to_y)):
                slot = k * n + z
                self.go(None, self.piece(self.outgo, slot), self.piece(self.income, slot), (k + 1) * n + z, (k + 1) * n + z, to)

        def line(z):
            self.got(None, self.piece(self.income, n + z), 2 * n + z)
            self.got(None, self.piece(self.income, 2 * n + z), 3 * n + z)
            self.line_wait(z, 1, 3 * n, 4 * n)
            away = p.z != z

            def body(here, cols):
                rows = pl.ds((2 * n + z) * r, r)
                total = (
                    self.full[rows, here]
                    + self.income[pl.ds((n + z) * r, r), here].astype(jnp.float32)
                    + self.income[pl.ds((2 * n + z) * r, r), here].astype(jnp.float32)
                )
                self.full[rows, here] = total

            self.columns(body)

            @pl.when(away)
            def _():
                def body(here, cols):
                    self.outgo[pl.ds((3 * n + z) * r, r), here] = (
                        self.full[pl.ds((2 * n + z) * r, r), here]
                        + self.income[pl.ds((3 * n + z) * r, r), here].astype(jnp.float32)
                    ).astype(jnp.bfloat16)

                self.columns(body)

            self.line_go(z, self.piece(self.outgo, 3 * n + z), 1, 3 * n, 4 * n)

        def end():
            self.line_end(1, 3 * n, 4 * n)
            own = pl.ds(pl.multiple_of((2 * n + p.z) * r, r), r)
            below = pl.ds(pl.multiple_of((3 * n + p.z) * r, r), r)
            above = pl.ds(4 * n * r, r)

            def body(here, cols):
                self.out[:, cols] = (
                    self.full[own, here]
                    + self.income[below, here].astype(jnp.float32)
                    + self.income[above, here].astype(jnp.float32)
                )

            self.columns(body)

        steps = [(0.0, far), (0.5, near)]
        for k, z in enumerate(self.order):
            steps.append((1 + k, functools.partial(cross, z)))
            steps.append((2.5 + k, functools.partial(line, z)))
        steps.append((9.0, end))
        return steps

    def line_steps(self):
        p, n, r = self.p, self.p.depth, self.rows

        def first():
            self.line_slots(4, 0)

        def line(z):
            places = [p.shard(z, y, p.c, x) for y in range(2) for x in range(2)]
            self.line_wait(z, 4, 0, 0)

            @pl.when(p.z != z)
            def _():
                def body(here, cols):
                    self.outgo[pl.ds(4 * z * r, 4 * r), here] = (
                        self.product(places, cols) + self.income[pl.ds(4 * z * r, 4 * r), here].astype(jnp.float32)
                    ).astype(jnp.bfloat16)

                self.columns(body)

            @pl.when(p.z == z)
            def _():
                def body(here, cols):
                    self.full[:, here] = self.product(places, cols)

                self.columns(body)

            self.line_go(z, self.piece(self.outgo, 4 * z, None, 4), 4, 0, 0)

        def spot(y, x):
            return pl.multiple_of((y * 2 + x) * r, r)

        sent, come = 4 * n, 4 * (n + 1)

        def meet():
            self.line_end(4, 0, 0)
            below = pl.ds(pl.multiple_of(4 * p.z * r, r), 4 * r)
            above = pl.ds(4 * n * r, 4 * r)
            far = pl.ds(spot(1 - p.y, 1 - p.x), r)

            def body(here, cols):
                self.full[:, here] = (
                    self.full[:, here]
                    + self.income[below, here].astype(jnp.float32)
                    + self.income[above, here].astype(jnp.float32)
                )
                self.outgo[pl.ds(sent * r, r), here] = self.full[far, here].astype(jnp.bfloat16)

            self.columns(body)
            self.go(None, self.piece(self.outgo, sent, 0), self.piece(self.income, come, 0), 8, 8, p.to_y)
            self.go(None, self.piece(self.outgo, sent, 1), self.piece(self.income, come, 1), 9, 9, p.to_x)

        def cross():
            self.got(None, self.piece(self.income, come, 0), 8)
            self.got(None, self.piece(self.income, come, 1), 9)
            h = r // 2
            spots = (spot(p.y, 1 - p.x), spot(1 - p.y, p.x))

            def body(here, cols):
                for k in range(2):
                    to = (sent + 1 + k) * r
                    with_half = pl.ds(pl.multiple_of(spots[k] + k * h, h), h)
                    plain = pl.ds(pl.multiple_of(spots[k] + (1 - k) * h, h), h)
                    self.outgo[pl.ds(to + k * h, h), here] = (
                        self.full[with_half, here] + self.income[pl.ds(come * r + k * h, h), here].astype(jnp.float32)
                    ).astype(jnp.bfloat16)
                    self.outgo[pl.ds(to + (1 - k) * h, h), here] = self.full[plain, here].astype(jnp.bfloat16)

            self.columns(body)
            for k, to in ((1, p.to_x), (2, p.to_y)):
                self.go(None, self.piece(self.outgo, sent + k), self.piece(self.income, come + k), 9 + k, 9 + k, to)

        def end():
            self.got(None, self.piece(self.income, come + 1), 10)
            self.got(None, self.piece(self.income, come + 2), 11)
            own = pl.ds(spot(p.y, p.x), r)

            def body(here, cols):
                self.out[:, cols] = (
                    self.full[own, here]
                    + self.income[pl.ds((come + 1) * r, r), here].astype(jnp.float32)
                    + self.income[pl.ds((come + 2) * r, r), here].astype(jnp.float32)
                )

            self.columns(body)

        steps = [(-1.0, first)]
        for k, z in enumerate(self.order):
            steps.append((0.2 + k, functools.partial(line, z)))
        steps += [(5.2, meet), (6.2, cross), (8.2, end)]
        return steps

    def finish(self):
        for wait in self.pending:
            wait()


VMEM_BYTES = 58 * 2**20


def kernel_params(number):
    return pltpu.CompilerParams(collective_id=number, has_side_effects=True, vmem_limit_bytes=VMEM_BYTES)


def in_vmem(count):
    return [pl.BlockSpec(memory_space=pltpu.VMEM)] * count


def in_any(count):
    return [pl.BlockSpec(memory_space=pl.ANY)] * count


def ranges(cols, cut):
    return [(0, cut, True), (cut, cols, False)] if cut else [(0, cols, False)]


def keep_own(p, pairs, sems):
    copies = []
    for k, (src, dst, rows) in enumerate(pairs):
        at = pl.multiple_of(p.shard(p.z, p.y, p.c, p.x) * rows, rows)
        copies.append(pltpu.make_async_copy(src, dst.at[pl.ds(at, rows)], sems.at[k]))
    for copy in copies:
        copy.start()
    return copies


class Exchange:
    def __init__(self, place, count, src, dst, sends, recvs, own):
        self.p, self.count, self.src, self.dst = place, count, src, dst
        self.sends, self.recvs, self.own = sends, recvs, own

    def copy(self, k):
        to = (self.p.b + k) % self.count
        return remote(
            self.src.at[to], self.dst.at[self.p.b], self.sends.at[k], self.recvs.at[k], (to, self.p.x)
        )

    def mine(self):
        return pltpu.make_async_copy(self.src.at[self.p.b], self.dst.at[self.p.b], self.own)

    def start(self):
        self.mine().start()
        for k in range(1, self.count):
            self.copy(k).start()

    def arrived(self):
        self.mine().wait()
        for k in range(1, self.count):
            came = (self.p.b + self.count - k) % self.count
            remote(
                self.dst.at[came], self.dst.at[came], self.sends.at[k], self.recvs.at[k], self.p.to_x
            ).wait_recv()

    def finish(self):
        for k in range(1, self.count):
            self.copy(k).wait_send()


def exchange_sems(count):
    return [
        pltpu.SemaphoreType.DMA((count,)),
        pltpu.SemaphoreType.DMA((count,)),
        pltpu.SemaphoreType.DMA,
    ]


def greet_plane(p, count):
    barrier = pltpu.get_barrier_semaphore()
    for k in range(1, count):
        pl.semaphore_signal(barrier, inc=1, device_id=((p.b + k) % count, p.x), device_id_type=MESH)
    pl.semaphore_signal(barrier, inc=1, device_id=p.to_x, device_id_type=MESH)
    pl.semaphore_wait(barrier, count)


def play(events):
    for event in events:
        event()


def open_kernel(depth, cuts, own_time, other_time, biases, w_mod, w_skip, w_qkv, skip_full, qkv_full, pack_full,
                times, got_time, pack, time_sems, sends, recvs, own_sems):
    p = Place(depth)
    p.greet()
    ask = remote(other_time, got_time, time_sems.at[0], time_sems.at[1], p.to_x)
    ask.start()
    gathers = []
    for src, dst, rows, cols, cut in (
        (w_skip, skip_full, w_skip.shape[0], w_skip.shape[1], cuts[0]),
        (w_qkv, qkv_full, w_qkv.shape[0], w_qkv.shape[1], cuts[1]),
    ):
        for lo, hi, first in ranges(cols, cut):
            k = len(gathers)
            gathers.append(Gather(p, src, dst, rows, lo, hi, True, first, sends.at[k], recvs.at[k]))
    k = len(gathers)
    width = pack.shape[1]
    packs = Gather(p, pack, pack_full, 8, 0, width, False, False, sends.at[k], recvs.at[k])

    def products():
        ask.wait_recv()
        both = own_time[...] + got_time[...]
        times[...] = both
        left = both[:, : w_mod.shape[0]].astype(jnp.bfloat16)
        model = w_skip.shape[1]
        row = lax.broadcasted_iota(jnp.int32, (8, model), 0) % 4
        total = jnp.zeros((8, model), jnp.float32)
        for part in range(4):
            made = jnp.dot(
                left, w_mod[:, part * model : (part + 1) * model], preferred_element_type=jnp.float32
            )
            total = jnp.where(row == part, made, total)
        pack[:, :model] = total
        pack[:, model:] = biases[...]

    events = [(t, k, f) for k, g in enumerate(gathers) for t, f in g.steps()]
    events.append((0.3, 0, products))
    events += [(t + 0.5, 9, f) for t, f in packs.steps()]
    events.sort(key=lambda e: (e[0], e[1]))
    owns = keep_own(p, ((w_skip, skip_full, w_skip.shape[0]), (w_qkv, qkv_full, w_qkv.shape[0])), own_sems)
    play([f for _, _, f in events])
    at = pl.multiple_of(p.shard(p.z, p.y, p.c, p.x) * 8, 8)
    last = pltpu.make_async_copy(pack, pack_full.at[pl.ds(at, 8)], own_sems.at[2])
    last.start()
    for g in gathers + [packs]:
        g.finish()
    for copy in owns:
        copy.wait()
    last.wait()
    ask.wait_send()


def open_call(depth, devices, own_time, other_time, biases, w_mod, w_skip, w_qkv):
    model = w_skip.shape[1]
    cuts = (model // 4, w_qkv.shape[1] // 4)
    width = model + 128
    return pl.pallas_call(
        functools.partial(open_kernel, depth, cuts),
        name="open",
        out_shape=[
            jax.ShapeDtypeStruct((devices * w_skip.shape[0], model), jnp.bfloat16),
            jax.ShapeDtypeStruct((devices * w_qkv.shape[0], w_qkv.shape[1]), jnp.bfloat16),
            jax.ShapeDtypeStruct((devices * 8, width), jnp.float32),
            jax.ShapeDtypeStruct((8, 128), jnp.float32),
        ],
        in_specs=in_vmem(4) + in_any(2),
        out_specs=in_any(3) + in_vmem(1),
        scratch_shapes=[
            pltpu.VMEM((8, 128), jnp.float32),
            pltpu.VMEM((8, width), jnp.float32),
            pltpu.SemaphoreType.DMA((2,)),
            *gather_sems(5),
            pltpu.SemaphoreType.DMA((3,)),
        ],
        compiler_params=kernel_params(1),
    )(own_time, other_time, biases, w_mod, w_skip, w_qkv)


def three_terms(v):
    a = v.astype(jnp.bfloat16).astype(jnp.float32)
    b = (v - a).astype(jnp.bfloat16).astype(jnp.float32)
    return a, b, v - a - b


def extra_rows(rows, length, width):
    shape = (length, width)
    row = lax.broadcasted_iota(jnp.int32, shape, 0)
    total = jnp.zeros(shape, jnp.float32)
    for k, values in enumerate(rows):
        total = jnp.where(row == k, values, total)
    return total.astype(jnp.bfloat16)


def attend(p, lengths, got, qkv, keys, mixed_out, lse, plain, block):
    count, _, span = got.shape
    frames = count * span
    for k in range(count):
        qkv[:, k * span : (k + 1) * span] = got[k]
    length = lengths[p.x]
    position = lax.broadcasted_iota(jnp.int32, (1, frames), 1)
    hidden_key = jnp.where(position < length, 0.0, -1e30)
    keys[...] = jnp.concatenate([qkv[HEAD_DIM : 2 * HEAD_DIM, :], extra_rows([hidden_key], HEAD_DIM, frames)], 0).T
    values = jnp.concatenate([qkv[2 * HEAD_DIM :, :], extra_rows([1.0], 16, frames)], 0)
    ones = extra_rows([1.0], HEAD_DIM, block)
    scaling = HEAD_DIM ** (-0.5)
    parts = block // span

    @pl.loop(0, frames // block)
    def _(j):
        here = pl.ds(pl.multiple_of(j * block, block), block)
        query = jnp.concatenate([qkv[:HEAD_DIM, here] * jnp.bfloat16(scaling), ones], 0)
        score = jnp.dot(keys[...], query, preferred_element_type=jnp.float32)
        peak = jnp.max(score, 0, keepdims=True)
        weights = jnp.exp(score - peak).astype(jnp.bfloat16)
        out = jnp.dot(values, weights, preferred_element_type=jnp.float32)
        total = out[HEAD_DIM : HEAD_DIM + 1]
        out = out[:HEAD_DIM] / total
        plain[:, here] = out
        lse[:, here] = peak + jnp.log(total)
        column = lax.broadcasted_iota(jnp.int32, (HEAD_DIM, block), 1) + j * block
        kept = jnp.where(column < length, out, 0.0).astype(jnp.bfloat16)
        for k in range(parts):
            mixed_out[j * parts + k] = kept[:, k * span : (k + 1) * span]


def forward_kernel(depth, cuts, lengths, heads_in, w_out, w_up, w_down, out_full, up_full, down_full, mixed, qkv, lse,
                   plain, got, keys, mixed_out, s1, r1, o1, s2, r2, o2, sends, recvs, own_sems):
    p = Place(depth)
    count = heads_in.shape[0]
    greet_plane(p, count)
    there = Exchange(p, count, heads_in, got, s1, r1, o1)
    back = Exchange(p, count, mixed_out, mixed, s2, r2, o2)
    gathers, owns = [], []
    for src, dst, cut in ((w_out, out_full, cuts[0]), (w_up, up_full, cuts[1]), (w_down, down_full, cuts[2])):
        for lo, hi, first in ranges(src.shape[1], cut):
            k = len(gathers)
            gathers.append(Gather(p, src, dst, src.shape[0], lo, hi, True, first, sends.at[k], recvs.at[k]))
        owns.append((src, dst, src.shape[0]))
    events = [(t, k, f) for k, g in enumerate(gathers) for t, f in g.steps()]

    def attention():
        there.arrived()
        attend(p, lengths, got, qkv, keys, mixed_out, lse, plain, 256)
        back.start()

    there.start()
    events.append((1.5, 0, attention))
    events.sort(key=lambda e: (e[0], e[1]))
    owns = keep_own(p, owns, own_sems)
    play([f for _, _, f in events])
    for g in gathers:
        g.finish()
    there.finish()
    back.arrived()
    back.finish()
    for copy in owns:
        copy.wait()


def forward_call(depth, devices, lengths, heads_in, w_out, w_up, w_down):
    count, depth3, span = heads_in.shape
    frames = count * span
    weights = (w_out, w_up, w_down)
    cuts = tuple(w.shape[1] // 4 for w in weights)
    return pl.pallas_call(
        functools.partial(forward_kernel, depth, cuts),
        name="forward",
        out_shape=[
            *[jax.ShapeDtypeStruct((devices * w.shape[0], w.shape[1]), jnp.bfloat16) for w in weights],
            jax.ShapeDtypeStruct((count, HEAD_DIM, span), jnp.bfloat16),
            jax.ShapeDtypeStruct((depth3, frames), jnp.bfloat16),
            jax.ShapeDtypeStruct((1, frames), jnp.float32),
            jax.ShapeDtypeStruct((HEAD_DIM, frames), jnp.float32),
        ],
        in_specs=[pl.BlockSpec(memory_space=pltpu.SMEM)] + in_any(4),
        out_specs=in_any(4) + in_vmem(3),
        scratch_shapes=[
            pltpu.VMEM((count, depth3, span), jnp.bfloat16),
            pltpu.VMEM((frames, 2 * HEAD_DIM), jnp.bfloat16),
            pltpu.VMEM((count, HEAD_DIM, span), jnp.bfloat16),
            *exchange_sems(count),
            *exchange_sems(count),
            *gather_sems(6),
            pltpu.SemaphoreType.DMA((3,)),
        ],
        compiler_params=kernel_params(2),
    )(lengths, heads_in, w_out, w_up, w_down)


def attend_back(p, lengths, got, qkv, lse, plain, keys, values, key_grad, value_grad, grads_out, block):
    count, _, span = got.shape
    frames = count * span
    length = lengths[p.x]
    position = lax.broadcasted_iota(jnp.int32, (1, frames), 1)
    hidden_key = jnp.where(position < length, 0.0, -1e30)
    keys[...] = jnp.concatenate(
        [qkv[HEAD_DIM : 2 * HEAD_DIM, :], extra_rows([hidden_key, 1.0, 1.0, 1.0], HEAD_DIM, frames)], 0
    ).T
    values[...] = jnp.concatenate(
        [qkv[2 * HEAD_DIM :, :], extra_rows([1.0, 1.0, 1.0], HEAD_DIM, frames)], 0
    ).T
    key_grad[...] = jnp.zeros_like(key_grad)
    value_grad[...] = jnp.zeros_like(value_grad)
    scaling = HEAD_DIM ** (-0.5)
    parts = block // span

    @pl.loop(0, frames // block)
    def _(j):
        here = pl.ds(pl.multiple_of(j * block, block), block)
        query = qkv[:HEAD_DIM, here] * jnp.bfloat16(scaling)
        upstream = jnp.concatenate([got[j * parts + k] for k in range(parts)], 1)
        delta = jnp.sum(upstream.astype(jnp.float32) * plain[:, here], 0, keepdims=True)
        left = jnp.concatenate(
            [query, extra_rows([1.0, *[-t for t in three_terms(lse[:, here])]], HEAD_DIM, block)], 0
        )
        right = jnp.concatenate([upstream, extra_rows([-t for t in three_terms(delta)], HEAD_DIM, block)], 0)
        weights = jnp.exp(jnp.dot(keys[...], left, preferred_element_type=jnp.float32))
        slope = jnp.dot(values[...], right, preferred_element_type=jnp.float32)
        slope = (weights * slope).astype(jnp.bfloat16)
        value_grad[...] += lax.dot_general(
            weights.astype(jnp.bfloat16), upstream, (((1,), (1,)), ((), ())), preferred_element_type=jnp.float32
        )
        key_grad[...] += lax.dot_general(
            slope, query, (((1,), (1,)), ((), ())), preferred_element_type=jnp.float32
        )
        query_grad = (
            jnp.dot(qkv[HEAD_DIM : 2 * HEAD_DIM, :], slope, preferred_element_type=jnp.float32) * scaling
        ).astype(jnp.bfloat16)
        for k in range(parts):
            grads_out[j * parts + k, :HEAD_DIM, :] = query_grad[:, k * span : (k + 1) * span]

    @pl.loop(0, count)
    def _(k):
        rows = pl.ds(pl.multiple_of(k * span, span), span)
        both = jnp.concatenate([key_grad[rows, :], value_grad[rows, :]], 1)
        grads_out[k, HEAD_DIM:, :] = both.T.astype(jnp.bfloat16)


class Shared:
    def __init__(self, p, src, dst, axis, sems):
        self.p, self.src, self.dst, self.axis, self.sems = p, src, dst, axis, sems

    def half(self, k):
        span = self.src.shape[self.axis]
        if self.axis:
            return self.dst.at[:, pl.ds(k * span, span)]
        return self.dst.at[pl.ds(k * span, span)]

    def here(self):
        return pltpu.make_async_copy(self.src, self.half(0), self.sems.at[0])

    def there(self):
        return remote(self.src, self.half(1), self.sems.at[1], self.sems.at[2], self.p.to_core)

    def start(self):
        self.here().start()
        self.there().start()

    def arrived(self):
        self.here().wait()
        self.there().wait_recv()

    def finish(self):
        self.there().wait_send()


def sum_specs(p_depth, shards):
    scratch = []
    for rows, cols, cut in shards:
        for lo, hi, first in ranges(cols, cut):
            scratch += Reduce.scratch(rows, hi - lo, p_depth, first)
    return scratch


def backward_kernel(depth, cuts, lengths, mixed_grad, qkv, lse, plain, pack, act, cot, normed2, inner_grad, mixed,
                    branch_grad, got_grads, down_grad, up_grad, out_grad, pack_full, got, keys, values, key_grad,
                    value_grad, grads_out, x0, g0, x1, g1, x2, g2, share_sems, s1, r1, o1, s2, r2, o2, sends, recvs,
                    own_sems, *rest):
    p = Place(depth)
    count = mixed_grad.shape[0]
    greet_plane(p, count)
    there = Exchange(p, count, mixed_grad, got, s1, r1, o1)
    back = Exchange(p, count, grads_out, got_grads, s2, r2, o2)
    there.start()
    shared = []
    for k, (src, dst, axis) in enumerate(
        ((act, x0, 1), (cot, g0, 0), (normed2, x1, 1), (inner_grad, g1, 1), (mixed, x2, 1), (branch_grad, g2, 0))
    ):
        shared.append(Shared(p, src, dst, axis, share_sems.at[k]))
        shared[-1].start()
    packs = Gather(p, pack, pack_full, 8, 0, pack.shape[1], False, False, sends.at[0], recvs.at[0])
    sums = []
    rest = list(rest)
    for x, g, turned, out, cut in (
        (x0, g0, False, down_grad, cuts[0]),
        (x1, g1, True, up_grad, cuts[1]),
        (x2, g2, False, out_grad, cuts[2]),
    ):
        for lo, hi, first in ranges(out.shape[1], cut):
            sums.append(Reduce(p, x, g, turned, out.shape[0], lo, hi, first, out, *rest[:5]))
            rest = rest[5:]

    def attention():
        there.arrived()
        attend_back(p, lengths, got, qkv, lse, plain, keys, values, key_grad, value_grad, grads_out, 256)
        back.start()

    at = pl.multiple_of(p.shard(p.z, p.y, p.c, p.x) * 8, 8)
    own = pltpu.make_async_copy(pack, pack_full.at[pl.ds(at, 8)], own_sems.at[0])
    own.start()
    for s in shared:
        s.arrived()
    events = [(t, k, f) for k, g in enumerate(sums) for t, f in g.steps()]
    events += [(t + 0.6, 9, f) for t, f in packs.steps()]
    events.append((0.7, 0, attention))
    events.sort(key=lambda e: (e[0], e[1]))
    play([f for _, _, f in events])
    for g in sums + [packs] + shared:
        g.finish()
    there.finish()
    back.arrived()
    back.finish()
    own.wait()


def backward_call(depth, devices, lengths, mixed_grad, qkv, lse, plain, pack, act, cot, normed2, inner_grad, mixed,
                  branch_grad):
    count, _, span = mixed_grad.shape
    frames = count * span
    model, ff = cot.shape[1], act.shape[0]
    shards = [
        (ff // devices, model, model // 4),
        (model // devices, ff, ff // 4),
        (model // devices, model, model // 4),
    ]
    pair = 2 * span
    return pl.pallas_call(
        functools.partial(backward_kernel, depth, tuple(s[2] for s in shards)),
        name="backward",
        out_shape=[
            jax.ShapeDtypeStruct((count, 3 * HEAD_DIM, span), jnp.bfloat16),
            *[jax.ShapeDtypeStruct(s[:2], jnp.float32) for s in shards],
            jax.ShapeDtypeStruct((devices * 8, pack.shape[1]), jnp.float32),
        ],
        in_specs=[pl.BlockSpec(memory_space=pltpu.SMEM)] + in_any(1) + in_vmem(4) + in_any(6),
        out_specs=in_any(1) + in_vmem(3) + in_any(1),
        scratch_shapes=[
            pltpu.VMEM((count, HEAD_DIM, span), jnp.bfloat16),
            pltpu.VMEM((frames, 2 * HEAD_DIM), jnp.bfloat16),
            pltpu.VMEM((frames, 2 * HEAD_DIM), jnp.bfloat16),
            pltpu.VMEM((frames, HEAD_DIM), jnp.float32),
            pltpu.VMEM((frames, HEAD_DIM), jnp.float32),
            pltpu.VMEM((count, 3 * HEAD_DIM, span), jnp.bfloat16),
            pltpu.VMEM((ff, pair), jnp.bfloat16),
            pltpu.VMEM((pair, model), jnp.bfloat16),
            pltpu.VMEM((model, pair), jnp.bfloat16),
            pltpu.VMEM((ff, pair), jnp.bfloat16),
            pltpu.VMEM((model, pair), jnp.bfloat16),
            pltpu.VMEM((pair, model), jnp.bfloat16),
            pltpu.SemaphoreType.DMA((6, 3)),
            *exchange_sems(count),
            *exchange_sems(count),
            *gather_sems(1),
            pltpu.SemaphoreType.DMA((1,)),
            *sum_specs(depth, shards),
        ],
        compiler_params=kernel_params(3),
    )(lengths, mixed_grad, qkv, lse, plain, pack, act, cot, normed2, inner_grad, mixed, branch_grad)


def close_kernel(depth, cuts, pack, late, w_mod, normed, grad, joined, base_grad, qkv_grad, skip_grad, sums_out,
                 times_full, pack_full, times, x0, g0, x1, g1, share_sems, sends, recvs, own_sems, *rest):
    p = Place(depth)
    p.greet()
    shared = []
    for k, (src, dst, axis) in enumerate(((normed, x0, 1), (grad, g0, 1), (joined, x1, 1), (base_grad, g1, 0))):
        shared.append(Shared(p, src, dst, axis, share_sems.at[k]))
        shared[-1].start()
    packs = Gather(p, pack, pack_full, 8, 0, pack.shape[1], False, False, sends.at[0], recvs.at[0])
    spread = Gather(p, times, times_full, 8, 0, 128, False, False, sends.at[1], recvs.at[1])
    sums = []
    rest = list(rest)
    for x, g, turned, out, cut in ((x0, g0, True, qkv_grad, cuts[0]), (x1, g1, False, skip_grad, cuts[1])):
        for lo, hi, first in ranges(out.shape[1], cut):
            sums.append(Reduce(p, x, g, turned, out.shape[0], lo, hi, first, out, *rest[:5]))
            rest = rest[5:]
    at = pl.multiple_of(p.shard(p.z, p.y, p.c, p.x) * 8, 8)
    own = pltpu.make_async_copy(pack, pack_full.at[pl.ds(at, 8)], own_sems.at[0])
    own.start()
    model = pack.shape[1]

    def modulations():
        own.wait()
        packs.finish()
        rows = [jnp.zeros((8, model), jnp.float32) for _ in range(2)]
        for k in range(pack_full.shape[0] // 8):
            rows[k % 2] = rows[k % 2] + pack_full[pl.ds(k * 8, 8), :]
        sums_out[0:8, :] = rows[0]
        sums_out[8:16, :] = rows[1]
        total = jnp.zeros((8, w_mod.shape[0]), jnp.float32)
        for part in range(4):
            values = []
            for r in range(2):
                if part < 2:
                    values.append(rows[r][part : part + 1])
                else:
                    values.append(late[2 * r + part - 2 : 2 * r + part - 1, :])
            terms = [*three_terms(values[0]), *three_terms(values[1])]
            left = extra_rows(terms, 8, model)
            total = total + lax.dot_general(
                left,
                w_mod[:, part * model : (part + 1) * model],
                (((1,), (1,)), ((), ())),
                preferred_element_type=jnp.float32,
            )
        first = total[0:1] + total[1:2] + total[2:3]
        second = total[3:4] + total[4:5] + total[5:6]
        made = jnp.concatenate([first, second, jnp.zeros((6, w_mod.shape[0]), jnp.float32)], 0)
        times[...] = jnp.concatenate([made, jnp.zeros((8, 128 - w_mod.shape[0]), jnp.float32)], 1)

    play([f for t, f in sorted(packs.steps(), key=lambda e: e[0])[:1]])
    for s in shared:
        s.arrived()
    events = [(t, k, f) for k, g in enumerate(sums) for t, f in g.steps()]
    events += [(t + 0.6, 9, f) for t, f in sorted(packs.steps(), key=lambda e: e[0])[1:]]
    events.append((6.8, 9, modulations))
    events += [(t + 6.9, 9, f) for t, f in spread.steps()]
    events.sort(key=lambda e: (e[0], e[1]))
    play([f for _, _, f in events])
    last = pltpu.make_async_copy(times, times_full.at[pl.ds(at, 8)], own_sems.at[1])
    last.start()
    for g in sums + [spread] + shared:
        g.finish()
    last.wait()


def close_call(depth, devices, pack, late, w_mod, normed, grad, joined, base_grad):
    model, span = normed.shape
    pair = 2 * span
    shards = [
        (model // devices, grad.shape[0], grad.shape[0] // 4),
        (joined.shape[0] // devices, model, model // 4),
    ]
    return pl.pallas_call(
        functools.partial(close_kernel, depth, tuple(s[2] for s in shards)),
        name="close",
        out_shape=[
            *[jax.ShapeDtypeStruct(s[:2], jnp.float32) for s in shards],
            jax.ShapeDtypeStruct((16, model), jnp.float32),
            jax.ShapeDtypeStruct((devices * 8, 128), jnp.float32),
        ],
        in_specs=in_vmem(3) + in_any(4),
        out_specs=in_vmem(3) + in_any(1),
        scratch_shapes=[
            pltpu.VMEM((devices * 8, model), jnp.float32),
            pltpu.VMEM((8, 128), jnp.float32),
            pltpu.VMEM((model, pair), jnp.bfloat16),
            pltpu.VMEM((grad.shape[0], pair), jnp.bfloat16),
            pltpu.VMEM((joined.shape[0], pair), jnp.bfloat16),
            pltpu.VMEM((pair, model), jnp.bfloat16),
            pltpu.SemaphoreType.DMA((4, 3)),
            *gather_sems(2),
            pltpu.SemaphoreType.DMA((2,)),
            *sum_specs(depth, shards),
        ],
        compiler_params=kernel_params(4),
    )(pack, late, w_mod, normed, grad, joined, base_grad)


def first_with_second(left, right, dims):
    return lax.dot_general(left, right, ((dims[:1], dims[1:]), ((), ())), preferred_element_type=jnp.float32)


def turn(values, cosine, sine):
    half = HEAD_DIM // 2
    first, second = values[..., :half, :], values[..., half:, :]
    return jnp.concatenate([first * cosine - second * sine, second * cosine + first * sine], -2)


def on_device(hidden, skip_in, time_embed, lengths, cotangent, w_skip, b_skip, w_mod, w_qkv, w_out, w_up, b_up,
              w_down, b_down):
    block, row = lax.axis_index("blk"), lax.axis_index("uly")
    blocks, rows = lax.axis_size("blk"), lax.axis_size("uly")
    devices, depth = blocks * rows, blocks // 4
    _, frames, model = hidden.shape
    position = block * frames + jnp.arange(frames, dtype=jnp.int32)
    length = lax.dynamic_index_in_dim(lengths, row, 0, keepdims=False)[0]
    valid = position < length
    kept = valid.astype(jnp.float32)

    number = block * rows + row
    share = w_mod.shape[0]
    time_row = time_embed[0, 0].astype(jnp.float32)
    mark = (jnp.arange(8) // 4 == row)[:, None]

    def time_part(index):
        part = lax.dynamic_slice_in_dim(time_row, index * share, share)
        return jnp.where(mark, jnp.pad(part, (0, 128 - share))[None], 0.0)

    tile = jnp.concatenate(
        [
            b_up.astype(jnp.float32)[None],
            jnp.pad(
                jnp.concatenate([b_skip, b_down]).astype(jnp.float32), (0, 128 - 2 * b_skip.shape[0])
            )[None],
            jnp.zeros((6, 128), jnp.float32),
        ]
    )
    skip_full, qkv_full, pack, times = open_call(
        depth, devices, time_part(number), time_part(block * rows + 1 - row), tile, w_mod, w_skip, w_qkv
    )
    pack = pack.reshape(devices, 8, model + 128)
    mods = lax.dynamic_slice_in_dim(jnp.sum(pack[:, :, :model], 0), row * 4, 4, 0)
    bup_full = pack[:, 0, model:].reshape(-1)
    each = b_skip.shape[0]
    bskip_full = pack[:, 1, model : model + each].reshape(-1)
    bdown_full = pack[:, 1, model + each : model + 2 * each].reshape(-1)

    joined = jnp.concatenate([hidden[0], skip_in[0]], 1)
    base = jnp.dot(joined, skip_full, preferred_element_type=jnp.float32) + bskip_full
    a_scale, a_shift, f_scale, f_shift = [kept[:, None] * mods[k][None] for k in range(4)]
    normed_full, norm_back = jax.vjp(modulate, base, a_scale, a_shift)
    normed = normed_full.astype(jnp.bfloat16)
    projected = first_with_second(qkv_full, normed, (0, 1)).reshape(3, HEADS, HEAD_DIM, frames)
    half = HEAD_DIM // 2
    freq = 10000.0 ** (-jnp.arange(half, dtype=jnp.float32) / half)
    offsets = jnp.where(valid, position, position - length).astype(jnp.float32)
    angle = freq[:, None] * offsets[None, :]
    cosine, sine = jnp.cos(angle), jnp.sin(angle)
    heads = jnp.concatenate(
        [turn(projected[0], cosine, sine), turn(projected[1], cosine, sine), projected[2]], 1
    ).astype(jnp.bfloat16)
    out_full, up_full, down_full, mixed, qkv, lse, plain = forward_call(
        depth, devices, lengths[:, 0], heads, w_out, w_up, w_down
    )
    mixed = mixed.reshape(model, frames)
    branch = first_with_second(mixed, out_full, (0, 0))
    middle = base + branch
    normed2_full, norm2_back = jax.vjp(modulate, middle, f_scale, f_shift)
    normed2 = normed2_full.astype(jnp.bfloat16)
    inner = first_with_second(up_full, normed2, (0, 1)) + bup_full[:, None]
    act_full, act_back = jax.vjp(gelu_exact, inner)
    act = act_full.astype(jnp.bfloat16)
    output = (middle + first_with_second(act, down_full, (0, 0)) + bdown_full).astype(jnp.bfloat16)[None]

    upstream = cotangent[0]
    upstream_full = upstream.astype(jnp.float32)
    grad_inner = act_back(first_with_second(down_full, upstream, (1, 1)))[0].astype(jnp.bfloat16)
    grad_normed2 = first_with_second(grad_inner, up_full, (0, 1))
    grad_mid_norm, grad_fscale, grad_fshift = norm2_back(grad_normed2)
    grad_middle = upstream_full + grad_mid_norm
    grad_branch = grad_middle.astype(jnp.bfloat16)
    grad_mixed = first_with_second(out_full, grad_branch, (1, 1)).astype(jnp.bfloat16)
    grad_mixed = grad_mixed * valid.astype(jnp.bfloat16)[None]
    early = jnp.concatenate(
        [
            jnp.sum(grad_fscale * kept[:, None], 0),
            jnp.sum(grad_fshift * kept[:, None], 0),
            jnp.sum(grad_inner.astype(jnp.float32), 1),
            jnp.sum(upstream_full, 0),
            jnp.zeros((model,), jnp.float32),
        ]
    ).reshape(8, model)
    head_grads, grad_down, grad_up, grad_out, early_full = backward_call(
        depth, devices, lengths[:, 0], grad_mixed.reshape(HEADS, HEAD_DIM, frames), qkv, lse, plain, early, act,
        upstream, normed2.T, grad_inner, mixed, grad_branch,
    )
    early_full = early_full.reshape(blocks, rows, 8, model)
    early_row = jnp.sum(early_full[:, :, :2], 0)
    early_bias = jnp.sum(early_full[:, :, 2:], (0, 1))
    head_grads = head_grads.astype(jnp.float32)
    grad_projected = jnp.stack(
        [
            turn(head_grads[:, :HEAD_DIM], cosine, -sine),
            turn(head_grads[:, HEAD_DIM : 2 * HEAD_DIM], cosine, -sine),
            head_grads[:, 2 * HEAD_DIM :],
        ]
    ).astype(jnp.bfloat16).reshape(3 * model, frames)
    grad_normed = first_with_second(grad_projected, qkv_full, (0, 1))
    grad_base_norm, grad_ascale, grad_ashift = norm_back(grad_normed)
    grad_base = (grad_middle + grad_base_norm).astype(jnp.bfloat16)
    grad_joined = first_with_second(grad_base, skip_full, (1, 1)).astype(jnp.bfloat16)
    late = jnp.concatenate(
        [
            jnp.sum(grad_ascale * kept[:, None], 0),
            jnp.sum(grad_ashift * kept[:, None], 0),
            jnp.sum(grad_base.astype(jnp.float32), 0),
            jnp.zeros((5 * model,), jnp.float32),
        ]
    ).reshape(8, model)
    early_mods = jnp.pad(early_row.reshape(2 * rows, model), ((0, 8 - 2 * rows), (0, 0)))
    grad_qkv, grad_skip, late_sums, time_parts = close_call(
        depth, devices, late, early_mods, w_mod, normed.T, grad_projected, joined.T, grad_base
    )
    late_sums = late_sums.reshape(2, 8, model)
    mod_grads = jnp.concatenate([late_sums[:, :2], early_row], 1).reshape(rows, 4 * model)
    own_times = times[::4, :share]
    grad_mod = jnp.sum(own_times[:, :, None] * mod_grads[:, None, :], 0)
    time_parts = time_parts.reshape(devices, 8, 128)[:, :, :share]
    time_grad = lax.dynamic_index_in_dim(time_parts, row, 1, keepdims=False).reshape(1, 1, model)
    grad_bskip = lax.dynamic_slice_in_dim(late_sums[0, 2] + late_sums[1, 2], number * each, each)
    ups = b_up.shape[0]
    grad_bup = lax.dynamic_slice_in_dim(early_bias[:4].reshape(-1), number * ups, ups)
    grad_bdown = lax.dynamic_slice_in_dim(early_bias[4], number * each, each)
    return (
        output,
        grad_joined[:, :model][None],
        grad_joined[:, model:][None],
        time_grad,
        grad_skip,
        grad_bskip,
        grad_mod,
        grad_qkv,
        grad_out,
        grad_up,
        grad_bup,
        grad_down,
        grad_bdown,
    )


def solution(mesh):
    placed = (
        P("uly", "blk", None),
        P("uly", "blk", None),
        P("uly", None, None),
        P(),
        P("uly", "blk", None),
        P(("blk", "uly"), None),
        P(("blk", "uly")),
        P(("blk", "uly"), None),
        P(("blk", "uly"), None),
        P(("blk", "uly"), None),
        P(("blk", "uly"), None),
        P(("blk", "uly")),
        P(("blk", "uly"), None),
        P(("blk", "uly")),
    )
    blocks = mesh.shape["blk"]
    special = mesh.shape["uly"] == 2 and blocks == HEADS and blocks % 4 == 0 and blocks > 4
    return jax.shard_map(
        on_device if special else per_device,
        mesh=mesh,
        in_specs=placed,
        out_specs=(
            P("uly", "blk", None),
            P("uly", "blk", None),
            P("uly", "blk", None),
            P("uly", None, None),
            P(("blk", "uly"), None),
            P(("blk", "uly")),
            P(("blk", "uly"), None),
            P(("blk", "uly"), None),
            P(("blk", "uly"), None),
            P(("blk", "uly"), None),
            P(("blk", "uly")),
            P(("blk", "uly"), None),
            P(("blk", "uly")),
        ),
        check_vma=False,
    )
```

```python
import functools
import math

import jax
import jax.numpy as jnp
from jax import lax
from jax.experimental import pallas as pl
from jax.experimental.pallas import tpu as pltpu
from jax.sharding import PartitionSpec as P

HEADS = 16
HEAD_DIM = 64


exact_mode = lax.Precision.HIGHEST
epsilon = 1e-05


def passed_along(x, axis, by):
    devices = lax.axis_size(axis)
    return lax.ppermute(x, axis, [(i, (i + by) % devices) for i in range(devices)])


def segment_info(len_row, positions):
    slots = len_row.shape[0]
    ends = jnp.cumsum(len_row)
    starts = ends - len_row
    total = ends[-1]
    seg_ids = jnp.sum((positions[:, None] >= ends[None, :]).astype(jnp.int32), axis=1)
    onehot = seg_ids[:, None] == jnp.arange(slots, dtype=jnp.int32)[None, :]
    begin = jnp.sum(jnp.where(onehot, starts[None, :], 0), axis=1)
    begin = begin + jnp.where(seg_ids == slots, total, 0)
    return (seg_ids, positions - begin, seg_ids < slots)


def rotary(values, offsets):
    half = values.shape[-1] // 2
    freq = 10000.0 ** (-jnp.arange(half, dtype=jnp.float32) / half)
    angle = offsets.astype(jnp.float32)[:, None] * freq[None, :]
    cosine = jnp.cos(angle)[:, None, :]
    sine = jnp.sin(angle)[:, None, :]
    first = values[..., :half]
    second = values[..., half:]
    return jnp.concatenate([first * cosine - second * sine, second * cosine + first * sine], -1)


def modulate(values, scale, shift):
    center = values - jnp.mean(values, -1, keepdims=True)
    spread = jnp.mean(center * center, -1, keepdims=True)
    return center * lax.rsqrt(spread + epsilon) * (1.0 + scale) + shift


def contract_rows(left, right):
    return lax.dot_general(
        left, right, (((0,), (0,)), ((), ())), preferred_element_type=jnp.float32
    )


def contract_cols(left, right):
    return lax.dot_general(
        left, right, (((1,), (1,)), ((), ())), preferred_element_type=jnp.float32
    )


def gelu_exact(values):
    return jax.nn.gelu(values, approximate=False)


def per_device(
    hidden,
    skip_in,
    time_embed,
    lengths,
    cotangent,
    w_skip,
    b_skip,
    w_mod,
    w_qkv,
    w_out,
    w_up,
    b_up,
    w_down,
    b_down,
):
    gathered = (
        lax.all_gather(w_skip, ("blk", "uly"), axis=0, tiled=True),
        lax.all_gather(b_skip, ("blk", "uly"), axis=0, tiled=True),
        lax.all_gather(w_mod, ("blk", "uly"), axis=0, tiled=True),
        lax.all_gather(w_qkv, ("blk", "uly"), axis=0, tiled=True),
        lax.all_gather(w_out, ("blk", "uly"), axis=0, tiled=True),
        lax.all_gather(w_up, ("blk", "uly"), axis=0, tiled=True),
        lax.all_gather(b_up, ("blk", "uly"), axis=0, tiled=True),
        lax.all_gather(w_down, ("blk", "uly"), axis=0, tiled=True),
        lax.all_gather(b_down, ("blk", "uly"), axis=0, tiled=True),
    )
    (
        skip_full,
        bskip_full,
        mod_full,
        qkv_full,
        out_full,
        up_full,
        bup_full,
        down_full,
        bdown_full,
    ) = gathered
    group_count = lax.axis_size("uly")
    cycle_size = lax.axis_size("blk")
    frame_count = hidden.shape[1]
    row_count = lengths.shape[0]
    slot_count = lengths.shape[1]
    local_heads = HEADS // group_count
    span = local_heads * HEAD_DIM
    scaling = HEAD_DIM ** (-0.5)
    block_index = lax.axis_index("blk")
    row_index = lax.axis_index("uly")
    frame_pos = block_index * frame_count + jnp.arange(frame_count, dtype=jnp.int32)
    all_seg, all_offsets, all_valid = jax.vmap(lambda len_row: segment_info(len_row, frame_pos))(
        lengths
    )
    own_seg = lax.dynamic_index_in_dim(all_seg, row_index, 0, keepdims=False)
    own_offsets = lax.dynamic_index_in_dim(all_offsets, row_index, 0, keepdims=False)
    joined = jnp.concatenate([hidden[0], skip_in[0]], 1)
    base = jnp.dot(joined, skip_full, preferred_element_type=jnp.float32) + bskip_full.astype(
        jnp.float32
    )
    time_row = time_embed[0]
    mods = jnp.dot(time_row, mod_full, preferred_element_type=jnp.float32)
    selector = (own_seg[:, None] == jnp.arange(slot_count, dtype=jnp.int32)[None, :]).astype(
        jnp.float32
    )
    frame_mod = jnp.dot(selector, mods, precision=exact_mode)
    a_scale, a_shift, f_scale, f_shift = jnp.split(frame_mod, 4, 1)
    normed_full, norm_back = jax.vjp(modulate, base, a_scale, a_shift)
    normed = normed_full.astype(jnp.bfloat16)
    projected = jnp.dot(normed, qkv_full, preferred_element_type=jnp.float32).reshape(
        frame_count, 3, HEADS, HEAD_DIM
    )

    def place(parts):
        return jnp.stack(
            [rotary(parts[:, 0], own_offsets), rotary(parts[:, 1], own_offsets), parts[:, 2]], 1
        )

    turned, unturn = jax.vjp(place, projected)
    sending = turned.astype(jnp.bfloat16).reshape(1, frame_count, 3, group_count, span)
    head_data = lax.all_to_all(sending, "uly", split_axis=3, concat_axis=0, tiled=True)
    query = head_data[:, :, 0, 0].reshape(row_count, frame_count, local_heads, HEAD_DIM)
    kv_pairs = head_data[:, :, 1:, 0]

    def key_segments(start, count):
        key_pos = start + jnp.arange(count, dtype=jnp.int32)
        return jax.vmap(lambda len_row: segment_info(len_row, key_pos)[0])(lengths)

    start_state = (
        jnp.full((row_count, local_heads, frame_count), -1e30, jnp.float32),
        jnp.zeros((row_count, local_heads, frame_count), jnp.float32),
        jnp.zeros((row_count, frame_count, local_heads, HEAD_DIM), jnp.float32),
    )
    piece = lax.all_gather(kv_pairs, "blk", axis=1, tiled=True)
    total = piece.shape[1]
    step = math.gcd(total, max(frame_count, 1024))

    def sub_step(step_index, state):
        run_max, run_total, run_acc = state
        offset = step_index * step
        section = lax.dynamic_slice_in_dim(piece, offset, step, 1)
        key_seg = key_segments(offset, step)
        key_part = section[:, :, 0].reshape(row_count, step, local_heads, HEAD_DIM)
        value_part = section[:, :, 1].reshape(row_count, step, local_heads, HEAD_DIM)
        mask = all_seg[:, None, :, None] == key_seg[:, None, None, :]
        score = (
            jnp.einsum("rqhd,rkhd->rhqk", query, key_part, preferred_element_type=jnp.float32)
            * scaling
        )
        masked = jnp.where(mask, score, -1e30)
        fresh = jnp.maximum(run_max, jnp.max(masked, -1))
        weights = jnp.where(mask, jnp.exp(masked - fresh[..., None]), 0.0)
        decay = jnp.exp(run_max - fresh)
        run_total = run_total * decay + jnp.sum(weights, -1)
        run_acc = run_acc * jnp.swapaxes(decay, 1, 2)[..., None] + jnp.einsum(
            "rhqk,rkhd->rqhd",
            weights.astype(jnp.bfloat16),
            value_part,
            preferred_element_type=jnp.float32,
        )
        return (fresh, run_total, run_acc)

    run_max, run_total, run_acc = lax.fori_loop(0, total // step, sub_step, start_state)
    attended = run_acc / jnp.swapaxes(run_total, 1, 2)[..., None]
    log_total = run_max + jnp.log(run_total)
    valid_half = all_valid.astype(jnp.bfloat16)[:, :, None, None]
    leaving = (attended * all_valid.astype(jnp.float32)[:, :, None, None]).astype(jnp.bfloat16)
    leaving = leaving.reshape(row_count, frame_count, 1, span)
    mixed = lax.all_to_all(leaving, "uly", split_axis=0, concat_axis=2, tiled=True).reshape(
        frame_count, HEADS * HEAD_DIM
    )
    branch = jnp.dot(mixed, out_full, preferred_element_type=jnp.float32)
    middle = base + branch
    normed2_full, norm2_back = jax.vjp(modulate, middle, f_scale, f_shift)
    normed2 = normed2_full.astype(jnp.bfloat16)
    inner = jnp.dot(normed2, up_full, preferred_element_type=jnp.float32) + bup_full.astype(
        jnp.float32
    )
    act_full, act_back = jax.vjp(gelu_exact, inner)
    act = act_full.astype(jnp.bfloat16)
    result = (
        middle
        + jnp.dot(act, down_full, preferred_element_type=jnp.float32)
        + bdown_full.astype(jnp.float32)
    )
    output = result.astype(jnp.bfloat16)[None]
    again = (
        lax.all_gather(w_skip, ("blk", "uly"), axis=0, tiled=True),
        lax.all_gather(w_mod, ("blk", "uly"), axis=0, tiled=True),
        lax.all_gather(w_qkv, ("blk", "uly"), axis=0, tiled=True),
        lax.all_gather(w_out, ("blk", "uly"), axis=0, tiled=True),
        lax.all_gather(w_up, ("blk", "uly"), axis=0, tiled=True),
        lax.all_gather(w_down, ("blk", "uly"), axis=0, tiled=True),
    )
    skip_back, mod_back, qkv_back, out_back, up_back, down_back = again
    upstream = cotangent[0]
    upstream_full = upstream.astype(jnp.float32)
    grad_down = contract_rows(act, upstream)
    grad_bdown = jnp.sum(upstream_full, 0)
    grad_act = contract_cols(upstream, down_back)
    grad_inner = act_back(grad_act)[0].astype(jnp.bfloat16)
    grad_up = contract_rows(normed2, grad_inner)
    grad_bup = jnp.sum(grad_inner.astype(jnp.float32), 0)
    grad_normed2 = contract_cols(grad_inner, up_back)
    grad_mid_norm, grad_fscale, grad_fshift = norm2_back(grad_normed2)
    grad_middle = upstream_full + grad_mid_norm
    grad_branch = grad_middle.astype(jnp.bfloat16)
    grad_out = contract_rows(mixed, grad_branch)
    grad_mixed = (
        contract_cols(grad_branch, out_back)
        .astype(jnp.bfloat16)
        .reshape(1, frame_count, group_count, span)
    )
    returning = lax.all_to_all(grad_mixed, "uly", split_axis=2, concat_axis=0, tiled=True)
    grad_attn = returning.reshape(row_count, frame_count, local_heads, HEAD_DIM) * valid_half
    delta_rows = jnp.swapaxes(jnp.sum(grad_attn.astype(jnp.float32) * attended, -1), 1, 2)

    def contribution(held_pairs, key_start):
        count = held_pairs.shape[1]
        key_seg = key_segments(key_start, count)
        key_part = held_pairs[:, :, 0].reshape(row_count, count, local_heads, HEAD_DIM)
        value_part = held_pairs[:, :, 1].reshape(row_count, count, local_heads, HEAD_DIM)
        mask = all_seg[:, None, :, None] == key_seg[:, None, None, :]
        score = (
            jnp.einsum("rqhd,rkhd->rhqk", query, key_part, preferred_element_type=jnp.float32)
            * scaling
        )
        weights = jnp.exp(jnp.where(mask, score - log_total[..., None], -1e30))
        grad_weights = jnp.einsum(
            "rqhd,rkhd->rhqk", grad_attn, value_part, preferred_element_type=jnp.float32
        )
        grad_score = (weights * (grad_weights - delta_rows[..., None])).astype(jnp.bfloat16)
        more_query = (
            jnp.einsum("rhqk,rkhd->rqhd", grad_score, key_part, preferred_element_type=jnp.float32)
            * scaling
        )
        more_key = (
            jnp.einsum("rhqk,rqhd->rkhd", grad_score, query, preferred_element_type=jnp.float32)
            * scaling
        )
        more_value = jnp.einsum(
            "rhqk,rqhd->rkhd",
            weights.astype(jnp.bfloat16),
            grad_attn,
            preferred_element_type=jnp.float32,
        )
        more_pairs = jnp.stack(
            [more_key.reshape(row_count, count, span), more_value.reshape(row_count, count, span)],
            2,
        )
        return (more_query, more_pairs)

    def pass_grads(held_grads):
        return passed_along(held_grads.astype(jnp.bfloat16), "blk", 1).astype(held_grads.dtype)

    def cycle_step(turn, state):
        held_pairs, held_grads, query_grad = state
        more_query, more_pairs = contribution(
            held_pairs, (block_index - turn) % cycle_size * frame_count
        )
        held_pairs = passed_along(held_pairs, "blk", 1)
        held_grads = pass_grads(held_grads + more_pairs)
        return (held_pairs, held_grads, query_grad + more_query)

    cycle_start = (
        kv_pairs,
        jnp.zeros((row_count, frame_count, 2, span), jnp.float32),
        jnp.zeros((row_count, frame_count, local_heads, HEAD_DIM), jnp.float32),
    )
    held_pairs, held_grads, query_grad = lax.fori_loop(0, cycle_size - 1, cycle_step, cycle_start)
    last_query, last_pairs = contribution(
        held_pairs, (block_index - (cycle_size - 1)) % cycle_size * frame_count
    )
    pair_grads = pass_grads(held_grads + last_pairs)
    query_grad = query_grad + last_query
    head_grads = jnp.concatenate(
        [
            query_grad.astype(jnp.bfloat16).reshape(row_count, frame_count, 1, span),
            pair_grads.astype(jnp.bfloat16),
        ],
        2,
    ).reshape(row_count, frame_count, 3, 1, span)
    frames_grad = lax.all_to_all(head_grads, "uly", split_axis=0, concat_axis=3, tiled=True)
    frames_grad = frames_grad.reshape(frame_count, 3, HEADS, HEAD_DIM).astype(jnp.float32)
    grad_projected = (
        unturn(frames_grad)[0].astype(jnp.bfloat16).reshape(frame_count, 3 * HEADS * HEAD_DIM)
    )
    grad_qkv = contract_rows(normed, grad_projected)
    grad_normed = contract_cols(grad_projected, qkv_back)
    grad_base_norm, grad_ascale, grad_ashift = norm_back(grad_normed)
    grad_base = (grad_middle + grad_base_norm).astype(jnp.bfloat16)
    grad_skip_w = contract_rows(joined, grad_base)
    grad_bskip = jnp.sum(grad_base.astype(jnp.float32), 0)
    grad_joined = contract_cols(grad_base, skip_back).astype(jnp.bfloat16)
    model_width = hidden.shape[2]
    hidden_grad = grad_joined[:, :model_width][None]
    skip_grad = grad_joined[:, model_width:][None]
    frame_mod_grad = jnp.concatenate([grad_ascale, grad_ashift, grad_fscale, grad_fshift], 1)
    slot_grad = lax.dot_general(
        selector, frame_mod_grad, (((0,), (0,)), ((), ())), precision=exact_mode
    )
    grad_mod = lax.dot_general(
        time_row.astype(jnp.float32), slot_grad, (((0,), (0,)), ((), ())), precision=exact_mode
    )
    slot_total = lax.psum(slot_grad, "blk")
    time_grad = lax.dot_general(
        slot_total, mod_back.astype(jnp.float32), (((1,), (1,)), ((), ())), precision=exact_mode
    )[None]
    owned = (
        lax.psum_scatter(grad_skip_w, ("blk", "uly"), scatter_dimension=0, tiled=True),
        lax.psum_scatter(grad_bskip, ("blk", "uly"), scatter_dimension=0, tiled=True),
        lax.psum_scatter(grad_mod, ("blk", "uly"), scatter_dimension=0, tiled=True),
        lax.psum_scatter(grad_qkv, ("blk", "uly"), scatter_dimension=0, tiled=True),
        lax.psum_scatter(grad_out, ("blk", "uly"), scatter_dimension=0, tiled=True),
        lax.psum_scatter(grad_up, ("blk", "uly"), scatter_dimension=0, tiled=True),
        lax.psum_scatter(grad_bup, ("blk", "uly"), scatter_dimension=0, tiled=True),
        lax.psum_scatter(grad_down, ("blk", "uly"), scatter_dimension=0, tiled=True),
        lax.psum_scatter(grad_bdown, ("blk", "uly"), scatter_dimension=0, tiled=True),
    )
    return (
        output,
        hidden_grad,
        skip_grad,
        time_grad,
        owned[0],
        owned[1],
        owned[2],
        owned[3],
        owned[4],
        owned[5],
        owned[6],
        owned[7],
        owned[8],
    )


MESH = pl.DeviceIdType.MESH


class Place:
    def __init__(self, depth):
        self.depth = depth
        self.b = lax.axis_index("blk")
        self.x = lax.axis_index("uly")
        self.z = self.b // 4
        self.y = (self.b // 2) % 2
        self.c = self.b % 2
        self.to_x = (self.b, 1 - self.x)
        self.to_y = (self.b + 2 - 4 * self.y, self.x)
        self.to_core = (self.b + 1 - 2 * self.c, self.x)
        self.to_far = (self.b + 3 - 4 * self.y - 2 * self.c, self.x)
        self.to_up = (self.b + 4, self.x)
        self.to_down = (self.b - 4, self.x)

    def shard(self, z, y, c, x):
        return ((z * 2 + y) * 2 + c) * 2 + x

    def greet(self):
        barrier = pltpu.get_barrier_semaphore()
        for to in (self.to_x, self.to_y, self.to_core, self.to_far):
            pl.semaphore_signal(barrier, inc=1, device_id=to, device_id_type=MESH)

        @pl.when(self.z < self.depth - 1)
        def _():
            pl.semaphore_signal(barrier, inc=1, device_id=self.to_up, device_id_type=MESH)

        @pl.when(self.z > 0)
        def _():
            pl.semaphore_signal(barrier, inc=1, device_id=self.to_down, device_id_type=MESH)

        top = self.depth - 1
        pl.semaphore_wait(barrier, 4 + (self.z + top - 1) // top + (2 * top - 1 - self.z) // top)


def remote(src, dst, send, recv, to):
    return pltpu.make_async_remote_copy(
        src_ref=src, dst_ref=dst, send_sem=send, recv_sem=recv, device_id=to, device_id_type=MESH
    )


class Gather:
    SENDS = 64
    RECVS = 48

    def __init__(self, place, src, dst, rows, lo, hi, split, plane_first, sends, recvs):
        self.p, self.src, self.dst, self.rows = place, src, dst, rows
        self.lo, self.hi, self.split, self.plane_first = lo, hi, split, plane_first
        self.sends, self.recvs = sends, recvs
        self.pending = []

    def part(self, z, y, c, x, half=None):
        base = self.p.shard(z, y, c, x) * self.rows
        rows = self.rows
        if half is not None:
            rows = rows // 2
            base = base + half * rows
        return self.dst.at[pl.ds(pl.multiple_of(base, rows), rows), pl.ds(self.lo, self.hi - self.lo)]

    def mine(self):
        return self.src.at[:, pl.ds(self.lo, self.hi - self.lo)]

    def go(self, when, src, dst, send, recv, to):
        def start():
            remote(src, dst, self.sends.at[send], self.recvs.at[recv], to).start()

        def finish():
            remote(src, dst, self.sends.at[send], self.recvs.at[recv], to).wait_send()

        if when is None:
            start()
            self.pending.append(finish)
        else:
            pl.when(when)(start)
            self.pending.append(lambda: pl.when(when)(finish))

    def got(self, dst, recv):
        remote(dst, dst, self.sends.at[0], self.recvs.at[recv], self.p.to_x).wait_recv()

    def share(self, when, src, z, y, x):
        slot = z * 4 + y * 2 + x
        self.go(when, src, self.part(z, y, self.p.c, x), slot, slot, self.p.to_core)

    def steps(self):
        return self.plane_steps() if self.plane_first else self.line_steps()

    def line_steps(self):
        p = self.p
        top = p.depth - 1

        def hand_on(when, src, z):
            whole = self.part(z, p.y, p.c, p.x)
            self.go(when, src, whole, 24 + z, 20 + z, p.to_x)
            self.go(when, src, whole, 28 + z, 24 + z, p.to_y)
            self.share(when, src, z, p.y, p.x)

        def own():
            src = self.mine()
            whole = self.part(p.z, p.y, p.c, p.x)
            self.go(p.z < top, src, whole, 16 + p.z, 16 + p.z, p.to_up)
            self.go(p.z > 0, src, whole, 20 + p.z, 16 + p.z, p.to_down)
            hand_on(None, src, p.z)

        def line(d):
            for side in (-1, 1):
                z = p.z + side * d
                here = (z >= 0) & (z <= top)
                whole = self.part(z, p.y, p.c, p.x)
                pl.when(here)(lambda: self.got(whole, 16 + z))
                if side < 0:
                    self.go(here & (p.z < top), whole, whole, 16 + z, 16 + z, p.to_up)
                else:
                    self.go(here & (p.z > 0), whole, whole, 20 + z, 16 + z, p.to_down)
                hand_on(here, whole, z)

        def origins(d):
            return [(None, p.z)] if d == 0 else [
                ((p.z + s * d >= 0) & (p.z + s * d <= top), p.z + s * d) for s in (-1, 1)
            ]

        def cond(when, f):
            f() if when is None else pl.when(when)(f)

        def cross(d):
            for when, z in origins(d):
                from_x = self.part(z, p.y, p.c, 1 - p.x)
                cond(when, lambda: self.got(from_x, 20 + z))
                self.share(when, from_x, z, p.y, 1 - p.x)
                if self.split:
                    part = self.part(z, p.y, p.c, 1 - p.x, 0)
                else:
                    part = from_x
                self.go(when, part, part, 32 + z, 28 + z, p.to_y)
                from_y = self.part(z, 1 - p.y, p.c, p.x)
                cond(when, lambda: self.got(from_y, 24 + z))
                self.share(when, from_y, z, 1 - p.y, p.x)
                if self.split:
                    part = self.part(z, 1 - p.y, p.c, p.x, 1)
                    self.go(when, part, part, 36 + z, 32 + z, p.to_x)

        def corner(d):
            for when, z in origins(d):
                whole = self.part(z, 1 - p.y, p.c, 1 - p.x)
                if self.split:
                    for half in (0, 1):
                        part = self.part(z, 1 - p.y, p.c, 1 - p.x, half)
                        cond(when, lambda: self.got(part, 28 + 4 * half + z))
                else:
                    cond(when, lambda: self.got(whole, 28 + z))
                self.share(when, whole, z, 1 - p.y, 1 - p.x)

        out = [(0, own)]
        for d in range(p.depth):
            if d:
                out.append((d, functools.partial(line, d)))
            out.append((d + 1, functools.partial(cross, d)))
            out.append((d + 2, functools.partial(corner, d)))
        return out

    def plane_steps(self):
        p = self.p
        top = p.depth - 1

        def along(when, src, z, y, x, up, down):
            slot = 20 + z * 4 + y * 2 + x
            whole = self.part(z, y, p.c, x)
            if up:
                w = p.z < top
                self.go(w if when is None else w & when, src, whole, slot, slot, p.to_up)
            if down:
                w = p.z > 0
                self.go(w if when is None else w & when, src, whole, slot + 16, slot, p.to_down)

        def own():
            src = self.mine()
            whole = self.part(p.z, p.y, p.c, p.x)
            self.go(None, src, whole, 16, 16, p.to_x)
            self.go(None, src, whole, 17, 17, p.to_y)
            along(None, src, p.z, p.y, p.x, True, True)
            self.share(None, src, p.z, p.y, p.x)

        def cross():
            from_x = self.part(p.z, p.y, p.c, 1 - p.x)
            self.got(from_x, 16)
            part = self.part(p.z, p.y, p.c, 1 - p.x, 0) if self.split else from_x
            self.go(None, part, part, 18, 18, p.to_y)
            along(None, from_x, p.z, p.y, 1 - p.x, True, True)
            self.share(None, from_x, p.z, p.y, 1 - p.x)
            from_y = self.part(p.z, 1 - p.y, p.c, p.x)
            self.got(from_y, 17)
            if self.split:
                part = self.part(p.z, 1 - p.y, p.c, p.x, 1)
                self.go(None, part, part, 19, 19, p.to_x)
            along(None, from_y, p.z, 1 - p.y, p.x, True, True)
            self.share(None, from_y, p.z, 1 - p.y, p.x)

        def corner():
            whole = self.part(p.z, 1 - p.y, p.c, 1 - p.x)
            if self.split:
                for half in (0, 1):
                    self.got(self.part(p.z, 1 - p.y, p.c, 1 - p.x, half), 18 + half)
            else:
                self.got(whole, 18)
            along(None, whole, p.z, 1 - p.y, 1 - p.x, True, True)
            self.share(None, whole, p.z, 1 - p.y, 1 - p.x)

        def line(d, k):
            y = p.y if k in (0, 1) else 1 - p.y
            x = p.x if k in (0, 2) else 1 - p.x
            for side in (-1, 1):
                z = p.z + side * d
                here = (z >= 0) & (z <= top)
                whole = self.part(z, y, p.c, x)
                pl.when(here)(lambda: self.got(whole, 20 + z * 4 + y * 2 + x))
                along(here, whole, z, y, x, side < 0, side > 0)
                self.share(here, whole, z, y, x)

        out = [(0, own), (1, cross), (2, corner)]
        for d in range(1, p.depth):
            for k in range(4):
                out.append((d + 0.1 + min(k, 2) * 0.9, functools.partial(line, d, k)))
        return out

    def shared(self):
        p = self.p
        for z in range(p.depth):
            for y in range(2):
                for x in range(2):
                    self.got(self.part(z, y, 1 - p.c, x), z * 4 + y * 2 + x)

    def sent(self):
        for wait in self.pending:
            wait()


class Quad:
    def __init__(self, p, src, dst, sems):
        self.p, self.src, self.dst, self.sems = p, src, dst, sems

    def to_core(self):
        return remote(self.src, self.dst(1), self.sems(0), self.sems(1), self.p.to_core)

    def to_y(self):
        return remote(self.src, self.dst(2), self.sems(2), self.sems(3), self.p.to_y)

    def on(self):
        return remote(self.dst(2), self.dst(3), self.sems(4), self.sems(5), self.p.to_core)

    def start(self):
        self.to_y().start()
        self.to_core().start()

    def relay(self):
        self.to_y().wait_recv()
        self.on().start()

    def arrived(self):
        self.to_core().wait_recv()
        self.on().wait_recv()

    def finish(self):
        self.to_y().wait_send()
        self.to_core().wait_send()
        self.on().wait_send()


class QuadRows:
    def __init__(self, p, src, dst, sems):
        self.p, self.src, self.dst, self.sems = p, src, dst, sems

    def mine(self, y, c):
        pair = self.dst.shape[2]
        return self.src.at[:, pl.ds(pl.multiple_of((y * 2 + c) * pair, pair), pair), :]

    def own(self):
        return pltpu.make_async_copy(self.mine(self.p.y, self.p.c), self.dst.at[0], self.sems.at[0])

    def copy(self, k):
        p = self.p
        y, c, to = (
            (p.y, 1 - p.c, p.to_core),
            (1 - p.y, p.c, p.to_y),
            (1 - p.y, 1 - p.c, p.to_far),
        )[k - 1]
        return remote(self.mine(y, c), self.dst.at[k], self.sems.at[2 * k - 1], self.sems.at[2 * k], to)

    def start(self):
        self.own().start()
        for k in (2, 3, 1):
            self.copy(k).start()

    def arrived(self):
        self.own().wait()
        for k in (1, 2, 3):
            self.copy(k).wait_recv()

    def finish(self):
        for k in (1, 2, 3):
            self.copy(k).wait_send()


class Reduce:
    CHUNK = 512

    def __init__(self, place, x, take, rows, lo, width, out, full, outgo, income, sends, recvs):
        self.p, self.x, self.take, self.rows = place, x, take, rows
        self.lo, self.width, self.out = lo, width, out
        self.full, self.outgo, self.income = full, outgo, income
        self.sends, self.recvs = sends, recvs

    @staticmethod
    def scratch(rows, width, depth):
        return [
            pltpu.VMEM((2 * depth * rows, width), jnp.bfloat16),
            pltpu.VMEM(((2 * depth + 1) * rows, width), jnp.bfloat16),
            pltpu.SemaphoreType.DMA((4,)),
            pltpu.SemaphoreType.DMA((4,)),
        ]

    def part(self, ref, lo, hi):
        return ref.at[pl.ds(lo * self.rows, (hi - lo) * self.rows)]

    def along_x(self):
        n = self.p.depth
        return remote(
            self.part(self.outgo, 0, n), self.part(self.income, 0, n), self.sends.at[0], self.recvs.at[0], self.p.to_x
        )

    def up(self, lo):
        n = self.p.depth
        return remote(
            self.part(self.outgo, n + lo, 2 * n),
            self.part(self.income, n + lo, 2 * n),
            self.sends.at[1],
            self.recvs.at[1],
            self.p.to_up,
        )

    def down(self, hi):
        n = self.p.depth
        return remote(
            self.part(self.outgo, n, n + hi),
            self.part(self.income, n, n + hi),
            self.sends.at[2],
            self.recvs.at[2],
            self.p.to_down,
        )

    def down_last(self, at):
        n = self.p.depth
        return remote(
            self.part(self.outgo, n + at, n + at + 1),
            self.part(self.income, 2 * n, 2 * n + 1),
            self.sends.at[3],
            self.recvs.at[3],
            self.p.to_down,
        )

    def columns(self, body):
        @pl.loop(0, self.width // self.CHUNK)
        def _(j):
            body(j, pl.ds(pl.multiple_of(j * self.CHUNK, self.CHUNK), self.CHUNK))

    def product(self, side, j):
        n, r = self.p.depth, self.rows
        side = pl.ds(pl.multiple_of(side * r, r), r)
        x = jnp.concatenate([self.x[k, :, side, :].reshape(n * r, self.x.shape[3]) for k in range(4)], 1)
        return jnp.dot(x, self.take(self.lo // self.CHUNK + j), preferred_element_type=jnp.float32)

    def begin(self):
        p, n, r = self.p, self.p.depth, self.rows

        def away(j, here):
            self.outgo[pl.ds(0, n * r), here] = self.product(1 - p.x, j).astype(jnp.bfloat16)

        self.columns(away)
        self.along_x().start()

        def near(j, here):
            self.full[pl.ds(0, n * r), here] = self.product(p.x, j)

        self.columns(near)

        @pl.when(p.z == 0)
        def _():
            ref = self.part(self.income, n, n + 1)
            ref[...] = jnp.zeros(ref.shape, ref.dtype)

        @pl.when(p.z == n - 1)
        def _():
            ref = self.part(self.income, 2 * n, 2 * n + 1)
            ref[...] = jnp.zeros(ref.shape, ref.dtype)

    def total(self, h, lo, hi):
        n, r = self.p.depth, self.rows

        def body(j, here):
            rows = pl.ds(lo * r, (hi - lo) * r)
            line = pl.ds((n + lo) * r, (hi - lo) * r)
            total = self.full[rows, here] + self.income[rows, here].astype(jnp.float32)
            if h:
                total = total + self.income[line, here].astype(jnp.float32)
            self.outgo[line, here] = total.astype(jnp.bfloat16)

        self.columns(body)

    def hop(self, h):
        p, n = self.p, self.p.depth
        if h == 0:
            self.along_x().wait_recv()

        @pl.when(p.z == h)
        def _():
            if h:
                self.up(h).wait_recv()
            self.total(h, h + 1, n)
            self.up(h + 1).start()

        @pl.when(p.z == n - 1 - h)
        def _():
            if h:
                self.down(n - 1 - h).wait_recv()
            self.total(h, 0, n - 1 - h)
            if h < n - 2:
                self.down(n - 2 - h).start()
            self.down_last(n - 2 - h).start()

    def end(self):
        p, n, r = self.p, self.p.depth, self.rows
        pl.when(p.z == n - 1)(lambda: self.up(n - 1).wait_recv())
        pl.when(p.z < n - 1)(lambda: self.down_last(0).wait_recv())
        own = pl.ds(pl.multiple_of(p.z * r, r), r)
        line = pl.ds(pl.multiple_of((n + p.z) * r, r), r)

        def body(j, here):
            there = pl.ds(pl.multiple_of(self.lo + j * self.CHUNK, self.CHUNK), self.CHUNK)
            self.out[:, there] = (
                self.full[own, here]
                + self.income[own, here].astype(jnp.float32)
                + self.income[line, here].astype(jnp.float32)
                + self.income[pl.ds(2 * n * r, r), here].astype(jnp.float32)
            )

        self.columns(body)

    def finish(self):
        p, n = self.p, self.p.depth
        self.along_x().wait_send()
        for h in range(n - 1):
            pl.when(p.z == h)(lambda: self.up(h + 1).wait_send())

            @pl.when(p.z == n - 1 - h)
            def _():
                if h < n - 2:
                    self.down(n - 2 - h).wait_send()
                self.down_last(n - 2 - h).wait_send()


VMEM_BYTES = 58 * 2**20


def kernel_params(number):
    return pltpu.CompilerParams(collective_id=number, has_side_effects=True, vmem_limit_bytes=VMEM_BYTES)


def in_vmem(count):
    return [pl.BlockSpec(memory_space=pltpu.VMEM)] * count


def in_any(count):
    return [pl.BlockSpec(memory_space=pl.ANY)] * count


def ranges(cols, cut):
    return [(0, cut, True), (cut, cols, False)] if cut else [(0, cols, False)]


def keep_own(p, pairs, sems):
    copies = []
    for k, (src, dst, rows) in enumerate(pairs):
        at = pl.multiple_of(p.shard(p.z, p.y, p.c, p.x) * rows, rows)
        copies.append(pltpu.make_async_copy(src, dst.at[pl.ds(at, rows)], sems.at[k]))
    for copy in copies:
        copy.start()
    return copies


class Exchange:
    def __init__(self, place, count, src, dst, sends, recvs, own):
        self.p, self.count, self.src, self.dst = place, count, src, dst
        self.sends, self.recvs, self.own = sends, recvs, own

    def copy(self, k):
        to = (self.p.b + k) % self.count
        return remote(
            self.src.at[to], self.dst.at[self.p.b], self.sends.at[k], self.recvs.at[k], (to, self.p.x)
        )

    def mine(self):
        return pltpu.make_async_copy(self.src.at[self.p.b], self.dst.at[self.p.b], self.own)

    def start(self):
        self.mine().start()
        for k in range(1, self.count):
            self.copy(k).start()

    def arrived(self):
        self.mine().wait()
        for k in range(1, self.count):
            came = (self.p.b + self.count - k) % self.count
            remote(
                self.dst.at[came], self.dst.at[came], self.sends.at[k], self.recvs.at[k], self.p.to_x
            ).wait_recv()

    def finish(self):
        for k in range(1, self.count):
            self.copy(k).wait_send()


def exchange_sems(count):
    return [
        pltpu.SemaphoreType.DMA((count,)),
        pltpu.SemaphoreType.DMA((count,)),
        pltpu.SemaphoreType.DMA,
    ]


def greet_plane(p, count):
    barrier = pltpu.get_barrier_semaphore()
    for k in range(1, count):
        pl.semaphore_signal(barrier, inc=1, device_id=((p.b + k) % count, p.x), device_id_type=MESH)
    pl.semaphore_signal(barrier, inc=1, device_id=p.to_x, device_id_type=MESH)
    pl.semaphore_wait(barrier, count)


def play(events):
    for event in events:
        event()


def three_terms(v):
    a = v.astype(jnp.bfloat16).astype(jnp.float32)
    b = (v - a).astype(jnp.bfloat16).astype(jnp.float32)
    return a, b, v - a - b


def extra_rows(rows, length, width):
    shape = (length, width)
    row = lax.broadcasted_iota(jnp.int32, shape, 0)
    total = jnp.zeros(shape, jnp.float32)
    for k, values in enumerate(rows):
        total = jnp.where(row == k, values, total)
    return total.astype(jnp.bfloat16)


def attend_open(p, lengths, got, qkv, keys, values):
    count, _, span = got.shape
    frames = count * span
    for k in range(count):
        qkv[:, k * span : (k + 1) * span] = got[k]
    position = lax.broadcasted_iota(jnp.int32, (1, frames), 1)
    hidden_key = jnp.where(position < lengths[p.x], 0.0, -1e30)
    keys[...] = jnp.concatenate([qkv[HEAD_DIM : 2 * HEAD_DIM, :], extra_rows([hidden_key], HEAD_DIM, frames)], 0).T
    values[...] = jnp.concatenate([qkv[2 * HEAD_DIM :, :], extra_rows([1.0], 16, frames)], 0)


def attend(p, lengths, got, qkv, keys, values, mixed_out, lse, plain, block, lo, hi):
    span = got.shape[2]
    length = lengths[p.x]
    ones = extra_rows([1.0], HEAD_DIM, block)
    scaling = HEAD_DIM ** (-0.5)
    parts = block // span

    @pl.loop(lo, hi)
    def _(j):
        here = pl.ds(pl.multiple_of(j * block, block), block)
        query = jnp.concatenate([qkv[:HEAD_DIM, here] * jnp.bfloat16(scaling), ones], 0)
        score = jnp.dot(keys[...], query, preferred_element_type=jnp.float32)
        peak = jnp.max(score, 0, keepdims=True)
        weights = jnp.exp(score - peak).astype(jnp.bfloat16)
        out = jnp.dot(values[...], weights, preferred_element_type=jnp.float32)
        total = out[HEAD_DIM : HEAD_DIM + 1]
        out = out[:HEAD_DIM] / total
        plain[:, here] = out
        lse[:, here] = peak + jnp.log(total)
        column = lax.broadcasted_iota(jnp.int32, (HEAD_DIM, block), 1) + j * block
        kept = jnp.where(column < length, out, 0.0).astype(jnp.bfloat16)
        for k in range(parts):
            mixed_out[j * parts + k] = kept[:, k * span : (k + 1) * span]


def attend_back_open(p, lengths, qkv, keys, values, sums):
    frames = qkv.shape[1]
    length = lengths[p.x]
    position = lax.broadcasted_iota(jnp.int32, (1, frames), 1)
    hidden_key = jnp.where(position < length, 0.0, -1e30)
    keys[...] = jnp.concatenate(
        [qkv[HEAD_DIM : 2 * HEAD_DIM, :], extra_rows([hidden_key, 1.0, 1.0, 1.0], HEAD_DIM, frames)], 0
    ).T
    values[...] = jnp.concatenate(
        [qkv[2 * HEAD_DIM :, :], extra_rows([1.0, 1.0, 1.0], HEAD_DIM, frames)], 0
    ).T
    sums[...] = jnp.zeros_like(sums)


def attend_back(got, qkv, lse, plain, keys, values, sums, grads_out, block, lo, hi):
    span = got.shape[2]
    scaling = HEAD_DIM ** (-0.5)
    parts = block // span

    @pl.loop(lo, hi)
    def _(j):
        here = pl.ds(pl.multiple_of(j * block, block), block)
        query = qkv[:HEAD_DIM, here] * jnp.bfloat16(scaling)
        upstream = jnp.concatenate([got[j * parts + k] for k in range(parts)], 1)
        delta = jnp.sum(upstream.astype(jnp.float32) * plain[:, here], 0, keepdims=True)
        left = jnp.concatenate(
            [query, extra_rows([1.0, *[-t for t in three_terms(lse[:, here])]], HEAD_DIM, block)], 0
        )
        right = jnp.concatenate([upstream, extra_rows([-t for t in three_terms(delta)], HEAD_DIM, block)], 0)
        weights = jnp.exp(jnp.dot(keys[...], left, preferred_element_type=jnp.float32))
        slope = jnp.dot(values[...], right, preferred_element_type=jnp.float32)
        slope = (weights * slope).astype(jnp.bfloat16)
        sums[:, HEAD_DIM:] += lax.dot_general(
            weights.astype(jnp.bfloat16), upstream, (((1,), (1,)), ((), ())), preferred_element_type=jnp.float32
        )
        sums[:, :HEAD_DIM] += lax.dot_general(
            slope, query, (((1,), (1,)), ((), ())), preferred_element_type=jnp.float32
        )
        query_grad = (
            jnp.dot(qkv[HEAD_DIM : 2 * HEAD_DIM, :], slope, preferred_element_type=jnp.float32) * scaling
        ).astype(jnp.bfloat16)
        for k in range(parts):
            grads_out[j * parts + k, :HEAD_DIM, :] = query_grad[:, k * span : (k + 1) * span]


def attend_back_close(sums, grads_out):
    count, _, span = grads_out.shape

    @pl.loop(0, count)
    def _(k):
        rows = pl.ds(pl.multiple_of(k * span, span), span)
        grads_out[k, HEAD_DIM:, :] = sums[rows, :].T.astype(jnp.bfloat16)


def others(p, count, k):
    number = (p.b * 2 + p.x + k) % (2 * count)
    return (number // 2, number % 2)


def nt(left, right):
    return lax.dot_general(left, right, (((1,), (1,)), ((), ())), preferred_element_type=jnp.float32)


def mean(v):
    return jnp.mean(v, -1, keepdims=True)


def normal(v):
    center = v - mean(v)
    rstd = lax.rsqrt(mean(center * center) + epsilon)
    return center * rstd, rstd


def normal_back(grad, hat, rstd, scale):
    gx = grad * (1.0 + scale)
    return rstd * (gx - mean(gx) - hat * mean(gx * hat))


def fold(v):
    width = v.shape[1] // 8
    return jnp.concatenate([v[:, k * width : (k + 1) * width] for k in range(8)], 0)


class Tiles:
    def __init__(self, p, src, dst, sends, recvs, each):
        self.p, self.src, self.dst, self.sends, self.recvs, self.each = p, src, dst, sends, recvs, each
        self.count = 4 * p.depth

    def number(self, k=0):
        return (self.p.b * 2 + self.p.x + k) % (2 * self.count)

    def copy(self, k):
        src = self.src.at[self.number(k)] if self.each else self.src
        return remote(src, self.dst.at[self.number()], self.sends.at[k], self.recvs.at[k], others(self.p, self.count, k))

    def start(self):
        for k in range(1, 2 * self.count):
            self.copy(k).start()
        if self.each:
            self.dst[self.number()] = self.src[self.number()]
        else:
            self.dst[self.number()] = self.src[...]

    def arrived(self):
        for k in range(1, 2 * self.count):
            came = self.dst.at[self.number(2 * self.count - k)]
            remote(came, came, self.sends.at[k], self.recvs.at[k], self.p.to_x).wait_recv()

    def finish(self):
        for k in range(1, 2 * self.count):
            self.copy(k).wait_send()


BACK_IN = [
    "lengths", "base", "mods", "b_up", "b_down", "cosine",
    "sine", "w_mod", "times", "qkv", "lse", "plain",
    "cot", "mixed", "joined", "normed", "w_out", "w_up",
    "w_down", "w_qkv", "w_skip",
]
BACK_OUT = [
    "output", "joined_grad", "skip_grad", "qkv_grad", "out_grad", "up_grad",
    "down_grad", "mod_grad", "sums_out", "times_full",
]
BACK_SCRATCH = [
    "wide", "weights", "middle", "total", "back", "normed2",
    "normed2_rows", "act_rows", "gcot", "gup", "gbranch", "xact",
    "xmix", "xn2", "xnormed", "xjoined", "mixed_grad", "got",
    "keys", "values", "kv_sums", "grads_out", "got_grads", "pack",
    "pack_full", "tiles", "tiles_full", "time_tile", "weight_sems", "row_sems", "act_sems",
    "cot_sems", "up_sems", "branch_sems", "late_sems", "s1", "r1",
    "o1", "s2", "r2", "o2", "s3", "r3",
    "s4", "r4", "s5", "r5", "own_sems",
]


def back_kernel(depth, shards, *refs):
    names = BACK_IN + BACK_OUT + BACK_SCRATCH
    r = Refs(names, refs)
    rest = list(refs[len(names) :])
    p = Place(depth)
    count = 4 * depth
    devices = 2 * count
    frames, model = r.base.shape
    ff = r.w_up.shape[1]
    half = model // 2
    chunk = 512
    chunks = ff // chunk
    bf = jnp.bfloat16

    barrier = pltpu.get_barrier_semaphore()
    for k in range(1, devices):
        pl.semaphore_signal(barrier, inc=1, device_id=others(p, count, k), device_id_type=MESH)

    def fetch_out(k):
        return pltpu.make_async_copy(r.w_out.at[:, pl.ds(k * chunk, chunk)], r.weights.at[k], r.weight_sems.at[k])

    def fetch_up(k):
        slot = 2 + k % 2
        at = pl.multiple_of(k * chunk, chunk)
        return pltpu.make_async_copy(r.w_up.at[:, pl.ds(at, chunk)], r.weights.at[slot], r.weight_sems.at[slot])

    def fetch_down(k, side):
        slot = 4 + k % 2
        at = pl.multiple_of(k * chunk, chunk)
        return pltpu.make_async_copy(
            r.w_down.at[pl.ds(at, chunk), pl.ds(side * half, half)],
            r.weights.at[slot, pl.ds(side * chunk, chunk)],
            r.weight_sems.at[slot + 2 * side],
        )

    def fetch_qkv(k):
        return pltpu.make_async_copy(r.w_qkv.at[:, pl.ds(k * chunk, chunk)], r.weights.at[k], r.weight_sems.at[k])

    def fetch_skip(k):
        return pltpu.make_async_copy(
            r.w_skip.at[pl.ds((k // 2) * model, model), pl.ds((k % 2) * chunk, chunk)],
            r.weights.at[k],
            r.weight_sems.at[k],
        )

    for k in range(2):
        fetch_out(k).start()
        fetch_up(k).start()
        fetch_down(k, 0).start()
        fetch_down(k, 1).start()
    own_cot = pltpu.make_async_copy(r.cot, r.gcot.at[0], r.own_sems.at[0])
    own_cot.start()
    pl.semaphore_wait(barrier, devices - 1)

    share_cot = Quad(p, r.cot, lambda k: r.gcot.at[k], lambda k: r.cot_sems.at[k])
    share_mixed = QuadRows(p, r.mixed, r.xmix, r.row_sems.at[0])
    share_n2 = QuadRows(p, r.normed2_rows, r.xn2, r.row_sems.at[1])
    share_normed = QuadRows(p, r.normed, r.xnormed, r.row_sems.at[3])
    share_joined = QuadRows(p, r.joined, r.xjoined, r.row_sems.at[4])

    def share_act(c, what):
        pair = chunk // 2
        z = c // 2

        def half(core):
            return r.act_rows.at[c, pl.ds(pl.multiple_of(core * pair, pair), pair)]

        def copy(core, k, to):
            return remote(half(core), r.xact.at[k, z], r.act_sems.at[z, 2 * k - 1], r.act_sems.at[z, 2 * k], to)

        own = pltpu.make_async_copy(half(p.c), r.xact.at[0, z], r.act_sems.at[z, 0])
        mine = p.y == c % 2
        if what == "start":

            @pl.when(mine)
            def _():
                own.start()
                copy(1 - p.c, 1, p.to_core).start()

            @pl.when(p.y != c % 2)
            def _():
                copy(p.c, 2, p.to_y).start()
                copy(1 - p.c, 3, p.to_far).start()

        elif what == "arrived":

            @pl.when(mine)
            def _():
                own.wait()
                copy(1 - p.c, 1, p.to_core).wait_recv()
                copy(p.c, 2, p.to_y).wait_recv()
                copy(1 - p.c, 3, p.to_far).wait_recv()

        else:
            pl.when(mine)(lambda: copy(1 - p.c, 1, p.to_core).wait_send())

            @pl.when(p.y != c % 2)
            def _():
                copy(p.c, 2, p.to_y).wait_send()
                copy(1 - p.c, 3, p.to_far).wait_send()

    share_branch = Quad(p, r.gbranch.at[0], lambda k: r.gbranch.at[k], lambda k: r.branch_sems.at[k])

    def share_up(c):
        return Quad(p, r.gup.at[0, c], lambda k: r.gup.at[k, c], lambda k: r.up_sems.at[c, k])

    def share_late(c):
        return Quad(p, r.gup.at[0, c], lambda k: r.gup.at[k, c], lambda k: r.late_sems.at[c, k])

    share_cot.start()
    share_mixed.start()

    length = r.lengths[p.x]
    position = p.b * frames
    kept = (position + lax.broadcasted_iota(jnp.int32, (frames, 1), 0) < length).astype(jnp.float32)
    kept_row = (position + lax.broadcasted_iota(jnp.int32, (1, frames), 1) < length).astype(jnp.float32)
    a_scale = kept * r.mods[0:1, :]
    f_scale = kept * r.mods[2:3, :]
    f_shift = kept * r.mods[3:4, :]
    mixed = r.mixed[...].reshape(model, frames).T
    for k in range(2):
        fetch_out(k).wait()
        cols = pl.ds(k * chunk, chunk)
        r.middle[:, cols] = r.base[:, cols] + jnp.dot(mixed, r.weights[k], preferred_element_type=jnp.float32)
    hat, rstd = normal(r.middle[...])
    normed2 = (hat * (1.0 + f_scale) + f_shift).astype(bf)
    r.normed2[...] = normed2
    r.normed2_rows[...] = normed2.T.reshape(r.normed2_rows.shape)
    share_n2.start()
    r.total[...] = jnp.zeros_like(r.total)
    r.back[...] = jnp.zeros_like(r.back)
    own_cot.wait()

    @pl.loop(0, chunks)
    def _(c):
        fetch_up(c).wait()
        fetch_down(c, 0).wait()
        fetch_down(c, 1).wait()
        up, down = r.weights.at[2 + c % 2], r.weights.at[4 + c % 2]
        here = pl.ds(pl.multiple_of(c * chunk, chunk), chunk)
        inner = jnp.dot(r.normed2[...], up[...], preferred_element_type=jnp.float32) + r.b_up[:, here]
        cdf = 0.5 * (1.0 + lax.erf(inner * (0.5**0.5)))
        act = (inner * cdf).astype(bf)
        slope = cdf + inner * (jnp.exp(-0.5 * inner * inner) * (1.0 / math.sqrt(2.0 * math.pi)))
        act_grad = nt(r.gcot[0, :, :half], down[:chunk, :]) + nt(r.gcot[0, :, half:], down[chunk:, :])
        inner_grad = (act_grad * slope).astype(bf)
        r.gup[0, c] = inner_grad
        rows = chunk // 4
        r.act_rows[c] = act.T
        share_act(c, "start")
        r.total[:, :half] += jnp.dot(act, down[:chunk, :], preferred_element_type=jnp.float32)
        r.total[:, half:] += jnp.dot(act, down[chunk:, :], preferred_element_type=jnp.float32)
        r.back[...] += nt(inner_grad, up[...])
        bias = jnp.sum(inner_grad.astype(jnp.float32), 0, keepdims=True)
        for k in range(4):
            r.tiles[c * 4 + k, 0:1, :] = bias[:, k * rows : (k + 1) * rows]

        @pl.when(c + 2 < chunks)
        def _():
            fetch_up(c + 2).start()
            fetch_down(c + 2, 0).start()
            fetch_down(c + 2, 1).start()

    middle = r.middle[...]
    r.output[...] = (middle + r.total[...] + r.b_down[...]).astype(bf)
    hat, rstd = normal(middle)
    grad = r.back[...]
    cot = r.gcot[0].astype(jnp.float32)
    middle_grad = cot + normal_back(grad, hat, rstd, f_scale)
    r.middle[...] = middle_grad
    branch_grad = middle_grad.astype(bf)
    r.gbranch[0] = branch_grad
    there = Exchange(p, count, r.mixed_grad, r.got, r.s1, r.r1, r.o1)
    back = Exchange(p, count, r.grads_out, r.got_grads, r.s2, r.r2, r.o2)
    mixed_grad = nt(r.weights[0], branch_grad[:, :half]) + nt(r.weights[1], branch_grad[:, half:])
    r.mixed_grad[...] = (mixed_grad.astype(bf) * kept_row.astype(bf)).reshape(r.mixed_grad.shape)
    there.start()
    for c in range(6):
        share_up(c).start()
    for k in range(6):
        fetch_qkv(k).start()
    f_scale_grad = jnp.sum(kept * grad * hat, 0, keepdims=True)
    f_shift_grad = jnp.sum(kept * grad, 0, keepdims=True)
    r.pack[:, 256:384] = fold(f_scale_grad)
    r.pack[:, 384:512] = fold(f_shift_grad)

    def columns_of(ref):
        def take(j):
            here = pl.ds(pl.multiple_of(j * chunk, chunk), chunk)
            return jnp.concatenate([ref[k, :, here] for k in range(4)], 0)

        return take

    def blocks_of(first):
        return lambda j: jnp.concatenate([r.gup[k, first + j] for k in range(4)], 0)

    sums = {}
    given = (
        ("up", r.xn2, blocks_of(0), r.up_grad),
        ("down", r.xact, columns_of(r.gcot), r.down_grad),
        ("out", r.xmix, columns_of(r.gbranch), r.out_grad),
        ("qkv", r.xnormed, blocks_of(0), r.qkv_grad),
        ("skip", r.xjoined, blocks_of(chunks), r.skip_grad),
    )
    full = {}
    for (name, x, take, out), (rows, cols, parts) in zip(given, shards):
        width = cols // parts
        sums[name] = []
        for k in range(parts):
            if name in ("up", "down", "out"):
                full[name, k] = rest.pop(0)
            mine = full[{"qkv": "up", "skip": "down"}.get(name, name), k]
            sums[name].append(Reduce(p, x, take, rows, k * width, width, out, mine, *rest[:4]))
            rest = rest[4:]
    up, down, out, qkv, skip = (sums[name] for name in ("up", "down", "out", "qkv", "skip"))

    def ready(shares):
        for share in shares:
            if isinstance(share, Quad):
                share.relay()
        for share in shares:
            share.arrived()

    blocks = 2048 // 256
    attend_back_open(p, r.lengths, r.qkv, r.keys, r.values, r.kv_sums)
    for c in range(chunks):
        share_act(c, "arrived")
    ready([share_cot])
    down[0].begin()
    down[1].begin()
    there.arrived()
    attend = functools.partial(
        attend_back, r.got, r.qkv, r.lse, r.plain, r.keys, r.values, r.kv_sums, r.grads_out, 256
    )
    attend(0, blocks // 2)
    ready([share_n2, share_up(0), share_up(1)])
    up[0].begin()
    down[0].hop(0)
    attend(blocks // 2, blocks)
    attend_back_close(r.kv_sums, r.grads_out)
    ready([share_up(2), share_up(3)])
    up[1].begin()
    ready([share_up(4), share_up(5)])
    up[2].begin()
    for c in range(6):
        share_up(c).finish()
    back.start()
    share_up(6).start()
    share_up(7).start()
    share_branch.start()
    share_normed.start()
    share_joined.start()
    down[0].hop(1)
    down[1].hop(0)
    up[0].hop(0)
    down[0].hop(2)
    down[1].hop(1)
    up[1].hop(0)
    ready([share_up(6), share_up(7)])
    up[3].begin()
    up[0].hop(1)
    down[0].end()
    down[1].hop(2)

    back.arrived()

    def unturned(at):
        h = r.got_grads[:, at : at + HEAD_DIM, :].astype(jnp.float32)
        first, second = h[:, : HEAD_DIM // 2, :], h[:, HEAD_DIM // 2 :, :]
        cosine, sine = r.cosine[...][None], r.sine[...][None]
        h = jnp.concatenate([first * cosine + second * sine, second * cosine - first * sine], 1)
        return h.astype(bf)

    for part in range(3):
        if part < 2:
            h = unturned(part * HEAD_DIM)
        else:
            h = r.got_grads[:, 2 * HEAD_DIM :, :]
        h = h.reshape(model, frames).T
        for k in range(2):
            r.gup[0, 2 * part + k] = h[:, k * chunk : (k + 1) * chunk]
            share_late(2 * part + k).start()
    for k in range(6):
        fetch_qkv(k).wait()
        made = nt(r.gup[0, k], r.weights[k])
        if k == 0:
            r.back[...] = made
        else:
            r.back[...] += made
    for k in range(4):
        fetch_skip(k).start()
    hat, rstd = normal(r.base[...])
    grad = r.back[...]
    base_grad = (r.middle[...] + normal_back(grad, hat, rstd, a_scale)).astype(bf)
    for k in range(2):
        r.gup[0, chunks + k] = base_grad[:, k * chunk : (k + 1) * chunk]
        share_late(chunks + k).start()
    r.pack[:, 0:128] = fold(jnp.sum(kept * grad * hat, 0, keepdims=True))
    r.pack[:, 128:256] = fold(jnp.sum(kept * grad, 0, keepdims=True))
    bias_down = jnp.sum(cot, 0, keepdims=True)
    bias_skip = jnp.sum(base_grad.astype(jnp.float32), 0, keepdims=True)
    each = model // devices
    for k in range(devices):
        r.tiles[k, 1:2, :each] = bias_down[:, k * each : (k + 1) * each]
        r.tiles[k, 1:2, each : 2 * each] = bias_skip[:, k * each : (k + 1) * each]
    packs = Tiles(p, r.pack, r.pack_full, r.s3, r.r3, False)
    tiles = Tiles(p, r.tiles, r.tiles_full, r.s4, r.r4, True)
    times = Tiles(p, r.time_tile, r.times_full, r.s5, r.r5, False)
    packs.start()
    tiles.start()
    for i in range(2):
        total = None
        for j in range(2):
            fetch_skip(2 * i + j).wait()
            made = nt(r.gup[0, chunks + j], r.weights[2 * i + j])
            total = made if total is None else total + made
        r.joined_grad[i] = total.astype(bf)

    ready([share_mixed, share_branch])
    out[0].begin()
    down[1].end()
    up[0].hop(2)
    up[1].hop(1)
    up[2].hop(0)
    ready([share_normed, share_late(0), share_late(1)])
    up[0].end()
    up[1].hop(2)
    up[2].hop(1)
    up[3].hop(0)
    qkv[0].begin()
    up[1].end()
    up[2].hop(2)
    up[3].hop(1)
    out[0].hop(0)
    ready([share_late(2), share_late(3)])
    qkv[1].begin()
    up[2].end()
    up[3].hop(2)
    out[0].hop(1)
    qkv[0].hop(0)
    ready([share_late(4), share_late(5)])
    qkv[2].begin()
    up[3].end()
    out[0].hop(2)
    qkv[0].hop(1)
    qkv[1].hop(0)
    ready([share_joined, share_late(chunks), share_late(chunks + 1)])
    skip[0].begin()
    skip[1].begin()
    out[0].end()
    qkv[0].hop(2)
    qkv[1].hop(1)
    qkv[2].hop(0)

    packs.arrived()
    rows = [jnp.zeros(r.pack.shape, jnp.float32) for _ in range(2)]
    for k in range(devices):
        rows[k % 2] = rows[k % 2] + r.pack_full[k]
    total = jnp.zeros((8, r.w_mod.shape[0]), jnp.float32)
    columns = r.times[...].T
    share = r.w_mod.shape[0]
    width = model // 8
    for part in range(4):
        for k in range(8):
            values = [rows[s][k : k + 1, part * width : (part + 1) * width] for s in range(2)]
            here = pl.ds(part * model + k * width, width)
            left = extra_rows([*three_terms(values[0]), *three_terms(values[1])], 8, width)
            total = total + nt(left, r.w_mod[:, here])
            r.mod_grad[:, here] = columns[:share, 0:1] * values[0] + columns[:share, 4:5] * values[1]
    first = total[0:1] + total[1:2] + total[2:3]
    second = total[3:4] + total[4:5] + total[5:6]
    made = jnp.concatenate([first, second, jnp.zeros((6, share), jnp.float32)], 0)
    r.time_tile[...] = jnp.concatenate([made, jnp.zeros((8, 128 - share), jnp.float32)], 1)
    times.start()
    qkv[0].end()
    qkv[1].hop(2)
    qkv[2].hop(1)
    skip[0].hop(0)
    skip[1].hop(0)
    tiles.arrived()
    total = r.tiles_full[0]
    for k in range(1, devices):
        total = total + r.tiles_full[k]
    r.sums_out[...] = total
    qkv[1].end()
    qkv[2].hop(2)
    skip[0].hop(1)
    skip[1].hop(1)
    qkv[2].end()
    skip[0].hop(2)
    skip[1].hop(2)
    skip[0].end()
    skip[1].end()
    times.arrived()
    for group in sums.values():
        for one in group:
            one.finish()
    for share in (share_cot, share_mixed, share_n2, share_normed, share_joined, share_branch):
        share.finish()
    for c in range(chunks):
        share_act(c, "sent")
    for c in (6, 7):
        share_up(c).finish()
    for c in [*range(6), chunks, chunks + 1]:
        share_late(c).finish()
    for one in (there, back, packs, tiles, times):
        one.finish()


def in_slices(x, depth):
    return x.reshape(depth, x.shape[0] // depth, x.shape[1])


def back_call(depth, devices, args):
    base, qkv = args["base"], args["qkv"]
    frames, model = base.shape
    count = devices // 2
    ff = args["w_up"].shape[1]
    bf, f32 = jnp.bfloat16, jnp.float32
    share = args["w_mod"].shape[0]
    shards = [
        (model // devices, ff, 4),
        (ff // devices, model, 2),
        (model // devices, model, 1),
        (model // devices, 3 * model, 3),
        (2 * model // devices, model, 2),
    ]
    sum_scratch = []
    for which, (rows, cols, parts) in enumerate(shards):
        for _ in range(parts):
            if which < 3:
                sum_scratch.append(pltpu.VMEM((depth * rows, cols // parts), f32))
            sum_scratch += Reduce.scratch(rows, cols // parts, depth)
    chunks = ff // 512
    dma = pltpu.SemaphoreType.DMA

    def rows(n):
        return pltpu.VMEM((4, depth, n // (4 * depth), frames), bf)

    scratch = dict(
        wide=pltpu.VMEM((8, 128), f32),
        weights=pltpu.VMEM((6, model, 512), bf),
        middle=pltpu.VMEM((frames, model), f32),
        total=pltpu.VMEM((frames, model), f32),
        back=pltpu.VMEM((frames, model), f32),
        normed2=pltpu.VMEM((frames, model), bf),
        normed2_rows=pltpu.VMEM((depth, model // depth, frames), bf),
        act_rows=pltpu.VMEM((chunks, 512, frames), bf),
        gcot=pltpu.VMEM((4, frames, model), bf),
        gup=pltpu.VMEM((4, chunks + 2, frames, 512), bf),
        gbranch=pltpu.VMEM((4, frames, model), bf),
        xact=rows(ff),
        xmix=rows(model),
        xn2=rows(model),
        xnormed=rows(model),
        xjoined=rows(2 * model),
        mixed_grad=pltpu.VMEM((count, HEAD_DIM, frames), bf),
        got=pltpu.VMEM((count, HEAD_DIM, frames), bf),
        keys=pltpu.VMEM((qkv.shape[1], 2 * HEAD_DIM), bf),
        values=pltpu.VMEM((qkv.shape[1], 2 * HEAD_DIM), bf),
        kv_sums=pltpu.VMEM((qkv.shape[1], 2 * HEAD_DIM), f32),
        grads_out=pltpu.VMEM((count, 3 * HEAD_DIM, frames), bf),
        got_grads=pltpu.VMEM((count, 3 * HEAD_DIM, frames), bf),
        pack=pltpu.VMEM((8, 512), f32),
        pack_full=pltpu.VMEM((devices, 8, 512), f32),
        tiles=pltpu.VMEM((devices, 8, 128), f32),
        tiles_full=pltpu.VMEM((devices, 8, 128), f32),
        time_tile=pltpu.VMEM((8, 128), f32),
        weight_sems=dma((8,)),
        row_sems=dma((5, 7)),
        act_sems=dma((depth, 7)),
        cot_sems=dma((6,)),
        up_sems=dma((chunks, 6)),
        branch_sems=dma((6,)),
        late_sems=dma((chunks + 2, 6)),
        s1=dma((count,)),
        r1=dma((count,)),
        o1=dma,
        s2=dma((count,)),
        r2=dma((count,)),
        o2=dma,
        s3=dma((devices,)),
        r3=dma((devices,)),
        s4=dma((devices,)),
        r4=dma((devices,)),
        s5=dma((devices,)),
        r5=dma((devices,)),
        own_sems=dma((1,)),
    )
    shape = jax.ShapeDtypeStruct
    outs = dict(
        output=shape((frames, model), bf),
        joined_grad=shape((2, frames, model), bf),
        skip_grad=shape((2 * model // devices, model), f32),
        qkv_grad=shape((model // devices, 3 * model), f32),
        out_grad=shape((model // devices, model), f32),
        up_grad=shape((model // devices, ff), f32),
        down_grad=shape((ff // devices, model), f32),
        mod_grad=shape((share, 4 * model), f32),
        sums_out=shape((8, 128), f32),
        times_full=shape((devices, 8, 128), f32),
    )
    made = pl.pallas_call(
        functools.partial(back_kernel, depth, shards),
        name="back",
        out_shape=[outs[name] for name in BACK_OUT],
        in_specs=[pl.BlockSpec(memory_space=pltpu.SMEM)] + in_vmem(11) + in_any(1) + in_vmem(1) + in_any(7),
        out_specs=in_vmem(len(BACK_OUT)),
        scratch_shapes=[scratch[name] for name in BACK_SCRATCH] + sum_scratch,
        compiler_params=kernel_params(3),
    )(*[args[name] for name in BACK_IN])
    return dict(zip(BACK_OUT, made))


FRONT_IN = (
    ["lengths", "time_row", "b_skip", "b_up_part", "b_down_part", "w_mod", "cosine", "sine", "hidden", "skip_in"]
    + ["w_skip", "w_qkv", "w_out", "w_up", "w_down"]
)
FRONT_OUT = (
    ["skip_full", "qkv_full", "out_full", "up_full", "down_full", "mixed"]
    + ["times", "mods", "b_up", "b_down", "base", "normed", "joined", "qkv", "lse", "plain"]
)
FRONT_SCRATCH = (
    ["own_time", "other_time", "got_time", "pack", "pack_full", "skip_here", "qkv_here", "heads_in", "got", "keys", "values", "mixed_out"]
    + ["time_sems", "load_sems", "own_sems", "sends", "recvs", "s1", "r1", "o1", "s2", "r2", "o2"]
)


class Refs:
    def __init__(self, names, refs):
        for name, ref in zip(names, refs):
            setattr(self, name, ref)


def front_kernel(depth, cuts, *refs):
    r = Refs(FRONT_IN + FRONT_OUT + FRONT_SCRATCH, refs)
    p = Place(depth)
    count = 4 * depth
    devices = 2 * count
    frames, model = r.hidden.shape
    bf = jnp.bfloat16
    share = r.w_mod.shape[0]
    tile = pl.ds(pl.multiple_of((p.b // 2) * 128, 128), 128)
    part = r.time_row[:, tile].astype(jnp.float32)
    mark = lax.broadcasted_iota(jnp.int32, (8, 128), 0) // 4 == p.x
    for ref, x in ((r.own_time, p.x), (r.other_time, 1 - p.x)):
        slot = p.c * 2 + x
        picked = part[:, 0:share]
        for k in range(1, 4):
            picked = jnp.where(slot == k, part[:, k * share : (k + 1) * share], picked)
        picked = jnp.concatenate([picked, jnp.zeros((1, 128 - share), jnp.float32)], 1)
        ref[...] = jnp.where(mark, picked, 0.0)
    greet_plane(p, count)
    ask = remote(r.other_time, r.got_time, r.time_sems.at[0], r.time_sems.at[1], p.to_x)
    ask.start()

    groups = {}
    number = 0
    owns = []
    for name, src, dst in (
        ("skip", r.w_skip, r.skip_full),
        ("qkv", r.w_qkv, r.qkv_full),
        ("out", r.w_out, r.out_full),
        ("up", r.w_up, r.up_full),
        ("down", r.w_down, r.down_full),
    ):
        groups[name] = []
        for lo, hi, first in ranges(src.shape[1], src.shape[1] // cuts[name] if cuts[name] else 0):
            groups[name].append(
                Gather(p, src, dst, src.shape[0], lo, hi, True, first, r.sends.at[number], r.recvs.at[number])
            )
            number += 1
        owns.append((src, dst, src.shape[0]))
    packs = Gather(
        p, r.pack, r.pack_full, 8, 0, r.pack.shape[1], False, False, r.sends.at[number], r.recvs.at[number]
    )
    number += 1
    there = Exchange(p, count, r.heads_in, r.got, r.s1, r.r1, r.o1)
    back = Exchange(p, count, r.mixed_out, r.mixed, r.s2, r.r2, r.o2)

    def products():
        ask.wait_recv()
        both = r.own_time[...] + r.got_time[...]
        r.times[...] = both
        left = both[:, : r.w_mod.shape[0]].astype(bf)
        row = lax.broadcasted_iota(jnp.int32, (8, model), 0) % 4
        total = jnp.zeros((8, model), jnp.float32)
        for part in range(4):
            made = jnp.dot(
                left, r.w_mod[:, part * model : (part + 1) * model], preferred_element_type=jnp.float32
            )
            total = jnp.where(row == part, made, total)
        r.pack[:, :model] = total
        each = r.b_skip.shape[1]
        r.pack[:, model:] = jnp.zeros((8, 128), jnp.float32)
        r.pack[0:1, model:] = r.b_up_part[...].astype(jnp.float32)
        r.pack[1:2, model : model + each] = r.b_skip[...].astype(jnp.float32)
        r.pack[1:2, model + each : model + 2 * each] = r.b_down_part[...].astype(jnp.float32)

    def turned_inputs():
        half = depth // 2
        rows = 2 * model // depth
        for k, ref in enumerate((r.hidden, r.skip_in)):
            r.joined[k * half : (k + 1) * half] = ref[...].T.reshape(half, rows, frames)

    def load_skip():
        return pltpu.make_async_copy(r.skip_full, r.skip_here, r.load_sems.at[0])

    def load_qkv():
        return pltpu.make_async_copy(r.qkv_full, r.qkv_here, r.load_sems.at[1])

    own_copies = []

    def complete(name):
        for g in groups[name]:
            g.shared()

    def begin_loads():
        own_copies[0].wait()
        complete("skip")
        load_skip().start()
        own_copies[1].wait()
        complete("qkv")
        load_qkv().start()

    def first_norm():
        at = pl.multiple_of(p.shard(p.z, p.y, p.c, p.x) * 8, 8)
        r.pack_full[pl.ds(at, 8), :] = r.pack[...]
        packs.shared()
        total = r.pack_full[0:8, :model]
        for k in range(1, devices):
            total = total + r.pack_full[k * 8 : (k + 1) * 8, :model]
        mods = jnp.where(p.x == 0, total[0:4], total[4:8])
        r.mods[0:4, :] = mods
        r.mods[4:8, :] = mods
        each = model // devices
        tiles = [r.pack_full[k * 8 : k * 8 + 2, model:] for k in range(devices)]
        for k in range(devices):
            r.b_up[:, k * 128 : (k + 1) * 128] = tiles[k][0:1]
        b_skip = jnp.concatenate([t[1:2, :each] for t in tiles], 1)
        r.b_down[...] = jnp.concatenate([t[1:2, each : 2 * each] for t in tiles], 1)
        length = r.lengths[p.x]
        kept = (p.b * frames + lax.broadcasted_iota(jnp.int32, (frames, 1), 0) < length).astype(jnp.float32)
        load_skip().wait()
        base = jnp.dot(r.hidden[...], r.skip_here[:model, :], preferred_element_type=jnp.float32)
        base = base + jnp.dot(r.skip_in[...], r.skip_here[model:, :], preferred_element_type=jnp.float32) + b_skip
        r.base[...] = base
        hat, _ = normal(base)
        normed = (hat * (1.0 + kept * mods[0:1]) + kept * mods[1:2]).astype(bf)
        r.normed[...] = normed.T.reshape(r.normed.shape)
        load_qkv().wait()
        cosine, sine = r.cosine[...][None], r.sine[...][None]
        for part in range(3):
            made = jnp.dot(
                normed, r.qkv_here[:, part * model : (part + 1) * model], preferred_element_type=jnp.float32
            )
            made = made.T.reshape(HEADS, HEAD_DIM, frames)
            if part < 2:
                made = turn(made, cosine, sine)
            r.heads_in[:, part * HEAD_DIM : (part + 1) * HEAD_DIM, :] = made.astype(bf)
        there.start()

    def attention(lo, hi):
        attend(p, r.lengths, r.got, r.qkv, r.keys, r.values, r.mixed_out, r.lse, r.plain, 256, lo, hi)

    blocks = 2048 // 256

    def first_half():
        there.arrived()
        attend_open(p, r.lengths, r.got, r.qkv, r.keys, r.values)
        attention(0, blocks // 2)

    def second_half():
        attention(blocks // 2, blocks)
        back.start()

    events = []
    for k, name in enumerate(("skip", "qkv")):
        events += [(t, k, f) for g in groups[name] for t, f in g.steps()]
    events.append((0.3, 0, products))
    events.append((0.35, 0, turned_inputs))
    events += [(t + 0.5, 9, f) for t, f in packs.steps()]
    for k, name in enumerate(("out", "up", "down")):
        for g in groups[name]:
            events += [((4.05 if t == 0 else 4.7 + t), k + 2, f) for t, f in g.steps()]
    events.append((5.6, 0, begin_loads))
    events.append((5.65, 0, first_norm))
    events.append((6.9, 0, first_half))
    events.append((7.9, 0, second_half))
    events.sort(key=lambda e: (e[0], e[1]))
    own_copies += keep_own(p, owns, r.own_sems)
    play([f for _, _, f in events])
    for name in ("out", "up", "down"):
        complete(name)
    for group in groups.values():
        for g in group:
            g.sent()
    packs.sent()
    there.finish()
    back.arrived()
    back.finish()
    for copy in own_copies[2:]:
        copy.wait()
    ask.wait_send()


def front_call(depth, devices, args):
    cuts = dict(skip=4, qkv=4, out=8, up=8, down=8)
    frames, model = args["hidden"].shape
    bf, f32 = jnp.bfloat16, jnp.float32
    count = devices // 2
    total = count * frames
    shape = jax.ShapeDtypeStruct

    def whole(name):
        rows, cols = args[name].shape
        return shape((devices * rows, cols), bf)

    outs = dict(
        skip_full=whole("w_skip"),
        qkv_full=whole("w_qkv"),
        out_full=whole("w_out"),
        up_full=whole("w_up"),
        down_full=whole("w_down"),
        mixed=shape((count, HEAD_DIM, frames), bf),
        times=shape((8, 128), f32),
        mods=shape((8, model), f32),
        b_up=shape((1, 4 * model), f32),
        b_down=shape((1, model), f32),
        base=shape((frames, model), f32),
        normed=shape((depth, model // depth, frames), bf),
        joined=shape((depth, 2 * model // depth, frames), bf),
        qkv=shape((3 * HEAD_DIM, total), bf),
        lse=shape((1, total), f32),
        plain=shape((HEAD_DIM, total), f32),
    )
    dma = pltpu.SemaphoreType.DMA
    gathers = 11
    scratch = dict(
        own_time=pltpu.VMEM((8, 128), f32),
        other_time=pltpu.VMEM((8, 128), f32),
        got_time=pltpu.VMEM((8, 128), f32),
        pack=pltpu.VMEM((8, model + 128), f32),
        pack_full=pltpu.VMEM((devices * 8, model + 128), f32),
        skip_here=pltpu.VMEM((2 * model, model), bf),
        qkv_here=pltpu.VMEM((model, 3 * model), bf),
        heads_in=pltpu.VMEM((count, 3 * HEAD_DIM, frames), bf),
        got=pltpu.VMEM((count, 3 * HEAD_DIM, frames), bf),
        keys=pltpu.VMEM((total, 2 * HEAD_DIM), bf),
        values=pltpu.VMEM((HEAD_DIM + 16, total), bf),
        mixed_out=pltpu.VMEM((count, HEAD_DIM, frames), bf),
        time_sems=dma((2,)),
        load_sems=dma((2,)),
        own_sems=dma((5,)),
        sends=dma((gathers, Gather.SENDS)),
        recvs=dma((gathers, Gather.RECVS)),
        s1=dma((count,)),
        r1=dma((count,)),
        o1=dma,
        s2=dma((count,)),
        r2=dma((count,)),
        o2=dma,
    )
    made = pl.pallas_call(
        functools.partial(front_kernel, depth, cuts),
        name="front",
        out_shape=[outs[name] for name in FRONT_OUT],
        in_specs=[pl.BlockSpec(memory_space=pltpu.SMEM)] + in_vmem(14),
        out_specs=in_any(6) + in_vmem(10),
        scratch_shapes=[scratch[name] for name in FRONT_SCRATCH],
        compiler_params=kernel_params(1),
    )(*[args[name] for name in FRONT_IN])
    return dict(zip(FRONT_OUT, made))


def write_kernel(count, times, sums, joined, *refs):
    ins, outs = refs[:count], refs[count:]
    for src, dst in zip(ins, outs):
        dst[...] = src[...]
    hidden_grad, skip_grad, time_grad, b_up, b_skip, b_down = outs[count:]
    hidden_grad[...] = joined[0]
    skip_grad[...] = joined[1]
    each = b_skip.shape[1]
    part = jnp.where(lax.axis_index("uly") == 0, times[:, 0, :each], times[:, 1, :each])
    time_grad[...] = jnp.concatenate([part[k : k + 1] for k in range(times.shape[0])], 1)
    b_up[...] = sums[0:1, :]
    b_down[...] = sums[1:2, :each]
    b_skip[...] = sums[1:2, each : 2 * each]


def write_call(made, names, each):
    shape = jax.ShapeDtypeStruct
    joined = made["joined_grad"]
    frames, model = joined.shape[1:]
    plain = [shape(made[name].shape, made[name].dtype) for name in names]
    return pl.pallas_call(
        functools.partial(write_kernel, len(names)),
        name="write",
        out_shape=plain
        + [shape((frames, model), joined.dtype)] * 2
        + [shape((1, model), jnp.float32), shape((1, 128), jnp.float32)]
        + [shape((1, each), jnp.float32)] * 2,
        in_specs=in_vmem(3 + len(names)),
        out_specs=in_vmem(6 + len(names)),
        compiler_params=pltpu.CompilerParams(vmem_limit_bytes=VMEM_BYTES),
    )(made["times_full"], made["sums_out"], joined, *[made[name] for name in names])


def first_with_second(left, right, dims):
    return lax.dot_general(left, right, ((dims[:1], dims[1:]), ((), ())), preferred_element_type=jnp.float32)


def turn(values, cosine, sine):
    half = HEAD_DIM // 2
    first, second = values[..., :half, :], values[..., half:, :]
    return jnp.concatenate([first * cosine - second * sine, second * cosine + first * sine], -2)


def on_device(hidden, skip_in, time_embed, lengths, cotangent, w_skip, b_skip, w_mod, w_qkv, w_out, w_up, b_up,
              w_down, b_down):
    block, row = lax.axis_index("blk"), lax.axis_index("uly")
    blocks, rows = lax.axis_size("blk"), lax.axis_size("uly")
    devices, depth = blocks * rows, blocks // 4
    _, frames, model = hidden.shape
    position = block * frames + jnp.arange(frames, dtype=jnp.int32)
    length = lax.dynamic_index_in_dim(lengths, row, 0, keepdims=False)[0]
    valid = position < length
    half = HEAD_DIM // 2
    freq = 10000.0 ** (-jnp.arange(half, dtype=jnp.float32) / half)
    offsets = jnp.where(valid, position, position - length).astype(jnp.float32)
    angle = freq[:, None] * offsets[None, :]
    cosine, sine = jnp.cos(angle), jnp.sin(angle)
    front = front_call(
        depth,
        devices,
        dict(
            lengths=lengths[:, 0],
            time_row=time_embed[0],
            b_skip=b_skip[None],
            b_up_part=b_up[None],
            b_down_part=b_down[None],
            w_mod=w_mod,
            cosine=cosine,
            sine=sine,
            hidden=hidden[0],
            skip_in=skip_in[0],
            w_skip=w_skip,
            w_qkv=w_qkv,
            w_out=w_out,
            w_up=w_up,
            w_down=w_down,
        ),
    )
    made = back_call(
        depth,
        devices,
        dict(
            lengths=lengths[:, 0],
            base=front["base"],
            mods=front["mods"],
            b_up=front["b_up"],
            b_down=front["b_down"],
            cosine=cosine,
            sine=sine,
            w_mod=w_mod,
            times=front["times"],
            qkv=front["qkv"],
            lse=front["lse"],
            plain=front["plain"],
            cot=cotangent[0],
            mixed=front["mixed"].reshape(depth, model // depth, frames),
            joined=front["joined"],
            normed=front["normed"],
            w_out=front["out_full"],
            w_up=front["up_full"],
            w_down=front["down_full"],
            w_qkv=front["qkv_full"],
            w_skip=front["skip_full"],
        ),
    )
    names = ["output", "skip_grad", "mod_grad", "qkv_grad", "out_grad", "up_grad", "down_grad"]
    output, skip_grad, mod_grad, qkv_grad, out_grad, up_grad, down_grad, *small = write_call(
        made, names, b_skip.shape[0]
    )
    hidden_grad, skip_in_grad, time_grad, b_up_grad, b_skip_grad, b_down_grad = small
    return (
        output[None],
        hidden_grad[None],
        skip_in_grad[None],
        time_grad[None],
        skip_grad,
        b_skip_grad[0],
        mod_grad,
        qkv_grad,
        out_grad,
        up_grad,
        b_up_grad[0],
        down_grad,
        b_down_grad[0],
    )


def solution(mesh):
    placed = (
        P("uly", "blk", None),
        P("uly", "blk", None),
        P("uly", None, None),
        P(),
        P("uly", "blk", None),
        P(("blk", "uly"), None),
        P(("blk", "uly")),
        P(("blk", "uly"), None),
        P(("blk", "uly"), None),
        P(("blk", "uly"), None),
        P(("blk", "uly"), None),
        P(("blk", "uly")),
        P(("blk", "uly"), None),
        P(("blk", "uly")),
    )
    blocks = mesh.shape["blk"]
    special = mesh.shape["uly"] == 2 and blocks == HEADS and blocks % 4 == 0 and blocks > 4
    return jax.shard_map(
        on_device if special else per_device,
        mesh=mesh,
        in_specs=placed,
        out_specs=(
            P("uly", "blk", None),
            P("uly", "blk", None),
            P("uly", "blk", None),
            P("uly", None, None),
            P(("blk", "uly"), None),
            P(("blk", "uly")),
            P(("blk", "uly"), None),
            P(("blk", "uly"), None),
            P(("blk", "uly"), None),
            P(("blk", "uly"), None),
            P(("blk", "uly")),
            P(("blk", "uly"), None),
            P(("blk", "uly")),
        ),
        check_vma=False,
    )
```

```python
import functools
import math

import jax
import jax.numpy as jnp
from jax import lax
from jax.experimental import pallas as pl
from jax.experimental.pallas import tpu as pltpu
from jax.sharding import PartitionSpec as P

HEADS = 16
HEAD_DIM = 64


exact_mode = lax.Precision.HIGHEST
epsilon = 1e-05


def passed_along(x, axis, by):
    devices = lax.axis_size(axis)
    return lax.ppermute(x, axis, [(i, (i + by) % devices) for i in range(devices)])


def segment_info(len_row, positions):
    slots = len_row.shape[0]
    ends = jnp.cumsum(len_row)
    starts = ends - len_row
    total = ends[-1]
    seg_ids = jnp.sum((positions[:, None] >= ends[None, :]).astype(jnp.int32), axis=1)
    onehot = seg_ids[:, None] == jnp.arange(slots, dtype=jnp.int32)[None, :]
    begin = jnp.sum(jnp.where(onehot, starts[None, :], 0), axis=1)
    begin = begin + jnp.where(seg_ids == slots, total, 0)
    return (seg_ids, positions - begin, seg_ids < slots)


def rotary(values, offsets):
    half = values.shape[-1] // 2
    freq = 10000.0 ** (-jnp.arange(half, dtype=jnp.float32) / half)
    angle = offsets.astype(jnp.float32)[:, None] * freq[None, :]
    cosine = jnp.cos(angle)[:, None, :]
    sine = jnp.sin(angle)[:, None, :]
    first = values[..., :half]
    second = values[..., half:]
    return jnp.concatenate([first * cosine - second * sine, second * cosine + first * sine], -1)


def modulate(values, scale, shift):
    center = values - jnp.mean(values, -1, keepdims=True)
    spread = jnp.mean(center * center, -1, keepdims=True)
    return center * lax.rsqrt(spread + epsilon) * (1.0 + scale) + shift


def contract_rows(left, right):
    return lax.dot_general(
        left, right, (((0,), (0,)), ((), ())), preferred_element_type=jnp.float32
    )


def contract_cols(left, right):
    return lax.dot_general(
        left, right, (((1,), (1,)), ((), ())), preferred_element_type=jnp.float32
    )


def gelu_exact(values):
    return jax.nn.gelu(values, approximate=False)


def per_device(
    hidden,
    skip_in,
    time_embed,
    lengths,
    cotangent,
    w_skip,
    b_skip,
    w_mod,
    w_qkv,
    w_out,
    w_up,
    b_up,
    w_down,
    b_down,
):
    gathered = (
        lax.all_gather(w_skip, ("blk", "uly"), axis=0, tiled=True),
        lax.all_gather(b_skip, ("blk", "uly"), axis=0, tiled=True),
        lax.all_gather(w_mod, ("blk", "uly"), axis=0, tiled=True),
        lax.all_gather(w_qkv, ("blk", "uly"), axis=0, tiled=True),
        lax.all_gather(w_out, ("blk", "uly"), axis=0, tiled=True),
        lax.all_gather(w_up, ("blk", "uly"), axis=0, tiled=True),
        lax.all_gather(b_up, ("blk", "uly"), axis=0, tiled=True),
        lax.all_gather(w_down, ("blk", "uly"), axis=0, tiled=True),
        lax.all_gather(b_down, ("blk", "uly"), axis=0, tiled=True),
    )
    (
        skip_full,
        bskip_full,
        mod_full,
        qkv_full,
        out_full,
        up_full,
        bup_full,
        down_full,
        bdown_full,
    ) = gathered
    group_count = lax.axis_size("uly")
    cycle_size = lax.axis_size("blk")
    frame_count = hidden.shape[1]
    row_count = lengths.shape[0]
    slot_count = lengths.shape[1]
    local_heads = HEADS // group_count
    span = local_heads * HEAD_DIM
    scaling = HEAD_DIM ** (-0.5)
    block_index = lax.axis_index("blk")
    row_index = lax.axis_index("uly")
    frame_pos = block_index * frame_count + jnp.arange(frame_count, dtype=jnp.int32)
    all_seg, all_offsets, all_valid = jax.vmap(lambda len_row: segment_info(len_row, frame_pos))(
        lengths
    )
    own_seg = lax.dynamic_index_in_dim(all_seg, row_index, 0, keepdims=False)
    own_offsets = lax.dynamic_index_in_dim(all_offsets, row_index, 0, keepdims=False)
    joined = jnp.concatenate([hidden[0], skip_in[0]], 1)
    base = jnp.dot(joined, skip_full, preferred_element_type=jnp.float32) + bskip_full.astype(
        jnp.float32
    )
    time_row = time_embed[0]
    mods = jnp.dot(time_row, mod_full, preferred_element_type=jnp.float32)
    selector = (own_seg[:, None] == jnp.arange(slot_count, dtype=jnp.int32)[None, :]).astype(
        jnp.float32
    )
    frame_mod = jnp.dot(selector, mods, precision=exact_mode)
    a_scale, a_shift, f_scale, f_shift = jnp.split(frame_mod, 4, 1)
    normed_full, norm_back = jax.vjp(modulate, base, a_scale, a_shift)
    normed = normed_full.astype(jnp.bfloat16)
    projected = jnp.dot(normed, qkv_full, preferred_element_type=jnp.float32).reshape(
        frame_count, 3, HEADS, HEAD_DIM
    )

    def place(parts):
        return jnp.stack(
            [rotary(parts[:, 0], own_offsets), rotary(parts[:, 1], own_offsets), parts[:, 2]], 1
        )

    turned, unturn = jax.vjp(place, projected)
    sending = turned.astype(jnp.bfloat16).reshape(1, frame_count, 3, group_count, span)
    head_data = lax.all_to_all(sending, "uly", split_axis=3, concat_axis=0, tiled=True)
    query = head_data[:, :, 0, 0].reshape(row_count, frame_count, local_heads, HEAD_DIM)
    kv_pairs = head_data[:, :, 1:, 0]

    def key_segments(start, count):
        key_pos = start + jnp.arange(count, dtype=jnp.int32)
        return jax.vmap(lambda len_row: segment_info(len_row, key_pos)[0])(lengths)

    start_state = (
        jnp.full((row_count, local_heads, frame_count), -1e30, jnp.float32),
        jnp.zeros((row_count, local_heads, frame_count), jnp.float32),
        jnp.zeros((row_count, frame_count, local_heads, HEAD_DIM), jnp.float32),
    )
    piece = lax.all_gather(kv_pairs, "blk", axis=1, tiled=True)
    total = piece.shape[1]
    step = math.gcd(total, max(frame_count, 1024))

    def sub_step(step_index, state):
        run_max, run_total, run_acc = state
        offset = step_index * step
        section = lax.dynamic_slice_in_dim(piece, offset, step, 1)
        key_seg = key_segments(offset, step)
        key_part = section[:, :, 0].reshape(row_count, step, local_heads, HEAD_DIM)
        value_part = section[:, :, 1].reshape(row_count, step, local_heads, HEAD_DIM)
        mask = all_seg[:, None, :, None] == key_seg[:, None, None, :]
        score = (
            jnp.einsum("rqhd,rkhd->rhqk", query, key_part, preferred_element_type=jnp.float32)
            * scaling
        )
        masked = jnp.where(mask, score, -1e30)
        fresh = jnp.maximum(run_max, jnp.max(masked, -1))
        weights = jnp.where(mask, jnp.exp(masked - fresh[..., None]), 0.0)
        decay = jnp.exp(run_max - fresh)
        run_total = run_total * decay + jnp.sum(weights, -1)
        run_acc = run_acc * jnp.swapaxes(decay, 1, 2)[..., None] + jnp.einsum(
            "rhqk,rkhd->rqhd",
            weights.astype(jnp.bfloat16),
            value_part,
            preferred_element_type=jnp.float32,
        )
        return (fresh, run_total, run_acc)

    run_max, run_total, run_acc = lax.fori_loop(0, total // step, sub_step, start_state)
    attended = run_acc / jnp.swapaxes(run_total, 1, 2)[..., None]
    log_total = run_max + jnp.log(run_total)
    valid_half = all_valid.astype(jnp.bfloat16)[:, :, None, None]
    leaving = (attended * all_valid.astype(jnp.float32)[:, :, None, None]).astype(jnp.bfloat16)
    leaving = leaving.reshape(row_count, frame_count, 1, span)
    mixed = lax.all_to_all(leaving, "uly", split_axis=0, concat_axis=2, tiled=True).reshape(
        frame_count, HEADS * HEAD_DIM
    )
    branch = jnp.dot(mixed, out_full, preferred_element_type=jnp.float32)
    middle = base + branch
    normed2_full, norm2_back = jax.vjp(modulate, middle, f_scale, f_shift)
    normed2 = normed2_full.astype(jnp.bfloat16)
    inner = jnp.dot(normed2, up_full, preferred_element_type=jnp.float32) + bup_full.astype(
        jnp.float32
    )
    act_full, act_back = jax.vjp(gelu_exact, inner)
    act = act_full.astype(jnp.bfloat16)
    result = (
        middle
        + jnp.dot(act, down_full, preferred_element_type=jnp.float32)
        + bdown_full.astype(jnp.float32)
    )
    output = result.astype(jnp.bfloat16)[None]
    again = (
        lax.all_gather(w_skip, ("blk", "uly"), axis=0, tiled=True),
        lax.all_gather(w_mod, ("blk", "uly"), axis=0, tiled=True),
        lax.all_gather(w_qkv, ("blk", "uly"), axis=0, tiled=True),
        lax.all_gather(w_out, ("blk", "uly"), axis=0, tiled=True),
        lax.all_gather(w_up, ("blk", "uly"), axis=0, tiled=True),
        lax.all_gather(w_down, ("blk", "uly"), axis=0, tiled=True),
    )
    skip_back, mod_back, qkv_back, out_back, up_back, down_back = again
    upstream = cotangent[0]
    upstream_full = upstream.astype(jnp.float32)
    grad_down = contract_rows(act, upstream)
    grad_bdown = jnp.sum(upstream_full, 0)
    grad_act = contract_cols(upstream, down_back)
    grad_inner = act_back(grad_act)[0].astype(jnp.bfloat16)
    grad_up = contract_rows(normed2, grad_inner)
    grad_bup = jnp.sum(grad_inner.astype(jnp.float32), 0)
    grad_normed2 = contract_cols(grad_inner, up_back)
    grad_mid_norm, grad_fscale, grad_fshift = norm2_back(grad_normed2)
    grad_middle = upstream_full + grad_mid_norm
    grad_branch = grad_middle.astype(jnp.bfloat16)
    grad_out = contract_rows(mixed, grad_branch)
    grad_mixed = (
        contract_cols(grad_branch, out_back)
        .astype(jnp.bfloat16)
        .reshape(1, frame_count, group_count, span)
    )
    returning = lax.all_to_all(grad_mixed, "uly", split_axis=2, concat_axis=0, tiled=True)
    grad_attn = returning.reshape(row_count, frame_count, local_heads, HEAD_DIM) * valid_half
    delta_rows = jnp.swapaxes(jnp.sum(grad_attn.astype(jnp.float32) * attended, -1), 1, 2)

    def contribution(held_pairs, key_start):
        count = held_pairs.shape[1]
        key_seg = key_segments(key_start, count)
        key_part = held_pairs[:, :, 0].reshape(row_count, count, local_heads, HEAD_DIM)
        value_part = held_pairs[:, :, 1].reshape(row_count, count, local_heads, HEAD_DIM)
        mask = all_seg[:, None, :, None] == key_seg[:, None, None, :]
        score = (
            jnp.einsum("rqhd,rkhd->rhqk", query, key_part, preferred_element_type=jnp.float32)
            * scaling
        )
        weights = jnp.exp(jnp.where(mask, score - log_total[..., None], -1e30))
        grad_weights = jnp.einsum(
            "rqhd,rkhd->rhqk", grad_attn, value_part, preferred_element_type=jnp.float32
        )
        grad_score = (weights * (grad_weights - delta_rows[..., None])).astype(jnp.bfloat16)
        more_query = (
            jnp.einsum("rhqk,rkhd->rqhd", grad_score, key_part, preferred_element_type=jnp.float32)
            * scaling
        )
        more_key = (
            jnp.einsum("rhqk,rqhd->rkhd", grad_score, query, preferred_element_type=jnp.float32)
            * scaling
        )
        more_value = jnp.einsum(
            "rhqk,rqhd->rkhd",
            weights.astype(jnp.bfloat16),
            grad_attn,
            preferred_element_type=jnp.float32,
        )
        more_pairs = jnp.stack(
            [more_key.reshape(row_count, count, span), more_value.reshape(row_count, count, span)],
            2,
        )
        return (more_query, more_pairs)

    def pass_grads(held_grads):
        return passed_along(held_grads.astype(jnp.bfloat16), "blk", 1).astype(held_grads.dtype)

    def cycle_step(turn, state):
        held_pairs, held_grads, query_grad = state
        more_query, more_pairs = contribution(
            held_pairs, (block_index - turn) % cycle_size * frame_count
        )
        held_pairs = passed_along(held_pairs, "blk", 1)
        held_grads = pass_grads(held_grads + more_pairs)
        return (held_pairs, held_grads, query_grad + more_query)

    cycle_start = (
        kv_pairs,
        jnp.zeros((row_count, frame_count, 2, span), jnp.float32),
        jnp.zeros((row_count, frame_count, local_heads, HEAD_DIM), jnp.float32),
    )
    held_pairs, held_grads, query_grad = lax.fori_loop(0, cycle_size - 1, cycle_step, cycle_start)
    last_query, last_pairs = contribution(
        held_pairs, (block_index - (cycle_size - 1)) % cycle_size * frame_count
    )
    pair_grads = pass_grads(held_grads + last_pairs)
    query_grad = query_grad + last_query
    head_grads = jnp.concatenate(
        [
            query_grad.astype(jnp.bfloat16).reshape(row_count, frame_count, 1, span),
            pair_grads.astype(jnp.bfloat16),
        ],
        2,
    ).reshape(row_count, frame_count, 3, 1, span)
    frames_grad = lax.all_to_all(head_grads, "uly", split_axis=0, concat_axis=3, tiled=True)
    frames_grad = frames_grad.reshape(frame_count, 3, HEADS, HEAD_DIM).astype(jnp.float32)
    grad_projected = (
        unturn(frames_grad)[0].astype(jnp.bfloat16).reshape(frame_count, 3 * HEADS * HEAD_DIM)
    )
    grad_qkv = contract_rows(normed, grad_projected)
    grad_normed = contract_cols(grad_projected, qkv_back)
    grad_base_norm, grad_ascale, grad_ashift = norm_back(grad_normed)
    grad_base = (grad_middle + grad_base_norm).astype(jnp.bfloat16)
    grad_skip_w = contract_rows(joined, grad_base)
    grad_bskip = jnp.sum(grad_base.astype(jnp.float32), 0)
    grad_joined = contract_cols(grad_base, skip_back).astype(jnp.bfloat16)
    model_width = hidden.shape[2]
    hidden_grad = grad_joined[:, :model_width][None]
    skip_grad = grad_joined[:, model_width:][None]
    frame_mod_grad = jnp.concatenate([grad_ascale, grad_ashift, grad_fscale, grad_fshift], 1)
    slot_grad = lax.dot_general(
        selector, frame_mod_grad, (((0,), (0,)), ((), ())), precision=exact_mode
    )
    grad_mod = lax.dot_general(
        time_row.astype(jnp.float32), slot_grad, (((0,), (0,)), ((), ())), precision=exact_mode
    )
    slot_total = lax.psum(slot_grad, "blk")
    time_grad = lax.dot_general(
        slot_total, mod_back.astype(jnp.float32), (((1,), (1,)), ((), ())), precision=exact_mode
    )[None]
    owned = (
        lax.psum_scatter(grad_skip_w, ("blk", "uly"), scatter_dimension=0, tiled=True),
        lax.psum_scatter(grad_bskip, ("blk", "uly"), scatter_dimension=0, tiled=True),
        lax.psum_scatter(grad_mod, ("blk", "uly"), scatter_dimension=0, tiled=True),
        lax.psum_scatter(grad_qkv, ("blk", "uly"), scatter_dimension=0, tiled=True),
        lax.psum_scatter(grad_out, ("blk", "uly"), scatter_dimension=0, tiled=True),
        lax.psum_scatter(grad_up, ("blk", "uly"), scatter_dimension=0, tiled=True),
        lax.psum_scatter(grad_bup, ("blk", "uly"), scatter_dimension=0, tiled=True),
        lax.psum_scatter(grad_down, ("blk", "uly"), scatter_dimension=0, tiled=True),
        lax.psum_scatter(grad_bdown, ("blk", "uly"), scatter_dimension=0, tiled=True),
    )
    return (
        output,
        hidden_grad,
        skip_grad,
        time_grad,
        owned[0],
        owned[1],
        owned[2],
        owned[3],
        owned[4],
        owned[5],
        owned[6],
        owned[7],
        owned[8],
    )


MESH = pl.DeviceIdType.MESH


class Place:
    def __init__(self, depth):
        self.depth = depth
        self.b = lax.axis_index("blk")
        self.x = lax.axis_index("uly")
        self.z = self.b // 4
        self.y = (self.b // 2) % 2
        self.c = self.b % 2
        self.to_x = (self.b, 1 - self.x)
        self.to_y = (self.b + 2 - 4 * self.y, self.x)
        self.to_core = (self.b + 1 - 2 * self.c, self.x)
        self.to_far = (self.b + 3 - 4 * self.y - 2 * self.c, self.x)
        self.to_across = (self.b + 2 - 4 * self.y, 1 - self.x)
        self.to_far_x = (self.b + 1 - 2 * self.c, 1 - self.x)
        self.to_up = (self.b + 4, self.x)
        self.to_down = (self.b - 4, self.x)

    def shard(self, z, y, c, x):
        return ((z * 2 + y) * 2 + c) * 2 + x

    def greet(self):
        barrier = pltpu.get_barrier_semaphore()
        for to in (self.to_x, self.to_y, self.to_core, self.to_far):
            pl.semaphore_signal(barrier, inc=1, device_id=to, device_id_type=MESH)

        @pl.when(self.z < self.depth - 1)
        def _():
            pl.semaphore_signal(barrier, inc=1, device_id=self.to_up, device_id_type=MESH)

        @pl.when(self.z > 0)
        def _():
            pl.semaphore_signal(barrier, inc=1, device_id=self.to_down, device_id_type=MESH)

        top = self.depth - 1
        pl.semaphore_wait(barrier, 4 + (self.z + top - 1) // top + (2 * top - 1 - self.z) // top)


def remote(src, dst, send, recv, to):
    return pltpu.make_async_remote_copy(
        src_ref=src, dst_ref=dst, send_sem=send, recv_sem=recv, device_id=to, device_id_type=MESH
    )


class Gather:
    SENDS = 64
    RECVS = 48

    def __init__(self, place, src, dst, rows, lo, hi, split, plane_first, sends, recvs):
        self.p, self.src, self.dst, self.rows = place, src, dst, rows
        self.lo, self.hi, self.split, self.plane_first = lo, hi, split, plane_first
        self.sends, self.recvs = sends, recvs
        self.pending = []

    def part(self, z, y, c, x, half=None):
        base = self.p.shard(z, y, c, x) * self.rows
        rows = self.rows
        if half is not None:
            rows = rows // 2
            base = base + half * rows
        return self.dst.at[pl.ds(pl.multiple_of(base, rows), rows), pl.ds(self.lo, self.hi - self.lo)]

    def mine(self):
        return self.src.at[:, pl.ds(self.lo, self.hi - self.lo)]

    def go(self, when, src, dst, send, recv, to):
        def start():
            remote(src, dst, self.sends.at[send], self.recvs.at[recv], to).start()

        def finish():
            remote(src, dst, self.sends.at[send], self.recvs.at[recv], to).wait_send()

        if when is None:
            start()
            self.pending.append(finish)
        else:
            pl.when(when)(start)
            self.pending.append(lambda: pl.when(when)(finish))

    def got(self, dst, recv):
        remote(dst, dst, self.sends.at[0], self.recvs.at[recv], self.p.to_x).wait_recv()

    def share(self, when, src, z, y, x):
        slot = z * 4 + y * 2 + x
        self.go(when, src, self.part(z, y, self.p.c, x), slot, slot, self.p.to_core)

    def steps(self):
        return self.plane_steps() if self.plane_first else self.line_steps()

    def line_steps(self):
        p = self.p
        top = p.depth - 1

        def hand_on(when, src, z):
            whole = self.part(z, p.y, p.c, p.x)
            self.go(when, src, whole, 24 + z, 20 + z, p.to_x)
            self.go(when, src, whole, 28 + z, 24 + z, p.to_y)
            self.share(when, src, z, p.y, p.x)

        def own():
            src = self.mine()
            whole = self.part(p.z, p.y, p.c, p.x)
            self.go(p.z < top, src, whole, 16 + p.z, 16 + p.z, p.to_up)
            self.go(p.z > 0, src, whole, 20 + p.z, 16 + p.z, p.to_down)
            hand_on(None, src, p.z)

        def line(d):
            for side in (-1, 1):
                z = p.z + side * d
                here = (z >= 0) & (z <= top)
                whole = self.part(z, p.y, p.c, p.x)
                pl.when(here)(lambda: self.got(whole, 16 + z))
                if side < 0:
                    self.go(here & (p.z < top), whole, whole, 16 + z, 16 + z, p.to_up)
                else:
                    self.go(here & (p.z > 0), whole, whole, 20 + z, 16 + z, p.to_down)
                hand_on(here, whole, z)

        def origins(d):
            return [(None, p.z)] if d == 0 else [
                ((p.z + s * d >= 0) & (p.z + s * d <= top), p.z + s * d) for s in (-1, 1)
            ]

        def cond(when, f):
            f() if when is None else pl.when(when)(f)

        def cross(d):
            for when, z in origins(d):
                from_x = self.part(z, p.y, p.c, 1 - p.x)
                cond(when, lambda: self.got(from_x, 20 + z))
                self.share(when, from_x, z, p.y, 1 - p.x)
                if self.split:
                    part = self.part(z, p.y, p.c, 1 - p.x, 0)
                else:
                    part = from_x
                self.go(when, part, part, 32 + z, 28 + z, p.to_y)
                from_y = self.part(z, 1 - p.y, p.c, p.x)
                cond(when, lambda: self.got(from_y, 24 + z))
                self.share(when, from_y, z, 1 - p.y, p.x)
                if self.split:
                    part = self.part(z, 1 - p.y, p.c, p.x, 1)
                    self.go(when, part, part, 36 + z, 32 + z, p.to_x)

        def corner(d):
            for when, z in origins(d):
                whole = self.part(z, 1 - p.y, p.c, 1 - p.x)
                if self.split:
                    for half in (0, 1):
                        part = self.part(z, 1 - p.y, p.c, 1 - p.x, half)
                        cond(when, lambda: self.got(part, 28 + 4 * half + z))
                else:
                    cond(when, lambda: self.got(whole, 28 + z))
                self.share(when, whole, z, 1 - p.y, 1 - p.x)

        out = [(0, own)]
        for d in range(p.depth):
            if d:
                out.append((d, functools.partial(line, d)))
            out.append((d + 1, functools.partial(cross, d)))
            out.append((d + 2, functools.partial(corner, d)))
        return out

    def plane_steps(self):
        p = self.p
        top = p.depth - 1

        def along(when, src, z, y, x, up, down):
            slot = 20 + z * 4 + y * 2 + x
            whole = self.part(z, y, p.c, x)
            if up:
                w = p.z < top
                self.go(w if when is None else w & when, src, whole, slot, slot, p.to_up)
            if down:
                w = p.z > 0
                self.go(w if when is None else w & when, src, whole, slot + 16, slot, p.to_down)

        def own():
            src = self.mine()
            whole = self.part(p.z, p.y, p.c, p.x)
            self.go(None, src, whole, 16, 16, p.to_x)
            self.go(None, src, whole, 17, 17, p.to_y)
            along(None, src, p.z, p.y, p.x, True, True)
            self.share(None, src, p.z, p.y, p.x)

        def cross():
            from_x = self.part(p.z, p.y, p.c, 1 - p.x)
            self.got(from_x, 16)
            part = self.part(p.z, p.y, p.c, 1 - p.x, 0) if self.split else from_x
            self.go(None, part, part, 18, 18, p.to_y)
            along(None, from_x, p.z, p.y, 1 - p.x, True, True)
            self.share(None, from_x, p.z, p.y, 1 - p.x)
            from_y = self.part(p.z, 1 - p.y, p.c, p.x)
            self.got(from_y, 17)
            if self.split:
                part = self.part(p.z, 1 - p.y, p.c, p.x, 1)
                self.go(None, part, part, 19, 19, p.to_x)
            along(None, from_y, p.z, 1 - p.y, p.x, True, True)
            self.share(None, from_y, p.z, 1 - p.y, p.x)

        def corner():
            whole = self.part(p.z, 1 - p.y, p.c, 1 - p.x)
            if self.split:
                for half in (0, 1):
                    self.got(self.part(p.z, 1 - p.y, p.c, 1 - p.x, half), 18 + half)
            else:
                self.got(whole, 18)
            along(None, whole, p.z, 1 - p.y, 1 - p.x, True, True)
            self.share(None, whole, p.z, 1 - p.y, 1 - p.x)

        def line(d, k):
            y = p.y if k in (0, 1) else 1 - p.y
            x = p.x if k in (0, 2) else 1 - p.x
            for side in (-1, 1):
                z = p.z + side * d
                here = (z >= 0) & (z <= top)
                whole = self.part(z, y, p.c, x)
                pl.when(here)(lambda: self.got(whole, 20 + z * 4 + y * 2 + x))
                along(here, whole, z, y, x, side < 0, side > 0)
                self.share(here, whole, z, y, x)

        out = [(0, own), (1, cross), (2, corner)]
        for d in range(1, p.depth):
            for k in range(4):
                out.append((d + 0.1 + min(k, 2) * 0.9, functools.partial(line, d, k)))
        return out

    def shared(self):
        p = self.p
        for z in range(p.depth):
            for y in range(2):
                for x in range(2):
                    self.got(self.part(z, y, 1 - p.c, x), z * 4 + y * 2 + x)

    def sent(self):
        for wait in self.pending:
            wait()


class LineGather:
    def __init__(self, place, src, piece, sends, recvs):
        self.p, self.src, self.piece, self.sends, self.recvs = place, src, piece, sends, recvs
        self.pending = []

    def go(self, when, src, dst, send, recv, to):
        def start():
            remote(src, dst, self.sends.at[send], self.recvs.at[recv], to).start()

        def finish():
            remote(src, dst, self.sends.at[send], self.recvs.at[recv], to).wait_send()

        if when is None:
            start()
            self.pending.append(finish)
        else:
            pl.when(when)(start)
            self.pending.append(lambda: pl.when(when)(finish))

    def got(self, dst, recv):
        remote(dst, dst, self.sends.at[0], self.recvs.at[recv], self.p.to_x).wait_recv()

    def own(self):
        p, n = self.p, self.p.depth
        dst = self.piece(p.z, p.c)
        self.go(p.z < n - 1, self.src, dst, p.z, p.z, p.to_up)
        self.go(p.z > 0, self.src, dst, n + p.z, p.z, p.to_down)
        self.go(None, self.src, dst, 2 * n + p.z, n + p.z, p.to_core)

    def line(self, d):
        p, n = self.p, self.p.depth
        for side in (-1, 1):
            z = p.z + side * d
            here = (z >= 0) & (z <= n - 1)
            dst = self.piece(z, p.c)
            pl.when(here)(lambda: self.got(dst, z))
            if side < 0:
                self.go(here & (p.z < n - 1), dst, dst, z, z, p.to_up)
            else:
                self.go(here & (p.z > 0), dst, dst, n + z, z, p.to_down)
            self.go(here, dst, dst, 2 * n + z, n + z, p.to_core)

    def shared(self):
        n = self.p.depth
        for z in range(n):
            self.got(self.piece(z, 1 - self.p.c), n + z)

    def sent(self):
        for wait in self.pending:
            wait()


class Plane:
    def __init__(self, place, src, dst, sends, recvs):
        self.p, self.src, self.dst, self.sends, self.recvs = place, src, dst, sends, recvs

    def to(self, q):
        p = self.p
        return (p.b + (2 - 4 * p.y) * (q // 2), p.x + (1 - 2 * p.x) * (q % 2))

    def copy(self, q):
        return remote(self.src(q), self.dst(q), self.sends.at[q], self.recvs.at[q], self.to(q))

    def start(self):
        for q in (3, 1, 2):
            self.copy(q).start()

    def arrived(self):
        for q in (1, 2, 3):
            self.copy(q).wait_recv()

    def finish(self):
        for q in (1, 2, 3):
            self.copy(q).wait_send()


class Rounds:
    def __init__(self, place, sends, recvs):
        self.p, self.sends, self.recvs = place, sends, recvs

    def one(self, k, src, dst, to):
        return remote(src, dst, self.sends.at[k], self.recvs.at[k], to)

    def line(self, k, d):
        p = self.p
        z = (p.z + d) % p.depth
        return (p.b + 4 * (z - p.z), p.x)


class Quad:
    def __init__(self, p, axis, src, dst, sems):
        self.p, self.src, self.dst, self.sems = p, src, dst, sems
        self.to_pair = p.to_y if axis == 0 else p.to_x

    def to_core(self):
        return remote(self.src, self.dst(1), self.sems(0), self.sems(1), self.p.to_core)

    def to_next(self):
        return remote(self.src, self.dst(2), self.sems(2), self.sems(3), self.to_pair)

    def on(self):
        return remote(self.dst(2), self.dst(3), self.sems(4), self.sems(5), self.p.to_core)

    def start(self):
        self.to_next().start()
        self.to_core().start()

    def relay(self):
        self.to_next().wait_recv()
        self.on().start()

    def arrived(self):
        self.to_core().wait_recv()
        self.on().wait_recv()

    def finish(self):
        self.to_next().wait_send()
        self.to_core().wait_send()
        self.on().wait_send()


class QuadRows:
    def __init__(self, p, axis, src, dst, sems):
        self.p, self.axis, self.src, self.dst, self.sems = p, axis, src, dst, sems

    def mine(self, side, c):
        return self.src.at[:, side, c] if self.axis == 0 else self.src.at[:, :, c, side]

    def own(self):
        p = self.p
        side = p.y if self.axis == 0 else p.x
        return pltpu.make_async_copy(self.mine(side, p.c), self.dst.at[0], self.sems.at[0])

    def copy(self, k):
        p = self.p
        side = p.y if self.axis == 0 else p.x
        pair, far = (p.to_y, p.to_far) if self.axis == 0 else (p.to_x, p.to_far_x)
        side, c, to = ((side, 1 - p.c, p.to_core), (1 - side, p.c, pair), (1 - side, 1 - p.c, far))[k - 1]
        return remote(self.mine(side, c), self.dst.at[k], self.sems.at[2 * k - 1], self.sems.at[2 * k], to)

    def start(self):
        self.own().start()
        for k in (2, 3, 1):
            self.copy(k).start()

    def arrived(self):
        self.own().wait()
        for k in (1, 2, 3):
            self.copy(k).wait_recv()

    def finish(self):
        for k in (1, 2, 3):
            self.copy(k).wait_send()


class Reduce:
    CHUNK = 512

    def __init__(self, place, axis, x, take, rows, lo, width, out, full, outgo, income, sends, recvs):
        self.p, self.x, self.take, self.rows = place, x, take, rows
        self.side = place.x if axis == 0 else place.y
        self.to_other = place.to_x if axis == 0 else place.to_y
        self.lo, self.width, self.out = lo, width, out
        self.full, self.outgo, self.income = full, outgo, income
        self.sends, self.recvs = sends, recvs
        self.first = place.depth
        self.chunk = min(self.CHUNK, width)

    @staticmethod
    def scratch(rows, width, depth):
        return [
            pltpu.VMEM((2 * depth * rows, width), jnp.bfloat16),
            pltpu.VMEM(((2 * depth + 1) * rows, width), jnp.bfloat16),
            pltpu.SemaphoreType.DMA((4,)),
            pltpu.SemaphoreType.DMA((4,)),
        ]

    def part(self, ref, lo, hi):
        return ref.at[pl.ds(lo * self.rows, (hi - lo) * self.rows)]

    def across(self):
        n = self.p.depth
        return remote(
            self.part(self.outgo, 0, n), self.part(self.income, 0, n), self.sends.at[0], self.recvs.at[0], self.to_other
        )

    def up(self, lo):
        f, n = self.first, self.p.depth
        return remote(
            self.part(self.outgo, f + lo, f + n),
            self.part(self.income, f + lo, f + n),
            self.sends.at[1],
            self.recvs.at[1],
            self.p.to_up,
        )

    def down(self, hi):
        f = self.first
        return remote(
            self.part(self.outgo, f, f + hi),
            self.part(self.income, f, f + hi),
            self.sends.at[2],
            self.recvs.at[2],
            self.p.to_down,
        )

    def down_last(self, at):
        f, n = self.first, self.p.depth
        return remote(
            self.part(self.outgo, f + at, f + at + 1),
            self.part(self.income, f + n, f + n + 1),
            self.sends.at[3],
            self.recvs.at[3],
            self.p.to_down,
        )

    def columns(self, body):
        @pl.loop(0, self.width // self.chunk)
        def _(j):
            body(j, pl.ds(pl.multiple_of(j * self.chunk, self.chunk), self.chunk))

    def product(self, side, j):
        n, r = self.p.depth, self.rows
        x = jnp.concatenate([self.x[k, :, side].reshape(n * r, self.x.shape[4]) for k in range(4)], 1)
        return jnp.dot(x, self.take(self.lo // self.chunk + j), preferred_element_type=jnp.float32)

    def begin(self):
        p, n, r = self.p, self.p.depth, self.rows

        def away(j, here):
            self.outgo[pl.ds(0, n * r), here] = self.product(1 - self.side, j).astype(jnp.bfloat16)

        self.columns(away)
        self.across().start()

        def near(j, here):
            self.full[pl.ds(0, n * r), here] = self.product(self.side, j)

        self.columns(near)

        self.zeros()

    def zeros(self):
        p, f, n = self.p, self.first, self.p.depth

        @pl.when(p.z == 0)
        def _():
            ref = self.part(self.income, f, f + 1)
            ref[...] = jnp.zeros(ref.shape, ref.dtype)

        @pl.when(p.z == n - 1)
        def _():
            ref = self.part(self.income, f + n, f + n + 1)
            ref[...] = jnp.zeros(ref.shape, ref.dtype)

    def total(self, h, lo, hi):
        f, r = self.first, self.rows

        def body(j, here):
            rows = pl.ds(lo * r, (hi - lo) * r)
            line = pl.ds((f + lo) * r, (hi - lo) * r)
            total = self.full[rows, here]
            if f:
                total = total + self.income[rows, here].astype(jnp.float32)
            if h:
                total = total + self.income[line, here].astype(jnp.float32)
            self.outgo[line, here] = total.astype(jnp.bfloat16)

        self.columns(body)

    def hop(self, h):
        p, n = self.p, self.p.depth
        if h == 0 and self.first:
            self.across().wait_recv()

        @pl.when(p.z == h)
        def _():
            if h:
                self.up(h).wait_recv()
            self.total(h, h + 1, n)
            self.up(h + 1).start()

        @pl.when(p.z == n - 1 - h)
        def _():
            if h:
                self.down(n - 1 - h).wait_recv()
            self.total(h, 0, n - 1 - h)
            if h < n - 2:
                self.down(n - 2 - h).start()
            self.down_last(n - 2 - h).start()

    def last_waits(self):
        p, n = self.p, self.p.depth
        pl.when(p.z == n - 1)(lambda: self.up(n - 1).wait_recv())
        pl.when(p.z < n - 1)(lambda: self.down_last(0).wait_recv())

    def end(self):
        p, n, r = self.p, self.p.depth, self.rows
        self.last_waits()
        own = pl.ds(pl.multiple_of(p.z * r, r), r)
        line = pl.ds(pl.multiple_of((n + p.z) * r, r), r)

        def body(j, here):
            there = pl.ds(pl.multiple_of(self.lo + j * self.chunk, self.chunk), self.chunk)
            self.out[:, there] = (
                self.full[own, here]
                + self.income[own, here].astype(jnp.float32)
                + self.income[line, here].astype(jnp.float32)
                + self.income[pl.ds(2 * n * r, r), here].astype(jnp.float32)
            )

        self.columns(body)

    def finish(self):
        p, n = self.p, self.p.depth
        if self.first:
            self.across().wait_send()
        for h in range(n - 1):
            pl.when(p.z == h)(lambda: self.up(h + 1).wait_send())

            @pl.when(p.z == n - 1 - h)
            def _():
                if h < n - 2:
                    self.down(n - 2 - h).wait_send()
                self.down_last(n - 2 - h).wait_send()


class LineReduce(Reduce):
    def __init__(self, place, product, rows, width, full, outgo, income, sends, recvs):
        self.p, self.make, self.rows, self.width = place, product, rows, width
        self.full, self.outgo, self.income = full, outgo, income
        self.sends, self.recvs = sends, recvs
        self.first = 0
        self.chunk = min(self.CHUNK, width)

    @staticmethod
    def scratch(rows, width, depth):
        return [
            pltpu.VMEM((depth * rows, width), jnp.bfloat16),
            pltpu.VMEM(((depth + 1) * rows, width), jnp.bfloat16),
            pltpu.SemaphoreType.DMA((4,)),
            pltpu.SemaphoreType.DMA((4,)),
        ]

    def begin(self):
        def near(j, here):
            self.full[:, here] = self.make(j)

        self.columns(near)
        self.zeros()

    def end(self, write):
        self.last_waits()
        n, r = self.p.depth, self.rows
        own = pl.ds(pl.multiple_of(self.p.z * r, r), r)

        def body(j, here):
            write(
                here,
                self.full[own, here]
                + self.income[own, here].astype(jnp.float32)
                + self.income[pl.ds(n * r, r), here].astype(jnp.float32),
            )

        self.columns(body)


VMEM_BYTES = 62 * 2**20


def kernel_params(number):
    return pltpu.CompilerParams(collective_id=number, has_side_effects=True, vmem_limit_bytes=VMEM_BYTES)


def in_vmem(count):
    return [pl.BlockSpec(memory_space=pltpu.VMEM)] * count


def in_any(count):
    return [pl.BlockSpec(memory_space=pl.ANY)] * count


def ranges(cols, cut):
    return [(0, cut, True), (cut, cols, False)] if cut else [(0, cols, False)]


def keep_own(p, pairs, sems):
    copies = []
    for k, (src, dst, rows) in enumerate(pairs):
        at = pl.multiple_of(p.shard(p.z, p.y, p.c, p.x) * rows, rows)
        copies.append(pltpu.make_async_copy(src, dst.at[pl.ds(at, rows)], sems.at[k]))
    for copy in copies:
        copy.start()
    return copies


class Exchange:
    def __init__(self, place, count, src, dst, sends, recvs, own):
        self.p, self.count, self.src, self.dst = place, count, src, dst
        self.sends, self.recvs, self.own = sends, recvs, own

    def copy(self, k):
        to = (self.p.b + k) % self.count
        return remote(
            self.src.at[to], self.dst.at[self.p.b], self.sends.at[k], self.recvs.at[k], (to, self.p.x)
        )

    def mine(self):
        return pltpu.make_async_copy(self.src.at[self.p.b], self.dst.at[self.p.b], self.own)

    def start(self):
        self.mine().start()
        for k in range(1, self.count):
            self.copy(k).start()

    def arrived(self):
        self.mine().wait()
        for k in range(1, self.count):
            came = (self.p.b + self.count - k) % self.count
            remote(
                self.dst.at[came], self.dst.at[came], self.sends.at[k], self.recvs.at[k], self.p.to_x
            ).wait_recv()

    def finish(self):
        for k in range(1, self.count):
            self.copy(k).wait_send()


def exchange_sems(count):
    return [
        pltpu.SemaphoreType.DMA((count,)),
        pltpu.SemaphoreType.DMA((count,)),
        pltpu.SemaphoreType.DMA,
    ]


def greet_plane(p, count, more):
    barrier = pltpu.get_barrier_semaphore()
    for to in more:
        pl.semaphore_signal(barrier, inc=1, device_id=to, device_id_type=MESH)
    for k in range(1, count):
        pl.semaphore_signal(barrier, inc=1, device_id=((p.b + k) % count, p.x), device_id_type=MESH)
    pl.semaphore_signal(barrier, inc=1, device_id=p.to_x, device_id_type=MESH)
    pl.semaphore_wait(barrier, count + len(more))


def play(events):
    for event in events:
        event()


def three_terms(v):
    a = v.astype(jnp.bfloat16).astype(jnp.float32)
    b = (v - a).astype(jnp.bfloat16).astype(jnp.float32)
    return a, b, v - a - b


def extra_rows(rows, length, width):
    shape = (length, width)
    row = lax.broadcasted_iota(jnp.int32, shape, 0)
    total = jnp.zeros(shape, jnp.float32)
    for k, values in enumerate(rows):
        total = jnp.where(row == k, values, total)
    return total.astype(jnp.bfloat16)


def attend_open(p, lengths, got, qkv, keys, values):
    count, _, span = got.shape
    frames = count * span
    for k in range(count):
        qkv[:, k * span : (k + 1) * span] = got[k]
    position = lax.broadcasted_iota(jnp.int32, (1, frames), 1)
    hidden_key = jnp.where(position < lengths[p.x], 0.0, -1e30)
    keys[...] = jnp.concatenate([qkv[HEAD_DIM : 2 * HEAD_DIM, :], extra_rows([hidden_key], HEAD_DIM, frames)], 0).T
    values[...] = jnp.concatenate([qkv[2 * HEAD_DIM :, :], extra_rows([1.0], 16, frames)], 0)


def attend(p, lengths, got, qkv, keys, values, mixed_out, lse, plain, block, lo, hi):
    span = got.shape[2]
    length = lengths[p.x]
    ones = extra_rows([1.0], HEAD_DIM, block)
    scaling = HEAD_DIM ** (-0.5)
    parts = block // span

    @pl.loop(lo, hi)
    def _(j):
        here = pl.ds(pl.multiple_of(j * block, block), block)
        query = jnp.concatenate([qkv[:HEAD_DIM, here] * jnp.bfloat16(scaling), ones], 0)
        score = jnp.dot(keys[...], query, preferred_element_type=jnp.float32)
        peak = jnp.max(score, 0, keepdims=True)
        weights = jnp.exp(score - peak).astype(jnp.bfloat16)
        out = jnp.dot(values[...], weights, preferred_element_type=jnp.float32)
        total = out[HEAD_DIM : HEAD_DIM + 1]
        out = out[:HEAD_DIM] / total
        plain[:, here] = out
        lse[:, here] = peak + jnp.log(total)
        column = lax.broadcasted_iota(jnp.int32, (HEAD_DIM, block), 1) + j * block
        kept = jnp.where(column < length, out, 0.0).astype(jnp.bfloat16)
        for k in range(parts):
            mixed_out[j * parts + k] = kept[:, k * span : (k + 1) * span]


def attend_back_open(p, lengths, qkv, keys, values, sums):
    frames = qkv.shape[1]
    length = lengths[p.x]
    position = lax.broadcasted_iota(jnp.int32, (1, frames), 1)
    hidden_key = jnp.where(position < length, 0.0, -1e30)
    keys[...] = jnp.concatenate(
        [qkv[HEAD_DIM : 2 * HEAD_DIM, :], extra_rows([hidden_key, 1.0, 1.0, 1.0], HEAD_DIM, frames)], 0
    ).T
    values[...] = jnp.concatenate(
        [qkv[2 * HEAD_DIM :, :], extra_rows([1.0, 1.0, 1.0], HEAD_DIM, frames)], 0
    ).T
    sums[...] = jnp.zeros_like(sums)


def attend_back(got, qkv, lse, plain, keys, values, sums, grads_out, block, lo, hi):
    span = got.shape[2]
    scaling = HEAD_DIM ** (-0.5)
    parts = block // span

    @pl.loop(lo, hi)
    def _(j):
        here = pl.ds(pl.multiple_of(j * block, block), block)
        query = qkv[:HEAD_DIM, here] * jnp.bfloat16(scaling)
        upstream = jnp.concatenate([got[j * parts + k] for k in range(parts)], 1)
        delta = jnp.sum(upstream.astype(jnp.float32) * plain[:, here], 0, keepdims=True)
        left = jnp.concatenate(
            [query, extra_rows([1.0, *[-t for t in three_terms(lse[:, here])]], HEAD_DIM, block)], 0
        )
        right = jnp.concatenate([upstream, extra_rows([-t for t in three_terms(delta)], HEAD_DIM, block)], 0)
        weights = jnp.exp(jnp.dot(keys[...], left, preferred_element_type=jnp.float32))
        slope = jnp.dot(values[...], right, preferred_element_type=jnp.float32)
        slope = (weights * slope).astype(jnp.bfloat16)
        sums[:, HEAD_DIM:] += lax.dot_general(
            weights.astype(jnp.bfloat16), upstream, (((1,), (1,)), ((), ())), preferred_element_type=jnp.float32
        )
        sums[:, :HEAD_DIM] += lax.dot_general(
            slope, query, (((1,), (1,)), ((), ())), preferred_element_type=jnp.float32
        )
        query_grad = (
            jnp.dot(qkv[HEAD_DIM : 2 * HEAD_DIM, :], slope, preferred_element_type=jnp.float32) * scaling
        ).astype(jnp.bfloat16)
        for k in range(parts):
            grads_out[j * parts + k, :HEAD_DIM, :] = query_grad[:, k * span : (k + 1) * span]


def attend_back_close(sums, grads_out):
    count, _, span = grads_out.shape

    @pl.loop(0, count)
    def _(k):
        rows = pl.ds(pl.multiple_of(k * span, span), span)
        grads_out[k, HEAD_DIM:, :] = sums[rows, :].T.astype(jnp.bfloat16)


def others(p, count, k):
    number = (p.b * 2 + p.x + k) % (2 * count)
    return (number // 2, number % 2)


def nt(left, right):
    return lax.dot_general(left, right, (((1,), (1,)), ((), ())), preferred_element_type=jnp.float32)


def mean(v):
    return jnp.mean(v, -1, keepdims=True)


def normal(v):
    center = v - mean(v)
    rstd = lax.rsqrt(mean(center * center) + epsilon)
    return center * rstd, rstd


def normal_back(grad, hat, rstd, scale):
    gx = grad * (1.0 + scale)
    return rstd * (gx - mean(gx) - hat * mean(gx * hat))


def fold(v):
    width = v.shape[1] // 8
    return jnp.concatenate([v[:, k * width : (k + 1) * width] for k in range(8)], 0)


class Refs:
    def __init__(self, names, refs):
        for name, ref in zip(names, refs):
            setattr(self, name, ref)


def back_kernel(depth, shards, names, *refs):
    r = Refs(names, refs)
    rest = list(refs[len(names) :])
    p = Place(depth)
    count = 4 * depth
    devices = 2 * count
    frames, model = r.base.shape
    half = model // 2
    chunk = 512
    bf = jnp.bfloat16
    units = r.w_up.shape[1]

    barrier = pltpu.get_barrier_semaphore()
    for k in range(1, devices):
        pl.semaphore_signal(barrier, inc=1, device_id=others(p, count, k), device_id_type=MESH)

    def fetch(src, slot):
        return pltpu.make_async_copy(src, r.weights.at[slot], r.weight_sems.at[slot])

    def columns(ref, k):
        return ref.at[:, pl.ds(k * chunk, chunk)]

    def fetch_first(slot):
        return fetch(columns((r.w_out, r.w_up, r.w_down)[slot // 2], slot % 2), slot)

    def fetch_qkv(slot):
        return fetch(columns(r.w_qkv, slot), slot)

    def fetch_skip(slot):
        return fetch(r.w_skip.at[pl.ds((slot // 2) * model, model), pl.ds((slot % 2) * chunk, chunk)], slot)

    for slot in range(6):
        fetch_first(slot).start()
    pl.semaphore_wait(barrier, devices - 1)

    def to_sibling(src, dst, k):
        return remote(src, dst, r.pair_sems.at[0, k], r.pair_sems.at[1, k], p.to_core)

    pair_cot = to_sibling(r.cot_all, r.cot_sib, 0)
    pair_n2 = to_sibling(r.n2_all, r.n2_sib, 1)
    pair_act = to_sibling(r.act.at[1 - p.c], r.act_sib, 2)
    pair_gin = to_sibling(r.gin.at[1 - p.c], r.gin_sib, 3)
    plane_n2 = Plane(p, lambda q: r.n2_all.at[0], lambda q: r.n2_all.at[q], r.n2_sems.at[0], r.n2_sems.at[1])
    plane_back = Plane(
        p, lambda q: r.part_back.at[q - 1], lambda q: r.got_back.at[q - 1], r.back_sems.at[0], r.back_sems.at[1]
    )
    plane_total = Plane(
        p, lambda q: r.part_total.at[q - 1], lambda q: r.got_total.at[q - 1], r.total_sems.at[0], r.total_sems.at[1]
    )
    share_mixed = QuadRows(p, 0, r.mixed, r.xmix, r.row_sems.at[0])
    share_branch = Quad(p, 0, r.gbranch.at[0], lambda k: r.gbranch.at[k], lambda k: r.branch_sems.at[k])

    def share_late(c):
        return Quad(p, c // 6, r.glate.at[0, c], lambda k: r.glate.at[k, c], lambda k: r.late_sems.at[c, k])

    pair_cot.start()

    length = r.lengths[p.x]
    position = p.b * frames
    kept = (position + lax.broadcasted_iota(jnp.int32, (frames, 1), 0) < length).astype(jnp.float32)
    kept_row = (position + lax.broadcasted_iota(jnp.int32, (1, frames), 1) < length).astype(jnp.float32)
    a_scale = kept * r.mods[0:1, :]
    f_scale = kept * r.mods[2:3, :]
    f_shift = kept * r.mods[3:4, :]
    mixed = r.mixed[...].reshape(model, frames).T
    for k in range(2):
        fetch_first(k).wait()
        cols = pl.ds(k * chunk, chunk)
        r.middle[:, cols] = r.base[:, cols] + jnp.dot(mixed, r.weights[k], preferred_element_type=jnp.float32)
    hat, rstd = normal(r.middle[...])
    r.n2_all[0] = (hat * (1.0 + f_scale) + f_shift).astype(bf)
    plane_n2.start()
    r.bias[...] = jnp.zeros_like(r.bias)
    for slot in range(2, 6):
        fetch_first(slot).wait()

    @pl.loop(0, 4)
    def _(q):
        pl.when(q > 0)(lambda: plane_n2.copy(q).wait_recv())
        acts, grads = [], []
        for u in range(2):
            cols = pl.ds(u * chunk, chunk)
            inner = jnp.dot(r.n2_all[q], r.weights[2 + u], preferred_element_type=jnp.float32) + r.b_up[:, cols]
            cdf = 0.5 * (1.0 + lax.erf(inner * (0.5**0.5)))
            act = (inner * cdf).astype(bf)
            slope = cdf + inner * (jnp.exp(-0.5 * inner * inner) * (1.0 / math.sqrt(2.0 * math.pi)))
            act_grad = nt(r.cot_all[q, :, :half], r.weights[4, cols, :]) + nt(
                r.cot_all[q, :, half:], r.weights[5, cols, :]
            )
            grad = (act_grad * slope).astype(bf)
            r.bias[:, cols] += jnp.sum(grad.astype(jnp.float32), 0, keepdims=True)
            for k in range(4):
                here = slice(k * 128, (k + 1) * 128)
                at = (2 * u + k // 2) * 128
                r.act[k % 2, q, :, at : at + 128] = act[:, here]
                r.gin[k % 2, q, :, at : at + 128] = grad[:, here]
            acts.append(act)
            grads.append(grad)
        back = nt(grads[0], r.weights[2]) + nt(grads[1], r.weights[3])

        @pl.when(q == 0)
        def _():
            r.back[...] = back

        @pl.when(q > 0)
        def _():
            r.part_back[q - 1] = back.astype(bf)
            plane_back.copy(q).start()

        for k in range(2):
            cols = slice(k * half, (k + 1) * half)
            total = jnp.dot(acts[0], r.weights[4 + k, :chunk, :], preferred_element_type=jnp.float32)
            total = total + jnp.dot(acts[1], r.weights[4 + k, chunk:, :], preferred_element_type=jnp.float32)

            @pl.when(q == 0)
            def _():
                r.total[:, cols] = total

            @pl.when(q > 0)
            def _():
                r.part_total[q - 1, :, cols] = total.astype(bf)

    pair_n2.start()
    pair_act.start()
    pair_gin.start()
    plane_back.arrived()
    middle = r.middle[...]
    hat, rstd = normal(middle)
    grad = r.back[...]
    for k in range(3):
        grad = grad + r.got_back[k].astype(jnp.float32)
    cot = r.cot_all[0].astype(jnp.float32)
    middle_grad = cot + normal_back(grad, hat, rstd, f_scale)
    r.back[...] = middle_grad
    branch_grad = middle_grad.astype(bf)
    r.gbranch[0] = branch_grad
    there = Exchange(p, count, r.mixed_grad, r.got, r.s1, r.r1, r.o1)
    back = Exchange(p, count, r.grads_out, r.got_grads, r.s2, r.r2, r.o2)
    mixed_grad = nt(r.weights[0], branch_grad[:, :half]) + nt(r.weights[1], branch_grad[:, half:])
    r.mixed_grad[...] = (mixed_grad.astype(bf) * kept_row.astype(bf)).reshape(r.mixed_grad.shape)
    there.start()
    plane_total.start()
    share_mixed.start()
    share_branch.start()
    for slot in range(6):
        fetch_qkv(slot).start()
    r.vectors[2:3, :] = jnp.sum(kept * grad * hat, 0, keepdims=True)
    r.vectors[3:4, :] = jnp.sum(kept * grad, 0, keepdims=True)

    def blocks_of(first):
        return lambda j: jnp.concatenate([r.glate[k, first + j] for k in range(4)], 0)

    def branch_columns(j):
        here = pl.ds(pl.multiple_of(j * chunk, chunk), chunk)
        return jnp.concatenate([r.gbranch[k, :, here] for k in range(4)], 0)

    def tn(left, right):
        return lax.dot_general(left, right, (((0,), (0,)), ((), ())), preferred_element_type=jnp.float32)

    def flat(v):
        return v.reshape(4 * frames, v.shape[2])

    def down_part(k):
        cols = slice(k * half, (k + 1) * half)

        def make(j):
            mine = tn(flat(r.act[p.c]), flat(r.cot_all[:, :, cols]))
            return mine + tn(flat(r.act_sib[...]), flat(r.cot_sib[:, :, cols]))

        return make

    def up_part(k):
        cols = slice(k * 256, (k + 1) * 256)

        def make(j):
            mine = tn(flat(r.n2_all[...]), flat(r.gin[p.c, :, :, cols]))
            return mine + tn(flat(r.n2_sib[...]), flat(r.gin_sib[:, :, cols]))

        return make

    down, up, out, qkv, skip = [], [], [], [], []
    group = model // depth
    for k in range(2):
        down.append(LineReduce(p, down_part(k), units // (2 * depth), half, *rest[:5]))
        rest = rest[5:]
    for k in range(2):
        up.append(LineReduce(p, up_part(k), group, 256, *rest[:5]))
        rest = rest[5:]
    for sums, axis, x, take, res, (rows, cols, parts) in (
        (out, 0, r.xmix, branch_columns, r.out_grad, shards[0]),
        (qkv, 0, r.xnormed, blocks_of(0), r.qkv_grad, shards[1]),
        (skip, 1, r.xjoined, blocks_of(6), r.skip_grad, shards[2]),
    ):
        width = cols // parts
        for k in range(parts):
            sums.append(Reduce(p, axis, x, take, rows, k * width, width, res, *rest[:5]))
            rest = rest[5:]

    def end_down(k):
        def write(here, total):
            r.down_grad[:, pl.ds(pl.multiple_of(k * half + here.start, 128), here.size)] = total

        down[k].end(write)

    def end_up(k):
        def write(here, total):
            r.up_out[:, :, k * 256 : (k + 1) * 256] = total.astype(bf).reshape(8, group // 8, 256)

        up[k].end(write)

    own_slot = p.y * 4 + p.c * 2 + p.x

    def up_copy(k):
        to = (own_slot + k) % 8
        device = (p.z * 4 + to // 2, to % 2)
        return remote(r.up_out.at[to], r.up_got.at[own_slot], r.up_sems.at[0, k], r.up_sems.at[1, k], device)

    def up_spread():
        for k in range(1, 8):
            up_copy(k).start()
        r.up_got[own_slot] = r.up_out[own_slot]

    def up_arrived():
        for k in range(1, 8):
            came = r.up_got.at[(own_slot + 8 - k) % 8]
            remote(came, came, r.up_sems.at[0, k], r.up_sems.at[1, k], p.to_x).wait_recv()
        for t in range(8):
            for z in range(depth):
                at = (z * 8 + t) * 128
                r.up_grad[:, at : at + 128] = r.up_got[t, :, z * 128 : (z + 1) * 128].astype(jnp.float32)

    def ready(shares):
        for share in shares:
            if isinstance(share, Quad):
                share.relay()
        for share in shares:
            share.arrived()

    blocks = r.qkv.shape[1] // 256
    attend_back_open(p, r.lengths, r.qkv, r.keys, r.values, r.kv_sums)
    pair_cot.wait_recv()
    pair_act.wait_recv()
    down[0].begin()
    down[0].hop(0)
    down[1].begin()
    there.arrived()
    attend = functools.partial(
        attend_back, r.got, r.qkv, r.lse, r.plain, r.keys, r.values, r.kv_sums, r.grads_out, 256
    )
    attend(0, blocks // 2)
    down[0].hop(1)
    down[1].hop(0)
    attend(blocks // 2, blocks)
    attend_back_close(r.kv_sums, r.grads_out)
    back.start()
    plane_total.arrived()
    total = r.middle[...] + r.total[...] + r.b_down[...]
    for k in range(3):
        total = total + r.got_total[k].astype(jnp.float32)
    r.output[...] = total.astype(bf)
    down[0].hop(2)
    down[1].hop(1)
    pair_n2.wait_recv()
    pair_gin.wait_recv()
    up[0].begin()
    up[0].hop(0)
    end_down(0)
    down[1].hop(2)
    up[1].begin()
    up[0].hop(1)
    up[1].hop(0)
    ready([share_mixed, share_branch])
    out[0].begin()
    end_down(1)
    up[0].hop(2)
    up[1].hop(1)

    back.arrived()

    def unturned(at):
        h = r.got_grads[:, at : at + HEAD_DIM, :].astype(jnp.float32)
        first, second = h[:, : HEAD_DIM // 2, :], h[:, HEAD_DIM // 2 :, :]
        cosine, sine = r.cosine[...][None], r.sine[...][None]
        h = jnp.concatenate([first * cosine + second * sine, second * cosine - first * sine], 1)
        return h.astype(bf)

    for part in range(3):
        if part < 2:
            h = unturned(part * HEAD_DIM)
        else:
            h = r.got_grads[:, 2 * HEAD_DIM :, :]
        h = h.reshape(model, frames).T
        for k in range(2):
            r.glate[0, 2 * part + k] = h[:, k * chunk : (k + 1) * chunk]
            share_late(2 * part + k).start()
    for k in range(6):
        fetch_qkv(k).wait()
        made = nt(r.glate[0, k], r.weights[k])
        if k == 0:
            r.total[...] = made
        else:
            r.total[...] += made
    for k in range(4):
        fetch_skip(k).start()
    hat, rstd = normal(r.base[...])
    grad = r.total[...]
    base_grad = (r.back[...] + normal_back(grad, hat, rstd, a_scale)).astype(bf)
    for k in range(2):
        r.glate[0, 6 + k] = base_grad[:, k * chunk : (k + 1) * chunk]
        share_late(6 + k).start()
    r.vectors[0:1, :] = jnp.sum(kept * grad * hat, 0, keepdims=True)
    r.vectors[1:2, :] = jnp.sum(kept * grad, 0, keepdims=True)

    r.vectors[4:5, :] = jnp.sum(cot, 0, keepdims=True)
    r.vectors[5:6, :] = jnp.sum(base_grad.astype(jnp.float32), 0, keepdims=True)
    r.vectors[6:7, :] = r.bias[...]
    r.vectors[7:8, :] = jnp.zeros((1, model), jnp.float32)
    small = Rounds(p, r.small_sems.at[0], r.small_sems.at[1])

    def small_core():
        return small.one(0, r.vectors, r.small_got.at[0], p.to_core)

    def small_line(d):
        return small.one(d, r.line_out, r.small_got.at[d], small.line(0, d))

    def small_y():
        return small.one(4, r.y_out, r.small_got.at[4], p.to_y)

    def small_x():
        return small.one(5, r.x_out, r.small_got.at[5], p.to_x)

    def after_core():
        small_core().wait_recv()
        r.line_out[...] = r.vectors[...] + r.small_got[0]
        for d in range(1, depth):
            small_line(d).start()

    def after_line():
        total = r.line_out[...]
        for d in range(1, depth):
            small_line(d).wait_recv()
            total = total + r.small_got[d]
        r.y_out[...] = total
        small_y().start()

    def after_y():
        small_y().wait_recv()
        r.x_out[...] = r.y_out[...] + r.small_got[4]
        small_x().start()

    small_core().start()

    def times_block(size):
        number = p.b * 2 + p.x
        return r.times_full.at[pl.ds(number // size * size, size)]

    def times_copy(k, size, to):
        return small.one(6 + k, times_block(size), times_block(size), to)

    def times_step(k):
        return times_copy(k, 1 << k, (p.to_x, p.to_core, p.to_y)[k])

    def times_line(d):
        return times_copy(2 + d, 8, small.line(0, d))

    for i in range(2):
        total = None
        for j in range(2):
            fetch_skip(2 * i + j).wait()
            made = nt(r.glate[0, 6 + j], r.weights[2 * i + j])
            total = made if total is None else total + made
        r.joined_grad[i] = total.astype(bf)

    after_core()
    end_up(0)
    up[1].hop(2)
    out[0].hop(0)
    ready([share_late(0), share_late(1)])
    qkv[0].begin()
    end_up(1)
    up_spread()
    after_line()
    out[0].hop(1)
    ready([share_late(6), share_late(7)])
    skip[0].begin()
    after_y()
    ready([share_late(2), share_late(3)])
    qkv[1].begin()
    qkv[0].hop(0)
    skip[1].begin()
    out[0].hop(2)
    up_arrived()

    small_x().wait_recv()
    mine, other = r.x_out[...], r.small_got[5]
    first, second = jnp.where(p.x == 0, mine, other), jnp.where(p.x == 0, other, mine)
    total = jnp.zeros((8, r.w_mod.shape[0]), jnp.float32)
    turned = r.times[...].T
    share = r.w_mod.shape[0]
    for part in range(4):
        values = [first[part : part + 1, :], second[part : part + 1, :]]
        here = pl.ds(part * model, model)
        left = extra_rows([*three_terms(values[0]), *three_terms(values[1])], 8, model)
        total = total + nt(left, r.w_mod[:, here])
        r.mod_grad[:, here] = turned[:share, 0:1] * values[0] + turned[:share, 4:5] * values[1]
    made = jnp.concatenate(
        [total[0:1] + total[1:2] + total[2:3], total[3:4] + total[4:5] + total[5:6], jnp.zeros((6, share), jnp.float32)]
    )
    number = p.b * 2 + p.x
    r.times_full[number] = jnp.concatenate([made, jnp.zeros((8, 128 - share), jnp.float32)], 1)
    times_step(0).start()
    r.sums_out[...] = jnp.zeros_like(r.sums_out)
    at = pl.multiple_of((p.z * 2 + p.c) * 128, 128)
    r.sums_out[0:1, :] = r.y_out[6:7, pl.ds(at, 128)]
    at = pl.multiple_of(number // 4 * 128, 128)
    near = r.x_out[4:6, pl.ds(at, 128)] + r.small_got[5, 4:6, pl.ds(at, 128)]
    each = model // devices
    own = near[:, :each]
    for k in range(1, 4):
        own = jnp.where(number % 4 == k, near[:, k * each : (k + 1) * each], own)
    r.sums_out[1:2, :each] = own[0:1]
    r.sums_out[1:2, each : 2 * each] = own[1:2]

    ready([share_late(4), share_late(5)])
    qkv[2].begin()
    qkv[0].hop(1)
    qkv[1].hop(0)
    skip[0].hop(0)
    out[0].end()
    times_step(0).wait_recv()
    times_step(1).start()
    qkv[0].hop(2)
    qkv[1].hop(1)
    qkv[2].hop(0)
    skip[0].hop(1)
    skip[1].hop(0)
    times_step(1).wait_recv()
    times_step(2).start()
    qkv[0].end()
    qkv[1].hop(2)
    qkv[2].hop(1)
    skip[0].hop(2)
    skip[1].hop(1)
    times_step(2).wait_recv()
    for d in range(1, depth):
        times_line(d).start()
    qkv[1].end()
    qkv[2].hop(2)
    skip[0].end()
    skip[1].hop(2)
    qkv[2].end()
    skip[1].end()
    for d in range(1, depth):
        times_line(d).wait_recv()
    for one in [*down, *up, *out, *qkv, *skip, share_mixed, share_branch, plane_n2, plane_back, plane_total]:
        one.finish()
    for c in range(8):
        share_late(c).finish()
    for k in range(1, 8):
        up_copy(k).wait_send()
    for one in (pair_cot, pair_n2, pair_act, pair_gin):
        one.wait_send()
    for one in (there, back):
        one.finish()
    for d in range(1, depth):
        small_line(d).wait_send()
        times_line(d).wait_send()
    for k in range(3):
        times_step(k).wait_send()
    for one in (small_core(), small_y(), small_x()):
        one.wait_send()


def back_call(depth, devices, args):
    base, qkv = args["base"], args["qkv"]
    frames, model = base.shape
    count = devices // 2
    units = args["w_up"].shape[1]
    ff = units * 4
    bf, f32 = jnp.bfloat16, jnp.float32
    share = args["w_mod"].shape[0]
    dma = pltpu.SemaphoreType.DMA
    sum_scratch = []
    for rows, width in [(units // (2 * depth), model // 2)] * 2 + [(model // depth, 256)] * 2:
        sum_scratch.append(pltpu.VMEM((depth * rows, width), f32))
        sum_scratch += LineReduce.scratch(rows, width, depth)
    shards = [
        (model // devices, model, 1),
        (model // devices, 3 * model, 3),
        (2 * model // devices, model, 2),
    ]
    for rows, cols, parts in shards:
        for _ in range(parts):
            sum_scratch.append(pltpu.VMEM((depth * rows, cols // parts), f32))
            sum_scratch += Reduce.scratch(rows, cols // parts, depth)

    def tall(n, *shape, kind=bf):
        return pltpu.VMEM((n, *shape), kind)

    scratch = dict(
        weights=tall(6, model, 512),
        middle=tall(frames, model, kind=f32),
        total=tall(frames, model, kind=f32),
        back=tall(frames, model, kind=f32),
        bias=tall(1, units, kind=f32),
        vectors=tall(8, model, kind=f32),
        n2_all=tall(4, frames, model),
        n2_sib=tall(4, frames, model),
        cot_sib=tall(4, frames, model),
        act=tall(2, 4, frames, units // 2),
        gin=tall(2, 4, frames, units // 2),
        act_sib=tall(4, frames, units // 2),
        gin_sib=tall(4, frames, units // 2),
        part_back=tall(3, frames, model),
        got_back=tall(3, frames, model),
        part_total=tall(3, frames, model),
        got_total=tall(3, frames, model),
        up_out=tall(8, model // devices, units // 2),
        up_got=tall(8, model // devices, units // 2),
        gbranch=tall(4, frames, model),
        glate=tall(4, 8, frames, 512),
        xmix=tall(4, depth, 2, model // devices, frames),
        mixed_grad=tall(count, HEAD_DIM, frames),
        got=tall(count, HEAD_DIM, frames),
        keys=tall(qkv.shape[1], 2 * HEAD_DIM),
        values=tall(qkv.shape[1], 2 * HEAD_DIM),
        kv_sums=tall(qkv.shape[1], 2 * HEAD_DIM, kind=f32),
        grads_out=tall(count, 3 * HEAD_DIM, frames),
        got_grads=tall(count, 3 * HEAD_DIM, frames),
        small_got=tall(6, 8, model, kind=f32),
        line_out=tall(8, model, kind=f32),
        y_out=tall(8, model, kind=f32),
        x_out=tall(8, model, kind=f32),
        weight_sems=dma((6,)),
        pair_sems=dma((2, 4)),
        n2_sems=dma((2, 4)),
        back_sems=dma((2, 4)),
        total_sems=dma((2, 4)),
        up_sems=dma((2, 8)),
        row_sems=dma((1, 7)),
        branch_sems=dma((6,)),
        late_sems=dma((8, 6)),
        s1=dma((count,)),
        r1=dma((count,)),
        o1=dma,
        s2=dma((count,)),
        r2=dma((count,)),
        o2=dma,
        small_sems=dma((2, 12)),
    )
    shape = jax.ShapeDtypeStruct
    outs = dict(
        output=shape((frames, model), bf),
        joined_grad=shape((2, frames, model), bf),
        skip_grad=shape((2 * model // devices, model), f32),
        qkv_grad=shape((model // devices, 3 * model), f32),
        out_grad=shape((model // devices, model), f32),
        up_grad=shape((model // devices, ff), f32),
        down_grad=shape((ff // devices, model), f32),
        mod_grad=shape((share, 4 * model), f32),
        sums_out=shape((8, 128), f32),
        times_full=shape((devices, 8, 128), f32),
    )
    names = [*args, *outs, *scratch]
    vmem = pl.BlockSpec(memory_space=pltpu.VMEM)
    specs = dict.fromkeys(args, vmem)
    specs["lengths"] = pl.BlockSpec(memory_space=pltpu.SMEM)
    for name in ("w_out", "w_up", "w_down", "w_qkv", "w_skip"):
        specs[name] = pl.BlockSpec(memory_space=pl.ANY)
    made = pl.pallas_call(
        functools.partial(back_kernel, depth, shards, names),
        name="back",
        out_shape=list(outs.values()),
        in_specs=list(specs.values()),
        out_specs=[vmem] * len(outs),
        scratch_shapes=list(scratch.values()) + sum_scratch,
        compiler_params=kernel_params(3),
    )(*args.values())
    return dict(zip(outs, made))


def front_kernel(depth, cuts, names, *refs):
    r = Refs(names, refs)
    p = Place(depth)
    count = 4 * depth
    devices = 2 * count
    frames, model = r.hidden.shape
    bf = jnp.bfloat16
    share = r.w_mod.shape[0]
    tile = pl.ds(pl.multiple_of((p.b // 2) * 128, 128), 128)
    part = r.time_row[:, tile].astype(jnp.float32)
    mark = lax.broadcasted_iota(jnp.int32, (8, 128), 0) // 4 == p.x
    for ref, x in ((r.own_time, p.x), (r.other_time, 1 - p.x)):
        slot = p.c * 2 + x
        picked = part[:, 0:share]
        for k in range(1, 4):
            picked = jnp.where(slot == k, part[:, k * share : (k + 1) * share], picked)
        picked = jnp.concatenate([picked, jnp.zeros((1, 128 - share), jnp.float32)], 1)
        ref[...] = jnp.where(mark, picked, 0.0)
    greet_plane(p, count, (p.to_across, p.to_far_x))
    ask = remote(r.other_time, r.got_time, r.time_sems.at[0], r.time_sems.at[1], p.to_x)
    ask.start()

    groups = {}
    number = 0
    owns = []
    for name, src, dst in (
        ("skip", r.w_skip, r.skip_full),
        ("qkv", r.w_qkv, r.qkv_full),
        ("out", r.w_out, r.out_full),
    ):
        groups[name] = []
        for lo, hi, first in ranges(src.shape[1], src.shape[1] // cuts[name] if cuts[name] else 0):
            groups[name].append(
                Gather(p, src, dst, src.shape[0], lo, hi, True, first, r.sends.at[number], r.recvs.at[number])
            )
            number += 1
        owns.append((src, dst, src.shape[0]))
    packs = Gather(
        p, r.pack, r.pack_full, 8, 0, r.pack.shape[1], False, False, r.sends.at[number], r.recvs.at[number]
    )
    number += 1
    units = 2 * depth * 128

    def spread_up():
        for q in range(4):
            y, x = (p.y + q // 2) % 2, (p.x + q % 2) % 2
            for z in range(depth):
                for c in range(2):
                    cols = pl.ds(pl.multiple_of(p.shard(z, y, c, x) * 128, 128), 128)
                    r.up_out[q, :, (z * 2 + c) * 128 : (z * 2 + c + 1) * 128] = r.w_up[:, cols]
        r.up_mid[p.y, pl.ds(pl.multiple_of(p.x * rows_up, rows_up), rows_up), :] = r.up_out[0]
        plane_up.start()

    rows_up = r.w_up.shape[0]
    plane_up = Plane(
        p,
        lambda q: r.up_out.at[q],
        lambda q: r.up_mid.at[p.y, pl.ds(pl.multiple_of(p.x * rows_up, rows_up), rows_up)],
        r.up_sems.at[0],
        r.up_sems.at[1],
    )
    plane_cot = Plane(p, lambda q: r.cot, lambda q: r.cot_all.at[q], r.cot_sems.at[0], r.cot_sems.at[1])
    line_up = LineGather(p, r.up_mid, lambda z, c: r.up_here.at[z, :, c], r.line_sems.at[0], r.line_sems.at[1])
    line_down = LineGather(p, r.w_down, lambda z, c: r.down_here.at[z, c], r.line_sems.at[2], r.line_sems.at[3])
    lines = (line_up, line_down)
    own_up = pltpu.make_async_copy(r.up_mid, r.up_here.at[p.z, :, p.c], r.own_sems.at[3])
    own_down = pltpu.make_async_copy(r.w_down, r.down_here.at[p.z, p.c], r.own_sems.at[4])
    own_cot = pltpu.make_async_copy(r.cot, r.cot_all.at[0], r.own_sems.at[5])
    share_joined = QuadRows(p, 1, r.joined, r.xjoined, r.row_sems.at[0])
    share_normed = QuadRows(p, 0, r.normed, r.xnormed, r.row_sems.at[1])

    def lines_own():
        plane_up.arrived()
        own_up.start()
        for line in lines:
            line.own()

    there = Exchange(p, count, r.heads_in, r.got, r.s1, r.r1, r.o1)
    back = Exchange(p, count, r.mixed_out, r.mixed, r.s2, r.r2, r.o2)

    def products():
        ask.wait_recv()
        both = r.own_time[...] + r.got_time[...]
        r.times[...] = both
        left = both[:, : r.w_mod.shape[0]].astype(bf)
        row = lax.broadcasted_iota(jnp.int32, (8, model), 0) % 4
        total = jnp.zeros((8, model), jnp.float32)
        for part in range(4):
            made = jnp.dot(
                left, r.w_mod[:, part * model : (part + 1) * model], preferred_element_type=jnp.float32
            )
            total = jnp.where(row == part, made, total)
        r.pack[:, :model] = total
        each = r.b_skip.shape[1]
        r.pack[:, model:] = jnp.zeros((8, 128), jnp.float32)
        r.pack[0:1, model:] = r.b_up_part[...].astype(jnp.float32)
        r.pack[1:2, model : model + each] = r.b_skip[...].astype(jnp.float32)
        r.pack[1:2, model + each : model + 2 * each] = r.b_down_part[...].astype(jnp.float32)

    def turned_inputs():
        half = depth // 2
        for k, ref in enumerate((r.hidden, r.skip_in)):
            r.joined[k * half : (k + 1) * half] = ref[...].T.reshape(half, *r.joined.shape[1:])

    def load_skip():
        return pltpu.make_async_copy(r.skip_full, r.skip_here, r.load_sems.at[0])

    def load_qkv():
        return pltpu.make_async_copy(r.qkv_full, r.qkv_here, r.load_sems.at[1])

    own_copies = []

    def complete(name):
        for g in groups[name]:
            g.shared()

    def first_norm():
        own_copies[0].wait()
        complete("skip")
        load_skip().start()
        at = pl.multiple_of(p.shard(p.z, p.y, p.c, p.x) * 8, 8)
        r.pack_full[pl.ds(at, 8), :] = r.pack[...]
        packs.shared()
        total = r.pack_full[0:8, :model]
        for k in range(1, devices):
            total = total + r.pack_full[k * 8 : (k + 1) * 8, :model]
        mods = jnp.where(p.x == 0, total[0:4], total[4:8])
        r.mods[0:4, :] = mods
        r.mods[4:8, :] = mods
        each = model // devices
        tiles = [r.pack_full[k * 8 : k * 8 + 2, model:] for k in range(devices)]
        for z in range(depth):
            for c in range(2):
                at = pl.multiple_of(p.shard(z, p.y, c, p.x) * 8, 8)
                here = (z * 2 + c) * 128
                r.b_up[:, here : here + 128] = r.pack_full[pl.ds(at, 8), model:][0:1]
        b_skip = jnp.concatenate([t[1:2, :each] for t in tiles], 1)
        r.b_down[...] = jnp.concatenate([t[1:2, each : 2 * each] for t in tiles], 1)
        length = r.lengths[p.x]
        kept = (p.b * frames + lax.broadcasted_iota(jnp.int32, (frames, 1), 0) < length).astype(jnp.float32)
        load_skip().wait()
        base = jnp.dot(r.hidden[...], r.skip_here[:model, :], preferred_element_type=jnp.float32)
        base = base + jnp.dot(r.skip_in[...], r.skip_here[model:, :], preferred_element_type=jnp.float32) + b_skip
        r.base[...] = base
        hat, _ = normal(base)
        normed = (hat * (1.0 + kept * mods[0:1]) + kept * mods[1:2]).astype(bf)
        r.normed[...] = normed.T.reshape(r.normed.shape)
        r.normed_here[...] = normed

    def projections():
        own_copies[1].wait()
        complete("qkv")
        load_qkv().start()
        share_normed.start()
        normed = r.normed_here[...]
        load_qkv().wait()
        cosine, sine = r.cosine[...][None], r.sine[...][None]
        for part in range(3):
            made = jnp.dot(
                normed, r.qkv_here[:, part * model : (part + 1) * model], preferred_element_type=jnp.float32
            )
            made = made.T.reshape(HEADS, HEAD_DIM, frames)
            if part < 2:
                made = turn(made, cosine, sine)
            r.heads_in[:, part * HEAD_DIM : (part + 1) * HEAD_DIM, :] = made.astype(bf)
        there.start()

    def attention(lo, hi):
        attend(p, r.lengths, r.got, r.qkv, r.keys, r.values, r.mixed_out, r.lse, r.plain, 256, lo, hi)

    blocks = 2048 // 256

    def first_half():
        there.arrived()
        attend_open(p, r.lengths, r.got, r.qkv, r.keys, r.values)
        attention(0, blocks // 2)

    def second_half():
        attention(blocks // 2, blocks)
        back.start()

    events = []
    for k, name in enumerate(("skip", "qkv")):
        events += [(t + 1.5 * k, k, f) for g in groups[name] for t, f in g.steps()]
    events.append((0.3, 0, products))
    events.append((0.35, 0, turned_inputs))
    events.append((0.36, 0, spread_up))
    events += [(t + 0.5, 9, f) for t, f in packs.steps()]
    events.append((3.2, 5, lines_own))
    for g in groups["out"]:
        events += [((5.56 if t == 0 else 6.2 + t), 2, f) for t, f in g.steps()]
    for k, line in enumerate(lines):
        events.append((5.55, 5 + k, functools.partial(line.line, 1)))
        events.append((8.72, 5 + k, functools.partial(line.line, 2)))
        events.append((9.6, 5 + k, functools.partial(line.line, 3)))
    events.append((5.6, 0, first_norm))
    events.append((5.65, 0, plane_cot.start))
    events.append((5.66, 0, share_joined.start))
    events.append((7.1, 0, projections))
    events.append((8.4, 0, first_half))
    events.append((9.4, 0, second_half))
    events.sort(key=lambda e: (e[0], e[1]))
    own_down.start()
    own_cot.start()
    own_copies += keep_own(p, owns, r.own_sems)
    play([f for _, _, f in events])
    complete("out")
    for line in lines:
        line.shared()
        line.sent()
    for group in groups.values():
        for g in group:
            g.sent()
    packs.sent()
    for one in (plane_up, there):
        one.finish()
    plane_cot.arrived()
    plane_cot.finish()
    for share in (share_joined, share_normed):
        share.arrived()
        share.finish()
    back.arrived()
    back.finish()
    for copy in (own_copies[2], own_up, own_down, own_cot):
        copy.wait()
    ask.wait_send()


def front_call(depth, devices, args):
    cuts = dict(skip=8, qkv=8, out=0)
    frames, model = args["hidden"].shape
    bf, f32 = jnp.bfloat16, jnp.float32
    count = devices // 2
    total = count * frames
    shape = jax.ShapeDtypeStruct
    vmem = pl.BlockSpec(memory_space=pltpu.VMEM)
    away = pl.BlockSpec(memory_space=pl.ANY)

    def whole(name):
        rows, cols = args[name].shape
        return shape((devices * rows, cols), bf)

    def by_owner(n):
        return (depth, 2, 2, 2, n // devices, frames)

    def quarter(n):
        return (4, depth, 2, n // devices, frames)

    units = 2 * depth * 128
    rows_up = args["w_up"].shape[0]
    far = dict(
        skip_full=whole("w_skip"),
        qkv_full=whole("w_qkv"),
        out_full=whole("w_out"),
        up_here=shape((depth, 2, 2, 2 * rows_up, units), bf),
        down_here=shape((depth, 2, 128, model), bf),
        cot_all=shape((4, frames, model), bf),
        xjoined=shape(quarter(2 * model), bf),
        xnormed=shape(quarter(model), bf),
        mixed=shape((count, HEAD_DIM, frames), bf),
    )
    near = dict(
        times=shape((8, 128), f32),
        mods=shape((8, model), f32),
        b_up=shape((1, units), f32),
        b_down=shape((1, model), f32),
        base=shape((frames, model), f32),
        qkv=shape((3 * HEAD_DIM, total), bf),
        lse=shape((1, total), f32),
        plain=shape((HEAD_DIM, total), f32),
    )
    dma = pltpu.SemaphoreType.DMA
    gathers = 6
    scratch = dict(
        own_time=pltpu.VMEM((8, 128), f32),
        other_time=pltpu.VMEM((8, 128), f32),
        got_time=pltpu.VMEM((8, 128), f32),
        pack=pltpu.VMEM((8, model + 128), f32),
        pack_full=pltpu.VMEM((devices * 8, model + 128), f32),
        skip_here=pltpu.VMEM((2 * model, model), bf),
        qkv_here=pltpu.VMEM((model, 3 * model), bf),
        joined=pltpu.VMEM(by_owner(2 * model), bf),
        normed=pltpu.VMEM(by_owner(model), bf),
        normed_here=pltpu.VMEM((frames, model), bf),
        up_out=pltpu.VMEM((4, rows_up, units), bf),
        up_mid=pltpu.VMEM((2, 2 * rows_up, units), bf),
        heads_in=pltpu.VMEM((count, 3 * HEAD_DIM, frames), bf),
        got=pltpu.VMEM((count, 3 * HEAD_DIM, frames), bf),
        keys=pltpu.VMEM((total, 2 * HEAD_DIM), bf),
        values=pltpu.VMEM((HEAD_DIM + 16, total), bf),
        mixed_out=pltpu.VMEM((count, HEAD_DIM, frames), bf),
        time_sems=dma((2,)),
        load_sems=dma((2,)),
        own_sems=dma((6,)),
        up_sems=dma((2, 4)),
        cot_sems=dma((2, 4)),
        line_sems=dma((4, 16)),
        row_sems=dma((2, 7)),
        sends=dma((gathers, Gather.SENDS)),
        recvs=dma((gathers, Gather.RECVS)),
        s1=dma((count,)),
        r1=dma((count,)),
        o1=dma,
        s2=dma((count,)),
        r2=dma((count,)),
        o2=dma,
    )
    names = [*args, *far, *near, *scratch]
    made = pl.pallas_call(
        functools.partial(front_kernel, depth, cuts, names),
        name="front",
        out_shape=[*far.values(), *near.values()],
        in_specs=[pl.BlockSpec(memory_space=pltpu.SMEM)] + [vmem] * (len(args) - 1),
        out_specs=[away] * len(far) + [vmem] * len(near),
        scratch_shapes=list(scratch.values()),
        compiler_params=kernel_params(1),
    )(*args.values())
    return dict(zip([*far, *near], made))


def write_kernel(count, times, sums, joined, *refs):
    ins, outs = refs[:count], refs[count:]
    for src, dst in zip(ins, outs):
        dst[...] = src[...]
    hidden_grad, skip_grad, time_grad, b_up, b_skip, b_down = outs[count:]
    hidden_grad[...] = joined[0]
    skip_grad[...] = joined[1]
    each = b_skip.shape[1]
    part = jnp.where(lax.axis_index("uly") == 0, times[:, 0, :each], times[:, 1, :each])
    time_grad[...] = jnp.concatenate([part[k : k + 1] for k in range(times.shape[0])], 1)
    b_up[...] = sums[0:1, :]
    b_down[...] = sums[1:2, :each]
    b_skip[...] = sums[1:2, each : 2 * each]


def write_call(made, names, each):
    shape = jax.ShapeDtypeStruct
    joined = made["joined_grad"]
    frames, model = joined.shape[1:]
    plain = [shape(made[name].shape, made[name].dtype) for name in names]
    return pl.pallas_call(
        functools.partial(write_kernel, len(names)),
        name="write",
        out_shape=plain
        + [shape((frames, model), joined.dtype)] * 2
        + [shape((1, model), jnp.float32), shape((1, 128), jnp.float32)]
        + [shape((1, each), jnp.float32)] * 2,
        in_specs=in_vmem(3 + len(names)),
        out_specs=in_vmem(6 + len(names)),
        compiler_params=pltpu.CompilerParams(vmem_limit_bytes=VMEM_BYTES),
    )(made["times_full"], made["sums_out"], joined, *[made[name] for name in names])


def first_with_second(left, right, dims):
    return lax.dot_general(left, right, ((dims[:1], dims[1:]), ((), ())), preferred_element_type=jnp.float32)


def turn(values, cosine, sine):
    half = HEAD_DIM // 2
    first, second = values[..., :half, :], values[..., half:, :]
    return jnp.concatenate([first * cosine - second * sine, second * cosine + first * sine], -2)


def on_device(hidden, skip_in, time_embed, lengths, cotangent, w_skip, b_skip, w_mod, w_qkv, w_out, w_up, b_up,
              w_down, b_down):
    block, row = lax.axis_index("blk"), lax.axis_index("uly")
    blocks, rows = lax.axis_size("blk"), lax.axis_size("uly")
    devices, depth = blocks * rows, blocks // 4
    _, frames, model = hidden.shape
    position = block * frames + jnp.arange(frames, dtype=jnp.int32)
    length = lax.dynamic_index_in_dim(lengths, row, 0, keepdims=False)[0]
    valid = position < length
    half = HEAD_DIM // 2
    freq = 10000.0 ** (-jnp.arange(half, dtype=jnp.float32) / half)
    offsets = jnp.where(valid, position, position - length).astype(jnp.float32)
    angle = freq[:, None] * offsets[None, :]
    cosine, sine = jnp.cos(angle), jnp.sin(angle)
    front = front_call(
        depth,
        devices,
        dict(
            lengths=lengths[:, 0],
            time_row=time_embed[0],
            b_skip=b_skip[None],
            b_up_part=b_up[None],
            b_down_part=b_down[None],
            cot=cotangent[0],
            w_mod=w_mod,
            cosine=cosine,
            sine=sine,
            hidden=hidden[0],
            skip_in=skip_in[0],
            w_skip=w_skip,
            w_qkv=w_qkv,
            w_out=w_out,
            w_up=w_up,
            w_down=w_down,
        ),
    )
    made = back_call(
        depth,
        devices,
        dict(
            lengths=lengths[:, 0],
            base=front["base"],
            mods=front["mods"],
            b_up=front["b_up"],
            b_down=front["b_down"],
            cosine=cosine,
            sine=sine,
            w_mod=w_mod,
            times=front["times"],
            qkv=front["qkv"],
            lse=front["lse"],
            plain=front["plain"],
            cot_all=front["cot_all"],
            mixed=front["mixed"].reshape(depth, 2, 2, 2, model // devices, frames),
            xjoined=front["xjoined"],
            xnormed=front["xnormed"],
            w_out=front["out_full"],
            w_up=front["up_here"].reshape(model, -1),
            w_down=front["down_here"].reshape(-1, model),
            w_qkv=front["qkv_full"],
            w_skip=front["skip_full"],
        ),
    )
    names = ["output", "skip_grad", "mod_grad", "qkv_grad", "out_grad", "up_grad", "down_grad"]
    output, skip_grad, mod_grad, qkv_grad, out_grad, up_grad, down_grad, *small = write_call(
        made, names, b_skip.shape[0]
    )
    hidden_grad, skip_in_grad, time_grad, b_up_grad, b_skip_grad, b_down_grad = small
    return (
        output[None],
        hidden_grad[None],
        skip_in_grad[None],
        time_grad[None],
        skip_grad,
        b_skip_grad[0],
        mod_grad,
        qkv_grad,
        out_grad,
        up_grad,
        b_up_grad[0],
        down_grad,
        b_down_grad[0],
    )


def solution(mesh):
    placed = (
        P("uly", "blk", None),
        P("uly", "blk", None),
        P("uly", None, None),
        P(),
        P("uly", "blk", None),
        P(("blk", "uly"), None),
        P(("blk", "uly")),
        P(("blk", "uly"), None),
        P(("blk", "uly"), None),
        P(("blk", "uly"), None),
        P(("blk", "uly"), None),
        P(("blk", "uly")),
        P(("blk", "uly"), None),
        P(("blk", "uly")),
    )
    blocks = mesh.shape["blk"]
    special = mesh.shape["uly"] == 2 and blocks == HEADS and blocks % 4 == 0 and blocks > 4
    return jax.shard_map(
        on_device if special else per_device,
        mesh=mesh,
        in_specs=placed,
        out_specs=(
            P("uly", "blk", None),
            P("uly", "blk", None),
            P("uly", "blk", None),
            P("uly", None, None),
            P(("blk", "uly"), None),
            P(("blk", "uly")),
            P(("blk", "uly"), None),
            P(("blk", "uly"), None),
            P(("blk", "uly"), None),
            P(("blk", "uly"), None),
            P(("blk", "uly")),
            P(("blk", "uly"), None),
            P(("blk", "uly")),
        ),
        check_vma=False,
    )
```

```python
import functools
import math

import jax
import jax.numpy as jnp
from jax import lax
from jax.experimental import pallas as pl
from jax.experimental.pallas import tpu as pltpu
from jax.sharding import PartitionSpec as P

HEADS = 16
HEAD_DIM = 64


exact_mode = lax.Precision.HIGHEST
epsilon = 1e-05


def passed_along(x, axis, by):
    devices = lax.axis_size(axis)
    return lax.ppermute(x, axis, [(i, (i + by) % devices) for i in range(devices)])


def segment_info(len_row, positions):
    slots = len_row.shape[0]
    ends = jnp.cumsum(len_row)
    starts = ends - len_row
    total = ends[-1]
    seg_ids = jnp.sum((positions[:, None] >= ends[None, :]).astype(jnp.int32), axis=1)
    onehot = seg_ids[:, None] == jnp.arange(slots, dtype=jnp.int32)[None, :]
    begin = jnp.sum(jnp.where(onehot, starts[None, :], 0), axis=1)
    begin = begin + jnp.where(seg_ids == slots, total, 0)
    return (seg_ids, positions - begin, seg_ids < slots)


def rotary(values, offsets):
    half = values.shape[-1] // 2
    freq = 10000.0 ** (-jnp.arange(half, dtype=jnp.float32) / half)
    angle = offsets.astype(jnp.float32)[:, None] * freq[None, :]
    cosine = jnp.cos(angle)[:, None, :]
    sine = jnp.sin(angle)[:, None, :]
    first = values[..., :half]
    second = values[..., half:]
    return jnp.concatenate([first * cosine - second * sine, second * cosine + first * sine], -1)


def modulate(values, scale, shift):
    center = values - jnp.mean(values, -1, keepdims=True)
    spread = jnp.mean(center * center, -1, keepdims=True)
    return center * lax.rsqrt(spread + epsilon) * (1.0 + scale) + shift


def contract_rows(left, right):
    return lax.dot_general(
        left, right, (((0,), (0,)), ((), ())), preferred_element_type=jnp.float32
    )


def contract_cols(left, right):
    return lax.dot_general(
        left, right, (((1,), (1,)), ((), ())), preferred_element_type=jnp.float32
    )


def gelu_exact(values):
    return jax.nn.gelu(values, approximate=False)


def per_device(
    hidden,
    skip_in,
    time_embed,
    lengths,
    cotangent,
    w_skip,
    b_skip,
    w_mod,
    w_qkv,
    w_out,
    w_up,
    b_up,
    w_down,
    b_down,
):
    gathered = (
        lax.all_gather(w_skip, ("blk", "uly"), axis=0, tiled=True),
        lax.all_gather(b_skip, ("blk", "uly"), axis=0, tiled=True),
        lax.all_gather(w_mod, ("blk", "uly"), axis=0, tiled=True),
        lax.all_gather(w_qkv, ("blk", "uly"), axis=0, tiled=True),
        lax.all_gather(w_out, ("blk", "uly"), axis=0, tiled=True),
        lax.all_gather(w_up, ("blk", "uly"), axis=0, tiled=True),
        lax.all_gather(b_up, ("blk", "uly"), axis=0, tiled=True),
        lax.all_gather(w_down, ("blk", "uly"), axis=0, tiled=True),
        lax.all_gather(b_down, ("blk", "uly"), axis=0, tiled=True),
    )
    (
        skip_full,
        bskip_full,
        mod_full,
        qkv_full,
        out_full,
        up_full,
        bup_full,
        down_full,
        bdown_full,
    ) = gathered
    group_count = lax.axis_size("uly")
    cycle_size = lax.axis_size("blk")
    frame_count = hidden.shape[1]
    row_count = lengths.shape[0]
    slot_count = lengths.shape[1]
    local_heads = HEADS // group_count
    span = local_heads * HEAD_DIM
    scaling = HEAD_DIM ** (-0.5)
    block_index = lax.axis_index("blk")
    row_index = lax.axis_index("uly")
    frame_pos = block_index * frame_count + jnp.arange(frame_count, dtype=jnp.int32)
    all_seg, all_offsets, all_valid = jax.vmap(lambda len_row: segment_info(len_row, frame_pos))(
        lengths
    )
    own_seg = lax.dynamic_index_in_dim(all_seg, row_index, 0, keepdims=False)
    own_offsets = lax.dynamic_index_in_dim(all_offsets, row_index, 0, keepdims=False)
    joined = jnp.concatenate([hidden[0], skip_in[0]], 1)
    base = jnp.dot(joined, skip_full, preferred_element_type=jnp.float32) + bskip_full.astype(
        jnp.float32
    )
    time_row = time_embed[0]
    mods = jnp.dot(time_row, mod_full, preferred_element_type=jnp.float32)
    selector = (own_seg[:, None] == jnp.arange(slot_count, dtype=jnp.int32)[None, :]).astype(
        jnp.float32
    )
    frame_mod = jnp.dot(selector, mods, precision=exact_mode)
    a_scale, a_shift, f_scale, f_shift = jnp.split(frame_mod, 4, 1)
    normed_full, norm_back = jax.vjp(modulate, base, a_scale, a_shift)
    normed = normed_full.astype(jnp.bfloat16)
    projected = jnp.dot(normed, qkv_full, preferred_element_type=jnp.float32).reshape(
        frame_count, 3, HEADS, HEAD_DIM
    )

    def place(parts):
        return jnp.stack(
            [rotary(parts[:, 0], own_offsets), rotary(parts[:, 1], own_offsets), parts[:, 2]], 1
        )

    turned, unturn = jax.vjp(place, projected)
    sending = turned.astype(jnp.bfloat16).reshape(1, frame_count, 3, group_count, span)
    head_data = lax.all_to_all(sending, "uly", split_axis=3, concat_axis=0, tiled=True)
    query = head_data[:, :, 0, 0].reshape(row_count, frame_count, local_heads, HEAD_DIM)
    kv_pairs = head_data[:, :, 1:, 0]

    def key_segments(start, count):
        key_pos = start + jnp.arange(count, dtype=jnp.int32)
        return jax.vmap(lambda len_row: segment_info(len_row, key_pos)[0])(lengths)

    start_state = (
        jnp.full((row_count, local_heads, frame_count), -1e30, jnp.float32),
        jnp.zeros((row_count, local_heads, frame_count), jnp.float32),
        jnp.zeros((row_count, frame_count, local_heads, HEAD_DIM), jnp.float32),
    )
    piece = lax.all_gather(kv_pairs, "blk", axis=1, tiled=True)
    total = piece.shape[1]
    step = math.gcd(total, max(frame_count, 1024))

    def sub_step(step_index, state):
        run_max, run_total, run_acc = state
        offset = step_index * step
        section = lax.dynamic_slice_in_dim(piece, offset, step, 1)
        key_seg = key_segments(offset, step)
        key_part = section[:, :, 0].reshape(row_count, step, local_heads, HEAD_DIM)
        value_part = section[:, :, 1].reshape(row_count, step, local_heads, HEAD_DIM)
        mask = all_seg[:, None, :, None] == key_seg[:, None, None, :]
        score = (
            jnp.einsum("rqhd,rkhd->rhqk", query, key_part, preferred_element_type=jnp.float32)
            * scaling
        )
        masked = jnp.where(mask, score, -1e30)
        fresh = jnp.maximum(run_max, jnp.max(masked, -1))
        weights = jnp.where(mask, jnp.exp(masked - fresh[..., None]), 0.0)
        decay = jnp.exp(run_max - fresh)
        run_total = run_total * decay + jnp.sum(weights, -1)
        run_acc = run_acc * jnp.swapaxes(decay, 1, 2)[..., None] + jnp.einsum(
            "rhqk,rkhd->rqhd",
            weights.astype(jnp.bfloat16),
            value_part,
            preferred_element_type=jnp.float32,
        )
        return (fresh, run_total, run_acc)

    run_max, run_total, run_acc = lax.fori_loop(0, total // step, sub_step, start_state)
    attended = run_acc / jnp.swapaxes(run_total, 1, 2)[..., None]
    log_total = run_max + jnp.log(run_total)
    valid_half = all_valid.astype(jnp.bfloat16)[:, :, None, None]
    leaving = (attended * all_valid.astype(jnp.float32)[:, :, None, None]).astype(jnp.bfloat16)
    leaving = leaving.reshape(row_count, frame_count, 1, span)
    mixed = lax.all_to_all(leaving, "uly", split_axis=0, concat_axis=2, tiled=True).reshape(
        frame_count, HEADS * HEAD_DIM
    )
    branch = jnp.dot(mixed, out_full, preferred_element_type=jnp.float32)
    middle = base + branch
    normed2_full, norm2_back = jax.vjp(modulate, middle, f_scale, f_shift)
    normed2 = normed2_full.astype(jnp.bfloat16)
    inner = jnp.dot(normed2, up_full, preferred_element_type=jnp.float32) + bup_full.astype(
        jnp.float32
    )
    act_full, act_back = jax.vjp(gelu_exact, inner)
    act = act_full.astype(jnp.bfloat16)
    result = (
        middle
        + jnp.dot(act, down_full, preferred_element_type=jnp.float32)
        + bdown_full.astype(jnp.float32)
    )
    output = result.astype(jnp.bfloat16)[None]
    again = (
        lax.all_gather(w_skip, ("blk", "uly"), axis=0, tiled=True),
        lax.all_gather(w_mod, ("blk", "uly"), axis=0, tiled=True),
        lax.all_gather(w_qkv, ("blk", "uly"), axis=0, tiled=True),
        lax.all_gather(w_out, ("blk", "uly"), axis=0, tiled=True),
        lax.all_gather(w_up, ("blk", "uly"), axis=0, tiled=True),
        lax.all_gather(w_down, ("blk", "uly"), axis=0, tiled=True),
    )
    skip_back, mod_back, qkv_back, out_back, up_back, down_back = again
    upstream = cotangent[0]
    upstream_full = upstream.astype(jnp.float32)
    grad_down = contract_rows(act, upstream)
    grad_bdown = jnp.sum(upstream_full, 0)
    grad_act = contract_cols(upstream, down_back)
    grad_inner = act_back(grad_act)[0].astype(jnp.bfloat16)
    grad_up = contract_rows(normed2, grad_inner)
    grad_bup = jnp.sum(grad_inner.astype(jnp.float32), 0)
    grad_normed2 = contract_cols(grad_inner, up_back)
    grad_mid_norm, grad_fscale, grad_fshift = norm2_back(grad_normed2)
    grad_middle = upstream_full + grad_mid_norm
    grad_branch = grad_middle.astype(jnp.bfloat16)
    grad_out = contract_rows(mixed, grad_branch)
    grad_mixed = (
        contract_cols(grad_branch, out_back)
        .astype(jnp.bfloat16)
        .reshape(1, frame_count, group_count, span)
    )
    returning = lax.all_to_all(grad_mixed, "uly", split_axis=2, concat_axis=0, tiled=True)
    grad_attn = returning.reshape(row_count, frame_count, local_heads, HEAD_DIM) * valid_half
    delta_rows = jnp.swapaxes(jnp.sum(grad_attn.astype(jnp.float32) * attended, -1), 1, 2)

    def contribution(held_pairs, key_start):
        count = held_pairs.shape[1]
        key_seg = key_segments(key_start, count)
        key_part = held_pairs[:, :, 0].reshape(row_count, count, local_heads, HEAD_DIM)
        value_part = held_pairs[:, :, 1].reshape(row_count, count, local_heads, HEAD_DIM)
        mask = all_seg[:, None, :, None] == key_seg[:, None, None, :]
        score = (
            jnp.einsum("rqhd,rkhd->rhqk", query, key_part, preferred_element_type=jnp.float32)
            * scaling
        )
        weights = jnp.exp(jnp.where(mask, score - log_total[..., None], -1e30))
        grad_weights = jnp.einsum(
            "rqhd,rkhd->rhqk", grad_attn, value_part, preferred_element_type=jnp.float32
        )
        grad_score = (weights * (grad_weights - delta_rows[..., None])).astype(jnp.bfloat16)
        more_query = (
            jnp.einsum("rhqk,rkhd->rqhd", grad_score, key_part, preferred_element_type=jnp.float32)
            * scaling
        )
        more_key = (
            jnp.einsum("rhqk,rqhd->rkhd", grad_score, query, preferred_element_type=jnp.float32)
            * scaling
        )
        more_value = jnp.einsum(
            "rhqk,rqhd->rkhd",
            weights.astype(jnp.bfloat16),
            grad_attn,
            preferred_element_type=jnp.float32,
        )
        more_pairs = jnp.stack(
            [more_key.reshape(row_count, count, span), more_value.reshape(row_count, count, span)],
            2,
        )
        return (more_query, more_pairs)

    def pass_grads(held_grads):
        return passed_along(held_grads.astype(jnp.bfloat16), "blk", 1).astype(held_grads.dtype)

    def cycle_step(turn, state):
        held_pairs, held_grads, query_grad = state
        more_query, more_pairs = contribution(
            held_pairs, (block_index - turn) % cycle_size * frame_count
        )
        held_pairs = passed_along(held_pairs, "blk", 1)
        held_grads = pass_grads(held_grads + more_pairs)
        return (held_pairs, held_grads, query_grad + more_query)

    cycle_start = (
        kv_pairs,
        jnp.zeros((row_count, frame_count, 2, span), jnp.float32),
        jnp.zeros((row_count, frame_count, local_heads, HEAD_DIM), jnp.float32),
    )
    held_pairs, held_grads, query_grad = lax.fori_loop(0, cycle_size - 1, cycle_step, cycle_start)
    last_query, last_pairs = contribution(
        held_pairs, (block_index - (cycle_size - 1)) % cycle_size * frame_count
    )
    pair_grads = pass_grads(held_grads + last_pairs)
    query_grad = query_grad + last_query
    head_grads = jnp.concatenate(
        [
            query_grad.astype(jnp.bfloat16).reshape(row_count, frame_count, 1, span),
            pair_grads.astype(jnp.bfloat16),
        ],
        2,
    ).reshape(row_count, frame_count, 3, 1, span)
    frames_grad = lax.all_to_all(head_grads, "uly", split_axis=0, concat_axis=3, tiled=True)
    frames_grad = frames_grad.reshape(frame_count, 3, HEADS, HEAD_DIM).astype(jnp.float32)
    grad_projected = (
        unturn(frames_grad)[0].astype(jnp.bfloat16).reshape(frame_count, 3 * HEADS * HEAD_DIM)
    )
    grad_qkv = contract_rows(normed, grad_projected)
    grad_normed = contract_cols(grad_projected, qkv_back)
    grad_base_norm, grad_ascale, grad_ashift = norm_back(grad_normed)
    grad_base = (grad_middle + grad_base_norm).astype(jnp.bfloat16)
    grad_skip_w = contract_rows(joined, grad_base)
    grad_bskip = jnp.sum(grad_base.astype(jnp.float32), 0)
    grad_joined = contract_cols(grad_base, skip_back).astype(jnp.bfloat16)
    model_width = hidden.shape[2]
    hidden_grad = grad_joined[:, :model_width][None]
    skip_grad = grad_joined[:, model_width:][None]
    frame_mod_grad = jnp.concatenate([grad_ascale, grad_ashift, grad_fscale, grad_fshift], 1)
    slot_grad = lax.dot_general(
        selector, frame_mod_grad, (((0,), (0,)), ((), ())), precision=exact_mode
    )
    grad_mod = lax.dot_general(
        time_row.astype(jnp.float32), slot_grad, (((0,), (0,)), ((), ())), precision=exact_mode
    )
    slot_total = lax.psum(slot_grad, "blk")
    time_grad = lax.dot_general(
        slot_total, mod_back.astype(jnp.float32), (((1,), (1,)), ((), ())), precision=exact_mode
    )[None]
    owned = (
        lax.psum_scatter(grad_skip_w, ("blk", "uly"), scatter_dimension=0, tiled=True),
        lax.psum_scatter(grad_bskip, ("blk", "uly"), scatter_dimension=0, tiled=True),
        lax.psum_scatter(grad_mod, ("blk", "uly"), scatter_dimension=0, tiled=True),
        lax.psum_scatter(grad_qkv, ("blk", "uly"), scatter_dimension=0, tiled=True),
        lax.psum_scatter(grad_out, ("blk", "uly"), scatter_dimension=0, tiled=True),
        lax.psum_scatter(grad_up, ("blk", "uly"), scatter_dimension=0, tiled=True),
        lax.psum_scatter(grad_bup, ("blk", "uly"), scatter_dimension=0, tiled=True),
        lax.psum_scatter(grad_down, ("blk", "uly"), scatter_dimension=0, tiled=True),
        lax.psum_scatter(grad_bdown, ("blk", "uly"), scatter_dimension=0, tiled=True),
    )
    return (
        output,
        hidden_grad,
        skip_grad,
        time_grad,
        owned[0],
        owned[1],
        owned[2],
        owned[3],
        owned[4],
        owned[5],
        owned[6],
        owned[7],
        owned[8],
    )


MESH = pl.DeviceIdType.MESH


class Place:
    def __init__(self, depth):
        self.depth = depth
        self.b = lax.axis_index("blk")
        self.x = lax.axis_index("uly")
        self.z = self.b // 4
        self.y = (self.b // 2) % 2
        self.c = self.b % 2
        self.to_x = (self.b, 1 - self.x)
        self.to_y = (self.b + 2 - 4 * self.y, self.x)
        self.to_core = (self.b + 1 - 2 * self.c, self.x)
        self.to_far = (self.b + 3 - 4 * self.y - 2 * self.c, self.x)
        self.to_across = (self.b + 2 - 4 * self.y, 1 - self.x)
        self.to_far_x = (self.b + 1 - 2 * self.c, 1 - self.x)
        self.to_up = (self.b + 4, self.x)
        self.to_down = (self.b - 4, self.x)

    def shard(self, z, y, c, x):
        return ((z * 2 + y) * 2 + c) * 2 + x

    def greet(self):
        barrier = pltpu.get_barrier_semaphore()
        for to in (self.to_x, self.to_y, self.to_core, self.to_far):
            pl.semaphore_signal(barrier, inc=1, device_id=to, device_id_type=MESH)

        @pl.when(self.z < self.depth - 1)
        def _():
            pl.semaphore_signal(barrier, inc=1, device_id=self.to_up, device_id_type=MESH)

        @pl.when(self.z > 0)
        def _():
            pl.semaphore_signal(barrier, inc=1, device_id=self.to_down, device_id_type=MESH)

        top = self.depth - 1
        pl.semaphore_wait(barrier, 4 + (self.z + top - 1) // top + (2 * top - 1 - self.z) // top)


def remote(src, dst, send, recv, to):
    return pltpu.make_async_remote_copy(
        src_ref=src, dst_ref=dst, send_sem=send, recv_sem=recv, device_id=to, device_id_type=MESH
    )


class Gather:
    SENDS = 64
    RECVS = 48

    def __init__(self, place, src, dst, rows, lo, hi, split, plane_first, sends, recvs):
        self.p, self.src, self.dst, self.rows = place, src, dst, rows
        self.lo, self.hi, self.split, self.plane_first = lo, hi, split, plane_first
        self.sends, self.recvs = sends, recvs
        self.pending = []

    def part(self, z, y, c, x, half=None):
        base = self.p.shard(z, y, c, x) * self.rows
        rows = self.rows
        if half is not None:
            rows = rows // 2
            base = base + half * rows
        return self.dst.at[pl.ds(pl.multiple_of(base, rows), rows), pl.ds(self.lo, self.hi - self.lo)]

    def mine(self):
        return self.src.at[:, pl.ds(self.lo, self.hi - self.lo)]

    def go(self, when, src, dst, send, recv, to):
        def start():
            remote(src, dst, self.sends.at[send], self.recvs.at[recv], to).start()

        def finish():
            remote(src, dst, self.sends.at[send], self.recvs.at[recv], to).wait_send()

        if when is None:
            start()
            self.pending.append(finish)
        else:
            pl.when(when)(start)
            self.pending.append(lambda: pl.when(when)(finish))

    def got(self, dst, recv):
        remote(dst, dst, self.sends.at[0], self.recvs.at[recv], self.p.to_x).wait_recv()

    def share(self, when, src, z, y, x):
        slot = z * 4 + y * 2 + x
        self.go(when, src, self.part(z, y, self.p.c, x), slot, slot, self.p.to_core)

    def steps(self):
        return self.plane_steps() if self.plane_first else self.line_steps()

    def line_steps(self):
        p = self.p
        top = p.depth - 1

        def hand_on(when, src, z):
            whole = self.part(z, p.y, p.c, p.x)
            self.go(when, src, whole, 24 + z, 20 + z, p.to_x)
            self.go(when, src, whole, 28 + z, 24 + z, p.to_y)
            self.share(when, src, z, p.y, p.x)

        def own():
            src = self.mine()
            whole = self.part(p.z, p.y, p.c, p.x)
            self.go(p.z < top, src, whole, 16 + p.z, 16 + p.z, p.to_up)
            self.go(p.z > 0, src, whole, 20 + p.z, 16 + p.z, p.to_down)
            hand_on(None, src, p.z)

        def line(d):
            for side in (-1, 1):
                z = p.z + side * d
                here = (z >= 0) & (z <= top)
                whole = self.part(z, p.y, p.c, p.x)
                pl.when(here)(lambda: self.got(whole, 16 + z))
                if side < 0:
                    self.go(here & (p.z < top), whole, whole, 16 + z, 16 + z, p.to_up)
                else:
                    self.go(here & (p.z > 0), whole, whole, 20 + z, 16 + z, p.to_down)
                hand_on(here, whole, z)

        def origins(d):
            return [(None, p.z)] if d == 0 else [
                ((p.z + s * d >= 0) & (p.z + s * d <= top), p.z + s * d) for s in (-1, 1)
            ]

        def cond(when, f):
            f() if when is None else pl.when(when)(f)

        def cross(d):
            for when, z in origins(d):
                from_x = self.part(z, p.y, p.c, 1 - p.x)
                cond(when, lambda: self.got(from_x, 20 + z))
                self.share(when, from_x, z, p.y, 1 - p.x)
                if self.split:
                    part = self.part(z, p.y, p.c, 1 - p.x, 0)
                else:
                    part = from_x
                self.go(when, part, part, 32 + z, 28 + z, p.to_y)
                from_y = self.part(z, 1 - p.y, p.c, p.x)
                cond(when, lambda: self.got(from_y, 24 + z))
                self.share(when, from_y, z, 1 - p.y, p.x)
                if self.split:
                    part = self.part(z, 1 - p.y, p.c, p.x, 1)
                    self.go(when, part, part, 36 + z, 32 + z, p.to_x)

        def corner(d):
            for when, z in origins(d):
                whole = self.part(z, 1 - p.y, p.c, 1 - p.x)
                if self.split:
                    for half in (0, 1):
                        part = self.part(z, 1 - p.y, p.c, 1 - p.x, half)
                        cond(when, lambda: self.got(part, 28 + 4 * half + z))
                else:
                    cond(when, lambda: self.got(whole, 28 + z))
                self.share(when, whole, z, 1 - p.y, 1 - p.x)

        out = [(0, own)]
        for d in range(p.depth):
            if d:
                out.append((d, functools.partial(line, d)))
            out.append((d + 1, functools.partial(cross, d)))
            out.append((d + 2, functools.partial(corner, d)))
        return out

    def plane_steps(self):
        p = self.p
        top = p.depth - 1

        def along(when, src, z, y, x, up, down):
            slot = 20 + z * 4 + y * 2 + x
            whole = self.part(z, y, p.c, x)
            if up:
                w = p.z < top
                self.go(w if when is None else w & when, src, whole, slot, slot, p.to_up)
            if down:
                w = p.z > 0
                self.go(w if when is None else w & when, src, whole, slot + 16, slot, p.to_down)

        def own():
            src = self.mine()
            whole = self.part(p.z, p.y, p.c, p.x)
            self.go(None, src, whole, 16, 16, p.to_x)
            self.go(None, src, whole, 17, 17, p.to_y)
            along(None, src, p.z, p.y, p.x, True, True)
            self.share(None, src, p.z, p.y, p.x)

        def cross():
            from_x = self.part(p.z, p.y, p.c, 1 - p.x)
            self.got(from_x, 16)
            part = self.part(p.z, p.y, p.c, 1 - p.x, 0) if self.split else from_x
            self.go(None, part, part, 18, 18, p.to_y)
            along(None, from_x, p.z, p.y, 1 - p.x, True, True)
            self.share(None, from_x, p.z, p.y, 1 - p.x)
            from_y = self.part(p.z, 1 - p.y, p.c, p.x)
            self.got(from_y, 17)
            if self.split:
                part = self.part(p.z, 1 - p.y, p.c, p.x, 1)
                self.go(None, part, part, 19, 19, p.to_x)
            along(None, from_y, p.z, 1 - p.y, p.x, True, True)
            self.share(None, from_y, p.z, 1 - p.y, p.x)

        def corner():
            whole = self.part(p.z, 1 - p.y, p.c, 1 - p.x)
            if self.split:
                for half in (0, 1):
                    self.got(self.part(p.z, 1 - p.y, p.c, 1 - p.x, half), 18 + half)
            else:
                self.got(whole, 18)
            along(None, whole, p.z, 1 - p.y, 1 - p.x, True, True)
            self.share(None, whole, p.z, 1 - p.y, 1 - p.x)

        def line(d, k):
            y = p.y if k in (0, 1) else 1 - p.y
            x = p.x if k in (0, 2) else 1 - p.x
            for side in (-1, 1):
                z = p.z + side * d
                here = (z >= 0) & (z <= top)
                whole = self.part(z, y, p.c, x)
                pl.when(here)(lambda: self.got(whole, 20 + z * 4 + y * 2 + x))
                along(here, whole, z, y, x, side < 0, side > 0)
                self.share(here, whole, z, y, x)

        out = [(0, own), (1, cross), (2, corner)]
        for d in range(1, p.depth):
            for k in range(4):
                out.append((d + 0.1 + min(k, 2) * 0.9, functools.partial(line, d, k)))
        return out

    def shared(self):
        p = self.p
        for z in range(p.depth):
            for y in range(2):
                for x in range(2):
                    self.got(self.part(z, y, 1 - p.c, x), z * 4 + y * 2 + x)

    def sent(self):
        for wait in self.pending:
            wait()


class LineGather:
    def __init__(self, place, src, piece, sends, recvs):
        self.p, self.src, self.piece, self.sends, self.recvs = place, src, piece, sends, recvs
        self.pending = []

    def go(self, when, src, dst, send, recv, to):
        def start():
            remote(src, dst, self.sends.at[send], self.recvs.at[recv], to).start()

        def finish():
            remote(src, dst, self.sends.at[send], self.recvs.at[recv], to).wait_send()

        if when is None:
            start()
            self.pending.append(finish)
        else:
            pl.when(when)(start)
            self.pending.append(lambda: pl.when(when)(finish))

    def got(self, dst, recv):
        remote(dst, dst, self.sends.at[0], self.recvs.at[recv], self.p.to_x).wait_recv()

    def own(self):
        p, n = self.p, self.p.depth
        dst = self.piece(p.z, p.c)
        self.go(p.z < n - 1, self.src, dst, p.z, p.z, p.to_up)
        self.go(p.z > 0, self.src, dst, n + p.z, p.z, p.to_down)
        self.go(None, self.src, dst, 2 * n + p.z, n + p.z, p.to_core)

    def line(self, d):
        p, n = self.p, self.p.depth
        for side in (-1, 1):
            z = p.z + side * d
            here = (z >= 0) & (z <= n - 1)
            dst = self.piece(z, p.c)
            pl.when(here)(lambda: self.got(dst, z))
            if side < 0:
                self.go(here & (p.z < n - 1), dst, dst, z, z, p.to_up)
            else:
                self.go(here & (p.z > 0), dst, dst, n + z, z, p.to_down)
            self.go(here, dst, dst, 2 * n + z, n + z, p.to_core)

    def shared(self):
        n = self.p.depth
        for z in range(n):
            self.got(self.piece(z, 1 - self.p.c), n + z)

    def sent(self):
        for wait in self.pending:
            wait()


class Plane:
    def __init__(self, place, src, dst, sends, recvs):
        self.p, self.src, self.dst, self.sends, self.recvs = place, src, dst, sends, recvs

    def to(self, q):
        p = self.p
        return (p.b + (2 - 4 * p.y) * (q // 2), p.x + (1 - 2 * p.x) * (q % 2))

    def copy(self, q):
        return remote(self.src(q), self.dst(q), self.sends.at[q], self.recvs.at[q], self.to(q))

    def start(self):
        for q in (1, 2, 3):
            self.copy(q).start()

    def arrived(self):
        for q in (1, 2, 3):
            self.copy(q).wait_recv()

    def finish(self):
        for q in (1, 2, 3):
            self.copy(q).wait_send()


class Rounds:
    def __init__(self, place, sends, recvs):
        self.p, self.sends, self.recvs = place, sends, recvs

    def one(self, k, src, dst, to):
        return remote(src, dst, self.sends.at[k], self.recvs.at[k], to)

    def line(self, k, d):
        p = self.p
        z = (p.z + d) % p.depth
        return (p.b + 4 * (z - p.z), p.x)


class Octet:
    def __init__(self, place, src, dst, sends, recvs):
        self.p, self.src, self.dst, self.sends, self.recvs = place, src, dst, sends, recvs
        self.slot = place.y * 4 + place.c * 2 + place.x

    def copy(self, k):
        to = (self.slot + k) % 8
        device = (self.p.z * 4 + to // 2, to % 2)
        return remote(self.src(to), self.dst(self.slot), self.sends.at[k], self.recvs.at[k], device)

    def start(self):
        for k in range(1, 8):
            self.copy(k).start()

    def arrived(self):
        for k in range(1, 8):
            came = self.dst((self.slot + 8 - k) % 8)
            remote(came, came, self.sends.at[k], self.recvs.at[k], self.p.to_x).wait_recv()

    def finish(self):
        for k in range(1, 8):
            self.copy(k).wait_send()


class Quad:
    def __init__(self, p, axis, src, dst, sems):
        self.p, self.src, self.dst, self.sems = p, src, dst, sems
        self.to_pair = p.to_y if axis == 0 else p.to_x

    def to_core(self):
        return remote(self.src, self.dst(1), self.sems(0), self.sems(1), self.p.to_core)

    def to_next(self):
        return remote(self.src, self.dst(2), self.sems(2), self.sems(3), self.to_pair)

    def on(self):
        return remote(self.dst(2), self.dst(3), self.sems(4), self.sems(5), self.p.to_core)

    def start(self):
        self.to_next().start()
        self.to_core().start()

    def relay(self):
        self.to_next().wait_recv()
        self.on().start()

    def arrived(self):
        self.to_core().wait_recv()
        self.on().wait_recv()

    def finish(self):
        self.to_next().wait_send()
        self.to_core().wait_send()
        self.on().wait_send()


class QuadRows:
    def __init__(self, p, axis, src, dst, sems):
        self.p, self.axis, self.src, self.dst, self.sems = p, axis, src, dst, sems

    def mine(self, side, c):
        return self.src.at[:, side, c] if self.axis == 0 else self.src.at[:, :, c, side]

    def own(self):
        p = self.p
        side = p.y if self.axis == 0 else p.x
        return pltpu.make_async_copy(self.mine(side, p.c), self.dst.at[0], self.sems.at[0])

    def copy(self, k):
        p = self.p
        side = p.y if self.axis == 0 else p.x
        pair, far = (p.to_y, p.to_far) if self.axis == 0 else (p.to_x, p.to_far_x)
        side, c, to = ((side, 1 - p.c, p.to_core), (1 - side, p.c, pair), (1 - side, 1 - p.c, far))[k - 1]
        return remote(self.mine(side, c), self.dst.at[k], self.sems.at[2 * k - 1], self.sems.at[2 * k], to)

    def start(self):
        self.own().start()
        for k in (2, 3, 1):
            self.copy(k).start()

    def arrived(self):
        self.own().wait()
        for k in (1, 2, 3):
            self.copy(k).wait_recv()

    def finish(self):
        for k in (1, 2, 3):
            self.copy(k).wait_send()


class Reduce:
    CHUNK = 512

    def __init__(self, place, axis, x, take, rows, lo, width, out, full, outgo, income, sends, recvs):
        self.p, self.x, self.take, self.rows = place, x, take, rows
        self.side = place.x if axis == 0 else place.y
        self.to_other = place.to_x if axis == 0 else place.to_y
        self.lo, self.width, self.out = lo, width, out
        self.full, self.outgo, self.income = full, outgo, income
        self.sends, self.recvs = sends, recvs
        self.first = place.depth
        self.chunk = min(self.CHUNK, width)

    @staticmethod
    def scratch(rows, width, depth):
        return [
            pltpu.VMEM((2 * depth * rows, width), jnp.bfloat16),
            pltpu.VMEM(((2 * depth + 1) * rows, width), jnp.bfloat16),
            pltpu.SemaphoreType.DMA((4,)),
            pltpu.SemaphoreType.DMA((4,)),
        ]

    def part(self, ref, lo, hi):
        return ref.at[pl.ds(lo * self.rows, (hi - lo) * self.rows)]

    def across(self):
        n = self.p.depth
        return remote(
            self.part(self.outgo, 0, n), self.part(self.income, 0, n), self.sends.at[0], self.recvs.at[0], self.to_other
        )

    def up(self, lo):
        f, n = self.first, self.p.depth
        return remote(
            self.part(self.outgo, f + lo, f + n),
            self.part(self.income, f + lo, f + n),
            self.sends.at[1],
            self.recvs.at[1],
            self.p.to_up,
        )

    def down(self, hi):
        f = self.first
        return remote(
            self.part(self.outgo, f, f + hi),
            self.part(self.income, f, f + hi),
            self.sends.at[2],
            self.recvs.at[2],
            self.p.to_down,
        )

    def down_last(self, at):
        f, n = self.first, self.p.depth
        return remote(
            self.part(self.outgo, f + at, f + at + 1),
            self.part(self.income, f + n, f + n + 1),
            self.sends.at[3],
            self.recvs.at[3],
            self.p.to_down,
        )

    def columns(self, body):
        @pl.loop(0, self.width // self.chunk)
        def _(j):
            body(j, pl.ds(pl.multiple_of(j * self.chunk, self.chunk), self.chunk))

    def product(self, side, j):
        n, r = self.p.depth, self.rows
        x = jnp.concatenate([self.x[k, :, side].reshape(n * r, self.x.shape[4]) for k in range(4)], 1)
        return jnp.dot(x, self.take(self.lo // self.chunk + j), preferred_element_type=jnp.float32)

    def begin(self):
        p, n, r = self.p, self.p.depth, self.rows

        def away(j, here):
            self.outgo[pl.ds(0, n * r), here] = self.product(1 - self.side, j).astype(jnp.bfloat16)

        self.columns(away)
        self.across().start()

        def near(j, here):
            self.full[pl.ds(0, n * r), here] = self.product(self.side, j)

        self.columns(near)

        self.zeros()

    def zeros(self):
        p, f, n = self.p, self.first, self.p.depth

        @pl.when(p.z == 0)
        def _():
            ref = self.part(self.income, f, f + 1)
            ref[...] = jnp.zeros(ref.shape, ref.dtype)

        @pl.when(p.z == n - 1)
        def _():
            ref = self.part(self.income, f + n, f + n + 1)
            ref[...] = jnp.zeros(ref.shape, ref.dtype)

    def total(self, h, lo, hi):
        f, r = self.first, self.rows

        def body(j, here):
            rows = pl.ds(lo * r, (hi - lo) * r)
            line = pl.ds((f + lo) * r, (hi - lo) * r)
            total = self.full[rows, here]
            if f:
                total = total + self.income[rows, here].astype(jnp.float32)
            if h:
                total = total + self.income[line, here].astype(jnp.float32)
            self.outgo[line, here] = total.astype(jnp.bfloat16)

        self.columns(body)

    def hop(self, h):
        p, n = self.p, self.p.depth
        if h == 0 and self.first:
            self.across().wait_recv()

        @pl.when(p.z == h)
        def _():
            if h:
                self.up(h).wait_recv()
            self.total(h, h + 1, n)
            self.up(h + 1).start()

        @pl.when(p.z == n - 1 - h)
        def _():
            if h:
                self.down(n - 1 - h).wait_recv()
            self.total(h, 0, n - 1 - h)
            if h < n - 2:
                self.down(n - 2 - h).start()
            self.down_last(n - 2 - h).start()

    def last_waits(self):
        p, n = self.p, self.p.depth
        pl.when(p.z == n - 1)(lambda: self.up(n - 1).wait_recv())
        pl.when(p.z < n - 1)(lambda: self.down_last(0).wait_recv())

    def end(self):
        p, n, r = self.p, self.p.depth, self.rows
        self.last_waits()
        own = pl.ds(pl.multiple_of(p.z * r, r), r)
        line = pl.ds(pl.multiple_of((n + p.z) * r, r), r)

        def body(j, here):
            there = pl.ds(pl.multiple_of(self.lo + j * self.chunk, self.chunk), self.chunk)
            self.out[:, there] = (
                self.full[own, here]
                + self.income[own, here].astype(jnp.float32)
                + self.income[line, here].astype(jnp.float32)
                + self.income[pl.ds(2 * n * r, r), here].astype(jnp.float32)
            )

        self.columns(body)

    def finish(self):
        p, n = self.p, self.p.depth
        if self.first:
            self.across().wait_send()
        for h in range(n - 1):
            pl.when(p.z == h)(lambda: self.up(h + 1).wait_send())

            @pl.when(p.z == n - 1 - h)
            def _():
                if h < n - 2:
                    self.down(n - 2 - h).wait_send()
                self.down_last(n - 2 - h).wait_send()


class LineReduce(Reduce):
    def __init__(self, place, product, rows, width, full, outgo, income, sends, recvs):
        self.p, self.make, self.rows, self.width = place, product, rows, width
        self.full, self.outgo, self.income = full, outgo, income
        self.sends, self.recvs = sends, recvs
        self.first = 0
        self.chunk = min(self.CHUNK, width)

    @staticmethod
    def scratch(rows, width, depth):
        return [
            pltpu.VMEM((depth * rows, width), jnp.bfloat16),
            pltpu.VMEM(((depth + 1) * rows, width), jnp.bfloat16),
            pltpu.SemaphoreType.DMA((4,)),
            pltpu.SemaphoreType.DMA((4,)),
        ]

    def begin(self):
        def near(j, here):
            self.full[:, here] = self.make(j)

        self.columns(near)
        self.zeros()

    def end(self, write):
        self.last_waits()
        n, r = self.p.depth, self.rows
        own = pl.ds(pl.multiple_of(self.p.z * r, r), r)

        def body(j, here):
            write(
                here,
                self.full[own, here]
                + self.income[own, here].astype(jnp.float32)
                + self.income[pl.ds(n * r, r), here].astype(jnp.float32),
            )

        self.columns(body)


VMEM_BYTES = 62 * 2**20


def kernel_params(number):
    return pltpu.CompilerParams(collective_id=number, has_side_effects=True, vmem_limit_bytes=VMEM_BYTES)


def in_vmem(count):
    return [pl.BlockSpec(memory_space=pltpu.VMEM)] * count


def in_any(count):
    return [pl.BlockSpec(memory_space=pl.ANY)] * count


def ranges(cols, cut):
    return [(0, cut, True), (cut, cols, False)] if cut else [(0, cols, False)]


def keep_own(p, pairs, sems):
    copies = []
    for k, (src, dst, rows) in enumerate(pairs):
        at = pl.multiple_of(p.shard(p.z, p.y, p.c, p.x) * rows, rows)
        copies.append(pltpu.make_async_copy(src, dst.at[pl.ds(at, rows)], sems.at[k]))
    for copy in copies:
        copy.start()
    return copies


class Exchange:
    def __init__(self, place, count, src, dst, sends, recvs, own):
        self.p, self.count, self.src, self.dst = place, count, src, dst
        self.sends, self.recvs, self.own = sends, recvs, own

    def copy(self, k):
        to = (self.p.b + k) % self.count
        return remote(
            self.src.at[to], self.dst.at[self.p.b], self.sends.at[k], self.recvs.at[k], (to, self.p.x)
        )

    def mine(self):
        return pltpu.make_async_copy(self.src.at[self.p.b], self.dst.at[self.p.b], self.own)

    def start(self):
        self.mine().start()
        for k in range(1, self.count):
            self.copy(k).start()

    def send_to(self, device):
        k = (device + self.count - self.p.b) % self.count
        pl.when(k > 0)(lambda: self.copy(k).start())
        pl.when(k == 0)(lambda: self.mine().start())

    def wait_from(self, device):
        k = (self.p.b + self.count - device) % self.count

        @pl.when(k > 0)
        def _():
            came = self.dst.at[device]
            remote(came, came, self.sends.at[k], self.recvs.at[k], self.p.to_x).wait_recv()

        pl.when(k == 0)(lambda: self.mine().wait())

    def arrived(self):
        self.mine().wait()
        for k in range(1, self.count):
            came = (self.p.b + self.count - k) % self.count
            remote(
                self.dst.at[came], self.dst.at[came], self.sends.at[k], self.recvs.at[k], self.p.to_x
            ).wait_recv()

    def finish(self):
        for k in range(1, self.count):
            self.copy(k).wait_send()


def exchange_sems(count):
    return [
        pltpu.SemaphoreType.DMA((count,)),
        pltpu.SemaphoreType.DMA((count,)),
        pltpu.SemaphoreType.DMA,
    ]


def greet_plane(p, count, more):
    barrier = pltpu.get_barrier_semaphore()
    for to in more:
        pl.semaphore_signal(barrier, inc=1, device_id=to, device_id_type=MESH)
    for k in range(1, count):
        pl.semaphore_signal(barrier, inc=1, device_id=((p.b + k) % count, p.x), device_id_type=MESH)
    pl.semaphore_signal(barrier, inc=1, device_id=p.to_x, device_id_type=MESH)
    pl.semaphore_wait(barrier, count + len(more))


def play(events):
    for event in events:
        event()


def three_terms(v):
    a = v.astype(jnp.bfloat16).astype(jnp.float32)
    b = (v - a).astype(jnp.bfloat16).astype(jnp.float32)
    return a, b, v - a - b


def extra_rows(rows, length, width):
    shape = (length, width)
    row = lax.broadcasted_iota(jnp.int32, shape, 0)
    total = jnp.zeros(shape, jnp.float32)
    for k, values in enumerate(rows):
        total = jnp.where(row == k, values, total)
    return total.astype(jnp.bfloat16)


def attend_open(p, lengths, got_kv, qkv, keys, values):
    count, _, span = got_kv.shape
    frames = count * span
    for k in range(count):
        qkv[HEAD_DIM:, k * span : (k + 1) * span] = got_kv[k]
    position = lax.broadcasted_iota(jnp.int32, (1, frames), 1)
    hidden_key = jnp.where(position < lengths[p.x], 0.0, -1e30)
    keys[...] = jnp.concatenate([qkv[HEAD_DIM : 2 * HEAD_DIM, :], extra_rows([hidden_key], HEAD_DIM, frames)], 0).T
    values[...] = jnp.concatenate([qkv[2 * HEAD_DIM :, :], extra_rows([1.0], 16, frames)], 0)


def in_turn(p, i, blocks):
    return (p.b // 2 + blocks - i) % blocks


def attend(p, lengths, queries, qkv, keys, values, results, lse, plain, lo, hi):
    count, _, span = queries.dst.shape
    block = 2 * span
    length = lengths[p.x]
    ones = extra_rows([1.0], HEAD_DIM, block)
    scaling = HEAD_DIM ** (-0.5)

    @pl.loop(lo, hi)
    def _(i):
        j = in_turn(p, i, count // 2)
        here = pl.ds(pl.multiple_of(j * block, block), block)
        for k in range(2):
            queries.wait_from(2 * j + k)
        query = jnp.concatenate([queries.dst[2 * j], queries.dst[2 * j + 1]], 1)
        qkv[:HEAD_DIM, here] = query
        query = jnp.concatenate([query * jnp.bfloat16(scaling), ones], 0)
        score = jnp.dot(keys[...], query, preferred_element_type=jnp.float32)
        peak = jnp.max(score, 0, keepdims=True)
        weights = jnp.exp(score - peak).astype(jnp.bfloat16)
        out = jnp.dot(values[...], weights, preferred_element_type=jnp.float32)
        total = out[HEAD_DIM : HEAD_DIM + 1]
        out = out[:HEAD_DIM] / total
        plain[:, here] = out
        lse[:, here] = peak + jnp.log(total)
        column = lax.broadcasted_iota(jnp.int32, (HEAD_DIM, block), 1) + j * block
        kept = jnp.where(column < length, out, 0.0).astype(jnp.bfloat16)
        for k in range(2):
            results.src[2 * j + k] = kept[:, k * span : (k + 1) * span]
            results.send_to(2 * j + k)


def attend_back_open(p, lengths, qkv, keys, values, sums):
    frames = qkv.shape[1]
    length = lengths[p.x]
    position = lax.broadcasted_iota(jnp.int32, (1, frames), 1)
    hidden_key = jnp.where(position < length, 0.0, -1e30)
    keys[...] = jnp.concatenate(
        [qkv[HEAD_DIM : 2 * HEAD_DIM, :], extra_rows([hidden_key, 1.0, 1.0, 1.0], HEAD_DIM, frames)], 0
    ).T
    values[...] = jnp.concatenate(
        [qkv[2 * HEAD_DIM :, :], extra_rows([1.0, 1.0, 1.0], HEAD_DIM, frames)], 0
    ).T
    sums[...] = jnp.zeros_like(sums)


def attend_back(p, upstreams, qkv, lse, plain, keys, values, sums, results, lo, hi):
    count, _, span = upstreams.dst.shape
    block = 2 * span
    scaling = HEAD_DIM ** (-0.5)

    @pl.loop(lo, hi)
    def _(i):
        j = in_turn(p, i, count // 2)
        here = pl.ds(pl.multiple_of(j * block, block), block)
        for k in range(2):
            upstreams.wait_from(2 * j + k)
        query = qkv[:HEAD_DIM, here] * jnp.bfloat16(scaling)
        upstream = jnp.concatenate([upstreams.dst[2 * j], upstreams.dst[2 * j + 1]], 1)
        delta = jnp.sum(upstream.astype(jnp.float32) * plain[:, here], 0, keepdims=True)
        left = jnp.concatenate(
            [query, extra_rows([1.0, *[-t for t in three_terms(lse[:, here])]], HEAD_DIM, block)], 0
        )
        right = jnp.concatenate([upstream, extra_rows([-t for t in three_terms(delta)], HEAD_DIM, block)], 0)
        weights = jnp.exp(jnp.dot(keys[...], left, preferred_element_type=jnp.float32))
        slope = jnp.dot(values[...], right, preferred_element_type=jnp.float32)
        slope = (weights * slope).astype(jnp.bfloat16)
        query_grad = (
            jnp.dot(qkv[HEAD_DIM : 2 * HEAD_DIM, :], slope, preferred_element_type=jnp.float32) * scaling
        ).astype(jnp.bfloat16)
        for k in range(2):
            results.src[2 * j + k] = query_grad[:, k * span : (k + 1) * span]
            results.send_to(2 * j + k)
        sums[:, HEAD_DIM:] += lax.dot_general(
            weights.astype(jnp.bfloat16), upstream, (((1,), (1,)), ((), ())), preferred_element_type=jnp.float32
        )
        sums[:, :HEAD_DIM] += lax.dot_general(
            slope, query, (((1,), (1,)), ((), ())), preferred_element_type=jnp.float32
        )


def attend_back_close(sums, grads_out):
    count, _, span = grads_out.shape

    @pl.loop(0, count)
    def _(k):
        rows = pl.ds(pl.multiple_of(k * span, span), span)
        grads_out[k] = sums[rows, :].T.astype(jnp.bfloat16)


def others(p, count, k):
    number = (p.b * 2 + p.x + k) % (2 * count)
    return (number // 2, number % 2)


def nt(left, right):
    return lax.dot_general(left, right, (((1,), (1,)), ((), ())), preferred_element_type=jnp.float32)


def mean(v):
    return jnp.mean(v, -1, keepdims=True)


def normal(v):
    center = v - mean(v)
    rstd = lax.rsqrt(mean(center * center) + epsilon)
    return center * rstd, rstd


def normal_back(grad, hat, rstd, scale):
    gx = grad * (1.0 + scale)
    return rstd * (gx - mean(gx) - hat * mean(gx * hat))


def fold(v):
    width = v.shape[1] // 8
    return jnp.concatenate([v[:, k * width : (k + 1) * width] for k in range(8)], 0)


class Refs:
    def __init__(self, names, refs):
        for name, ref in zip(names, refs):
            setattr(self, name, ref)


def back_kernel(depth, shards, names, *refs):
    r = Refs(names, refs)
    rest = list(refs[len(names) :])
    p = Place(depth)
    count = 4 * depth
    devices = 2 * count
    frames, model = r.base.shape
    half = model // 2
    chunk = 512
    bf = jnp.bfloat16
    units = r.w_up.shape[1]

    barrier = pltpu.get_barrier_semaphore()
    for k in range(1, devices):
        pl.semaphore_signal(barrier, inc=1, device_id=others(p, count, k), device_id_type=MESH)

    def fetch(src, slot):
        return pltpu.make_async_copy(src, r.weights.at[slot], r.weight_sems.at[slot])

    def columns(ref, k):
        return ref.at[:, pl.ds(k * chunk, chunk)]

    def fetch_first(slot):
        return fetch(columns((r.w_out, r.w_up, r.w_down)[slot // 2], slot % 2), slot)

    def fetch_qkv(slot):
        return fetch(columns(r.w_qkv, slot), slot)

    def fetch_skip(slot):
        return fetch(r.w_skip.at[pl.ds((slot // 2) * model, model), pl.ds((slot % 2) * chunk, chunk)], slot)

    late_loads = [
        pltpu.make_async_copy(src, dst, r.load_sems.at[k])
        for k, (src, dst) in enumerate(
            ((r.cot_far, r.cot_all), (r.qkv_far, r.qkv), (r.plain_far, r.plain), (r.xnormed_far, r.xnormed),
             (r.xjoined_far, r.xjoined))
        )
    ]
    for slot in range(6):
        fetch_first(slot).start()
    for copy in late_loads:
        copy.start()
    pl.semaphore_wait(barrier, devices - 1)

    def to_sibling(src, dst, k):
        return remote(src, dst, r.pair_sems.at[0, k], r.pair_sems.at[1, k], p.to_core)

    pair_cot = to_sibling(r.cot_all, r.cot_sib, 0)
    pair_n2 = to_sibling(r.n2_all, r.n2_sib, 1)
    pair_act = to_sibling(r.act.at[1 - p.c], r.act_sib, 2)
    pair_gin = to_sibling(r.gin.at[1 - p.c], r.gin_sib, 3)
    plane_n2 = Plane(p, lambda q: r.n2_all.at[0], lambda q: r.n2_all.at[q], r.n2_sems.at[0], r.n2_sems.at[1])
    plane_back = Plane(
        p, lambda q: r.part_back.at[q - 1], lambda q: r.got_back.at[q - 1], r.back_sems.at[0], r.back_sems.at[1]
    )
    plane_total = Plane(
        p, lambda q: r.part_total.at[q - 1], lambda q: r.got_total.at[q - 1], r.total_sems.at[0], r.total_sems.at[1]
    )
    share_mixed = QuadRows(p, 0, r.mixed, r.xmix, r.row_sems.at[0])
    share_branch = Quad(p, 0, r.gbranch.at[0], lambda k: r.gbranch.at[k], lambda k: r.branch_sems.at[k])

    def share_late(c):
        return Quad(p, c // 6, r.glate.at[0, c], lambda k: r.glate.at[k, c], lambda k: r.late_sems.at[c, k])

    length = r.lengths[p.x]
    position = p.b * frames
    kept = (position + lax.broadcasted_iota(jnp.int32, (frames, 1), 0) < length).astype(jnp.float32)
    kept_row = (position + lax.broadcasted_iota(jnp.int32, (1, frames), 1) < length).astype(jnp.float32)
    a_scale = kept * r.mods[0:1, :]
    f_scale = kept * r.mods[2:3, :]
    f_shift = kept * r.mods[3:4, :]
    mixed = r.mixed[...].reshape(model, frames).T
    for k in range(2):
        fetch_first(k).wait()
        cols = pl.ds(k * chunk, chunk)
        r.middle[:, cols] = r.base[:, cols] + jnp.dot(mixed, r.weights[k], preferred_element_type=jnp.float32)
    hat, rstd = normal(r.middle[...])
    r.n2_all[0] = (hat * (1.0 + f_scale) + f_shift).astype(bf)
    plane_n2.start()
    r.bias[...] = jnp.zeros_like(r.bias)
    for slot in range(2, 6):
        fetch_first(slot).wait()
    for copy in late_loads:
        copy.wait()
    pair_cot.start()

    @pl.loop(0, 4)
    def _(q):
        pl.when(q > 0)(lambda: plane_n2.copy(q).wait_recv())
        acts, grads = [], []
        for u in range(2):
            cols = pl.ds(u * chunk, chunk)
            inner = jnp.dot(r.n2_all[q], r.weights[2 + u], preferred_element_type=jnp.float32) + r.b_up[:, cols]
            cdf = 0.5 * (1.0 + lax.erf(inner * (0.5**0.5)))
            act = (inner * cdf).astype(bf)
            slope = cdf + inner * (jnp.exp(-0.5 * inner * inner) * (1.0 / math.sqrt(2.0 * math.pi)))
            act_grad = nt(r.cot_all[q, :, :half], r.weights[4, cols, :]) + nt(
                r.cot_all[q, :, half:], r.weights[5, cols, :]
            )
            grad = (act_grad * slope).astype(bf)
            r.bias[:, cols] += jnp.sum(grad.astype(jnp.float32), 0, keepdims=True)
            for k in range(4):
                here = slice(k * 128, (k + 1) * 128)
                at = (2 * u + k // 2) * 128
                r.act[k % 2, q, :, at : at + 128] = act[:, here]
                r.gin[k % 2, q, :, at : at + 128] = grad[:, here]
            acts.append(act)
            grads.append(grad)
        back = nt(grads[0], r.weights[2]) + nt(grads[1], r.weights[3])

        @pl.when(q == 0)
        def _():
            r.back[...] = back

        @pl.when(q > 0)
        def _():
            r.part_back[q - 1] = back.astype(bf)
            plane_back.copy(q).start()

        for k in range(2):
            cols = slice(k * half, (k + 1) * half)
            total = jnp.dot(acts[0], r.weights[4 + k, :chunk, :], preferred_element_type=jnp.float32)
            total = total + jnp.dot(acts[1], r.weights[4 + k, chunk:, :], preferred_element_type=jnp.float32)

            @pl.when(q == 0)
            def _():
                r.own_total[:, cols] = total

            @pl.when(q > 0)
            def _():
                r.part_total[q - 1, :, cols] = total.astype(bf)

    def blocks_of(first):
        return lambda j: jnp.concatenate([r.glate[k, first + j] for k in range(4)], 0)

    def branch_columns(j):
        here = pl.ds(pl.multiple_of(j * chunk, chunk), chunk)
        return jnp.concatenate([r.gbranch[k, :, here] for k in range(4)], 0)

    def tn(left, right):
        return lax.dot_general(left, right, (((0,), (0,)), ((), ())), preferred_element_type=jnp.float32)

    def flat(v):
        return v.reshape(4 * frames, v.shape[2])

    def down_part(k):
        cols = slice(k * half, (k + 1) * half)

        def make(j):
            mine = tn(flat(r.act[p.c]), flat(r.cot_all[:, :, cols]))
            return mine + tn(flat(r.act_sib[...]), flat(r.cot_sib[:, :, cols]))

        return make

    def up_part(k):
        cols = slice(k * 256, (k + 1) * 256)

        def make(j):
            mine = tn(flat(r.n2_all[...]), flat(r.gin[p.c, :, :, cols]))
            return mine + tn(flat(r.n2_sib[...]), flat(r.gin_sib[:, :, cols]))

        return make

    down, up, out, qkv, skip = [], [], [], [], []
    group = model // depth
    for k in range(2):
        down.append(LineReduce(p, down_part(k), units // (2 * depth), half, *rest[:5]))
        rest = rest[5:]
    for k in range(2):
        up.append(LineReduce(p, up_part(k), group, 256, *rest[:5]))
        rest = rest[5:]
    for sums, axis, x, take, res, (rows, cols, parts) in (
        (out, 0, r.xmix, branch_columns, r.out_grad, shards[0]),
        (qkv, 0, r.xnormed, blocks_of(0), r.qkv_grad, shards[1]),
        (skip, 1, r.xjoined, blocks_of(6), r.skip_grad, shards[2]),
    ):
        width = cols // parts
        for k in range(parts):
            sums.append(Reduce(p, axis, x, take, rows, k * width, width, res, *rest[:5]))
            rest = rest[5:]

    pair_act.start()
    pair_n2.start()
    pair_gin.start()
    pair_cot.wait_recv()
    pair_act.wait_recv()
    down[0].begin()
    down[0].hop(0)
    plane_back.arrived()
    middle = r.middle[...]
    hat, rstd = normal(middle)
    grad = r.back[...]
    for k in range(3):
        grad = grad + r.got_back[k].astype(jnp.float32)
    cot = r.cot_all[0].astype(jnp.float32)
    middle_grad = cot + normal_back(grad, hat, rstd, f_scale)
    r.back[...] = middle_grad
    branch_grad = middle_grad.astype(bf)
    r.gbranch[0] = branch_grad
    there = Exchange(p, count, r.mixed_grad, r.got, r.s1, r.r1, r.o1)
    back = Exchange(p, count, r.grads_out, r.got_grads, r.s2, r.r2, r.o2)
    queries = Exchange(p, count, r.queries_out, r.got_queries, r.s3, r.r3, r.o3)
    mixed_grad = nt(r.weights[0], branch_grad[:, :half]) + nt(r.weights[1], branch_grad[:, half:])
    r.mixed_grad[...] = (mixed_grad.astype(bf) * kept_row.astype(bf)).reshape(r.mixed_grad.shape)
    there.start()
    plane_total.start()
    share_mixed.start()
    share_branch.start()
    for slot in range(6):
        fetch_qkv(slot).start()
    r.vectors[2:3, :] = jnp.sum(kept * grad * hat, 0, keepdims=True)
    r.vectors[3:4, :] = jnp.sum(kept * grad, 0, keepdims=True)

    def end_down(k):
        def write(here, total):
            r.down_grad[:, pl.ds(pl.multiple_of(k * half + here.start, 128), here.size)] = total

        down[k].end(write)

    def end_up(k):
        def write(here, total):
            r.up_out[:, :, k * 256 : (k + 1) * 256] = total.astype(bf).reshape(8, group // 8, 256)

        up[k].end(write)

    ups = Octet(p, lambda to: r.up_out.at[to], lambda slot: r.up_got.at[slot], r.up_sems.at[0], r.up_sems.at[1])

    def up_spread():
        ups.start()
        r.up_got[ups.slot] = r.up_out[ups.slot]

    def up_arrived():
        ups.arrived()
        for t in range(8):
            for z in range(depth):
                at = (z * 8 + t) * 128
                r.up_grad[:, at : at + 128] = r.up_got[t, :, z * 128 : (z + 1) * 128].astype(jnp.float32)

    def ready(shares):
        for share in shares:
            if isinstance(share, Quad):
                share.relay()
        for share in shares:
            share.arrived()

    blocks = r.qkv.shape[1] // 256
    attend_back_open(p, r.lengths, r.qkv, r.keys, r.values, r.kv_sums)
    attend = functools.partial(
        attend_back, p, there, r.qkv, r.lse, r.plain, r.keys, r.values, r.kv_sums, queries
    )
    down[1].begin()
    down[1].hop(0)
    attend(0, blocks // 2)
    down[0].hop(1)
    attend(blocks // 2, blocks)
    attend_back_close(r.kv_sums, r.grads_out)
    back.start()
    down[1].hop(1)

    cosine, sine = r.cosine[...][None], r.sine[...][None]

    def send_part(part, h):
        h = h.reshape(model, frames).T
        for k in range(2):
            r.glate[0, 2 * part + k] = h[:, k * chunk : (k + 1) * chunk]
            share_late(2 * part + k).start()

    queries.arrived()
    send_part(0, turn(r.got_queries[...].astype(jnp.float32), cosine, -sine).astype(bf))
    for k in range(2):
        fetch_qkv(k).wait()
        made = nt(r.glate[0, k], r.weights[k])
        if k == 0:
            r.total[...] = made
        else:
            r.total[...] += made
    down[0].hop(2)
    pair_n2.wait_recv()
    pair_gin.wait_recv()
    up[0].begin()
    up[0].hop(0)
    plane_total.arrived()
    total = r.middle[...] + r.own_total[...] + r.b_down[...]
    for k in range(3):
        total = total + r.got_total[k].astype(jnp.float32)
    r.output[...] = total.astype(bf)
    ready([share_mixed, share_branch])
    out[0].begin()
    up[1].begin()
    up[1].hop(0)
    ready([share_late(0), share_late(1)])
    qkv[0].begin()
    back.arrived()
    send_part(1, turn(r.got_grads[:, :HEAD_DIM, :].astype(jnp.float32), cosine, -sine).astype(bf))
    send_part(2, r.got_grads[:, HEAD_DIM:, :])
    for k in range(2, 6):
        fetch_qkv(k).wait()
        r.total[...] += nt(r.glate[0, k], r.weights[k])
    for k in range(4):
        fetch_skip(k).start()
    hat, rstd = normal(r.base[...])
    grad = r.total[...]
    base_grad = (r.back[...] + normal_back(grad, hat, rstd, a_scale)).astype(bf)
    for k in range(2):
        r.glate[0, 6 + k] = base_grad[:, k * chunk : (k + 1) * chunk]
        share_late(6 + k).start()
    r.vectors[0:1, :] = jnp.sum(kept * grad * hat, 0, keepdims=True)
    r.vectors[1:2, :] = jnp.sum(kept * grad, 0, keepdims=True)

    r.vectors[4:5, :] = jnp.sum(cot, 0, keepdims=True)
    r.vectors[5:6, :] = jnp.sum(base_grad.astype(jnp.float32), 0, keepdims=True)
    r.vectors[6:7, :] = r.bias[...]
    r.vectors[7:8, :] = jnp.zeros((1, model), jnp.float32)
    smalls = Octet(p, lambda to: r.vectors, lambda slot: r.plane_got.at[slot], r.small_sems.at[0], r.small_sems.at[1])
    small = Rounds(p, r.line_sems.at[0], r.line_sems.at[1])

    def small_line(d):
        return small.one(d, r.line_out, r.line_got.at[d], small.line(0, d))

    def after_plane():
        r.plane_got[smalls.slot] = r.vectors[...]
        smalls.arrived()
        halves = []
        for x in range(2):
            total = r.plane_got[x]
            for k in range(1, 4):
                total = total + r.plane_got[2 * k + x]
            halves.append(total)
            r.line_out[4 * x : 4 * x + 4, :] = total[0:4]
        r.line_out[8:10, :] = halves[0][4:6] + halves[1][4:6]
        chip = p.y * 4 + p.x
        r.line_out[10:11, :] = r.plane_got[chip, 6:7, :] + r.plane_got[chip + 2, 6:7, :]
        r.line_out[11:16, :] = jnp.zeros((5, model), jnp.float32)
        for d in range(1, depth):
            small_line(d).start()

    smalls.start()
    down[1].hop(2)
    end_down(0)
    out[0].hop(0)
    up[0].hop(1)

    number = p.b * 2 + p.x
    timers = Octet(
        p,
        lambda to: r.times_full.at[number],
        lambda slot: r.times_full.at[p.z * 8 + slot],
        r.small_sems.at[2],
        r.small_sems.at[3],
    )

    def times_line(d):
        block = r.times_full.at[pl.ds(p.z * 8, 8)]
        return small.one(3 + d, block, block, small.line(0, d))

    def times_came(d):
        z = (p.z + depth - d) % depth
        block = r.times_full.at[pl.ds(z * 8, 8)]
        return small.one(3 + d, block, block, small.line(0, d))

    for i in range(2):
        total = None
        for j in range(2):
            fetch_skip(2 * i + j).wait()
            made = nt(r.glate[0, 6 + j], r.weights[2 * i + j])
            total = made if total is None else total + made
        r.joined_grad[i] = total.astype(bf)

    qkv[0].hop(0)
    end_down(1)
    up[1].hop(1)
    after_plane()
    out[0].hop(1)
    ready([share_late(6), share_late(7)])
    skip[0].begin()
    skip[1].begin()
    ready([share_late(2), share_late(3)])
    qkv[1].begin()
    up[0].hop(2)
    ready([share_late(4), share_late(5)])
    qkv[2].begin()
    out[0].hop(2)
    qkv[0].hop(1)
    up[1].hop(2)

    total = r.line_out[...]
    for d in range(1, depth):
        small_line(d).wait_recv()
        total = total + r.line_got[d]
    first, second = total[0:4], total[4:8]
    r.line_sum[...] = total
    total = jnp.zeros((8, r.w_mod.shape[0]), jnp.float32)
    turned = r.times[...].T
    share = r.w_mod.shape[0]
    for part in range(4):
        values = [first[part : part + 1, :], second[part : part + 1, :]]
        here = pl.ds(part * model, model)
        left = extra_rows([*three_terms(values[0]), *three_terms(values[1])], 8, model)
        total = total + nt(left, r.w_mod[:, here])
        r.mod_grad[:, here] = turned[:share, 0:1] * values[0] + turned[:share, 4:5] * values[1]
    made = jnp.concatenate(
        [total[0:1] + total[1:2] + total[2:3], total[3:4] + total[4:5] + total[5:6], jnp.zeros((6, share), jnp.float32)]
    )
    r.times_full[number] = jnp.concatenate([made, jnp.zeros((8, 128 - share), jnp.float32)], 1)
    timers.start()
    skip[0].hop(0)
    qkv[1].hop(0)
    qkv[0].hop(2)
    end_up(0)
    skip[1].hop(0)
    skip[0].hop(1)
    qkv[1].hop(1)
    qkv[2].hop(0)
    end_up(1)
    up_spread()
    timers.arrived()
    for d in range(1, depth):
        times_line(d).start()
    r.sums_out[...] = jnp.zeros_like(r.sums_out)
    at = pl.multiple_of((p.z * 2 + p.c) * 128, 128)
    r.sums_out[0:1, :] = r.line_sum[10:11, pl.ds(at, 128)]
    at = pl.multiple_of(number // 4 * 128, 128)
    near = r.line_sum[8:10, pl.ds(at, 128)]
    each = model // devices
    own = near[:, :each]
    for k in range(1, 4):
        own = jnp.where(number % 4 == k, near[:, k * each : (k + 1) * each], own)
    r.sums_out[1:2, :each] = own[0:1]
    r.sums_out[1:2, each : 2 * each] = own[1:2]
    out[0].end()
    qkv[0].end()
    skip[0].hop(2)
    skip[1].hop(1)
    qkv[1].hop(2)
    qkv[2].hop(1)
    skip[0].end()
    skip[1].hop(2)
    qkv[1].end()
    qkv[2].hop(2)
    skip[1].end()
    up_arrived()
    qkv[2].end()
    for d in range(1, depth):
        times_came(d).wait_recv()
    for one in [*down, *up, *out, *qkv, *skip, share_mixed, share_branch, plane_n2, plane_back, plane_total]:
        one.finish()
    for c in range(8):
        share_late(c).finish()
    for one in (pair_cot, pair_n2, pair_act, pair_gin):
        one.wait_send()
    for one in (there, back, queries, ups, smalls, timers):
        one.finish()
    for d in range(1, depth):
        small_line(d).wait_send()
        times_line(d).wait_send()


def back_call(depth, devices, args):
    base, qkv = args["base"], args["qkv_far"]
    frames, model = base.shape
    count = devices // 2
    units = args["w_up"].shape[1]
    ff = units * 4
    bf, f32 = jnp.bfloat16, jnp.float32
    share = args["w_mod"].shape[0]
    dma = pltpu.SemaphoreType.DMA
    sum_scratch = []
    for rows, width in [(units // (2 * depth), model // 2)] * 2 + [(model // depth, 256)] * 2:
        sum_scratch.append(pltpu.VMEM((depth * rows, width), f32))
        sum_scratch += LineReduce.scratch(rows, width, depth)
    shards = [
        (model // devices, model, 1),
        (model // devices, 3 * model, 3),
        (2 * model // devices, model, 2),
    ]
    for rows, cols, parts in shards:
        for _ in range(parts):
            sum_scratch.append(pltpu.VMEM((depth * rows, cols // parts), f32))
            sum_scratch += Reduce.scratch(rows, cols // parts, depth)

    def tall(n, *shape, kind=bf):
        return pltpu.VMEM((n, *shape), kind)

    scratch = dict(
        cot_all=tall(4, frames, model),
        qkv=tall(*qkv.shape),
        plain=tall(HEAD_DIM, qkv.shape[1], kind=f32),
        xnormed=tall(4, depth, 2, model // devices, frames),
        xjoined=tall(4, depth, 2, 2 * model // devices, frames),
        load_sems=dma((5,)),
        weights=tall(6, model, 512),
        middle=tall(frames, model, kind=f32),
        total=tall(frames, model, kind=f32),
        own_total=tall(frames, model, kind=f32),
        back=tall(frames, model, kind=f32),
        bias=tall(1, units, kind=f32),
        vectors=tall(8, model, kind=f32),
        n2_all=tall(4, frames, model),
        n2_sib=tall(4, frames, model),
        cot_sib=tall(4, frames, model),
        act=tall(2, 4, frames, units // 2),
        gin=tall(2, 4, frames, units // 2),
        act_sib=tall(4, frames, units // 2),
        gin_sib=tall(4, frames, units // 2),
        part_back=tall(3, frames, model),
        got_back=tall(3, frames, model),
        part_total=tall(3, frames, model),
        got_total=tall(3, frames, model),
        up_out=tall(8, model // devices, units // 2),
        up_got=tall(8, model // devices, units // 2),
        gbranch=tall(4, frames, model),
        glate=tall(4, 8, frames, 512),
        xmix=tall(4, depth, 2, model // devices, frames),
        mixed_grad=tall(count, HEAD_DIM, frames),
        got=tall(count, HEAD_DIM, frames),
        keys=tall(qkv.shape[1], 2 * HEAD_DIM),
        values=tall(qkv.shape[1], 2 * HEAD_DIM),
        kv_sums=tall(qkv.shape[1], 2 * HEAD_DIM, kind=f32),
        grads_out=tall(count, 2 * HEAD_DIM, frames),
        got_grads=tall(count, 2 * HEAD_DIM, frames),
        queries_out=tall(count, HEAD_DIM, frames),
        got_queries=tall(count, HEAD_DIM, frames),
        plane_got=tall(8, 8, model, kind=f32),
        line_out=tall(16, model, kind=f32),
        line_got=tall(depth, 16, model, kind=f32),
        line_sum=tall(16, model, kind=f32),
        weight_sems=dma((6,)),
        pair_sems=dma((2, 4)),
        n2_sems=dma((2, 4)),
        back_sems=dma((2, 4)),
        total_sems=dma((2, 4)),
        up_sems=dma((2, 8)),
        row_sems=dma((1, 7)),
        branch_sems=dma((6,)),
        late_sems=dma((8, 6)),
        s1=dma((count,)),
        r1=dma((count,)),
        o1=dma,
        s2=dma((count,)),
        r2=dma((count,)),
        o2=dma,
        s3=dma((count,)),
        r3=dma((count,)),
        o3=dma,
        small_sems=dma((4, 8)),
        line_sems=dma((2, 8)),
    )
    shape = jax.ShapeDtypeStruct
    outs = dict(
        output=shape((frames, model), bf),
        joined_grad=shape((2, frames, model), bf),
        skip_grad=shape((2 * model // devices, model), f32),
        qkv_grad=shape((model // devices, 3 * model), f32),
        out_grad=shape((model // devices, model), f32),
        up_grad=shape((model // devices, ff), f32),
        down_grad=shape((ff // devices, model), f32),
        mod_grad=shape((share, 4 * model), f32),
        sums_out=shape((8, 128), f32),
        times_full=shape((devices, 8, 128), f32),
    )
    names = [*args, *outs, *scratch]
    vmem = pl.BlockSpec(memory_space=pltpu.VMEM)
    specs = dict.fromkeys(args, vmem)
    specs["lengths"] = pl.BlockSpec(memory_space=pltpu.SMEM)
    for name in args:
        if name.startswith("w_") and name != "w_mod" or name.endswith("_far"):
            specs[name] = pl.BlockSpec(memory_space=pl.ANY)
    made = pl.pallas_call(
        functools.partial(back_kernel, depth, shards, names),
        name="back",
        out_shape=list(outs.values()),
        in_specs=list(specs.values()),
        out_specs=[vmem] * len(outs),
        scratch_shapes=list(scratch.values()) + sum_scratch,
        compiler_params=kernel_params(3),
    )(*args.values())
    return dict(zip(outs, made))


def front_kernel(depth, cuts, names, *refs):
    r = Refs(names, refs)
    p = Place(depth)
    count = 4 * depth
    devices = 2 * count
    frames, model = r.hidden.shape
    bf = jnp.bfloat16
    share = r.w_mod.shape[0]
    tile = pl.ds(pl.multiple_of((p.b // 2) * 128, 128), 128)
    part = r.time_row[:, tile].astype(jnp.float32)
    mark = lax.broadcasted_iota(jnp.int32, (8, 128), 0) // 4 == p.x
    for ref, x in ((r.own_time, p.x), (r.other_time, 1 - p.x)):
        slot = p.c * 2 + x
        picked = part[:, 0:share]
        for k in range(1, 4):
            picked = jnp.where(slot == k, part[:, k * share : (k + 1) * share], picked)
        picked = jnp.concatenate([picked, jnp.zeros((1, 128 - share), jnp.float32)], 1)
        ref[...] = jnp.where(mark, picked, 0.0)
    half = HEAD_DIM // 2
    position = p.b * frames + lax.broadcasted_iota(jnp.int32, (half, frames), 1)
    length = r.lengths[p.x]
    offset = jnp.where(position < length, position, position - length).astype(jnp.float32)
    index = lax.broadcasted_iota(jnp.int32, (half, frames), 0).astype(jnp.float32)
    angle = offset * jnp.exp(index * (-math.log(10000.0) / half))
    r.cosine[...] = jnp.cos(angle)
    r.sine[...] = jnp.sin(angle)
    greet_plane(p, count, (p.to_across, p.to_far_x))
    ask = remote(r.other_time, r.got_time, r.time_sems.at[0], r.time_sems.at[1], p.to_x)
    ask.start()

    groups = {}
    number = 0
    owns = []
    for name, src, dst in (
        ("skip", r.w_skip, r.skip_full),
        ("qkv", r.w_qkv, r.qkv_full),
        ("out", r.w_out, r.out_full),
    ):
        groups[name] = []
        for lo, hi, first in ranges(src.shape[1], src.shape[1] // cuts[name] if cuts[name] else 0):
            groups[name].append(
                Gather(p, src, dst, src.shape[0], lo, hi, True, first, r.sends.at[number], r.recvs.at[number])
            )
            number += 1
        owns.append((src, dst, src.shape[0]))
    packs = Gather(
        p, r.pack, r.pack_full, 8, 0, r.pack.shape[1], False, False, r.sends.at[number], r.recvs.at[number]
    )
    number += 1
    units = 2 * depth * 128

    def spread_up():
        for q in range(4):
            y, x = (p.y + q // 2) % 2, (p.x + q % 2) % 2
            for z in range(depth):
                for c in range(2):
                    cols = pl.ds(pl.multiple_of(p.shard(z, y, c, x) * 128, 128), 128)
                    r.up_out[q, :, (z * 2 + c) * 128 : (z * 2 + c + 1) * 128] = r.w_up[:, cols]
        r.up_mid[p.y, pl.ds(pl.multiple_of(p.x * rows_up, rows_up), rows_up), :] = r.up_out[0]
        plane_up.start()

    rows_up = r.w_up.shape[0]
    plane_up = Plane(
        p,
        lambda q: r.up_out.at[q],
        lambda q: r.up_mid.at[p.y, pl.ds(pl.multiple_of(p.x * rows_up, rows_up), rows_up)],
        r.up_sems.at[0],
        r.up_sems.at[1],
    )
    plane_cot = Plane(p, lambda q: r.cot, lambda q: r.cot_all.at[q], r.cot_sems.at[0], r.cot_sems.at[1])
    line_up = LineGather(p, r.up_mid, lambda z, c: r.up_here.at[z, :, c], r.line_sems.at[0], r.line_sems.at[1])
    line_down = LineGather(p, r.w_down, lambda z, c: r.down_here.at[z, c], r.line_sems.at[2], r.line_sems.at[3])
    lines = (line_up, line_down)
    own_up = pltpu.make_async_copy(r.up_mid, r.up_here.at[p.z, :, p.c], r.own_sems.at[3])
    own_down = pltpu.make_async_copy(r.w_down, r.down_here.at[p.z, p.c], r.own_sems.at[4])
    own_cot = pltpu.make_async_copy(r.cot, r.cot_all.at[0], r.own_sems.at[5])
    share_joined = QuadRows(p, 1, r.joined, r.xjoined, r.row_sems.at[0])
    share_normed = QuadRows(p, 0, r.normed, r.xnormed, r.row_sems.at[1])

    def lines_own():
        plane_up.arrived()
        own_up.start()
        for line in lines:
            line.own()

    queries = Exchange(p, count, r.queries_in, r.got_queries, r.s1, r.r1, r.o1)
    there = Exchange(p, count, r.heads_in, r.got, r.s3, r.r3, r.o3)
    back = Exchange(p, count, r.mixed_out, r.mixed, r.s2, r.r2, r.o2)

    def products():
        ask.wait_recv()
        both = r.own_time[...] + r.got_time[...]
        r.times[...] = both
        left = both[:, : r.w_mod.shape[0]].astype(bf)
        row = lax.broadcasted_iota(jnp.int32, (8, model), 0) % 4
        total = jnp.zeros((8, model), jnp.float32)
        for part in range(4):
            made = jnp.dot(
                left, r.w_mod[:, part * model : (part + 1) * model], preferred_element_type=jnp.float32
            )
            total = jnp.where(row == part, made, total)
        r.mods_part[0] = total
        small.one(0, r.mods_part.at[0], r.mods_got.at[0], p.to_core).start()

    def bias_tile():
        each = r.b_skip.shape[1]
        r.pack[...] = jnp.zeros((8, 128), jnp.float32)
        r.pack[0:1, :] = r.b_up_part[...].astype(jnp.float32)
        r.pack[1:2, :each] = r.b_skip[...].astype(jnp.float32)
        r.pack[1:2, each : 2 * each] = r.b_down_part[...].astype(jnp.float32)

    small = Rounds(p, r.small_sems.at[0], r.small_sems.at[1])

    def small_line(d):
        return small.one(d, r.mods_part.at[1], r.mods_got.at[d], small.line(0, d))

    def after_core():
        small.one(0, r.mods_part.at[0], r.mods_got.at[0], p.to_core).wait_recv()
        r.mods_part[1] = r.mods_part[0] + r.mods_got[0]
        for d in range(1, depth):
            small_line(d).start()

    def after_line():
        total = r.mods_part[1]
        for d in range(1, depth):
            small_line(d).wait_recv()
            total = total + r.mods_got[d]
        r.mods_part[2] = total
        small.one(4, r.mods_part.at[2], r.mods_got.at[4], p.to_y).start()

    def after_y():
        small.one(4, r.mods_part.at[2], r.mods_got.at[4], p.to_y).wait_recv()
        r.mods_part[3] = r.mods_part[2] + r.mods_got[4]
        small.one(5, r.mods_part.at[3], r.mods_got.at[5], p.to_x).start()

    def turned_inputs():
        half = depth // 2
        for k, ref in enumerate((r.hidden, r.skip_in)):
            r.joined[k * half : (k + 1) * half] = ref[...].T.reshape(half, *r.joined.shape[1:])

    def load_skip():
        return pltpu.make_async_copy(r.skip_full, r.skip_here, r.load_sems.at[0])

    def load_qkv():
        return pltpu.make_async_copy(r.qkv_full, r.qkv_here, r.load_sems.at[1])

    own_copies = []

    def complete(name):
        for g in groups[name]:
            g.shared()

    def first_norm():
        own_copies[0].wait()
        complete("skip")
        load_skip().start()
        at = pl.multiple_of(p.shard(p.z, p.y, p.c, p.x) * 8, 8)
        r.pack_full[pl.ds(at, 8), :] = r.pack[...]
        packs.shared()
        small.one(5, r.mods_part.at[3], r.mods_got.at[5], p.to_x).wait_recv()
        total = r.mods_part[3] + r.mods_got[5]
        mods = jnp.where(p.x == 0, total[0:4], total[4:8])
        r.mods[0:4, :] = mods
        r.mods[4:8, :] = mods
        each = model // devices
        tiles = [r.pack_full[k * 8 : k * 8 + 2, :] for k in range(devices)]
        for z in range(depth):
            for c in range(2):
                at = pl.multiple_of(p.shard(z, p.y, c, p.x) * 8, 8)
                here = (z * 2 + c) * 128
                r.b_up[:, here : here + 128] = r.pack_full[pl.ds(at, 8), :][0:1]
        b_skip = jnp.concatenate([t[1:2, :each] for t in tiles], 1)
        r.b_down[...] = jnp.concatenate([t[1:2, each : 2 * each] for t in tiles], 1)
        length = r.lengths[p.x]
        kept = (p.b * frames + lax.broadcasted_iota(jnp.int32, (frames, 1), 0) < length).astype(jnp.float32)
        load_skip().wait()
        base = jnp.dot(r.hidden[...], r.skip_here[:model, :], preferred_element_type=jnp.float32)
        base = base + jnp.dot(r.skip_in[...], r.skip_here[model:, :], preferred_element_type=jnp.float32) + b_skip
        r.base[...] = base
        hat, _ = normal(base)
        normed = (hat * (1.0 + kept * mods[0:1]) + kept * mods[1:2]).astype(bf)
        r.normed[...] = normed.T.reshape(r.normed.shape)
        r.normed_here[...] = normed

    def projections():
        own_copies[1].wait()
        complete("qkv")
        load_qkv().start()
        share_normed.start()
        normed = r.normed_here[...]
        load_qkv().wait()
        cosine, sine = r.cosine[...][None], r.sine[...][None]
        for part in (1, 2, 0):
            made = jnp.dot(
                normed, r.qkv_here[:, part * model : (part + 1) * model], preferred_element_type=jnp.float32
            )
            made = made.T.reshape(HEADS, HEAD_DIM, frames)
            if part < 2:
                made = turn(made, cosine, sine)
            if part == 0:
                r.queries_in[...] = made.astype(bf)
                queries.start()
            else:
                r.heads_in[:, (part - 1) * HEAD_DIM : part * HEAD_DIM, :] = made.astype(bf)
            if part == 2:
                there.start()

    def attention(lo, hi):
        attend(p, r.lengths, queries, r.qkv, r.keys, r.values, back, r.lse, r.plain, lo, hi)

    blocks = count // 2

    def first_half():
        there.arrived()
        attend_open(p, r.lengths, r.got, r.qkv, r.keys, r.values)
        attention(0, blocks // 2)

    def second_half():
        attention(blocks // 2, blocks)

    events = []
    for k, name in enumerate(("skip", "qkv")):
        events += [(t + 1.5 * k, k, f) for g in groups[name] for t, f in g.steps()]
    events.append((0.3, 0, products))
    events.append((0.31, 0, bias_tile))
    events.append((0.35, 0, turned_inputs))
    events.append((0.36, 0, spread_up))
    events.append((0.9, 0, after_core))
    events.append((2.05, 9, after_line))
    events.append((3.05, 9, after_y))
    events += [(t + 0.5, 9, f) for t, f in packs.steps()]
    events.append((3.2, 5, lines_own))
    for g in groups["out"]:
        times = {0: 3.25, 1: 5.56, 2: 7.0, 3: 7.16, 4: 8.73, 5: 9.45}
        events += [(times[t], 2, f) for t, f in g.steps()]
    for k, line in enumerate(lines):
        events.append((5.55, 5 + k, functools.partial(line.line, 1)))
        events.append((7.15, 5 + k, functools.partial(line.line, 2)))
        events.append((8.72, 5 + k, functools.partial(line.line, 3)))
    events.append((5.6, 0, first_norm))
    events.append((5.65, 0, plane_cot.start))
    events.append((5.66, 0, share_joined.start))
    events.append((7.1, 0, projections))
    events.append((8.4, 0, first_half))
    events.append((9.4, 0, second_half))
    events.sort(key=lambda e: (e[0], e[1]))
    own_down.start()
    own_cot.start()
    own_copies += keep_own(p, owns, r.own_sems)
    play([f for _, _, f in events])
    complete("out")
    for line in lines:
        line.shared()
        line.sent()
    for group in groups.values():
        for g in group:
            g.sent()
    packs.sent()
    for one in (plane_up, there, queries):
        one.finish()
    plane_cot.arrived()
    plane_cot.finish()
    for share in (share_joined, share_normed):
        share.arrived()
        share.finish()
    back.arrived()
    back.finish()
    for copy in (own_copies[2], own_up, own_down, own_cot):
        copy.wait()
    ask.wait_send()
    small.one(0, r.mods_part.at[0], r.mods_got.at[0], p.to_core).wait_send()
    for d in range(1, depth):
        small_line(d).wait_send()
    small.one(4, r.mods_part.at[2], r.mods_got.at[4], p.to_y).wait_send()
    small.one(5, r.mods_part.at[3], r.mods_got.at[5], p.to_x).wait_send()


def front_call(depth, devices, args):
    cuts = dict(skip=8, qkv=8, out=0)
    frames, model = args["hidden"].shape
    bf, f32 = jnp.bfloat16, jnp.float32
    count = devices // 2
    total = count * frames
    shape = jax.ShapeDtypeStruct
    vmem = pl.BlockSpec(memory_space=pltpu.VMEM)
    away = pl.BlockSpec(memory_space=pl.ANY)

    def whole(name):
        rows, cols = args[name].shape
        return shape((devices * rows, cols), bf)

    def by_owner(n):
        return (depth, 2, 2, 2, n // devices, frames)

    def quarter(n):
        return (4, depth, 2, n // devices, frames)

    units = 2 * depth * 128
    rows_up = args["w_up"].shape[0]
    far = dict(
        skip_full=whole("w_skip"),
        qkv_full=whole("w_qkv"),
        out_full=whole("w_out"),
        up_here=shape((depth, 2, 2, 2 * rows_up, units), bf),
        down_here=shape((depth, 2, 128, model), bf),
        cot_all=shape((4, frames, model), bf),
        xjoined=shape(quarter(2 * model), bf),
        xnormed=shape(quarter(model), bf),
        mixed=shape((count, HEAD_DIM, frames), bf),
    )
    half = HEAD_DIM // 2
    near = dict(
        cosine=shape((half, frames), f32),
        sine=shape((half, frames), f32),
        times=shape((8, 128), f32),
        mods=shape((8, model), f32),
        b_up=shape((1, units), f32),
        b_down=shape((1, model), f32),
        base=shape((frames, model), f32),
        qkv=shape((3 * HEAD_DIM, total), bf),
        lse=shape((1, total), f32),
        plain=shape((HEAD_DIM, total), f32),
    )
    dma = pltpu.SemaphoreType.DMA
    gathers = 6
    scratch = dict(
        own_time=pltpu.VMEM((8, 128), f32),
        other_time=pltpu.VMEM((8, 128), f32),
        got_time=pltpu.VMEM((8, 128), f32),
        pack=pltpu.VMEM((8, 128), f32),
        pack_full=pltpu.VMEM((devices * 8, 128), f32),
        mods_part=pltpu.VMEM((4, 8, model), f32),
        mods_got=pltpu.VMEM((6, 8, model), f32),
        small_sems=dma((2, 6)),
        skip_here=pltpu.VMEM((2 * model, model), bf),
        qkv_here=pltpu.VMEM((model, 3 * model), bf),
        joined=pltpu.VMEM(by_owner(2 * model), bf),
        normed=pltpu.VMEM(by_owner(model), bf),
        normed_here=pltpu.VMEM((frames, model), bf),
        up_out=pltpu.VMEM((4, rows_up, units), bf),
        up_mid=pltpu.VMEM((2, 2 * rows_up, units), bf),
        queries_in=pltpu.VMEM((count, HEAD_DIM, frames), bf),
        got_queries=pltpu.VMEM((count, HEAD_DIM, frames), bf),
        heads_in=pltpu.VMEM((count, 2 * HEAD_DIM, frames), bf),
        got=pltpu.VMEM((count, 2 * HEAD_DIM, frames), bf),
        keys=pltpu.VMEM((total, 2 * HEAD_DIM), bf),
        values=pltpu.VMEM((HEAD_DIM + 16, total), bf),
        mixed_out=pltpu.VMEM((count, HEAD_DIM, frames), bf),
        time_sems=dma((2,)),
        load_sems=dma((2,)),
        own_sems=dma((6,)),
        up_sems=dma((2, 4)),
        cot_sems=dma((2, 4)),
        line_sems=dma((4, 16)),
        row_sems=dma((2, 7)),
        sends=dma((gathers, Gather.SENDS)),
        recvs=dma((gathers, Gather.RECVS)),
        s1=dma((count,)),
        r1=dma((count,)),
        o1=dma,
        s2=dma((count,)),
        r2=dma((count,)),
        o2=dma,
        s3=dma((count,)),
        r3=dma((count,)),
        o3=dma,
    )
    names = [*args, *far, *near, *scratch]
    made = pl.pallas_call(
        functools.partial(front_kernel, depth, cuts, names),
        name="front",
        out_shape=[*far.values(), *near.values()],
        in_specs=[pl.BlockSpec(memory_space=pltpu.SMEM)] + [vmem] * (len(args) - 1),
        out_specs=[away] * len(far) + [vmem] * len(near),
        scratch_shapes=list(scratch.values()),
        compiler_params=kernel_params(1),
    )(*args.values())
    return dict(zip([*far, *near], made))


def write_kernel(count, times, sums, joined, *refs):
    ins, outs = refs[:count], refs[count:]
    for src, dst in zip(ins, outs):
        dst[...] = src[...]
    hidden_grad, skip_grad, time_grad, b_up, b_skip, b_down = outs[count:]
    hidden_grad[...] = joined[0]
    skip_grad[...] = joined[1]
    each = b_skip.shape[1]
    part = jnp.where(lax.axis_index("uly") == 0, times[:, 0, :each], times[:, 1, :each])
    time_grad[...] = jnp.concatenate([part[k : k + 1] for k in range(times.shape[0])], 1)
    b_up[...] = sums[0:1, :]
    b_down[...] = sums[1:2, :each]
    b_skip[...] = sums[1:2, each : 2 * each]


def write_call(made, names, each):
    shape = jax.ShapeDtypeStruct
    joined = made["joined_grad"]
    frames, model = joined.shape[1:]
    plain = [shape(made[name].shape, made[name].dtype) for name in names]
    return pl.pallas_call(
        functools.partial(write_kernel, len(names)),
        name="write",
        out_shape=plain
        + [shape((frames, model), joined.dtype)] * 2
        + [shape((1, model), jnp.float32), shape((1, 128), jnp.float32)]
        + [shape((1, each), jnp.float32)] * 2,
        in_specs=in_vmem(3 + len(names)),
        out_specs=in_vmem(6 + len(names)),
        compiler_params=pltpu.CompilerParams(vmem_limit_bytes=VMEM_BYTES),
    )(made["times_full"], made["sums_out"], joined, *[made[name] for name in names])


def first_with_second(left, right, dims):
    return lax.dot_general(left, right, ((dims[:1], dims[1:]), ((), ())), preferred_element_type=jnp.float32)


def turn(values, cosine, sine):
    half = HEAD_DIM // 2
    first, second = values[..., :half, :], values[..., half:, :]
    return jnp.concatenate([first * cosine - second * sine, second * cosine + first * sine], -2)


def on_device(hidden, skip_in, time_embed, lengths, cotangent, w_skip, b_skip, w_mod, w_qkv, w_out, w_up, b_up,
              w_down, b_down):
    blocks, rows = lax.axis_size("blk"), lax.axis_size("uly")
    devices, depth = blocks * rows, blocks // 4
    _, frames, model = hidden.shape
    front = front_call(
        depth,
        devices,
        dict(
            lengths=lengths[:, 0],
            time_row=time_embed[0],
            b_skip=b_skip[None],
            b_up_part=b_up[None],
            b_down_part=b_down[None],
            cot=cotangent[0],
            w_mod=w_mod,
            hidden=hidden[0],
            skip_in=skip_in[0],
            w_skip=w_skip,
            w_qkv=w_qkv,
            w_out=w_out,
            w_up=w_up,
            w_down=w_down,
        ),
    )
    made = back_call(
        depth,
        devices,
        dict(
            lengths=lengths[:, 0],
            base=front["base"],
            mods=front["mods"],
            b_up=front["b_up"],
            b_down=front["b_down"],
            cosine=front["cosine"],
            sine=front["sine"],
            w_mod=w_mod,
            times=front["times"],
            qkv_far=front["qkv"],
            lse=front["lse"],
            plain_far=front["plain"],
            cot_far=front["cot_all"],
            mixed=front["mixed"].reshape(depth, 2, 2, 2, model // devices, frames),
            xjoined_far=front["xjoined"],
            xnormed_far=front["xnormed"],
            w_out=front["out_full"],
            w_up=front["up_here"].reshape(model, -1),
            w_down=front["down_here"].reshape(-1, model),
            w_qkv=front["qkv_full"],
            w_skip=front["skip_full"],
        ),
    )
    names = ["output", "skip_grad", "mod_grad", "qkv_grad", "out_grad", "up_grad", "down_grad"]
    output, skip_grad, mod_grad, qkv_grad, out_grad, up_grad, down_grad, *small = write_call(
        made, names, b_skip.shape[0]
    )
    hidden_grad, skip_in_grad, time_grad, b_up_grad, b_skip_grad, b_down_grad = small
    return (
        output[None],
        hidden_grad[None],
        skip_in_grad[None],
        time_grad[None],
        skip_grad,
        b_skip_grad[0],
        mod_grad,
        qkv_grad,
        out_grad,
        up_grad,
        b_up_grad[0],
        down_grad,
        b_down_grad[0],
    )


def solution(mesh):
    placed = (
        P("uly", "blk", None),
        P("uly", "blk", None),
        P("uly", None, None),
        P(),
        P("uly", "blk", None),
        P(("blk", "uly"), None),
        P(("blk", "uly")),
        P(("blk", "uly"), None),
        P(("blk", "uly"), None),
        P(("blk", "uly"), None),
        P(("blk", "uly"), None),
        P(("blk", "uly")),
        P(("blk", "uly"), None),
        P(("blk", "uly")),
    )
    blocks = mesh.shape["blk"]
    special = mesh.shape["uly"] == 2 and blocks == HEADS and blocks % 4 == 0 and blocks > 4
    return jax.shard_map(
        on_device if special else per_device,
        mesh=mesh,
        in_specs=placed,
        out_specs=(
            P("uly", "blk", None),
            P("uly", "blk", None),
            P("uly", "blk", None),
            P("uly", None, None),
            P(("blk", "uly"), None),
            P(("blk", "uly")),
            P(("blk", "uly"), None),
            P(("blk", "uly"), None),
            P(("blk", "uly"), None),
            P(("blk", "uly"), None),
            P(("blk", "uly")),
            P(("blk", "uly"), None),
            P(("blk", "uly")),
        ),
        check_vma=False,
    )
```

```python
import functools
import math

import jax
import jax.numpy as jnp
from jax import lax
from jax.experimental import pallas as pl
from jax.experimental.pallas import tpu as pltpu
from jax.sharding import PartitionSpec as P

HEADS = 16
HEAD_DIM = 64


exact_mode = lax.Precision.HIGHEST
epsilon = 1e-05


def passed_along(x, axis, by):
    devices = lax.axis_size(axis)
    return lax.ppermute(x, axis, [(i, (i + by) % devices) for i in range(devices)])


def segment_info(len_row, positions):
    slots = len_row.shape[0]
    ends = jnp.cumsum(len_row)
    starts = ends - len_row
    total = ends[-1]
    seg_ids = jnp.sum((positions[:, None] >= ends[None, :]).astype(jnp.int32), axis=1)
    onehot = seg_ids[:, None] == jnp.arange(slots, dtype=jnp.int32)[None, :]
    begin = jnp.sum(jnp.where(onehot, starts[None, :], 0), axis=1)
    begin = begin + jnp.where(seg_ids == slots, total, 0)
    return (seg_ids, positions - begin, seg_ids < slots)


def rotary(values, offsets):
    half = values.shape[-1] // 2
    freq = 10000.0 ** (-jnp.arange(half, dtype=jnp.float32) / half)
    angle = offsets.astype(jnp.float32)[:, None] * freq[None, :]
    cosine = jnp.cos(angle)[:, None, :]
    sine = jnp.sin(angle)[:, None, :]
    first = values[..., :half]
    second = values[..., half:]
    return jnp.concatenate([first * cosine - second * sine, second * cosine + first * sine], -1)


def modulate(values, scale, shift):
    center = values - jnp.mean(values, -1, keepdims=True)
    spread = jnp.mean(center * center, -1, keepdims=True)
    return center * lax.rsqrt(spread + epsilon) * (1.0 + scale) + shift


def contract_rows(left, right):
    return lax.dot_general(
        left, right, (((0,), (0,)), ((), ())), preferred_element_type=jnp.float32
    )


def contract_cols(left, right):
    return lax.dot_general(
        left, right, (((1,), (1,)), ((), ())), preferred_element_type=jnp.float32
    )


def gelu_exact(values):
    return jax.nn.gelu(values, approximate=False)


def per_device(
    hidden,
    skip_in,
    time_embed,
    lengths,
    cotangent,
    w_skip,
    b_skip,
    w_mod,
    w_qkv,
    w_out,
    w_up,
    b_up,
    w_down,
    b_down,
):
    gathered = (
        lax.all_gather(w_skip, ("blk", "uly"), axis=0, tiled=True),
        lax.all_gather(b_skip, ("blk", "uly"), axis=0, tiled=True),
        lax.all_gather(w_mod, ("blk", "uly"), axis=0, tiled=True),
        lax.all_gather(w_qkv, ("blk", "uly"), axis=0, tiled=True),
        lax.all_gather(w_out, ("blk", "uly"), axis=0, tiled=True),
        lax.all_gather(w_up, ("blk", "uly"), axis=0, tiled=True),
        lax.all_gather(b_up, ("blk", "uly"), axis=0, tiled=True),
        lax.all_gather(w_down, ("blk", "uly"), axis=0, tiled=True),
        lax.all_gather(b_down, ("blk", "uly"), axis=0, tiled=True),
    )
    (
        skip_full,
        bskip_full,
        mod_full,
        qkv_full,
        out_full,
        up_full,
        bup_full,
        down_full,
        bdown_full,
    ) = gathered
    group_count = lax.axis_size("uly")
    cycle_size = lax.axis_size("blk")
    frame_count = hidden.shape[1]
    row_count = lengths.shape[0]
    slot_count = lengths.shape[1]
    local_heads = HEADS // group_count
    span = local_heads * HEAD_DIM
    scaling = HEAD_DIM ** (-0.5)
    block_index = lax.axis_index("blk")
    row_index = lax.axis_index("uly")
    frame_pos = block_index * frame_count + jnp.arange(frame_count, dtype=jnp.int32)
    all_seg, all_offsets, all_valid = jax.vmap(lambda len_row: segment_info(len_row, frame_pos))(
        lengths
    )
    own_seg = lax.dynamic_index_in_dim(all_seg, row_index, 0, keepdims=False)
    own_offsets = lax.dynamic_index_in_dim(all_offsets, row_index, 0, keepdims=False)
    joined = jnp.concatenate([hidden[0], skip_in[0]], 1)
    base = jnp.dot(joined, skip_full, preferred_element_type=jnp.float32) + bskip_full.astype(
        jnp.float32
    )
    time_row = time_embed[0]
    mods = jnp.dot(time_row, mod_full, preferred_element_type=jnp.float32)
    selector = (own_seg[:, None] == jnp.arange(slot_count, dtype=jnp.int32)[None, :]).astype(
        jnp.float32
    )
    frame_mod = jnp.dot(selector, mods, precision=exact_mode)
    a_scale, a_shift, f_scale, f_shift = jnp.split(frame_mod, 4, 1)
    normed_full, norm_back = jax.vjp(modulate, base, a_scale, a_shift)
    normed = normed_full.astype(jnp.bfloat16)
    projected = jnp.dot(normed, qkv_full, preferred_element_type=jnp.float32).reshape(
        frame_count, 3, HEADS, HEAD_DIM
    )

    def place(parts):
        return jnp.stack(
            [rotary(parts[:, 0], own_offsets), rotary(parts[:, 1], own_offsets), parts[:, 2]], 1
        )

    turned, unturn = jax.vjp(place, projected)
    sending = turned.astype(jnp.bfloat16).reshape(1, frame_count, 3, group_count, span)
    head_data = lax.all_to_all(sending, "uly", split_axis=3, concat_axis=0, tiled=True)
    query = head_data[:, :, 0, 0].reshape(row_count, frame_count, local_heads, HEAD_DIM)
    kv_pairs = head_data[:, :, 1:, 0]

    def key_segments(start, count):
        key_pos = start + jnp.arange(count, dtype=jnp.int32)
        return jax.vmap(lambda len_row: segment_info(len_row, key_pos)[0])(lengths)

    start_state = (
        jnp.full((row_count, local_heads, frame_count), -1e30, jnp.float32),
        jnp.zeros((row_count, local_heads, frame_count), jnp.float32),
        jnp.zeros((row_count, frame_count, local_heads, HEAD_DIM), jnp.float32),
    )
    piece = lax.all_gather(kv_pairs, "blk", axis=1, tiled=True)
    total = piece.shape[1]
    step = math.gcd(total, max(frame_count, 1024))

    def sub_step(step_index, state):
        run_max, run_total, run_acc = state
        offset = step_index * step
        section = lax.dynamic_slice_in_dim(piece, offset, step, 1)
        key_seg = key_segments(offset, step)
        key_part = section[:, :, 0].reshape(row_count, step, local_heads, HEAD_DIM)
        value_part = section[:, :, 1].reshape(row_count, step, local_heads, HEAD_DIM)
        mask = all_seg[:, None, :, None] == key_seg[:, None, None, :]
        score = (
            jnp.einsum("rqhd,rkhd->rhqk", query, key_part, preferred_element_type=jnp.float32)
            * scaling
        )
        masked = jnp.where(mask, score, -1e30)
        fresh = jnp.maximum(run_max, jnp.max(masked, -1))
        weights = jnp.where(mask, jnp.exp(masked - fresh[..., None]), 0.0)
        decay = jnp.exp(run_max - fresh)
        run_total = run_total * decay + jnp.sum(weights, -1)
        run_acc = run_acc * jnp.swapaxes(decay, 1, 2)[..., None] + jnp.einsum(
            "rhqk,rkhd->rqhd",
            weights.astype(jnp.bfloat16),
            value_part,
            preferred_element_type=jnp.float32,
        )
        return (fresh, run_total, run_acc)

    run_max, run_total, run_acc = lax.fori_loop(0, total // step, sub_step, start_state)
    attended = run_acc / jnp.swapaxes(run_total, 1, 2)[..., None]
    log_total = run_max + jnp.log(run_total)
    valid_half = all_valid.astype(jnp.bfloat16)[:, :, None, None]
    leaving = (attended * all_valid.astype(jnp.float32)[:, :, None, None]).astype(jnp.bfloat16)
    leaving = leaving.reshape(row_count, frame_count, 1, span)
    mixed = lax.all_to_all(leaving, "uly", split_axis=0, concat_axis=2, tiled=True).reshape(
        frame_count, HEADS * HEAD_DIM
    )
    branch = jnp.dot(mixed, out_full, preferred_element_type=jnp.float32)
    middle = base + branch
    normed2_full, norm2_back = jax.vjp(modulate, middle, f_scale, f_shift)
    normed2 = normed2_full.astype(jnp.bfloat16)
    inner = jnp.dot(normed2, up_full, preferred_element_type=jnp.float32) + bup_full.astype(
        jnp.float32
    )
    act_full, act_back = jax.vjp(gelu_exact, inner)
    act = act_full.astype(jnp.bfloat16)
    result = (
        middle
        + jnp.dot(act, down_full, preferred_element_type=jnp.float32)
        + bdown_full.astype(jnp.float32)
    )
    output = result.astype(jnp.bfloat16)[None]
    again = (
        lax.all_gather(w_skip, ("blk", "uly"), axis=0, tiled=True),
        lax.all_gather(w_mod, ("blk", "uly"), axis=0, tiled=True),
        lax.all_gather(w_qkv, ("blk", "uly"), axis=0, tiled=True),
        lax.all_gather(w_out, ("blk", "uly"), axis=0, tiled=True),
        lax.all_gather(w_up, ("blk", "uly"), axis=0, tiled=True),
        lax.all_gather(w_down, ("blk", "uly"), axis=0, tiled=True),
    )
    skip_back, mod_back, qkv_back, out_back, up_back, down_back = again
    upstream = cotangent[0]
    upstream_full = upstream.astype(jnp.float32)
    grad_down = contract_rows(act, upstream)
    grad_bdown = jnp.sum(upstream_full, 0)
    grad_act = contract_cols(upstream, down_back)
    grad_inner = act_back(grad_act)[0].astype(jnp.bfloat16)
    grad_up = contract_rows(normed2, grad_inner)
    grad_bup = jnp.sum(grad_inner.astype(jnp.float32), 0)
    grad_normed2 = contract_cols(grad_inner, up_back)
    grad_mid_norm, grad_fscale, grad_fshift = norm2_back(grad_normed2)
    grad_middle = upstream_full + grad_mid_norm
    grad_branch = grad_middle.astype(jnp.bfloat16)
    grad_out = contract_rows(mixed, grad_branch)
    grad_mixed = (
        contract_cols(grad_branch, out_back)
        .astype(jnp.bfloat16)
        .reshape(1, frame_count, group_count, span)
    )
    returning = lax.all_to_all(grad_mixed, "uly", split_axis=2, concat_axis=0, tiled=True)
    grad_attn = returning.reshape(row_count, frame_count, local_heads, HEAD_DIM) * valid_half
    delta_rows = jnp.swapaxes(jnp.sum(grad_attn.astype(jnp.float32) * attended, -1), 1, 2)

    def contribution(held_pairs, key_start):
        count = held_pairs.shape[1]
        key_seg = key_segments(key_start, count)
        key_part = held_pairs[:, :, 0].reshape(row_count, count, local_heads, HEAD_DIM)
        value_part = held_pairs[:, :, 1].reshape(row_count, count, local_heads, HEAD_DIM)
        mask = all_seg[:, None, :, None] == key_seg[:, None, None, :]
        score = (
            jnp.einsum("rqhd,rkhd->rhqk", query, key_part, preferred_element_type=jnp.float32)
            * scaling
        )
        weights = jnp.exp(jnp.where(mask, score - log_total[..., None], -1e30))
        grad_weights = jnp.einsum(
            "rqhd,rkhd->rhqk", grad_attn, value_part, preferred_element_type=jnp.float32
        )
        grad_score = (weights * (grad_weights - delta_rows[..., None])).astype(jnp.bfloat16)
        more_query = (
            jnp.einsum("rhqk,rkhd->rqhd", grad_score, key_part, preferred_element_type=jnp.float32)
            * scaling
        )
        more_key = (
            jnp.einsum("rhqk,rqhd->rkhd", grad_score, query, preferred_element_type=jnp.float32)
            * scaling
        )
        more_value = jnp.einsum(
            "rhqk,rqhd->rkhd",
            weights.astype(jnp.bfloat16),
            grad_attn,
            preferred_element_type=jnp.float32,
        )
        more_pairs = jnp.stack(
            [more_key.reshape(row_count, count, span), more_value.reshape(row_count, count, span)],
            2,
        )
        return (more_query, more_pairs)

    def pass_grads(held_grads):
        return passed_along(held_grads.astype(jnp.bfloat16), "blk", 1).astype(held_grads.dtype)

    def cycle_step(turn, state):
        held_pairs, held_grads, query_grad = state
        more_query, more_pairs = contribution(
            held_pairs, (block_index - turn) % cycle_size * frame_count
        )
        held_pairs = passed_along(held_pairs, "blk", 1)
        held_grads = pass_grads(held_grads + more_pairs)
        return (held_pairs, held_grads, query_grad + more_query)

    cycle_start = (
        kv_pairs,
        jnp.zeros((row_count, frame_count, 2, span), jnp.float32),
        jnp.zeros((row_count, frame_count, local_heads, HEAD_DIM), jnp.float32),
    )
    held_pairs, held_grads, query_grad = lax.fori_loop(0, cycle_size - 1, cycle_step, cycle_start)
    last_query, last_pairs = contribution(
        held_pairs, (block_index - (cycle_size - 1)) % cycle_size * frame_count
    )
    pair_grads = pass_grads(held_grads + last_pairs)
    query_grad = query_grad + last_query
    head_grads = jnp.concatenate(
        [
            query_grad.astype(jnp.bfloat16).reshape(row_count, frame_count, 1, span),
            pair_grads.astype(jnp.bfloat16),
        ],
        2,
    ).reshape(row_count, frame_count, 3, 1, span)
    frames_grad = lax.all_to_all(head_grads, "uly", split_axis=0, concat_axis=3, tiled=True)
    frames_grad = frames_grad.reshape(frame_count, 3, HEADS, HEAD_DIM).astype(jnp.float32)
    grad_projected = (
        unturn(frames_grad)[0].astype(jnp.bfloat16).reshape(frame_count, 3 * HEADS * HEAD_DIM)
    )
    grad_qkv = contract_rows(normed, grad_projected)
    grad_normed = contract_cols(grad_projected, qkv_back)
    grad_base_norm, grad_ascale, grad_ashift = norm_back(grad_normed)
    grad_base = (grad_middle + grad_base_norm).astype(jnp.bfloat16)
    grad_skip_w = contract_rows(joined, grad_base)
    grad_bskip = jnp.sum(grad_base.astype(jnp.float32), 0)
    grad_joined = contract_cols(grad_base, skip_back).astype(jnp.bfloat16)
    model_width = hidden.shape[2]
    hidden_grad = grad_joined[:, :model_width][None]
    skip_grad = grad_joined[:, model_width:][None]
    frame_mod_grad = jnp.concatenate([grad_ascale, grad_ashift, grad_fscale, grad_fshift], 1)
    slot_grad = lax.dot_general(
        selector, frame_mod_grad, (((0,), (0,)), ((), ())), precision=exact_mode
    )
    grad_mod = lax.dot_general(
        time_row.astype(jnp.float32), slot_grad, (((0,), (0,)), ((), ())), precision=exact_mode
    )
    slot_total = lax.psum(slot_grad, "blk")
    time_grad = lax.dot_general(
        slot_total, mod_back.astype(jnp.float32), (((1,), (1,)), ((), ())), precision=exact_mode
    )[None]
    owned = (
        lax.psum_scatter(grad_skip_w, ("blk", "uly"), scatter_dimension=0, tiled=True),
        lax.psum_scatter(grad_bskip, ("blk", "uly"), scatter_dimension=0, tiled=True),
        lax.psum_scatter(grad_mod, ("blk", "uly"), scatter_dimension=0, tiled=True),
        lax.psum_scatter(grad_qkv, ("blk", "uly"), scatter_dimension=0, tiled=True),
        lax.psum_scatter(grad_out, ("blk", "uly"), scatter_dimension=0, tiled=True),
        lax.psum_scatter(grad_up, ("blk", "uly"), scatter_dimension=0, tiled=True),
        lax.psum_scatter(grad_bup, ("blk", "uly"), scatter_dimension=0, tiled=True),
        lax.psum_scatter(grad_down, ("blk", "uly"), scatter_dimension=0, tiled=True),
        lax.psum_scatter(grad_bdown, ("blk", "uly"), scatter_dimension=0, tiled=True),
    )
    return (
        output,
        hidden_grad,
        skip_grad,
        time_grad,
        owned[0],
        owned[1],
        owned[2],
        owned[3],
        owned[4],
        owned[5],
        owned[6],
        owned[7],
        owned[8],
    )


MESH = pl.DeviceIdType.MESH


class Place:
    def __init__(self, depth):
        self.depth = depth
        self.b = lax.axis_index("blk")
        self.x = lax.axis_index("uly")
        self.z = self.b // 4
        self.y = (self.b // 2) % 2
        self.c = self.b % 2
        self.to_x = (self.b, 1 - self.x)
        self.to_y = (self.b + 2 - 4 * self.y, self.x)
        self.to_core = (self.b + 1 - 2 * self.c, self.x)
        self.to_far = (self.b + 3 - 4 * self.y - 2 * self.c, self.x)
        self.to_across = (self.b + 2 - 4 * self.y, 1 - self.x)
        self.to_far_x = (self.b + 1 - 2 * self.c, 1 - self.x)
        self.to_up = (self.b + 4, self.x)
        self.to_down = (self.b - 4, self.x)

    def shard(self, z, y, c, x):
        return ((z * 2 + y) * 2 + c) * 2 + x

    def greet(self):
        barrier = pltpu.get_barrier_semaphore()
        for to in (self.to_x, self.to_y, self.to_core, self.to_far):
            pl.semaphore_signal(barrier, inc=1, device_id=to, device_id_type=MESH)

        @pl.when(self.z < self.depth - 1)
        def _():
            pl.semaphore_signal(barrier, inc=1, device_id=self.to_up, device_id_type=MESH)

        @pl.when(self.z > 0)
        def _():
            pl.semaphore_signal(barrier, inc=1, device_id=self.to_down, device_id_type=MESH)

        top = self.depth - 1
        pl.semaphore_wait(barrier, 4 + (self.z + top - 1) // top + (2 * top - 1 - self.z) // top)


def remote(src, dst, send, recv, to):
    return pltpu.make_async_remote_copy(
        src_ref=src, dst_ref=dst, send_sem=send, recv_sem=recv, device_id=to, device_id_type=MESH
    )


class Gather:
    SENDS = 64
    RECVS = 48

    def __init__(self, place, src, dst, rows, lo, hi, split, plane_first, sends, recvs):
        self.p, self.src, self.dst, self.rows = place, src, dst, rows
        self.lo, self.hi, self.split, self.plane_first = lo, hi, split, plane_first
        self.sends, self.recvs = sends, recvs
        self.pending = []

    def part(self, z, y, c, x, half=None):
        base = self.p.shard(z, y, c, x) * self.rows
        rows = self.rows
        if half is not None:
            rows = rows // 2
            base = base + half * rows
        return self.dst.at[pl.ds(pl.multiple_of(base, rows), rows), pl.ds(self.lo, self.hi - self.lo)]

    def mine(self):
        return self.src.at[:, pl.ds(self.lo, self.hi - self.lo)]

    def go(self, when, src, dst, send, recv, to):
        def start():
            remote(src, dst, self.sends.at[send], self.recvs.at[recv], to).start()

        def finish():
            remote(src, dst, self.sends.at[send], self.recvs.at[recv], to).wait_send()

        if when is None:
            start()
            self.pending.append(finish)
        else:
            pl.when(when)(start)
            self.pending.append(lambda: pl.when(when)(finish))

    def got(self, dst, recv):
        remote(dst, dst, self.sends.at[0], self.recvs.at[recv], self.p.to_x).wait_recv()

    def share(self, when, src, z, y, x):
        slot = z * 4 + y * 2 + x
        self.go(when, src, self.part(z, y, self.p.c, x), slot, slot, self.p.to_core)

    def steps(self):
        return self.plane_steps() if self.plane_first else self.line_steps()

    def line_steps(self):
        p = self.p
        top = p.depth - 1

        def hand_on(when, src, z):
            whole = self.part(z, p.y, p.c, p.x)
            self.go(when, src, whole, 24 + z, 20 + z, p.to_x)
            self.go(when, src, whole, 28 + z, 24 + z, p.to_y)
            self.share(when, src, z, p.y, p.x)

        def own():
            src = self.mine()
            whole = self.part(p.z, p.y, p.c, p.x)
            self.go(p.z < top, src, whole, 16 + p.z, 16 + p.z, p.to_up)
            self.go(p.z > 0, src, whole, 20 + p.z, 16 + p.z, p.to_down)
            hand_on(None, src, p.z)

        def line(d):
            for side in (-1, 1):
                z = p.z + side * d
                here = (z >= 0) & (z <= top)
                whole = self.part(z, p.y, p.c, p.x)
                pl.when(here)(lambda: self.got(whole, 16 + z))
                if side < 0:
                    self.go(here & (p.z < top), whole, whole, 16 + z, 16 + z, p.to_up)
                else:
                    self.go(here & (p.z > 0), whole, whole, 20 + z, 16 + z, p.to_down)
                hand_on(here, whole, z)

        def origins(d):
            return [(None, p.z)] if d == 0 else [
                ((p.z + s * d >= 0) & (p.z + s * d <= top), p.z + s * d) for s in (-1, 1)
            ]

        def cond(when, f):
            f() if when is None else pl.when(when)(f)

        def cross(d):
            for when, z in origins(d):
                from_x = self.part(z, p.y, p.c, 1 - p.x)
                cond(when, lambda: self.got(from_x, 20 + z))
                self.share(when, from_x, z, p.y, 1 - p.x)
                if self.split:
                    part = self.part(z, p.y, p.c, 1 - p.x, 0)
                else:
                    part = from_x
                self.go(when, part, part, 32 + z, 28 + z, p.to_y)
                from_y = self.part(z, 1 - p.y, p.c, p.x)
                cond(when, lambda: self.got(from_y, 24 + z))
                self.share(when, from_y, z, 1 - p.y, p.x)
                if self.split:
                    part = self.part(z, 1 - p.y, p.c, p.x, 1)
                    self.go(when, part, part, 36 + z, 32 + z, p.to_x)

        def corner(d):
            for when, z in origins(d):
                whole = self.part(z, 1 - p.y, p.c, 1 - p.x)
                if self.split:
                    for half in (0, 1):
                        part = self.part(z, 1 - p.y, p.c, 1 - p.x, half)
                        cond(when, lambda: self.got(part, 28 + 4 * half + z))
                else:
                    cond(when, lambda: self.got(whole, 28 + z))
                self.share(when, whole, z, 1 - p.y, 1 - p.x)

        out = [(0, own)]
        for d in range(p.depth):
            if d:
                out.append((d, functools.partial(line, d)))
            out.append((d + 1, functools.partial(cross, d)))
            out.append((d + 2, functools.partial(corner, d)))
        return out

    def plane_steps(self):
        p = self.p
        top = p.depth - 1

        def along(when, src, z, y, x, up, down):
            slot = 20 + z * 4 + y * 2 + x
            whole = self.part(z, y, p.c, x)
            if up:
                w = p.z < top
                self.go(w if when is None else w & when, src, whole, slot, slot, p.to_up)
            if down:
                w = p.z > 0
                self.go(w if when is None else w & when, src, whole, slot + 16, slot, p.to_down)

        def own():
            src = self.mine()
            whole = self.part(p.z, p.y, p.c, p.x)
            self.go(None, src, whole, 16, 16, p.to_x)
            self.go(None, src, whole, 17, 17, p.to_y)
            along(None, src, p.z, p.y, p.x, True, True)
            self.share(None, src, p.z, p.y, p.x)

        def cross():
            from_x = self.part(p.z, p.y, p.c, 1 - p.x)
            self.got(from_x, 16)
            part = self.part(p.z, p.y, p.c, 1 - p.x, 0) if self.split else from_x
            self.go(None, part, part, 18, 18, p.to_y)
            along(None, from_x, p.z, p.y, 1 - p.x, True, True)
            self.share(None, from_x, p.z, p.y, 1 - p.x)
            from_y = self.part(p.z, 1 - p.y, p.c, p.x)
            self.got(from_y, 17)
            if self.split:
                part = self.part(p.z, 1 - p.y, p.c, p.x, 1)
                self.go(None, part, part, 19, 19, p.to_x)
            along(None, from_y, p.z, 1 - p.y, p.x, True, True)
            self.share(None, from_y, p.z, 1 - p.y, p.x)

        def corner():
            whole = self.part(p.z, 1 - p.y, p.c, 1 - p.x)
            if self.split:
                for half in (0, 1):
                    self.got(self.part(p.z, 1 - p.y, p.c, 1 - p.x, half), 18 + half)
            else:
                self.got(whole, 18)
            along(None, whole, p.z, 1 - p.y, 1 - p.x, True, True)
            self.share(None, whole, p.z, 1 - p.y, 1 - p.x)

        def line(d, k):
            y = p.y if k in (0, 1) else 1 - p.y
            x = p.x if k in (0, 2) else 1 - p.x
            for side in (-1, 1):
                z = p.z + side * d
                here = (z >= 0) & (z <= top)
                whole = self.part(z, y, p.c, x)
                pl.when(here)(lambda: self.got(whole, 20 + z * 4 + y * 2 + x))
                along(here, whole, z, y, x, side < 0, side > 0)
                self.share(here, whole, z, y, x)

        out = [(0, own), (1, cross), (2, corner)]
        for d in range(1, p.depth):
            for k in range(4):
                out.append((d + 0.1 + min(k, 2) * 0.9, functools.partial(line, d, k)))
        return out

    def shared(self):
        p = self.p
        for z in range(p.depth):
            for y in range(2):
                for x in range(2):
                    self.got(self.part(z, y, 1 - p.c, x), z * 4 + y * 2 + x)

    def sent(self):
        for wait in self.pending:
            wait()


class LineGather:
    def __init__(self, place, src, piece, sends, recvs):
        self.p, self.src, self.piece, self.sends, self.recvs = place, src, piece, sends, recvs
        self.pending = []

    def go(self, when, src, dst, send, recv, to):
        def start():
            remote(src, dst, self.sends.at[send], self.recvs.at[recv], to).start()

        def finish():
            remote(src, dst, self.sends.at[send], self.recvs.at[recv], to).wait_send()

        if when is None:
            start()
            self.pending.append(finish)
        else:
            pl.when(when)(start)
            self.pending.append(lambda: pl.when(when)(finish))

    def got(self, dst, recv):
        remote(dst, dst, self.sends.at[0], self.recvs.at[recv], self.p.to_x).wait_recv()

    def own(self):
        p, n = self.p, self.p.depth
        dst = self.piece(p.z, p.c)
        self.go(p.z < n - 1, self.src, dst, p.z, p.z, p.to_up)
        self.go(p.z > 0, self.src, dst, n + p.z, p.z, p.to_down)
        self.go(None, self.src, dst, 2 * n + p.z, n + p.z, p.to_core)

    def line(self, d):
        p, n = self.p, self.p.depth
        for side in (-1, 1):
            z = p.z + side * d
            here = (z >= 0) & (z <= n - 1)
            dst = self.piece(z, p.c)
            pl.when(here)(lambda: self.got(dst, z))
            if side < 0:
                self.go(here & (p.z < n - 1), dst, dst, z, z, p.to_up)
            else:
                self.go(here & (p.z > 0), dst, dst, n + z, z, p.to_down)
            self.go(here, dst, dst, 2 * n + z, n + z, p.to_core)

    def shared(self):
        n = self.p.depth
        for z in range(n):
            self.got(self.piece(z, 1 - self.p.c), n + z)

    def sent(self):
        for wait in self.pending:
            wait()


class Plane:
    def __init__(self, place, src, dst, sends, recvs):
        self.p, self.src, self.dst, self.sends, self.recvs = place, src, dst, sends, recvs

    def to(self, q):
        p = self.p
        return (p.b + (2 - 4 * p.y) * (q // 2), p.x + (1 - 2 * p.x) * (q % 2))

    def copy(self, q):
        return remote(self.src(q), self.dst(q), self.sends.at[q], self.recvs.at[q], self.to(q))

    def start(self):
        for q in (1, 2, 3):
            self.copy(q).start()

    def arrived(self):
        for q in (1, 2, 3):
            self.copy(q).wait_recv()

    def finish(self):
        for q in (1, 2, 3):
            self.copy(q).wait_send()


class Rounds:
    def __init__(self, place, sends, recvs):
        self.p, self.sends, self.recvs = place, sends, recvs

    def one(self, k, src, dst, to):
        return remote(src, dst, self.sends.at[k], self.recvs.at[k], to)

    def line(self, k, d):
        p = self.p
        z = (p.z + d) % p.depth
        return (p.b + 4 * (z - p.z), p.x)


class Octet:
    def __init__(self, place, src, dst, sends, recvs):
        self.p, self.src, self.dst, self.sends, self.recvs = place, src, dst, sends, recvs
        self.slot = place.y * 4 + place.c * 2 + place.x

    def copy(self, k):
        to = (self.slot + k) % 8
        device = (self.p.z * 4 + to // 2, to % 2)
        return remote(self.src(to), self.dst(self.slot), self.sends.at[k], self.recvs.at[k], device)

    def start(self):
        for k in range(1, 8):
            self.copy(k).start()

    def arrived(self):
        for k in range(1, 8):
            came = self.dst((self.slot + 8 - k) % 8)
            remote(came, came, self.sends.at[k], self.recvs.at[k], self.p.to_x).wait_recv()

    def finish(self):
        for k in range(1, 8):
            self.copy(k).wait_send()


class Quad:
    def __init__(self, p, axis, src, dst, sems):
        self.p, self.src, self.dst, self.sems = p, src, dst, sems
        self.to_pair = p.to_y if axis == 0 else p.to_x

    def to_core(self):
        return remote(self.src, self.dst(1), self.sems(0), self.sems(1), self.p.to_core)

    def to_next(self):
        return remote(self.src, self.dst(2), self.sems(2), self.sems(3), self.to_pair)

    def on(self):
        return remote(self.dst(2), self.dst(3), self.sems(4), self.sems(5), self.p.to_core)

    def start(self):
        self.to_next().start()
        self.to_core().start()

    def relay(self):
        self.to_next().wait_recv()
        self.on().start()

    def arrived(self):
        self.to_core().wait_recv()
        self.on().wait_recv()

    def finish(self):
        self.to_next().wait_send()
        self.to_core().wait_send()
        self.on().wait_send()


class QuadRows:
    def __init__(self, p, axis, src, dst, sems):
        self.p, self.axis, self.src, self.dst, self.sems = p, axis, src, dst, sems

    def mine(self, side, c):
        return self.src.at[:, side, c] if self.axis == 0 else self.src.at[:, :, c, side]

    def own(self):
        p = self.p
        side = p.y if self.axis == 0 else p.x
        return pltpu.make_async_copy(self.mine(side, p.c), self.dst.at[0], self.sems.at[0])

    def copy(self, k):
        p = self.p
        side = p.y if self.axis == 0 else p.x
        pair, far = (p.to_y, p.to_far) if self.axis == 0 else (p.to_x, p.to_far_x)
        side, c, to = ((side, 1 - p.c, p.to_core), (1 - side, p.c, pair), (1 - side, 1 - p.c, far))[k - 1]
        return remote(self.mine(side, c), self.dst.at[k], self.sems.at[2 * k - 1], self.sems.at[2 * k], to)

    def start(self):
        self.own().start()
        for k in (2, 3, 1):
            self.copy(k).start()

    def arrived(self):
        self.own().wait()
        for k in (1, 2, 3):
            self.copy(k).wait_recv()

    def finish(self):
        for k in (1, 2, 3):
            self.copy(k).wait_send()


class Reduce:
    CHUNK = 512

    def __init__(self, place, axis, x, take, rows, lo, width, out, full, outgo, income, sends, recvs):
        self.p, self.x, self.take, self.rows = place, x, take, rows
        self.side = place.x if axis == 0 else place.y
        self.to_other = place.to_x if axis == 0 else place.to_y
        self.lo, self.width, self.out = lo, width, out
        self.full, self.outgo, self.income = full, outgo, income
        self.sends, self.recvs = sends, recvs
        self.first = place.depth
        self.chunk = min(self.CHUNK, width)

    @staticmethod
    def scratch(rows, width, depth):
        return [
            pltpu.VMEM((2 * depth * rows, width), jnp.bfloat16),
            pltpu.VMEM(((2 * depth + 1) * rows, width), jnp.bfloat16),
            pltpu.SemaphoreType.DMA((4,)),
            pltpu.SemaphoreType.DMA((4,)),
        ]

    def part(self, ref, lo, hi):
        return ref.at[pl.ds(lo * self.rows, (hi - lo) * self.rows)]

    def across(self):
        n = self.p.depth
        return remote(
            self.part(self.outgo, 0, n), self.part(self.income, 0, n), self.sends.at[0], self.recvs.at[0], self.to_other
        )

    def up(self, lo):
        f, n = self.first, self.p.depth
        return remote(
            self.part(self.outgo, f + lo, f + n),
            self.part(self.income, f + lo, f + n),
            self.sends.at[1],
            self.recvs.at[1],
            self.p.to_up,
        )

    def down(self, hi):
        f = self.first
        return remote(
            self.part(self.outgo, f, f + hi),
            self.part(self.income, f, f + hi),
            self.sends.at[2],
            self.recvs.at[2],
            self.p.to_down,
        )

    def down_last(self, at):
        f, n = self.first, self.p.depth
        return remote(
            self.part(self.outgo, f + at, f + at + 1),
            self.part(self.income, f + n, f + n + 1),
            self.sends.at[3],
            self.recvs.at[3],
            self.p.to_down,
        )

    def columns(self, body):
        @pl.loop(0, self.width // self.chunk)
        def _(j):
            body(j, pl.ds(pl.multiple_of(j * self.chunk, self.chunk), self.chunk))

    def product(self, side, j):
        n, r = self.p.depth, self.rows
        x = jnp.concatenate([self.x[k, :, side].reshape(n * r, self.x.shape[4]) for k in range(4)], 1)
        return jnp.dot(x, self.take(self.lo // self.chunk + j), preferred_element_type=jnp.float32)

    def begin(self):
        p, n, r = self.p, self.p.depth, self.rows

        def away(j, here):
            self.outgo[pl.ds(0, n * r), here] = self.product(1 - self.side, j).astype(jnp.bfloat16)

        self.columns(away)
        self.across().start()

        def near(j, here):
            self.full[pl.ds(0, n * r), here] = self.product(self.side, j)

        self.columns(near)

        self.zeros()

    def zeros(self):
        p, f, n = self.p, self.first, self.p.depth

        @pl.when(p.z == 0)
        def _():
            ref = self.part(self.income, f, f + 1)
            ref[...] = jnp.zeros(ref.shape, ref.dtype)

        @pl.when(p.z == n - 1)
        def _():
            ref = self.part(self.income, f + n, f + n + 1)
            ref[...] = jnp.zeros(ref.shape, ref.dtype)

    def total(self, h, lo, hi):
        f, r = self.first, self.rows

        def body(j, here):
            rows = pl.ds(lo * r, (hi - lo) * r)
            line = pl.ds((f + lo) * r, (hi - lo) * r)
            total = self.full[rows, here]
            if f:
                total = total + self.income[rows, here].astype(jnp.float32)
            if h:
                total = total + self.income[line, here].astype(jnp.float32)
            self.outgo[line, here] = total.astype(jnp.bfloat16)

        self.columns(body)

    def hop(self, h):
        p, n = self.p, self.p.depth
        if h == 0 and self.first:
            self.across().wait_recv()

        @pl.when(p.z == h)
        def _():
            if h:
                self.up(h).wait_recv()
            self.total(h, h + 1, n)
            self.up(h + 1).start()

        @pl.when(p.z == n - 1 - h)
        def _():
            if h:
                self.down(n - 1 - h).wait_recv()
            self.total(h, 0, n - 1 - h)
            if h < n - 2:
                self.down(n - 2 - h).start()
            self.down_last(n - 2 - h).start()

    def last_waits(self):
        p, n = self.p, self.p.depth
        pl.when(p.z == n - 1)(lambda: self.up(n - 1).wait_recv())
        pl.when(p.z < n - 1)(lambda: self.down_last(0).wait_recv())

    def end(self):
        p, n, r = self.p, self.p.depth, self.rows
        self.last_waits()
        own = pl.ds(pl.multiple_of(p.z * r, r), r)
        line = pl.ds(pl.multiple_of((n + p.z) * r, r), r)

        def body(j, here):
            there = pl.ds(pl.multiple_of(self.lo + j * self.chunk, self.chunk), self.chunk)
            self.out[:, there] = (
                self.full[own, here]
                + self.income[own, here].astype(jnp.float32)
                + self.income[line, here].astype(jnp.float32)
                + self.income[pl.ds(2 * n * r, r), here].astype(jnp.float32)
            )

        self.columns(body)

    def finish(self):
        p, n = self.p, self.p.depth
        if self.first:
            self.across().wait_send()
        for h in range(n - 1):
            pl.when(p.z == h)(lambda: self.up(h + 1).wait_send())

            @pl.when(p.z == n - 1 - h)
            def _():
                if h < n - 2:
                    self.down(n - 2 - h).wait_send()
                self.down_last(n - 2 - h).wait_send()


class LineReduce(Reduce):
    def __init__(self, place, product, rows, width, full, outgo, income, sends, recvs):
        self.p, self.make, self.rows, self.width = place, product, rows, width
        self.full, self.outgo, self.income = full, outgo, income
        self.sends, self.recvs = sends, recvs
        self.first = 0
        self.chunk = min(self.CHUNK, width)

    @staticmethod
    def scratch(rows, width, depth):
        return [
            pltpu.VMEM((depth * rows, width), jnp.bfloat16),
            pltpu.VMEM(((depth + 1) * rows, width), jnp.bfloat16),
            pltpu.SemaphoreType.DMA((4,)),
            pltpu.SemaphoreType.DMA((4,)),
        ]

    def begin(self):
        def near(j, here):
            self.full[:, here] = self.make(j)

        self.columns(near)
        self.zeros()

    def end(self, write):
        self.last_waits()
        n, r = self.p.depth, self.rows
        own = pl.ds(pl.multiple_of(self.p.z * r, r), r)

        def body(j, here):
            write(
                here,
                self.full[own, here]
                + self.income[own, here].astype(jnp.float32)
                + self.income[pl.ds(n * r, r), here].astype(jnp.float32),
            )

        self.columns(body)


VMEM_BYTES = 62 * 2**20


def kernel_params(number):
    return pltpu.CompilerParams(collective_id=number, has_side_effects=True, vmem_limit_bytes=VMEM_BYTES)


def in_vmem(count):
    return [pl.BlockSpec(memory_space=pltpu.VMEM)] * count


def in_any(count):
    return [pl.BlockSpec(memory_space=pl.ANY)] * count


def ranges(cols, cut):
    return [(0, cut, True), (cut, cols, False)] if cut else [(0, cols, False)]


def keep_own(p, pairs, sems):
    copies = []
    for k, (src, dst, rows) in enumerate(pairs):
        at = pl.multiple_of(p.shard(p.z, p.y, p.c, p.x) * rows, rows)
        copies.append(pltpu.make_async_copy(src, dst.at[pl.ds(at, rows)], sems.at[k]))
    for copy in copies:
        copy.start()
    return copies


class Exchange:
    def __init__(self, place, count, src, dst, sends, recvs, own):
        self.p, self.count, self.src, self.dst = place, count, src, dst
        self.sends, self.recvs, self.own = sends, recvs, own

    def copy(self, k):
        to = (self.p.b + k) % self.count
        return remote(
            self.src.at[to], self.dst.at[self.p.b], self.sends.at[k], self.recvs.at[k], (to, self.p.x)
        )

    def mine(self):
        return pltpu.make_async_copy(self.src.at[self.p.b], self.dst.at[self.p.b], self.own)

    def start(self):
        self.mine().start()
        for k in range(1, self.count):
            self.copy(k).start()

    def send_to(self, device):
        k = (device + self.count - self.p.b) % self.count
        pl.when(k > 0)(lambda: self.copy(k).start())
        pl.when(k == 0)(lambda: self.mine().start())

    def wait_from(self, device):
        k = (self.p.b + self.count - device) % self.count

        @pl.when(k > 0)
        def _():
            came = self.dst.at[device]
            remote(came, came, self.sends.at[k], self.recvs.at[k], self.p.to_x).wait_recv()

        pl.when(k == 0)(lambda: self.mine().wait())

    def arrived(self):
        self.mine().wait()
        for k in range(1, self.count):
            came = (self.p.b + self.count - k) % self.count
            remote(
                self.dst.at[came], self.dst.at[came], self.sends.at[k], self.recvs.at[k], self.p.to_x
            ).wait_recv()

    def finish(self):
        for k in range(1, self.count):
            self.copy(k).wait_send()


def exchange_sems(count):
    return [
        pltpu.SemaphoreType.DMA((count,)),
        pltpu.SemaphoreType.DMA((count,)),
        pltpu.SemaphoreType.DMA,
    ]


def greet_plane(p, count, more):
    barrier = pltpu.get_barrier_semaphore()
    for to in more:
        pl.semaphore_signal(barrier, inc=1, device_id=to, device_id_type=MESH)
    for k in range(1, count):
        pl.semaphore_signal(barrier, inc=1, device_id=((p.b + k) % count, p.x), device_id_type=MESH)
    pl.semaphore_signal(barrier, inc=1, device_id=p.to_x, device_id_type=MESH)
    pl.semaphore_wait(barrier, count + len(more))


def play(events):
    for event in events:
        event()


def three_terms(v):
    a = v.astype(jnp.bfloat16).astype(jnp.float32)
    b = (v - a).astype(jnp.bfloat16).astype(jnp.float32)
    return a, b, v - a - b


def extra_rows(rows, length, width):
    shape = (length, width)
    row = lax.broadcasted_iota(jnp.int32, shape, 0)
    total = jnp.zeros(shape, jnp.float32)
    for k, values in enumerate(rows):
        total = jnp.where(row == k, values, total)
    return total.astype(jnp.bfloat16)


def attend_open(p, lengths, got_kv, qkv, keys, values):
    count, _, span = got_kv.shape
    frames = count * span
    for k in range(count):
        qkv[HEAD_DIM:, k * span : (k + 1) * span] = got_kv[k]
    position = lax.broadcasted_iota(jnp.int32, (1, frames), 1)
    hidden_key = jnp.where(position < lengths[p.x], 0.0, -1e30)
    keys[...] = jnp.concatenate([qkv[HEAD_DIM : 2 * HEAD_DIM, :], extra_rows([hidden_key], HEAD_DIM, frames)], 0).T
    values[...] = jnp.concatenate([qkv[2 * HEAD_DIM :, :], extra_rows([1.0], 16, frames)], 0)


def in_turn(p, i, blocks):
    return (p.b // 2 + blocks - i) % blocks


def attend(p, lengths, queries, qkv, keys, values, results, lse, plain, lo, hi):
    count, _, span = queries.dst.shape
    block = 2 * span
    length = lengths[p.x]
    ones = extra_rows([1.0], HEAD_DIM, block)
    scaling = HEAD_DIM ** (-0.5)

    @pl.loop(lo, hi)
    def _(i):
        j = in_turn(p, i, count // 2)
        here = pl.ds(pl.multiple_of(j * block, block), block)
        for k in range(2):
            queries.wait_from(2 * j + k)
        query = jnp.concatenate([queries.dst[2 * j], queries.dst[2 * j + 1]], 1)
        qkv[:HEAD_DIM, here] = query
        query = jnp.concatenate([query * jnp.bfloat16(scaling), ones], 0)
        score = jnp.dot(keys[...], query, preferred_element_type=jnp.float32)
        peak = jnp.max(score, 0, keepdims=True)
        weights = jnp.exp(score - peak).astype(jnp.bfloat16)
        out = jnp.dot(values[...], weights, preferred_element_type=jnp.float32)
        total = out[HEAD_DIM : HEAD_DIM + 1]
        out = out[:HEAD_DIM] / total
        plain[:, here] = out
        lse[:, here] = peak + jnp.log(total)
        column = lax.broadcasted_iota(jnp.int32, (HEAD_DIM, block), 1) + j * block
        kept = jnp.where(column < length, out, 0.0).astype(jnp.bfloat16)
        for k in range(2):
            results.src[2 * j + k] = kept[:, k * span : (k + 1) * span]
            results.send_to(2 * j + k)


def attend_back_open(p, lengths, qkv, keys, values, sums):
    frames = qkv.shape[1]
    length = lengths[p.x]
    position = lax.broadcasted_iota(jnp.int32, (1, frames), 1)
    hidden_key = jnp.where(position < length, 0.0, -1e30)
    keys[...] = jnp.concatenate(
        [qkv[HEAD_DIM : 2 * HEAD_DIM, :], extra_rows([hidden_key, 1.0, 1.0, 1.0], HEAD_DIM, frames)], 0
    ).T
    values[...] = jnp.concatenate(
        [qkv[2 * HEAD_DIM :, :], extra_rows([1.0, 1.0, 1.0], HEAD_DIM, frames)], 0
    ).T
    sums[...] = jnp.zeros_like(sums)


def attend_back(p, upstreams, qkv, lse, plain, keys, values, sums, results, lo, hi):
    count, _, span = upstreams.dst.shape
    block = 2 * span
    scaling = HEAD_DIM ** (-0.5)

    @pl.loop(lo, hi)
    def _(i):
        j = in_turn(p, i, count // 2)
        here = pl.ds(pl.multiple_of(j * block, block), block)
        for k in range(2):
            upstreams.wait_from(2 * j + k)
        query = qkv[:HEAD_DIM, here] * jnp.bfloat16(scaling)
        upstream = jnp.concatenate([upstreams.dst[2 * j], upstreams.dst[2 * j + 1]], 1)
        delta = jnp.sum(upstream.astype(jnp.float32) * plain[:, here], 0, keepdims=True)
        left = jnp.concatenate(
            [query, extra_rows([1.0, *[-t for t in three_terms(lse[:, here])]], HEAD_DIM, block)], 0
        )
        right = jnp.concatenate([upstream, extra_rows([-t for t in three_terms(delta)], HEAD_DIM, block)], 0)
        weights = jnp.exp(jnp.dot(keys[...], left, preferred_element_type=jnp.float32))
        slope = jnp.dot(values[...], right, preferred_element_type=jnp.float32)
        slope = (weights * slope).astype(jnp.bfloat16)
        query_grad = (
            jnp.dot(qkv[HEAD_DIM : 2 * HEAD_DIM, :], slope, preferred_element_type=jnp.float32) * scaling
        ).astype(jnp.bfloat16)
        for k in range(2):
            results.src[2 * j + k] = query_grad[:, k * span : (k + 1) * span]
            results.send_to(2 * j + k)
        sums[:, HEAD_DIM:] += lax.dot_general(
            weights.astype(jnp.bfloat16), upstream, (((1,), (1,)), ((), ())), preferred_element_type=jnp.float32
        )
        sums[:, :HEAD_DIM] += lax.dot_general(
            slope, query, (((1,), (1,)), ((), ())), preferred_element_type=jnp.float32
        )


def attend_back_close(sums, grads_out):
    count, _, span = grads_out.shape

    @pl.loop(0, count)
    def _(k):
        rows = pl.ds(pl.multiple_of(k * span, span), span)
        grads_out[k] = sums[rows, :].T.astype(jnp.bfloat16)


def others(p, count, k):
    number = (p.b * 2 + p.x + k) % (2 * count)
    return (number // 2, number % 2)


def nt(left, right):
    return lax.dot_general(left, right, (((1,), (1,)), ((), ())), preferred_element_type=jnp.float32)


def mean(v):
    return jnp.mean(v, -1, keepdims=True)


def normal(v):
    center = v - mean(v)
    rstd = lax.rsqrt(mean(center * center) + epsilon)
    return center * rstd, rstd


def normal_back(grad, hat, rstd, scale):
    gx = grad * (1.0 + scale)
    return rstd * (gx - mean(gx) - hat * mean(gx * hat))


def fold(v):
    width = v.shape[1] // 8
    return jnp.concatenate([v[:, k * width : (k + 1) * width] for k in range(8)], 0)


class Refs:
    def __init__(self, names, refs):
        for name, ref in zip(names, refs):
            setattr(self, name, ref)


def back_kernel(depth, shards, names, *refs):
    r = Refs(names, refs)
    rest = list(refs[len(names) :])
    p = Place(depth)
    count = 4 * depth
    devices = 2 * count
    frames, model = r.base.shape
    half = model // 2
    chunk = 512
    bf = jnp.bfloat16
    units = r.w_up.shape[1]

    barrier = pltpu.get_barrier_semaphore()
    for k in range(1, devices):
        pl.semaphore_signal(barrier, inc=1, device_id=others(p, count, k), device_id_type=MESH)

    def fetch(src, slot):
        return pltpu.make_async_copy(src, r.weights.at[slot], r.weight_sems.at[slot])

    def columns(ref, k):
        return ref.at[:, pl.ds(k * chunk, chunk)]

    def fetch_first(slot):
        return fetch(columns((r.w_out, r.w_up, r.w_down)[slot // 2], slot % 2), slot)

    def fetch_qkv(slot):
        return fetch(columns(r.w_qkv, slot), slot)

    def fetch_skip(slot):
        return fetch(r.w_skip.at[pl.ds((slot // 2) * model, model), pl.ds((slot % 2) * chunk, chunk)], slot)

    late_loads = [
        pltpu.make_async_copy(src, dst, r.load_sems.at[k])
        for k, (src, dst) in enumerate(
            ((r.cot_far, r.cot_all), (r.qkv_far, r.qkv), (r.plain_far, r.plain), (r.xnormed_far, r.xnormed),
             (r.xjoined_far, r.xjoined))
        )
    ]
    for slot in range(6):
        fetch_first(slot).start()
    for copy in late_loads:
        copy.start()
    pl.semaphore_wait(barrier, devices - 1)

    def to_sibling(src, dst, k):
        return remote(src, dst, r.pair_sems.at[0, k], r.pair_sems.at[1, k], p.to_core)

    pair_cot = to_sibling(r.cot_all, r.cot_sib, 0)
    pair_n2 = to_sibling(r.n2_all, r.n2_sib, 1)
    pair_act = to_sibling(r.act.at[1 - p.c], r.act_sib, 2)
    pair_gin = to_sibling(r.gin.at[1 - p.c], r.gin_sib, 3)
    plane_n2 = Plane(p, lambda q: r.n2_all.at[0], lambda q: r.n2_all.at[q], r.n2_sems.at[0], r.n2_sems.at[1])
    plane_back = Plane(
        p, lambda q: r.part_back.at[q - 1], lambda q: r.got_back.at[q - 1], r.back_sems.at[0], r.back_sems.at[1]
    )
    plane_total = Plane(
        p, lambda q: r.part_total.at[q - 1], lambda q: r.got_total.at[q - 1], r.total_sems.at[0], r.total_sems.at[1]
    )
    share_mixed = QuadRows(p, 0, r.mixed, r.xmix, r.row_sems.at[0])
    share_branch = Quad(p, 0, r.gbranch.at[0], lambda k: r.gbranch.at[k], lambda k: r.branch_sems.at[k])

    def share_late(c):
        return Quad(p, c // 6, r.glate.at[0, c], lambda k: r.glate.at[k, c], lambda k: r.late_sems.at[c, k])

    length = r.lengths[p.x]
    position = p.b * frames
    kept = (position + lax.broadcasted_iota(jnp.int32, (frames, 1), 0) < length).astype(jnp.float32)
    kept_row = (position + lax.broadcasted_iota(jnp.int32, (1, frames), 1) < length).astype(jnp.float32)
    a_scale = kept * r.mods[0:1, :]
    f_scale = kept * r.mods[2:3, :]
    f_shift = kept * r.mods[3:4, :]
    mixed = r.mixed[...].reshape(model, frames).T
    for k in range(2):
        fetch_first(k).wait()
        cols = pl.ds(k * chunk, chunk)
        r.middle[:, cols] = r.base[:, cols] + jnp.dot(mixed, r.weights[k], preferred_element_type=jnp.float32)
    hat, rstd = normal(r.middle[...])
    r.n2_all[0] = (hat * (1.0 + f_scale) + f_shift).astype(bf)
    plane_n2.start()
    r.bias[...] = jnp.zeros_like(r.bias)
    for slot in range(2, 6):
        fetch_first(slot).wait()
    for copy in late_loads:
        copy.wait()
    pair_cot.start()

    @pl.loop(0, 4)
    def _(q):
        pl.when(q > 0)(lambda: plane_n2.copy(q).wait_recv())
        acts, grads = [], []
        for u in range(2):
            cols = pl.ds(u * chunk, chunk)
            inner = jnp.dot(r.n2_all[q], r.weights[2 + u], preferred_element_type=jnp.float32) + r.b_up[:, cols]
            cdf = 0.5 * (1.0 + lax.erf(inner * (0.5**0.5)))
            act = (inner * cdf).astype(bf)
            slope = cdf + inner * (jnp.exp(-0.5 * inner * inner) * (1.0 / math.sqrt(2.0 * math.pi)))
            act_grad = nt(r.cot_all[q, :, :half], r.weights[4, cols, :]) + nt(
                r.cot_all[q, :, half:], r.weights[5, cols, :]
            )
            grad = (act_grad * slope).astype(bf)
            r.bias[:, cols] += jnp.sum(grad.astype(jnp.float32), 0, keepdims=True)
            for k in range(4):
                here = slice(k * 128, (k + 1) * 128)
                at = (2 * u + k // 2) * 128
                r.act[k % 2, q, :, at : at + 128] = act[:, here]
                r.gin[k % 2, q, :, at : at + 128] = grad[:, here]
            acts.append(act)
            grads.append(grad)
        back = nt(grads[0], r.weights[2]) + nt(grads[1], r.weights[3])

        @pl.when(q == 0)
        def _():
            r.back[...] = back

        @pl.when(q > 0)
        def _():
            r.part_back[q - 1] = back.astype(bf)
            plane_back.copy(q).start()

        for k in range(2):
            cols = slice(k * half, (k + 1) * half)
            total = jnp.dot(acts[0], r.weights[4 + k, :chunk, :], preferred_element_type=jnp.float32)
            total = total + jnp.dot(acts[1], r.weights[4 + k, chunk:, :], preferred_element_type=jnp.float32)

            @pl.when(q == 0)
            def _():
                r.own_total[:, cols] = total

            @pl.when(q > 0)
            def _():
                r.part_total[q - 1, :, cols] = total.astype(bf)

    def blocks_of(first):
        return lambda j: jnp.concatenate([r.glate[k, first + j] for k in range(4)], 0)

    def branch_columns(j):
        here = pl.ds(pl.multiple_of(j * chunk, chunk), chunk)
        return jnp.concatenate([r.gbranch[k, :, here] for k in range(4)], 0)

    def tn(left, right):
        return lax.dot_general(left, right, (((0,), (0,)), ((), ())), preferred_element_type=jnp.float32)

    def flat(v):
        return v.reshape(4 * frames, v.shape[2])

    def down_part(k):
        cols = slice(k * half, (k + 1) * half)

        def make(j):
            mine = tn(flat(r.act[p.c]), flat(r.cot_all[:, :, cols]))
            return mine + tn(flat(r.act_sib[...]), flat(r.cot_sib[:, :, cols]))

        return make

    def up_part(k):
        cols = slice(k * 256, (k + 1) * 256)

        def make(j):
            mine = tn(flat(r.n2_all[...]), flat(r.gin[p.c, :, :, cols]))
            return mine + tn(flat(r.n2_sib[...]), flat(r.gin_sib[:, :, cols]))

        return make

    down, up, out, qkv, skip = [], [], [], [], []
    group = model // depth
    for k in range(2):
        down.append(LineReduce(p, down_part(k), units // (2 * depth), half, *rest[:5]))
        rest = rest[5:]
    for k in range(2):
        up.append(LineReduce(p, up_part(k), group, 256, *rest[:5]))
        rest = rest[5:]
    for sums, axis, x, take, res, (rows, cols, parts) in (
        (out, 0, r.xmix, branch_columns, r.out_grad, shards[0]),
        (qkv, 0, r.xnormed, blocks_of(0), r.qkv_grad, shards[1]),
        (skip, 1, r.xjoined, blocks_of(6), r.skip_grad, shards[2]),
    ):
        width = cols // parts
        for k in range(parts):
            sums.append(Reduce(p, axis, x, take, rows, k * width, width, res, *rest[:5]))
            rest = rest[5:]

    pair_act.start()
    pair_n2.start()
    pair_gin.start()
    pair_cot.wait_recv()
    pair_act.wait_recv()
    down[0].begin()
    down[0].hop(0)
    plane_back.arrived()
    middle = r.middle[...]
    hat, rstd = normal(middle)
    grad = r.back[...]
    for k in range(3):
        grad = grad + r.got_back[k].astype(jnp.float32)
    cot = r.cot_all[0].astype(jnp.float32)
    middle_grad = cot + normal_back(grad, hat, rstd, f_scale)
    r.back[...] = middle_grad
    branch_grad = middle_grad.astype(bf)
    r.gbranch[0] = branch_grad
    there = Exchange(p, count, r.mixed_grad, r.got, r.s1, r.r1, r.o1)
    back = Exchange(p, count, r.grads_out, r.got_grads, r.s2, r.r2, r.o2)
    queries = Exchange(p, count, r.queries_out, r.got_queries, r.s3, r.r3, r.o3)
    mixed_grad = nt(r.weights[0], branch_grad[:, :half]) + nt(r.weights[1], branch_grad[:, half:])
    r.mixed_grad[...] = (mixed_grad.astype(bf) * kept_row.astype(bf)).reshape(r.mixed_grad.shape)
    there.start()
    plane_total.start()
    share_mixed.start()
    share_branch.start()
    for slot in range(6):
        fetch_qkv(slot).start()
    r.vectors[2:3, :] = jnp.sum(kept * grad * hat, 0, keepdims=True)
    r.vectors[3:4, :] = jnp.sum(kept * grad, 0, keepdims=True)

    def end_down(k):
        def write(here, total):
            r.down_grad[:, pl.ds(pl.multiple_of(k * half + here.start, 128), here.size)] = total

        down[k].end(write)

    def end_up(k):
        def write(here, total):
            r.up_out[:, :, k * 256 : (k + 1) * 256] = total.astype(bf).reshape(8, group // 8, 256)

        up[k].end(write)

    ups = Octet(p, lambda to: r.up_out.at[to], lambda slot: r.up_got.at[slot], r.up_sems.at[0], r.up_sems.at[1])

    def up_spread():
        ups.start()
        r.up_got[ups.slot] = r.up_out[ups.slot]

    def up_arrived():
        ups.arrived()
        for t in range(8):
            for z in range(depth):
                at = (z * 8 + t) * 128
                r.up_grad[:, at : at + 128] = r.up_got[t, :, z * 128 : (z + 1) * 128].astype(jnp.float32)

    def ready(shares):
        for share in shares:
            if isinstance(share, Quad):
                share.relay()
        for share in shares:
            share.arrived()

    blocks = r.qkv.shape[1] // 256
    attend_back_open(p, r.lengths, r.qkv, r.keys, r.values, r.kv_sums)
    attend = functools.partial(
        attend_back, p, there, r.qkv, r.lse, r.plain, r.keys, r.values, r.kv_sums, queries
    )
    down[1].begin()
    down[1].hop(0)
    attend(0, blocks // 2)
    down[0].hop(1)
    attend(blocks // 2, blocks)
    attend_back_close(r.kv_sums, r.grads_out)
    back.start()
    down[1].hop(1)

    cosine, sine = r.cosine[...][None], r.sine[...][None]

    def send_part(part, h):
        h = h.reshape(model, frames).T
        for k in range(2):
            r.glate[0, 2 * part + k] = h[:, k * chunk : (k + 1) * chunk]
            share_late(2 * part + k).start()

    queries.arrived()
    send_part(0, turn(r.got_queries[...].astype(jnp.float32), cosine, -sine).astype(bf))
    for k in range(2):
        fetch_qkv(k).wait()
        made = nt(r.glate[0, k], r.weights[k])
        if k == 0:
            r.total[...] = made
        else:
            r.total[...] += made
    down[0].hop(2)
    pair_n2.wait_recv()
    pair_gin.wait_recv()
    up[0].begin()
    up[0].hop(0)
    plane_total.arrived()
    total = r.middle[...] + r.own_total[...] + r.b_down[...]
    for k in range(3):
        total = total + r.got_total[k].astype(jnp.float32)
    r.output[...] = total.astype(bf)
    ready([share_mixed, share_branch])
    out[0].begin()
    up[1].begin()
    up[1].hop(0)
    ready([share_late(0), share_late(1)])
    qkv[0].begin()
    back.arrived()
    send_part(1, turn(r.got_grads[:, :HEAD_DIM, :].astype(jnp.float32), cosine, -sine).astype(bf))
    send_part(2, r.got_grads[:, HEAD_DIM:, :])
    for k in range(2, 6):
        fetch_qkv(k).wait()
        r.total[...] += nt(r.glate[0, k], r.weights[k])
    for k in range(4):
        fetch_skip(k).start()
    hat, rstd = normal(r.base[...])
    grad = r.total[...]
    base_grad = (r.back[...] + normal_back(grad, hat, rstd, a_scale)).astype(bf)
    for k in range(2):
        r.glate[0, 6 + k] = base_grad[:, k * chunk : (k + 1) * chunk]
        share_late(6 + k).start()
    r.vectors[0:1, :] = jnp.sum(kept * grad * hat, 0, keepdims=True)
    r.vectors[1:2, :] = jnp.sum(kept * grad, 0, keepdims=True)

    r.vectors[4:5, :] = jnp.sum(cot, 0, keepdims=True)
    r.vectors[5:6, :] = jnp.sum(base_grad.astype(jnp.float32), 0, keepdims=True)
    r.vectors[6:7, :] = r.bias[...]
    r.vectors[7:8, :] = jnp.zeros((1, model), jnp.float32)
    smalls = Octet(p, lambda to: r.vectors, lambda slot: r.plane_got.at[slot], r.small_sems.at[0], r.small_sems.at[1])
    small = Rounds(p, r.line_sems.at[0], r.line_sems.at[1])

    def small_line(d):
        return small.one(d, r.line_out, r.line_got.at[d], small.line(0, d))

    def after_plane():
        r.plane_got[smalls.slot] = r.vectors[...]
        smalls.arrived()
        halves = []
        for x in range(2):
            total = r.plane_got[x]
            for k in range(1, 4):
                total = total + r.plane_got[2 * k + x]
            halves.append(total)
            r.line_out[4 * x : 4 * x + 4, :] = total[0:4]
        r.line_out[8:10, :] = halves[0][4:6] + halves[1][4:6]
        chip = p.y * 4 + p.x
        r.line_out[10:11, :] = r.plane_got[chip, 6:7, :] + r.plane_got[chip + 2, 6:7, :]
        r.line_out[11:16, :] = jnp.zeros((5, model), jnp.float32)
        for d in range(1, depth):
            small_line(d).start()

    smalls.start()
    down[1].hop(2)
    end_down(0)
    out[0].hop(0)
    up[0].hop(1)

    number = p.b * 2 + p.x
    timers = Octet(
        p,
        lambda to: r.times_full.at[number],
        lambda slot: r.times_full.at[p.z * 8 + slot],
        r.small_sems.at[2],
        r.small_sems.at[3],
    )

    def times_line(d):
        block = r.times_full.at[pl.ds(p.z * 8, 8)]
        return small.one(3 + d, block, block, small.line(0, d))

    def times_came(d):
        z = (p.z + depth - d) % depth
        block = r.times_full.at[pl.ds(z * 8, 8)]
        return small.one(3 + d, block, block, small.line(0, d))

    for i in range(2):
        total = None
        for j in range(2):
            fetch_skip(2 * i + j).wait()
            made = nt(r.glate[0, 6 + j], r.weights[2 * i + j])
            total = made if total is None else total + made
        r.joined_grad[i] = total.astype(bf)

    qkv[0].hop(0)
    end_down(1)
    up[1].hop(1)
    after_plane()
    out[0].hop(1)
    ready([share_late(6), share_late(7)])
    skip[0].begin()
    skip[1].begin()
    ready([share_late(2), share_late(3)])
    qkv[1].begin()
    up[0].hop(2)
    ready([share_late(4), share_late(5)])
    qkv[2].begin()
    out[0].hop(2)
    qkv[0].hop(1)
    up[1].hop(2)

    total = r.line_out[...]
    for d in range(1, depth):
        small_line(d).wait_recv()
        total = total + r.line_got[d]
    first, second = total[0:4], total[4:8]
    r.line_sum[...] = total
    total = jnp.zeros((8, r.w_mod.shape[0]), jnp.float32)
    turned = r.times[...].T
    share = r.w_mod.shape[0]
    for part in range(4):
        values = [first[part : part + 1, :], second[part : part + 1, :]]
        here = pl.ds(part * model, model)
        left = extra_rows([*three_terms(values[0]), *three_terms(values[1])], 8, model)
        total = total + nt(left, r.w_mod[:, here])
        r.mod_grad[:, here] = turned[:share, 0:1] * values[0] + turned[:share, 4:5] * values[1]
    made = jnp.concatenate(
        [total[0:1] + total[1:2] + total[2:3], total[3:4] + total[4:5] + total[5:6], jnp.zeros((6, share), jnp.float32)]
    )
    r.times_full[number] = jnp.concatenate([made, jnp.zeros((8, 128 - share), jnp.float32)], 1)
    timers.start()
    skip[0].hop(0)
    qkv[1].hop(0)
    qkv[0].hop(2)
    end_up(0)
    skip[1].hop(0)
    skip[0].hop(1)
    qkv[1].hop(1)
    qkv[2].hop(0)
    end_up(1)
    up_spread()
    timers.arrived()
    for d in range(1, depth):
        times_line(d).start()
    r.sums_out[...] = jnp.zeros_like(r.sums_out)
    at = pl.multiple_of((p.z * 2 + p.c) * 128, 128)
    r.sums_out[0:1, :] = r.line_sum[10:11, pl.ds(at, 128)]
    at = pl.multiple_of(number // 4 * 128, 128)
    near = r.line_sum[8:10, pl.ds(at, 128)]
    each = model // devices
    own = near[:, :each]
    for k in range(1, 4):
        own = jnp.where(number % 4 == k, near[:, k * each : (k + 1) * each], own)
    r.sums_out[1:2, :each] = own[0:1]
    r.sums_out[1:2, each : 2 * each] = own[1:2]
    out[0].end()
    qkv[0].end()
    skip[0].hop(2)
    skip[1].hop(1)
    qkv[1].hop(2)
    qkv[2].hop(1)
    skip[0].end()
    skip[1].hop(2)
    qkv[1].end()
    qkv[2].hop(2)
    skip[1].end()
    up_arrived()
    qkv[2].end()
    for d in range(1, depth):
        times_came(d).wait_recv()
    for one in [*down, *up, *out, *qkv, *skip, share_mixed, share_branch, plane_n2, plane_back, plane_total]:
        one.finish()
    for c in range(8):
        share_late(c).finish()
    for one in (pair_cot, pair_n2, pair_act, pair_gin):
        one.wait_send()
    for one in (there, back, queries, ups, smalls, timers):
        one.finish()
    for d in range(1, depth):
        small_line(d).wait_send()
        times_line(d).wait_send()


def back_call(depth, devices, args):
    base, qkv = args["base"], args["qkv_far"]
    frames, model = base.shape
    count = devices // 2
    units = args["w_up"].shape[1]
    ff = units * 4
    bf, f32 = jnp.bfloat16, jnp.float32
    share = args["w_mod"].shape[0]
    dma = pltpu.SemaphoreType.DMA
    sum_scratch = []
    for rows, width in [(units // (2 * depth), model // 2)] * 2 + [(model // depth, 256)] * 2:
        sum_scratch.append(pltpu.VMEM((depth * rows, width), f32))
        sum_scratch += LineReduce.scratch(rows, width, depth)
    shards = [
        (model // devices, model, 1),
        (model // devices, 3 * model, 3),
        (2 * model // devices, model, 2),
    ]
    for rows, cols, parts in shards:
        for _ in range(parts):
            sum_scratch.append(pltpu.VMEM((depth * rows, cols // parts), f32))
            sum_scratch += Reduce.scratch(rows, cols // parts, depth)

    def tall(n, *shape, kind=bf):
        return pltpu.VMEM((n, *shape), kind)

    scratch = dict(
        cot_all=tall(4, frames, model),
        qkv=tall(*qkv.shape),
        plain=tall(HEAD_DIM, qkv.shape[1], kind=f32),
        xnormed=tall(4, depth, 2, model // devices, frames),
        xjoined=tall(4, depth, 2, 2 * model // devices, frames),
        load_sems=dma((5,)),
        weights=tall(6, model, 512),
        middle=tall(frames, model, kind=f32),
        total=tall(frames, model, kind=f32),
        own_total=tall(frames, model, kind=f32),
        back=tall(frames, model, kind=f32),
        bias=tall(1, units, kind=f32),
        vectors=tall(8, model, kind=f32),
        n2_all=tall(4, frames, model),
        n2_sib=tall(4, frames, model),
        cot_sib=tall(4, frames, model),
        act=tall(2, 4, frames, units // 2),
        gin=tall(2, 4, frames, units // 2),
        act_sib=tall(4, frames, units // 2),
        gin_sib=tall(4, frames, units // 2),
        part_back=tall(3, frames, model),
        got_back=tall(3, frames, model),
        part_total=tall(3, frames, model),
        got_total=tall(3, frames, model),
        up_out=tall(8, model // devices, units // 2),
        up_got=tall(8, model // devices, units // 2),
        gbranch=tall(4, frames, model),
        glate=tall(4, 8, frames, 512),
        xmix=tall(4, depth, 2, model // devices, frames),
        mixed_grad=tall(count, HEAD_DIM, frames),
        got=tall(count, HEAD_DIM, frames),
        keys=tall(qkv.shape[1], 2 * HEAD_DIM),
        values=tall(qkv.shape[1], 2 * HEAD_DIM),
        kv_sums=tall(qkv.shape[1], 2 * HEAD_DIM, kind=f32),
        grads_out=tall(count, 2 * HEAD_DIM, frames),
        got_grads=tall(count, 2 * HEAD_DIM, frames),
        queries_out=tall(count, HEAD_DIM, frames),
        got_queries=tall(count, HEAD_DIM, frames),
        plane_got=tall(8, 8, model, kind=f32),
        line_out=tall(16, model, kind=f32),
        line_got=tall(depth, 16, model, kind=f32),
        line_sum=tall(16, model, kind=f32),
        weight_sems=dma((6,)),
        pair_sems=dma((2, 4)),
        n2_sems=dma((2, 4)),
        back_sems=dma((2, 4)),
        total_sems=dma((2, 4)),
        up_sems=dma((2, 8)),
        row_sems=dma((1, 7)),
        branch_sems=dma((6,)),
        late_sems=dma((8, 6)),
        s1=dma((count,)),
        r1=dma((count,)),
        o1=dma,
        s2=dma((count,)),
        r2=dma((count,)),
        o2=dma,
        s3=dma((count,)),
        r3=dma((count,)),
        o3=dma,
        small_sems=dma((4, 8)),
        line_sems=dma((2, 8)),
    )
    shape = jax.ShapeDtypeStruct
    outs = dict(
        output=shape((frames, model), bf),
        joined_grad=shape((2, frames, model), bf),
        skip_grad=shape((2 * model // devices, model), f32),
        qkv_grad=shape((model // devices, 3 * model), f32),
        out_grad=shape((model // devices, model), f32),
        up_grad=shape((model // devices, ff), f32),
        down_grad=shape((ff // devices, model), f32),
        mod_grad=shape((share, 4 * model), f32),
        sums_out=shape((8, 128), f32),
        times_full=shape((devices, 8, 128), f32),
    )
    names = [*args, *outs, *scratch]
    vmem = pl.BlockSpec(memory_space=pltpu.VMEM)
    specs = dict.fromkeys(args, vmem)
    specs["lengths"] = pl.BlockSpec(memory_space=pltpu.SMEM)
    for name in args:
        if name.startswith("w_") and name != "w_mod" or name.endswith("_far"):
            specs[name] = pl.BlockSpec(memory_space=pl.ANY)
    made = pl.pallas_call(
        functools.partial(back_kernel, depth, shards, names),
        name="back",
        out_shape=list(outs.values()),
        in_specs=list(specs.values()),
        out_specs=[vmem] * len(outs),
        scratch_shapes=list(scratch.values()) + sum_scratch,
        compiler_params=kernel_params(3),
    )(*args.values())
    return dict(zip(outs, made))


def front_kernel(depth, cuts, names, *refs):
    r = Refs(names, refs)
    p = Place(depth)
    count = 4 * depth
    devices = 2 * count
    frames, model = r.hidden.shape
    bf = jnp.bfloat16
    share = r.w_mod.shape[0]
    tile = pl.ds(pl.multiple_of((p.b // 2) * 128, 128), 128)
    part = r.time_row[:, tile].astype(jnp.float32)
    mark = lax.broadcasted_iota(jnp.int32, (8, 128), 0) // 4 == p.x
    for ref, x in ((r.own_time, p.x), (r.other_time, 1 - p.x)):
        slot = p.c * 2 + x
        picked = part[:, 0:share]
        for k in range(1, 4):
            picked = jnp.where(slot == k, part[:, k * share : (k + 1) * share], picked)
        picked = jnp.concatenate([picked, jnp.zeros((1, 128 - share), jnp.float32)], 1)
        ref[...] = jnp.where(mark, picked, 0.0)
    half = HEAD_DIM // 2
    position = p.b * frames + lax.broadcasted_iota(jnp.int32, (half, frames), 1)
    length = r.lengths[p.x]
    offset = jnp.where(position < length, position, position - length).astype(jnp.float32)
    index = lax.broadcasted_iota(jnp.int32, (half, frames), 0).astype(jnp.float32)
    angle = offset * jnp.exp(index * (-math.log(10000.0) / half))
    r.cosine[...] = jnp.cos(angle)
    r.sine[...] = jnp.sin(angle)
    greet_plane(p, count, (p.to_across, p.to_far_x))
    ask = remote(r.other_time, r.got_time, r.time_sems.at[0], r.time_sems.at[1], p.to_x)
    ask.start()

    groups = {}
    number = 0
    owns = []
    for name, src, dst in (
        ("skip", r.w_skip, r.skip_here),
        ("qkv", r.w_qkv, r.qkv_here),
        ("out", r.w_out, r.out_full),
    ):
        groups[name] = []
        for lo, hi, first in ranges(src.shape[1], src.shape[1] // cuts[name] if cuts[name] else 0):
            groups[name].append(
                Gather(p, src, dst, src.shape[0], lo, hi, True, first, r.sends.at[number], r.recvs.at[number])
            )
            number += 1
        owns.append((src, dst, src.shape[0]))
    packs = Gather(
        p, r.pack, r.pack_full, 8, 0, r.pack.shape[1], False, False, r.sends.at[number], r.recvs.at[number]
    )
    number += 1
    units = 2 * depth * 128

    def spread_up():
        for q in range(4):
            y, x = (p.y + q // 2) % 2, (p.x + q % 2) % 2
            for z in range(depth):
                for c in range(2):
                    cols = pl.ds(pl.multiple_of(p.shard(z, y, c, x) * 128, 128), 128)
                    r.up_out[q, :, (z * 2 + c) * 128 : (z * 2 + c + 1) * 128] = r.w_up[:, cols]
        r.up_mid[p.y, pl.ds(pl.multiple_of(p.x * rows_up, rows_up), rows_up), :] = r.up_out[0]
        plane_up.start()

    rows_up = r.w_up.shape[0]
    plane_up = Plane(
        p,
        lambda q: r.up_out.at[q],
        lambda q: r.up_mid.at[p.y, pl.ds(pl.multiple_of(p.x * rows_up, rows_up), rows_up)],
        r.up_sems.at[0],
        r.up_sems.at[1],
    )
    plane_cot = Plane(p, lambda q: r.cot, lambda q: r.cot_all.at[q], r.cot_sems.at[0], r.cot_sems.at[1])
    line_up = LineGather(p, r.up_mid, lambda z, c: r.up_here.at[z, :, c], r.line_sems.at[0], r.line_sems.at[1])
    line_down = LineGather(p, r.w_down, lambda z, c: r.down_here.at[z, c], r.line_sems.at[2], r.line_sems.at[3])
    lines = (line_up, line_down)
    own_up = pltpu.make_async_copy(r.up_mid, r.up_here.at[p.z, :, p.c], r.own_sems.at[3])
    own_down = pltpu.make_async_copy(r.w_down, r.down_here.at[p.z, p.c], r.own_sems.at[4])
    own_cot = pltpu.make_async_copy(r.cot, r.cot_all.at[0], r.own_sems.at[5])
    share_joined = QuadRows(p, 1, r.joined, r.xjoined, r.row_sems.at[0])
    share_normed = QuadRows(p, 0, r.normed, r.xnormed, r.row_sems.at[1])

    def lines_own():
        plane_up.arrived()
        own_up.start()
        for line in lines:
            line.own()

    queries = Exchange(p, count, r.queries_in, r.got_queries, r.s1, r.r1, r.o1)
    there = Exchange(p, count, r.heads_in, r.got, r.s3, r.r3, r.o3)
    back = Exchange(p, count, r.mixed_out, r.mixed, r.s2, r.r2, r.o2)

    def products():
        ask.wait_recv()
        both = r.own_time[...] + r.got_time[...]
        r.times[...] = both
        left = both[:, : r.w_mod.shape[0]].astype(bf)
        row = lax.broadcasted_iota(jnp.int32, (8, model), 0) % 4
        total = jnp.zeros((8, model), jnp.float32)
        for part in range(4):
            made = jnp.dot(
                left, r.w_mod[:, part * model : (part + 1) * model], preferred_element_type=jnp.float32
            )
            total = jnp.where(row == part, made, total)
        r.mods_part[0] = total
        small.one(0, r.mods_part.at[0], r.mods_got.at[0], p.to_core).start()

    def bias_tile():
        each = r.b_skip.shape[1]
        r.pack[...] = jnp.zeros((8, 128), jnp.float32)
        r.pack[0:1, :] = r.b_up_part[...].astype(jnp.float32)
        r.pack[1:2, :each] = r.b_skip[...].astype(jnp.float32)
        r.pack[1:2, each : 2 * each] = r.b_down_part[...].astype(jnp.float32)

    small = Rounds(p, r.small_sems.at[0], r.small_sems.at[1])

    def small_line(d):
        return small.one(d, r.mods_part.at[1], r.mods_got.at[d], small.line(0, d))

    def after_core():
        small.one(0, r.mods_part.at[0], r.mods_got.at[0], p.to_core).wait_recv()
        r.mods_part[1] = r.mods_part[0] + r.mods_got[0]
        for d in range(1, depth):
            small_line(d).start()

    def after_line():
        total = r.mods_part[1]
        for d in range(1, depth):
            small_line(d).wait_recv()
            total = total + r.mods_got[d]
        r.mods_part[2] = total
        small.one(4, r.mods_part.at[2], r.mods_got.at[4], p.to_y).start()

    def after_y():
        small.one(4, r.mods_part.at[2], r.mods_got.at[4], p.to_y).wait_recv()
        r.mods_part[3] = r.mods_part[2] + r.mods_got[4]
        small.one(5, r.mods_part.at[3], r.mods_got.at[5], p.to_x).start()

    def turned_inputs():
        half = depth // 2
        for k, ref in enumerate((r.hidden, r.skip_in)):
            r.joined[k * half : (k + 1) * half] = ref[...].T.reshape(half, *r.joined.shape[1:])

    def keep_skip():
        return pltpu.make_async_copy(r.skip_here, r.skip_full, r.load_sems.at[0])

    def keep_qkv():
        return pltpu.make_async_copy(r.qkv_here, r.qkv_full, r.load_sems.at[1])

    own_copies = []

    def complete(name):
        for g in groups[name]:
            g.shared()

    def first_norm():
        own_copies[0].wait()
        complete("skip")
        at = pl.multiple_of(p.shard(p.z, p.y, p.c, p.x) * 8, 8)
        r.pack_full[pl.ds(at, 8), :] = r.pack[...]
        packs.shared()
        small.one(5, r.mods_part.at[3], r.mods_got.at[5], p.to_x).wait_recv()
        total = r.mods_part[3] + r.mods_got[5]
        mods = jnp.where(p.x == 0, total[0:4], total[4:8])
        r.mods[0:4, :] = mods
        r.mods[4:8, :] = mods
        each = model // devices
        tiles = [r.pack_full[k * 8 : k * 8 + 2, :] for k in range(devices)]
        for z in range(depth):
            for c in range(2):
                at = pl.multiple_of(p.shard(z, p.y, c, p.x) * 8, 8)
                here = (z * 2 + c) * 128
                r.b_up[:, here : here + 128] = r.pack_full[pl.ds(at, 8), :][0:1]
        b_skip = jnp.concatenate([t[1:2, :each] for t in tiles], 1)
        r.b_down[...] = jnp.concatenate([t[1:2, each : 2 * each] for t in tiles], 1)
        length = r.lengths[p.x]
        kept = (p.b * frames + lax.broadcasted_iota(jnp.int32, (frames, 1), 0) < length).astype(jnp.float32)
        base = jnp.dot(r.hidden[...], r.skip_here[:model, :], preferred_element_type=jnp.float32)
        base = base + jnp.dot(r.skip_in[...], r.skip_here[model:, :], preferred_element_type=jnp.float32) + b_skip
        r.base[...] = base
        hat, _ = normal(base)
        normed = (hat * (1.0 + kept * mods[0:1]) + kept * mods[1:2]).astype(bf)
        r.normed[...] = normed.T.reshape(r.normed.shape)
        r.normed_here[...] = normed

    def projections():
        own_copies[1].wait()
        complete("qkv")
        share_normed.start()
        normed = r.normed_here[...]
        cosine, sine = r.cosine[...][None], r.sine[...][None]
        for part in (1, 2, 0):
            made = jnp.dot(
                normed, r.qkv_here[:, part * model : (part + 1) * model], preferred_element_type=jnp.float32
            )
            made = made.T.reshape(HEADS, HEAD_DIM, frames)
            if part < 2:
                made = turn(made, cosine, sine)
            if part == 0:
                r.queries_in[...] = made.astype(bf)
                queries.start()
                keep_skip().start()
                keep_qkv().start()
            else:
                r.heads_in[:, (part - 1) * HEAD_DIM : part * HEAD_DIM, :] = made.astype(bf)
            if part == 2:
                there.start()

    def attention(lo, hi):
        attend(p, r.lengths, queries, r.qkv, r.keys, r.values, back, r.lse, r.plain, lo, hi)

    blocks = count // 2

    def first_half():
        there.arrived()
        attend_open(p, r.lengths, r.got, r.qkv, r.keys, r.values)
        attention(0, blocks // 2)

    def second_half():
        attention(blocks // 2, blocks)

    events = []
    for k, name in enumerate(("skip", "qkv")):
        events += [(t + 1.5 * k, k, f) for g in groups[name] for t, f in g.steps()]
    events.append((0.3, 0, products))
    events.append((0.31, 0, bias_tile))
    events.append((0.35, 0, turned_inputs))
    events.append((0.36, 0, spread_up))
    events.append((0.9, 0, after_core))
    events.append((2.05, 9, after_line))
    events.append((3.05, 9, after_y))
    events += [(t + 0.5, 9, f) for t, f in packs.steps()]
    events.append((3.2, 5, lines_own))
    for g in groups["out"]:
        times = {0: 3.25, 1: 5.56, 2: 7.0, 3: 7.16, 4: 8.73, 5: 9.45}
        events += [(times[t], 2, f) for t, f in g.steps()]
    for k, line in enumerate(lines):
        events.append((5.55, 5 + k, functools.partial(line.line, 1)))
        events.append((7.15, 5 + k, functools.partial(line.line, 2)))
        events.append((8.72, 5 + k, functools.partial(line.line, 3)))
    events.append((5.6, 0, first_norm))
    events.append((5.65, 0, plane_cot.start))
    events.append((5.66, 0, share_joined.start))
    events.append((7.1, 0, projections))
    events.append((8.4, 0, first_half))
    events.append((9.4, 0, second_half))
    events.sort(key=lambda e: (e[0], e[1]))
    own_down.start()
    own_cot.start()
    own_copies += keep_own(p, owns, r.own_sems)
    play([f for _, _, f in events])
    complete("out")
    for line in lines:
        line.shared()
        line.sent()
    for group in groups.values():
        for g in group:
            g.sent()
    packs.sent()
    for one in (plane_up, there, queries):
        one.finish()
    plane_cot.arrived()
    plane_cot.finish()
    for share in (share_joined, share_normed):
        share.arrived()
        share.finish()
    back.arrived()
    back.finish()
    for copy in (own_copies[2], own_up, own_down, own_cot, keep_skip(), keep_qkv()):
        copy.wait()
    ask.wait_send()
    small.one(0, r.mods_part.at[0], r.mods_got.at[0], p.to_core).wait_send()
    for d in range(1, depth):
        small_line(d).wait_send()
    small.one(4, r.mods_part.at[2], r.mods_got.at[4], p.to_y).wait_send()
    small.one(5, r.mods_part.at[3], r.mods_got.at[5], p.to_x).wait_send()


def front_call(depth, devices, args):
    cuts = dict(skip=8, qkv=8, out=0)
    frames, model = args["hidden"].shape
    bf, f32 = jnp.bfloat16, jnp.float32
    count = devices // 2
    total = count * frames
    shape = jax.ShapeDtypeStruct
    vmem = pl.BlockSpec(memory_space=pltpu.VMEM)
    away = pl.BlockSpec(memory_space=pl.ANY)

    def whole(name):
        rows, cols = args[name].shape
        return shape((devices * rows, cols), bf)

    def by_owner(n):
        return (depth, 2, 2, 2, n // devices, frames)

    def quarter(n):
        return (4, depth, 2, n // devices, frames)

    units = 2 * depth * 128
    rows_up = args["w_up"].shape[0]
    far = dict(
        skip_full=whole("w_skip"),
        qkv_full=whole("w_qkv"),
        out_full=whole("w_out"),
        up_here=shape((depth, 2, 2, 2 * rows_up, units), bf),
        down_here=shape((depth, 2, 128, model), bf),
        cot_all=shape((4, frames, model), bf),
        xjoined=shape(quarter(2 * model), bf),
        xnormed=shape(quarter(model), bf),
        mixed=shape((count, HEAD_DIM, frames), bf),
    )
    half = HEAD_DIM // 2
    near = dict(
        cosine=shape((half, frames), f32),
        sine=shape((half, frames), f32),
        times=shape((8, 128), f32),
        mods=shape((8, model), f32),
        b_up=shape((1, units), f32),
        b_down=shape((1, model), f32),
        base=shape((frames, model), f32),
        qkv=shape((3 * HEAD_DIM, total), bf),
        lse=shape((1, total), f32),
        plain=shape((HEAD_DIM, total), f32),
    )
    dma = pltpu.SemaphoreType.DMA
    gathers = 6
    scratch = dict(
        own_time=pltpu.VMEM((8, 128), f32),
        other_time=pltpu.VMEM((8, 128), f32),
        got_time=pltpu.VMEM((8, 128), f32),
        pack=pltpu.VMEM((8, 128), f32),
        pack_full=pltpu.VMEM((devices * 8, 128), f32),
        mods_part=pltpu.VMEM((4, 8, model), f32),
        mods_got=pltpu.VMEM((6, 8, model), f32),
        small_sems=dma((2, 6)),
        skip_here=pltpu.VMEM((2 * model, model), bf),
        qkv_here=pltpu.VMEM((model, 3 * model), bf),
        joined=pltpu.VMEM(by_owner(2 * model), bf),
        normed=pltpu.VMEM(by_owner(model), bf),
        normed_here=pltpu.VMEM((frames, model), bf),
        up_out=pltpu.VMEM((4, rows_up, units), bf),
        up_mid=pltpu.VMEM((2, 2 * rows_up, units), bf),
        queries_in=pltpu.VMEM((count, HEAD_DIM, frames), bf),
        got_queries=pltpu.VMEM((count, HEAD_DIM, frames), bf),
        heads_in=pltpu.VMEM((count, 2 * HEAD_DIM, frames), bf),
        got=pltpu.VMEM((count, 2 * HEAD_DIM, frames), bf),
        keys=pltpu.VMEM((total, 2 * HEAD_DIM), bf),
        values=pltpu.VMEM((HEAD_DIM + 16, total), bf),
        mixed_out=pltpu.VMEM((count, HEAD_DIM, frames), bf),
        time_sems=dma((2,)),
        load_sems=dma((2,)),
        own_sems=dma((6,)),
        up_sems=dma((2, 4)),
        cot_sems=dma((2, 4)),
        line_sems=dma((4, 16)),
        row_sems=dma((2, 7)),
        sends=dma((gathers, Gather.SENDS)),
        recvs=dma((gathers, Gather.RECVS)),
        s1=dma((count,)),
        r1=dma((count,)),
        o1=dma,
        s2=dma((count,)),
        r2=dma((count,)),
        o2=dma,
        s3=dma((count,)),
        r3=dma((count,)),
        o3=dma,
    )
    names = [*args, *far, *near, *scratch]
    made = pl.pallas_call(
        functools.partial(front_kernel, depth, cuts, names),
        name="front",
        out_shape=[*far.values(), *near.values()],
        in_specs=[pl.BlockSpec(memory_space=pltpu.SMEM)] + [vmem] * (len(args) - 1),
        out_specs=[away] * len(far) + [vmem] * len(near),
        scratch_shapes=list(scratch.values()),
        compiler_params=kernel_params(1),
    )(*args.values())
    return dict(zip([*far, *near], made))


def write_kernel(count, times, sums, joined, *refs):
    ins, outs = refs[:count], refs[count:]
    for src, dst in zip(ins, outs):
        dst[...] = src[...]
    hidden_grad, skip_grad, time_grad, b_up, b_skip, b_down = outs[count:]
    hidden_grad[...] = joined[0]
    skip_grad[...] = joined[1]
    each = b_skip.shape[1]
    part = jnp.where(lax.axis_index("uly") == 0, times[:, 0, :each], times[:, 1, :each])
    time_grad[...] = jnp.concatenate([part[k : k + 1] for k in range(times.shape[0])], 1)
    b_up[...] = sums[0:1, :]
    b_down[...] = sums[1:2, :each]
    b_skip[...] = sums[1:2, each : 2 * each]


def write_call(made, names, each):
    shape = jax.ShapeDtypeStruct
    joined = made["joined_grad"]
    frames, model = joined.shape[1:]
    plain = [shape(made[name].shape, made[name].dtype) for name in names]
    return pl.pallas_call(
        functools.partial(write_kernel, len(names)),
        name="write",
        out_shape=plain
        + [shape((frames, model), joined.dtype)] * 2
        + [shape((1, model), jnp.float32), shape((1, 128), jnp.float32)]
        + [shape((1, each), jnp.float32)] * 2,
        in_specs=in_vmem(3 + len(names)),
        out_specs=in_vmem(6 + len(names)),
        compiler_params=pltpu.CompilerParams(vmem_limit_bytes=VMEM_BYTES),
    )(made["times_full"], made["sums_out"], joined, *[made[name] for name in names])


def first_with_second(left, right, dims):
    return lax.dot_general(left, right, ((dims[:1], dims[1:]), ((), ())), preferred_element_type=jnp.float32)


def turn(values, cosine, sine):
    half = HEAD_DIM // 2
    first, second = values[..., :half, :], values[..., half:, :]
    return jnp.concatenate([first * cosine - second * sine, second * cosine + first * sine], -2)


def on_device(hidden, skip_in, time_embed, lengths, cotangent, w_skip, b_skip, w_mod, w_qkv, w_out, w_up, b_up,
              w_down, b_down):
    blocks, rows = lax.axis_size("blk"), lax.axis_size("uly")
    devices, depth = blocks * rows, blocks // 4
    _, frames, model = hidden.shape
    front = front_call(
        depth,
        devices,
        dict(
            lengths=lengths[:, 0],
            time_row=time_embed[0],
            b_skip=b_skip[None],
            b_up_part=b_up[None],
            b_down_part=b_down[None],
            cot=cotangent[0],
            w_mod=w_mod,
            hidden=hidden[0],
            skip_in=skip_in[0],
            w_skip=w_skip,
            w_qkv=w_qkv,
            w_out=w_out,
            w_up=w_up,
            w_down=w_down,
        ),
    )
    made = back_call(
        depth,
        devices,
        dict(
            lengths=lengths[:, 0],
            base=front["base"],
            mods=front["mods"],
            b_up=front["b_up"],
            b_down=front["b_down"],
            cosine=front["cosine"],
            sine=front["sine"],
            w_mod=w_mod,
            times=front["times"],
            qkv_far=front["qkv"],
            lse=front["lse"],
            plain_far=front["plain"],
            cot_far=front["cot_all"],
            mixed=front["mixed"].reshape(depth, 2, 2, 2, model // devices, frames),
            xjoined_far=front["xjoined"],
            xnormed_far=front["xnormed"],
            w_out=front["out_full"],
            w_up=front["up_here"].reshape(model, -1),
            w_down=front["down_here"].reshape(-1, model),
            w_qkv=front["qkv_full"],
            w_skip=front["skip_full"],
        ),
    )
    names = ["output", "skip_grad", "mod_grad", "qkv_grad", "out_grad", "up_grad", "down_grad"]
    output, skip_grad, mod_grad, qkv_grad, out_grad, up_grad, down_grad, *small = write_call(
        made, names, b_skip.shape[0]
    )
    hidden_grad, skip_in_grad, time_grad, b_up_grad, b_skip_grad, b_down_grad = small
    return (
        output[None],
        hidden_grad[None],
        skip_in_grad[None],
        time_grad[None],
        skip_grad,
        b_skip_grad[0],
        mod_grad,
        qkv_grad,
        out_grad,
        up_grad,
        b_up_grad[0],
        down_grad,
        b_down_grad[0],
    )


def solution(mesh):
    placed = (
        P("uly", "blk", None),
        P("uly", "blk", None),
        P("uly", None, None),
        P(),
        P("uly", "blk", None),
        P(("blk", "uly"), None),
        P(("blk", "uly")),
        P(("blk", "uly"), None),
        P(("blk", "uly"), None),
        P(("blk", "uly"), None),
        P(("blk", "uly"), None),
        P(("blk", "uly")),
        P(("blk", "uly"), None),
        P(("blk", "uly")),
    )
    blocks = mesh.shape["blk"]
    special = mesh.shape["uly"] == 2 and blocks == HEADS and blocks % 4 == 0 and blocks > 4
    return jax.shard_map(
        on_device if special else per_device,
        mesh=mesh,
        in_specs=placed,
        out_specs=(
            P("uly", "blk", None),
            P("uly", "blk", None),
            P("uly", "blk", None),
            P("uly", None, None),
            P(("blk", "uly"), None),
            P(("blk", "uly")),
            P(("blk", "uly"), None),
            P(("blk", "uly"), None),
            P(("blk", "uly"), None),
            P(("blk", "uly"), None),
            P(("blk", "uly")),
            P(("blk", "uly"), None),
            P(("blk", "uly")),
        ),
        check_vma=False,
    )
```

```python
import functools
import math

import jax
import jax.numpy as jnp
from jax import lax
from jax.experimental import pallas as pl
from jax.experimental.pallas import tpu as pltpu
from jax.sharding import PartitionSpec as P

HEADS = 16
HEAD_DIM = 64


exact_mode = lax.Precision.HIGHEST
epsilon = 1e-05


def passed_along(x, axis, by):
    devices = lax.axis_size(axis)
    return lax.ppermute(x, axis, [(i, (i + by) % devices) for i in range(devices)])


def segment_info(len_row, positions):
    slots = len_row.shape[0]
    ends = jnp.cumsum(len_row)
    starts = ends - len_row
    total = ends[-1]
    seg_ids = jnp.sum((positions[:, None] >= ends[None, :]).astype(jnp.int32), axis=1)
    onehot = seg_ids[:, None] == jnp.arange(slots, dtype=jnp.int32)[None, :]
    begin = jnp.sum(jnp.where(onehot, starts[None, :], 0), axis=1)
    begin = begin + jnp.where(seg_ids == slots, total, 0)
    return (seg_ids, positions - begin, seg_ids < slots)


def rotary(values, offsets):
    half = values.shape[-1] // 2
    freq = 10000.0 ** (-jnp.arange(half, dtype=jnp.float32) / half)
    angle = offsets.astype(jnp.float32)[:, None] * freq[None, :]
    cosine = jnp.cos(angle)[:, None, :]
    sine = jnp.sin(angle)[:, None, :]
    first = values[..., :half]
    second = values[..., half:]
    return jnp.concatenate([first * cosine - second * sine, second * cosine + first * sine], -1)


def modulate(values, scale, shift):
    center = values - jnp.mean(values, -1, keepdims=True)
    spread = jnp.mean(center * center, -1, keepdims=True)
    return center * lax.rsqrt(spread + epsilon) * (1.0 + scale) + shift


def contract_rows(left, right):
    return lax.dot_general(
        left, right, (((0,), (0,)), ((), ())), preferred_element_type=jnp.float32
    )


def contract_cols(left, right):
    return lax.dot_general(
        left, right, (((1,), (1,)), ((), ())), preferred_element_type=jnp.float32
    )


def gelu_exact(values):
    return jax.nn.gelu(values, approximate=False)


def per_device(
    hidden,
    skip_in,
    time_embed,
    lengths,
    cotangent,
    w_skip,
    b_skip,
    w_mod,
    w_qkv,
    w_out,
    w_up,
    b_up,
    w_down,
    b_down,
):
    gathered = (
        lax.all_gather(w_skip, ("blk", "uly"), axis=0, tiled=True),
        lax.all_gather(b_skip, ("blk", "uly"), axis=0, tiled=True),
        lax.all_gather(w_mod, ("blk", "uly"), axis=0, tiled=True),
        lax.all_gather(w_qkv, ("blk", "uly"), axis=0, tiled=True),
        lax.all_gather(w_out, ("blk", "uly"), axis=0, tiled=True),
        lax.all_gather(w_up, ("blk", "uly"), axis=0, tiled=True),
        lax.all_gather(b_up, ("blk", "uly"), axis=0, tiled=True),
        lax.all_gather(w_down, ("blk", "uly"), axis=0, tiled=True),
        lax.all_gather(b_down, ("blk", "uly"), axis=0, tiled=True),
    )
    (
        skip_full,
        bskip_full,
        mod_full,
        qkv_full,
        out_full,
        up_full,
        bup_full,
        down_full,
        bdown_full,
    ) = gathered
    group_count = lax.axis_size("uly")
    cycle_size = lax.axis_size("blk")
    frame_count = hidden.shape[1]
    row_count = lengths.shape[0]
    slot_count = lengths.shape[1]
    local_heads = HEADS // group_count
    span = local_heads * HEAD_DIM
    scaling = HEAD_DIM ** (-0.5)
    block_index = lax.axis_index("blk")
    row_index = lax.axis_index("uly")
    frame_pos = block_index * frame_count + jnp.arange(frame_count, dtype=jnp.int32)
    all_seg, all_offsets, all_valid = jax.vmap(lambda len_row: segment_info(len_row, frame_pos))(
        lengths
    )
    own_seg = lax.dynamic_index_in_dim(all_seg, row_index, 0, keepdims=False)
    own_offsets = lax.dynamic_index_in_dim(all_offsets, row_index, 0, keepdims=False)
    joined = jnp.concatenate([hidden[0], skip_in[0]], 1)
    base = jnp.dot(joined, skip_full, preferred_element_type=jnp.float32) + bskip_full.astype(
        jnp.float32
    )
    time_row = time_embed[0]
    mods = jnp.dot(time_row, mod_full, preferred_element_type=jnp.float32)
    selector = (own_seg[:, None] == jnp.arange(slot_count, dtype=jnp.int32)[None, :]).astype(
        jnp.float32
    )
    frame_mod = jnp.dot(selector, mods, precision=exact_mode)
    a_scale, a_shift, f_scale, f_shift = jnp.split(frame_mod, 4, 1)
    normed_full, norm_back = jax.vjp(modulate, base, a_scale, a_shift)
    normed = normed_full.astype(jnp.bfloat16)
    projected = jnp.dot(normed, qkv_full, preferred_element_type=jnp.float32).reshape(
        frame_count, 3, HEADS, HEAD_DIM
    )

    def place(parts):
        return jnp.stack(
            [rotary(parts[:, 0], own_offsets), rotary(parts[:, 1], own_offsets), parts[:, 2]], 1
        )

    turned, unturn = jax.vjp(place, projected)
    sending = turned.astype(jnp.bfloat16).reshape(1, frame_count, 3, group_count, span)
    head_data = lax.all_to_all(sending, "uly", split_axis=3, concat_axis=0, tiled=True)
    query = head_data[:, :, 0, 0].reshape(row_count, frame_count, local_heads, HEAD_DIM)
    kv_pairs = head_data[:, :, 1:, 0]

    def key_segments(start, count):
        key_pos = start + jnp.arange(count, dtype=jnp.int32)
        return jax.vmap(lambda len_row: segment_info(len_row, key_pos)[0])(lengths)

    start_state = (
        jnp.full((row_count, local_heads, frame_count), -1e30, jnp.float32),
        jnp.zeros((row_count, local_heads, frame_count), jnp.float32),
        jnp.zeros((row_count, frame_count, local_heads, HEAD_DIM), jnp.float32),
    )
    piece = lax.all_gather(kv_pairs, "blk", axis=1, tiled=True)
    total = piece.shape[1]
    step = math.gcd(total, max(frame_count, 1024))

    def sub_step(step_index, state):
        run_max, run_total, run_acc = state
        offset = step_index * step
        section = lax.dynamic_slice_in_dim(piece, offset, step, 1)
        key_seg = key_segments(offset, step)
        key_part = section[:, :, 0].reshape(row_count, step, local_heads, HEAD_DIM)
        value_part = section[:, :, 1].reshape(row_count, step, local_heads, HEAD_DIM)
        mask = all_seg[:, None, :, None] == key_seg[:, None, None, :]
        score = (
            jnp.einsum("rqhd,rkhd->rhqk", query, key_part, preferred_element_type=jnp.float32)
            * scaling
        )
        masked = jnp.where(mask, score, -1e30)
        fresh = jnp.maximum(run_max, jnp.max(masked, -1))
        weights = jnp.where(mask, jnp.exp(masked - fresh[..., None]), 0.0)
        decay = jnp.exp(run_max - fresh)
        run_total = run_total * decay + jnp.sum(weights, -1)
        run_acc = run_acc * jnp.swapaxes(decay, 1, 2)[..., None] + jnp.einsum(
            "rhqk,rkhd->rqhd",
            weights.astype(jnp.bfloat16),
            value_part,
            preferred_element_type=jnp.float32,
        )
        return (fresh, run_total, run_acc)

    run_max, run_total, run_acc = lax.fori_loop(0, total // step, sub_step, start_state)
    attended = run_acc / jnp.swapaxes(run_total, 1, 2)[..., None]
    log_total = run_max + jnp.log(run_total)
    valid_half = all_valid.astype(jnp.bfloat16)[:, :, None, None]
    leaving = (attended * all_valid.astype(jnp.float32)[:, :, None, None]).astype(jnp.bfloat16)
    leaving = leaving.reshape(row_count, frame_count, 1, span)
    mixed = lax.all_to_all(leaving, "uly", split_axis=0, concat_axis=2, tiled=True).reshape(
        frame_count, HEADS * HEAD_DIM
    )
    branch = jnp.dot(mixed, out_full, preferred_element_type=jnp.float32)
    middle = base + branch
    normed2_full, norm2_back = jax.vjp(modulate, middle, f_scale, f_shift)
    normed2 = normed2_full.astype(jnp.bfloat16)
    inner = jnp.dot(normed2, up_full, preferred_element_type=jnp.float32) + bup_full.astype(
        jnp.float32
    )
    act_full, act_back = jax.vjp(gelu_exact, inner)
    act = act_full.astype(jnp.bfloat16)
    result = (
        middle
        + jnp.dot(act, down_full, preferred_element_type=jnp.float32)
        + bdown_full.astype(jnp.float32)
    )
    output = result.astype(jnp.bfloat16)[None]
    again = (
        lax.all_gather(w_skip, ("blk", "uly"), axis=0, tiled=True),
        lax.all_gather(w_mod, ("blk", "uly"), axis=0, tiled=True),
        lax.all_gather(w_qkv, ("blk", "uly"), axis=0, tiled=True),
        lax.all_gather(w_out, ("blk", "uly"), axis=0, tiled=True),
        lax.all_gather(w_up, ("blk", "uly"), axis=0, tiled=True),
        lax.all_gather(w_down, ("blk", "uly"), axis=0, tiled=True),
    )
    skip_back, mod_back, qkv_back, out_back, up_back, down_back = again
    upstream = cotangent[0]
    upstream_full = upstream.astype(jnp.float32)
    grad_down = contract_rows(act, upstream)
    grad_bdown = jnp.sum(upstream_full, 0)
    grad_act = contract_cols(upstream, down_back)
    grad_inner = act_back(grad_act)[0].astype(jnp.bfloat16)
    grad_up = contract_rows(normed2, grad_inner)
    grad_bup = jnp.sum(grad_inner.astype(jnp.float32), 0)
    grad_normed2 = contract_cols(grad_inner, up_back)
    grad_mid_norm, grad_fscale, grad_fshift = norm2_back(grad_normed2)
    grad_middle = upstream_full + grad_mid_norm
    grad_branch = grad_middle.astype(jnp.bfloat16)
    grad_out = contract_rows(mixed, grad_branch)
    grad_mixed = (
        contract_cols(grad_branch, out_back)
        .astype(jnp.bfloat16)
        .reshape(1, frame_count, group_count, span)
    )
    returning = lax.all_to_all(grad_mixed, "uly", split_axis=2, concat_axis=0, tiled=True)
    grad_attn = returning.reshape(row_count, frame_count, local_heads, HEAD_DIM) * valid_half
    delta_rows = jnp.swapaxes(jnp.sum(grad_attn.astype(jnp.float32) * attended, -1), 1, 2)

    def contribution(held_pairs, key_start):
        count = held_pairs.shape[1]
        key_seg = key_segments(key_start, count)
        key_part = held_pairs[:, :, 0].reshape(row_count, count, local_heads, HEAD_DIM)
        value_part = held_pairs[:, :, 1].reshape(row_count, count, local_heads, HEAD_DIM)
        mask = all_seg[:, None, :, None] == key_seg[:, None, None, :]
        score = (
            jnp.einsum("rqhd,rkhd->rhqk", query, key_part, preferred_element_type=jnp.float32)
            * scaling
        )
        weights = jnp.exp(jnp.where(mask, score - log_total[..., None], -1e30))
        grad_weights = jnp.einsum(
            "rqhd,rkhd->rhqk", grad_attn, value_part, preferred_element_type=jnp.float32
        )
        grad_score = (weights * (grad_weights - delta_rows[..., None])).astype(jnp.bfloat16)
        more_query = (
            jnp.einsum("rhqk,rkhd->rqhd", grad_score, key_part, preferred_element_type=jnp.float32)
            * scaling
        )
        more_key = (
            jnp.einsum("rhqk,rqhd->rkhd", grad_score, query, preferred_element_type=jnp.float32)
            * scaling
        )
        more_value = jnp.einsum(
            "rhqk,rqhd->rkhd",
            weights.astype(jnp.bfloat16),
            grad_attn,
            preferred_element_type=jnp.float32,
        )
        more_pairs = jnp.stack(
            [more_key.reshape(row_count, count, span), more_value.reshape(row_count, count, span)],
            2,
        )
        return (more_query, more_pairs)

    def pass_grads(held_grads):
        return passed_along(held_grads.astype(jnp.bfloat16), "blk", 1).astype(held_grads.dtype)

    def cycle_step(turn, state):
        held_pairs, held_grads, query_grad = state
        more_query, more_pairs = contribution(
            held_pairs, (block_index - turn) % cycle_size * frame_count
        )
        held_pairs = passed_along(held_pairs, "blk", 1)
        held_grads = pass_grads(held_grads + more_pairs)
        return (held_pairs, held_grads, query_grad + more_query)

    cycle_start = (
        kv_pairs,
        jnp.zeros((row_count, frame_count, 2, span), jnp.float32),
        jnp.zeros((row_count, frame_count, local_heads, HEAD_DIM), jnp.float32),
    )
    held_pairs, held_grads, query_grad = lax.fori_loop(0, cycle_size - 1, cycle_step, cycle_start)
    last_query, last_pairs = contribution(
        held_pairs, (block_index - (cycle_size - 1)) % cycle_size * frame_count
    )
    pair_grads = pass_grads(held_grads + last_pairs)
    query_grad = query_grad + last_query
    head_grads = jnp.concatenate(
        [
            query_grad.astype(jnp.bfloat16).reshape(row_count, frame_count, 1, span),
            pair_grads.astype(jnp.bfloat16),
        ],
        2,
    ).reshape(row_count, frame_count, 3, 1, span)
    frames_grad = lax.all_to_all(head_grads, "uly", split_axis=0, concat_axis=3, tiled=True)
    frames_grad = frames_grad.reshape(frame_count, 3, HEADS, HEAD_DIM).astype(jnp.float32)
    grad_projected = (
        unturn(frames_grad)[0].astype(jnp.bfloat16).reshape(frame_count, 3 * HEADS * HEAD_DIM)
    )
    grad_qkv = contract_rows(normed, grad_projected)
    grad_normed = contract_cols(grad_projected, qkv_back)
    grad_base_norm, grad_ascale, grad_ashift = norm_back(grad_normed)
    grad_base = (grad_middle + grad_base_norm).astype(jnp.bfloat16)
    grad_skip_w = contract_rows(joined, grad_base)
    grad_bskip = jnp.sum(grad_base.astype(jnp.float32), 0)
    grad_joined = contract_cols(grad_base, skip_back).astype(jnp.bfloat16)
    model_width = hidden.shape[2]
    hidden_grad = grad_joined[:, :model_width][None]
    skip_grad = grad_joined[:, model_width:][None]
    frame_mod_grad = jnp.concatenate([grad_ascale, grad_ashift, grad_fscale, grad_fshift], 1)
    slot_grad = lax.dot_general(
        selector, frame_mod_grad, (((0,), (0,)), ((), ())), precision=exact_mode
    )
    grad_mod = lax.dot_general(
        time_row.astype(jnp.float32), slot_grad, (((0,), (0,)), ((), ())), precision=exact_mode
    )
    slot_total = lax.psum(slot_grad, "blk")
    time_grad = lax.dot_general(
        slot_total, mod_back.astype(jnp.float32), (((1,), (1,)), ((), ())), precision=exact_mode
    )[None]
    owned = (
        lax.psum_scatter(grad_skip_w, ("blk", "uly"), scatter_dimension=0, tiled=True),
        lax.psum_scatter(grad_bskip, ("blk", "uly"), scatter_dimension=0, tiled=True),
        lax.psum_scatter(grad_mod, ("blk", "uly"), scatter_dimension=0, tiled=True),
        lax.psum_scatter(grad_qkv, ("blk", "uly"), scatter_dimension=0, tiled=True),
        lax.psum_scatter(grad_out, ("blk", "uly"), scatter_dimension=0, tiled=True),
        lax.psum_scatter(grad_up, ("blk", "uly"), scatter_dimension=0, tiled=True),
        lax.psum_scatter(grad_bup, ("blk", "uly"), scatter_dimension=0, tiled=True),
        lax.psum_scatter(grad_down, ("blk", "uly"), scatter_dimension=0, tiled=True),
        lax.psum_scatter(grad_bdown, ("blk", "uly"), scatter_dimension=0, tiled=True),
    )
    return (
        output,
        hidden_grad,
        skip_grad,
        time_grad,
        owned[0],
        owned[1],
        owned[2],
        owned[3],
        owned[4],
        owned[5],
        owned[6],
        owned[7],
        owned[8],
    )


MESH = pl.DeviceIdType.MESH


class Place:
    def __init__(self, depth):
        self.depth = depth
        self.b = lax.axis_index("blk")
        self.x = lax.axis_index("uly")
        self.z = self.b // 4
        self.y = (self.b // 2) % 2
        self.c = self.b % 2
        self.to_x = (self.b, 1 - self.x)
        self.to_y = (self.b + 2 - 4 * self.y, self.x)
        self.to_core = (self.b + 1 - 2 * self.c, self.x)
        self.to_far = (self.b + 3 - 4 * self.y - 2 * self.c, self.x)
        self.to_across = (self.b + 2 - 4 * self.y, 1 - self.x)
        self.to_far_x = (self.b + 1 - 2 * self.c, 1 - self.x)
        self.to_up = (self.b + 4, self.x)
        self.to_down = (self.b - 4, self.x)

    def shard(self, z, y, c, x):
        return ((z * 2 + y) * 2 + c) * 2 + x

    def greet(self):
        barrier = pltpu.get_barrier_semaphore()
        for to in (self.to_x, self.to_y, self.to_core, self.to_far):
            pl.semaphore_signal(barrier, inc=1, device_id=to, device_id_type=MESH)

        @pl.when(self.z < self.depth - 1)
        def _():
            pl.semaphore_signal(barrier, inc=1, device_id=self.to_up, device_id_type=MESH)

        @pl.when(self.z > 0)
        def _():
            pl.semaphore_signal(barrier, inc=1, device_id=self.to_down, device_id_type=MESH)

        top = self.depth - 1
        pl.semaphore_wait(barrier, 4 + (self.z + top - 1) // top + (2 * top - 1 - self.z) // top)


def remote(src, dst, send, recv, to):
    return pltpu.make_async_remote_copy(
        src_ref=src, dst_ref=dst, send_sem=send, recv_sem=recv, device_id=to, device_id_type=MESH
    )


class Gather:
    SENDS = 64
    RECVS = 48

    def __init__(self, place, src, dst, rows, lo, hi, split, plane_first, sends, recvs):
        self.p, self.src, self.dst, self.rows = place, src, dst, rows
        self.lo, self.hi, self.split, self.plane_first = lo, hi, split, plane_first
        self.sends, self.recvs = sends, recvs
        self.pending = []

    def part(self, z, y, c, x, half=None):
        base = self.p.shard(z, y, c, x) * self.rows
        rows = self.rows
        if half is not None:
            rows = rows // 2
            base = base + half * rows
        return self.dst.at[pl.ds(pl.multiple_of(base, rows), rows), pl.ds(self.lo, self.hi - self.lo)]

    def mine(self):
        return self.src.at[:, pl.ds(self.lo, self.hi - self.lo)]

    def go(self, when, src, dst, send, recv, to):
        def start():
            remote(src, dst, self.sends.at[send], self.recvs.at[recv], to).start()

        def finish():
            remote(src, dst, self.sends.at[send], self.recvs.at[recv], to).wait_send()

        if when is None:
            start()
            self.pending.append(finish)
        else:
            pl.when(when)(start)
            self.pending.append(lambda: pl.when(when)(finish))

    def got(self, dst, recv):
        remote(dst, dst, self.sends.at[0], self.recvs.at[recv], self.p.to_x).wait_recv()

    def share(self, when, src, z, y, x):
        slot = z * 4 + y * 2 + x
        self.go(when, src, self.part(z, y, self.p.c, x), slot, slot, self.p.to_core)

    def steps(self):
        return self.plane_steps() if self.plane_first else self.line_steps()

    def line_steps(self):
        p = self.p
        top = p.depth - 1

        def hand_on(when, src, z):
            whole = self.part(z, p.y, p.c, p.x)
            self.go(when, src, whole, 24 + z, 20 + z, p.to_x)
            self.go(when, src, whole, 28 + z, 24 + z, p.to_y)
            self.share(when, src, z, p.y, p.x)

        def own():
            src = self.mine()
            whole = self.part(p.z, p.y, p.c, p.x)
            self.go(p.z < top, src, whole, 16 + p.z, 16 + p.z, p.to_up)
            self.go(p.z > 0, src, whole, 20 + p.z, 16 + p.z, p.to_down)
            hand_on(None, src, p.z)

        def line(d):
            for side in (-1, 1):
                z = p.z + side * d
                here = (z >= 0) & (z <= top)
                whole = self.part(z, p.y, p.c, p.x)
                pl.when(here)(lambda: self.got(whole, 16 + z))
                if side < 0:
                    self.go(here & (p.z < top), whole, whole, 16 + z, 16 + z, p.to_up)
                else:
                    self.go(here & (p.z > 0), whole, whole, 20 + z, 16 + z, p.to_down)
                hand_on(here, whole, z)

        def origins(d):
            return [(None, p.z)] if d == 0 else [
                ((p.z + s * d >= 0) & (p.z + s * d <= top), p.z + s * d) for s in (-1, 1)
            ]

        def cond(when, f):
            f() if when is None else pl.when(when)(f)

        def cross(d):
            for when, z in origins(d):
                from_x = self.part(z, p.y, p.c, 1 - p.x)
                cond(when, lambda: self.got(from_x, 20 + z))
                self.share(when, from_x, z, p.y, 1 - p.x)
                if self.split:
                    part = self.part(z, p.y, p.c, 1 - p.x, 0)
                else:
                    part = from_x
                self.go(when, part, part, 32 + z, 28 + z, p.to_y)
                from_y = self.part(z, 1 - p.y, p.c, p.x)
                cond(when, lambda: self.got(from_y, 24 + z))
                self.share(when, from_y, z, 1 - p.y, p.x)
                if self.split:
                    part = self.part(z, 1 - p.y, p.c, p.x, 1)
                    self.go(when, part, part, 36 + z, 32 + z, p.to_x)

        def corner(d):
            for when, z in origins(d):
                whole = self.part(z, 1 - p.y, p.c, 1 - p.x)
                if self.split:
                    for half in (0, 1):
                        part = self.part(z, 1 - p.y, p.c, 1 - p.x, half)
                        cond(when, lambda: self.got(part, 28 + 4 * half + z))
                else:
                    cond(when, lambda: self.got(whole, 28 + z))
                self.share(when, whole, z, 1 - p.y, 1 - p.x)

        out = [(0, own)]
        for d in range(p.depth):
            if d:
                out.append((d, functools.partial(line, d)))
            out.append((d + 1, functools.partial(cross, d)))
            out.append((d + 2, functools.partial(corner, d)))
        return out

    def plane_steps(self):
        p = self.p
        top = p.depth - 1

        def along(when, src, z, y, x, up, down):
            slot = 20 + z * 4 + y * 2 + x
            whole = self.part(z, y, p.c, x)
            if up:
                w = p.z < top
                self.go(w if when is None else w & when, src, whole, slot, slot, p.to_up)
            if down:
                w = p.z > 0
                self.go(w if when is None else w & when, src, whole, slot + 16, slot, p.to_down)

        def own():
            src = self.mine()
            whole = self.part(p.z, p.y, p.c, p.x)
            self.go(None, src, whole, 16, 16, p.to_x)
            self.go(None, src, whole, 17, 17, p.to_y)
            along(None, src, p.z, p.y, p.x, True, True)
            self.share(None, src, p.z, p.y, p.x)

        def cross():
            from_x = self.part(p.z, p.y, p.c, 1 - p.x)
            self.got(from_x, 16)
            part = self.part(p.z, p.y, p.c, 1 - p.x, 0) if self.split else from_x
            self.go(None, part, part, 18, 18, p.to_y)
            along(None, from_x, p.z, p.y, 1 - p.x, True, True)
            self.share(None, from_x, p.z, p.y, 1 - p.x)
            from_y = self.part(p.z, 1 - p.y, p.c, p.x)
            self.got(from_y, 17)
            if self.split:
                part = self.part(p.z, 1 - p.y, p.c, p.x, 1)
                self.go(None, part, part, 19, 19, p.to_x)
            along(None, from_y, p.z, 1 - p.y, p.x, True, True)
            self.share(None, from_y, p.z, 1 - p.y, p.x)

        def corner():
            whole = self.part(p.z, 1 - p.y, p.c, 1 - p.x)
            if self.split:
                for half in (0, 1):
                    self.got(self.part(p.z, 1 - p.y, p.c, 1 - p.x, half), 18 + half)
            else:
                self.got(whole, 18)
            along(None, whole, p.z, 1 - p.y, 1 - p.x, True, True)
            self.share(None, whole, p.z, 1 - p.y, 1 - p.x)

        def line(d, k):
            y = p.y if k in (0, 1) else 1 - p.y
            x = p.x if k in (0, 2) else 1 - p.x
            for side in (-1, 1):
                z = p.z + side * d
                here = (z >= 0) & (z <= top)
                whole = self.part(z, y, p.c, x)
                pl.when(here)(lambda: self.got(whole, 20 + z * 4 + y * 2 + x))
                along(here, whole, z, y, x, side < 0, side > 0)
                self.share(here, whole, z, y, x)

        out = [(0, own), (1, cross), (2, corner)]
        for d in range(1, p.depth):
            for k in range(4):
                out.append((d + 0.1 + min(k, 2) * 0.9, functools.partial(line, d, k)))
        return out

    def shared(self):
        p = self.p
        for z in range(p.depth):
            for y in range(2):
                for x in range(2):
                    self.got(self.part(z, y, 1 - p.c, x), z * 4 + y * 2 + x)

    def sent(self):
        for wait in self.pending:
            wait()


class LineGather:
    def __init__(self, place, src, piece, sends, recvs):
        self.p, self.src, self.piece, self.sends, self.recvs = place, src, piece, sends, recvs
        self.pending = []

    def go(self, when, src, dst, send, recv, to):
        def start():
            remote(src, dst, self.sends.at[send], self.recvs.at[recv], to).start()

        def finish():
            remote(src, dst, self.sends.at[send], self.recvs.at[recv], to).wait_send()

        if when is None:
            start()
            self.pending.append(finish)
        else:
            pl.when(when)(start)
            self.pending.append(lambda: pl.when(when)(finish))

    def got(self, dst, recv):
        remote(dst, dst, self.sends.at[0], self.recvs.at[recv], self.p.to_x).wait_recv()

    def own(self):
        p, n = self.p, self.p.depth
        dst = self.piece(p.z, p.c)
        self.go(p.z < n - 1, self.src, dst, p.z, p.z, p.to_up)
        self.go(p.z > 0, self.src, dst, n + p.z, p.z, p.to_down)
        self.go(None, self.src, dst, 2 * n + p.z, n + p.z, p.to_core)

    def line(self, d):
        p, n = self.p, self.p.depth
        for side in (-1, 1):
            z = p.z + side * d
            here = (z >= 0) & (z <= n - 1)
            dst = self.piece(z, p.c)
            pl.when(here)(lambda: self.got(dst, z))
            if side < 0:
                self.go(here & (p.z < n - 1), dst, dst, z, z, p.to_up)
            else:
                self.go(here & (p.z > 0), dst, dst, n + z, z, p.to_down)
            self.go(here, dst, dst, 2 * n + z, n + z, p.to_core)

    def shared(self):
        n = self.p.depth
        for z in range(n):
            self.got(self.piece(z, 1 - self.p.c), n + z)

    def sent(self):
        for wait in self.pending:
            wait()


class Plane:
    def __init__(self, place, src, dst, sends, recvs):
        self.p, self.src, self.dst, self.sends, self.recvs = place, src, dst, sends, recvs

    def to(self, q):
        p = self.p
        return (p.b + (2 - 4 * p.y) * (q // 2), p.x + (1 - 2 * p.x) * (q % 2))

    def copy(self, q):
        return remote(self.src(q), self.dst(q), self.sends.at[q], self.recvs.at[q], self.to(q))

    def start(self):
        for q in (1, 2, 3):
            self.copy(q).start()

    def arrived(self):
        for q in (1, 2, 3):
            self.copy(q).wait_recv()

    def finish(self):
        for q in (1, 2, 3):
            self.copy(q).wait_send()


class Rounds:
    def __init__(self, place, sends, recvs):
        self.p, self.sends, self.recvs = place, sends, recvs

    def one(self, k, src, dst, to):
        return remote(src, dst, self.sends.at[k], self.recvs.at[k], to)

    def line(self, k, d):
        p = self.p
        z = (p.z + d) % p.depth
        return (p.b + 4 * (z - p.z), p.x)


class Octet:
    def __init__(self, place, src, dst, sends, recvs):
        self.p, self.src, self.dst, self.sends, self.recvs = place, src, dst, sends, recvs
        self.slot = place.y * 4 + place.c * 2 + place.x

    def copy(self, k):
        to = (self.slot + k) % 8
        device = (self.p.z * 4 + to // 2, to % 2)
        return remote(self.src(to), self.dst(self.slot), self.sends.at[k], self.recvs.at[k], device)

    def start(self):
        for k in range(1, 8):
            self.copy(k).start()

    def arrived(self):
        for k in range(1, 8):
            came = self.dst((self.slot + 8 - k) % 8)
            remote(came, came, self.sends.at[k], self.recvs.at[k], self.p.to_x).wait_recv()

    def finish(self):
        for k in range(1, 8):
            self.copy(k).wait_send()


class Quad:
    def __init__(self, p, axis, src, dst, sems):
        self.p, self.src, self.dst, self.sems = p, src, dst, sems
        self.to_pair = p.to_y if axis == 0 else p.to_x

    def to_core(self):
        return remote(self.src, self.dst(1), self.sems(0), self.sems(1), self.p.to_core)

    def to_next(self):
        return remote(self.src, self.dst(2), self.sems(2), self.sems(3), self.to_pair)

    def on(self):
        return remote(self.dst(2), self.dst(3), self.sems(4), self.sems(5), self.p.to_core)

    def start(self):
        self.to_next().start()
        self.to_core().start()

    def relay(self):
        self.to_next().wait_recv()
        self.on().start()

    def arrived(self):
        self.to_core().wait_recv()
        self.on().wait_recv()

    def finish(self):
        self.to_next().wait_send()
        self.to_core().wait_send()
        self.on().wait_send()


class QuadRows:
    def __init__(self, p, axis, src, dst, sems):
        self.p, self.axis, self.src, self.dst, self.sems = p, axis, src, dst, sems

    def mine(self, side, c):
        return self.src.at[:, side, c] if self.axis == 0 else self.src.at[:, :, c, side]

    def own(self):
        p = self.p
        side = p.y if self.axis == 0 else p.x
        return pltpu.make_async_copy(self.mine(side, p.c), self.dst.at[0], self.sems.at[0])

    def copy(self, k):
        p = self.p
        side = p.y if self.axis == 0 else p.x
        pair, far = (p.to_y, p.to_far) if self.axis == 0 else (p.to_x, p.to_far_x)
        side, c, to = ((side, 1 - p.c, p.to_core), (1 - side, p.c, pair), (1 - side, 1 - p.c, far))[k - 1]
        return remote(self.mine(side, c), self.dst.at[k], self.sems.at[2 * k - 1], self.sems.at[2 * k], to)

    def start(self):
        self.own().start()
        for k in (2, 3, 1):
            self.copy(k).start()

    def arrived(self):
        self.own().wait()
        for k in (1, 2, 3):
            self.copy(k).wait_recv()

    def finish(self):
        for k in (1, 2, 3):
            self.copy(k).wait_send()


class Reduce:
    CHUNK = 512

    def __init__(self, place, axis, x, take, rows, lo, width, out, full, outgo, income, sends, recvs):
        self.p, self.x, self.take, self.rows = place, x, take, rows
        self.side = place.x if axis == 0 else place.y
        self.to_other = place.to_x if axis == 0 else place.to_y
        self.lo, self.width, self.out = lo, width, out
        self.full, self.outgo, self.income = full, outgo, income
        self.sends, self.recvs = sends, recvs
        self.first = place.depth
        self.chunk = min(self.CHUNK, width)

    @staticmethod
    def scratch(rows, width, depth):
        return [
            pltpu.VMEM((2 * depth * rows, width), jnp.bfloat16),
            pltpu.VMEM(((2 * depth + 1) * rows, width), jnp.bfloat16),
            pltpu.SemaphoreType.DMA((4,)),
            pltpu.SemaphoreType.DMA((4,)),
        ]

    def part(self, ref, lo, hi):
        return ref.at[pl.ds(lo * self.rows, (hi - lo) * self.rows)]

    def across(self):
        n = self.p.depth
        return remote(
            self.part(self.outgo, 0, n), self.part(self.income, 0, n), self.sends.at[0], self.recvs.at[0], self.to_other
        )

    def up(self, lo):
        f, n = self.first, self.p.depth
        return remote(
            self.part(self.outgo, f + lo, f + n),
            self.part(self.income, f + lo, f + n),
            self.sends.at[1],
            self.recvs.at[1],
            self.p.to_up,
        )

    def down(self, hi):
        f = self.first
        return remote(
            self.part(self.outgo, f, f + hi),
            self.part(self.income, f, f + hi),
            self.sends.at[2],
            self.recvs.at[2],
            self.p.to_down,
        )

    def down_last(self, at):
        f, n = self.first, self.p.depth
        return remote(
            self.part(self.outgo, f + at, f + at + 1),
            self.part(self.income, f + n, f + n + 1),
            self.sends.at[3],
            self.recvs.at[3],
            self.p.to_down,
        )

    def columns(self, body):
        @pl.loop(0, self.width // self.chunk)
        def _(j):
            body(j, pl.ds(pl.multiple_of(j * self.chunk, self.chunk), self.chunk))

    def product(self, side, j):
        n, r = self.p.depth, self.rows
        x = jnp.concatenate([self.x[k, :, side].reshape(n * r, self.x.shape[4]) for k in range(4)], 1)
        return jnp.dot(x, self.take(self.lo // self.chunk + j), preferred_element_type=jnp.float32)

    def begin(self):
        p, n, r = self.p, self.p.depth, self.rows

        def away(j, here):
            self.outgo[pl.ds(0, n * r), here] = self.product(1 - self.side, j).astype(jnp.bfloat16)

        self.columns(away)
        self.across().start()

        def near(j, here):
            self.full[pl.ds(0, n * r), here] = self.product(self.side, j)

        self.columns(near)

        self.zeros()

    def zeros(self):
        p, f, n = self.p, self.first, self.p.depth

        @pl.when(p.z == 0)
        def _():
            ref = self.part(self.income, f, f + 1)
            ref[...] = jnp.zeros(ref.shape, ref.dtype)

        @pl.when(p.z == n - 1)
        def _():
            ref = self.part(self.income, f + n, f + n + 1)
            ref[...] = jnp.zeros(ref.shape, ref.dtype)

    def total(self, h, lo, hi):
        f, r = self.first, self.rows

        def body(j, here):
            rows = pl.ds(lo * r, (hi - lo) * r)
            line = pl.ds((f + lo) * r, (hi - lo) * r)
            total = self.full[rows, here]
            if f:
                total = total + self.income[rows, here].astype(jnp.float32)
            if h:
                total = total + self.income[line, here].astype(jnp.float32)
            self.outgo[line, here] = total.astype(jnp.bfloat16)

        self.columns(body)

    def hop(self, h):
        p, n = self.p, self.p.depth
        if h == 0 and self.first:
            self.across().wait_recv()

        @pl.when(p.z == h)
        def _():
            if h:
                self.up(h).wait_recv()
            self.total(h, h + 1, n)
            self.up(h + 1).start()

        @pl.when(p.z == n - 1 - h)
        def _():
            if h:
                self.down(n - 1 - h).wait_recv()
            self.total(h, 0, n - 1 - h)
            if h < n - 2:
                self.down(n - 2 - h).start()
            self.down_last(n - 2 - h).start()

    def last_waits(self):
        p, n = self.p, self.p.depth
        pl.when(p.z == n - 1)(lambda: self.up(n - 1).wait_recv())
        pl.when(p.z < n - 1)(lambda: self.down_last(0).wait_recv())

    def end(self):
        p, n, r = self.p, self.p.depth, self.rows
        self.last_waits()
        own = pl.ds(pl.multiple_of(p.z * r, r), r)
        line = pl.ds(pl.multiple_of((n + p.z) * r, r), r)

        def body(j, here):
            there = pl.ds(pl.multiple_of(self.lo + j * self.chunk, self.chunk), self.chunk)
            self.out[:, there] = (
                self.full[own, here]
                + self.income[own, here].astype(jnp.float32)
                + self.income[line, here].astype(jnp.float32)
                + self.income[pl.ds(2 * n * r, r), here].astype(jnp.float32)
            )

        self.columns(body)

    def finish(self):
        p, n = self.p, self.p.depth
        if self.first:
            self.across().wait_send()
        for h in range(n - 1):
            pl.when(p.z == h)(lambda: self.up(h + 1).wait_send())

            @pl.when(p.z == n - 1 - h)
            def _():
                if h < n - 2:
                    self.down(n - 2 - h).wait_send()
                self.down_last(n - 2 - h).wait_send()


class LineReduce(Reduce):
    def __init__(self, place, product, rows, width, full, outgo, income, sends, recvs):
        self.p, self.make, self.rows, self.width = place, product, rows, width
        self.full, self.outgo, self.income = full, outgo, income
        self.sends, self.recvs = sends, recvs
        self.first = 0
        self.chunk = min(self.CHUNK, width)

    @staticmethod
    def scratch(rows, width, depth):
        return [
            pltpu.VMEM((depth * rows, width), jnp.bfloat16),
            pltpu.VMEM(((depth + 1) * rows, width), jnp.bfloat16),
            pltpu.SemaphoreType.DMA((4,)),
            pltpu.SemaphoreType.DMA((4,)),
        ]

    def begin(self):
        def near(j, here):
            self.full[:, here] = self.make(j)

        self.columns(near)
        self.zeros()

    def end(self, write):
        self.last_waits()
        n, r = self.p.depth, self.rows
        own = pl.ds(pl.multiple_of(self.p.z * r, r), r)

        def body(j, here):
            write(
                here,
                self.full[own, here]
                + self.income[own, here].astype(jnp.float32)
                + self.income[pl.ds(n * r, r), here].astype(jnp.float32),
            )

        self.columns(body)


VMEM_BYTES = 62 * 2**20


def kernel_params(number):
    return pltpu.CompilerParams(collective_id=number, has_side_effects=True, vmem_limit_bytes=VMEM_BYTES)


def in_vmem(count):
    return [pl.BlockSpec(memory_space=pltpu.VMEM)] * count


def in_any(count):
    return [pl.BlockSpec(memory_space=pl.ANY)] * count


def ranges(cols, cut):
    return [(0, cut, True), (cut, cols, False)] if cut else [(0, cols, False)]


def keep_own(p, pairs, sems):
    copies = []
    for k, (src, dst, rows) in enumerate(pairs):
        at = pl.multiple_of(p.shard(p.z, p.y, p.c, p.x) * rows, rows)
        copies.append(pltpu.make_async_copy(src, dst.at[pl.ds(at, rows)], sems.at[k]))
    for copy in copies:
        copy.start()
    return copies


class Exchange:
    def __init__(self, place, count, src, dst, sends, recvs, own):
        self.p, self.count, self.src, self.dst = place, count, src, dst
        self.sends, self.recvs, self.own = sends, recvs, own

    def copy(self, k):
        to = (self.p.b + k) % self.count
        return remote(
            self.src.at[to], self.dst.at[self.p.b], self.sends.at[k], self.recvs.at[k], (to, self.p.x)
        )

    def mine(self):
        return pltpu.make_async_copy(self.src.at[self.p.b], self.dst.at[self.p.b], self.own)

    def start(self):
        self.mine().start()
        for k in range(1, self.count):
            self.copy(k).start()

    def send_to(self, device):
        k = (device + self.count - self.p.b) % self.count
        pl.when(k > 0)(lambda: self.copy(k).start())
        pl.when(k == 0)(lambda: self.mine().start())

    def wait_from(self, device):
        k = (self.p.b + self.count - device) % self.count

        @pl.when(k > 0)
        def _():
            came = self.dst.at[device]
            remote(came, came, self.sends.at[k], self.recvs.at[k], self.p.to_x).wait_recv()

        pl.when(k == 0)(lambda: self.mine().wait())

    def arrived(self):
        self.mine().wait()
        for k in range(1, self.count):
            came = (self.p.b + self.count - k) % self.count
            remote(
                self.dst.at[came], self.dst.at[came], self.sends.at[k], self.recvs.at[k], self.p.to_x
            ).wait_recv()

    def finish(self):
        for k in range(1, self.count):
            self.copy(k).wait_send()


def exchange_sems(count):
    return [
        pltpu.SemaphoreType.DMA((count,)),
        pltpu.SemaphoreType.DMA((count,)),
        pltpu.SemaphoreType.DMA,
    ]


def greet_plane(p, count, more):
    barrier = pltpu.get_barrier_semaphore()
    for to in more:
        pl.semaphore_signal(barrier, inc=1, device_id=to, device_id_type=MESH)
    for k in range(1, count):
        pl.semaphore_signal(barrier, inc=1, device_id=((p.b + k) % count, p.x), device_id_type=MESH)
    pl.semaphore_signal(barrier, inc=1, device_id=p.to_x, device_id_type=MESH)
    pl.semaphore_wait(barrier, count + len(more))


def play(events):
    for event in events:
        event()


def three_terms(v):
    a = v.astype(jnp.bfloat16).astype(jnp.float32)
    b = (v - a).astype(jnp.bfloat16).astype(jnp.float32)
    return a, b, v - a - b


def extra_rows(rows, length, width):
    shape = (length, width)
    row = lax.broadcasted_iota(jnp.int32, shape, 0)
    total = jnp.zeros(shape, jnp.float32)
    for k, values in enumerate(rows):
        total = jnp.where(row == k, values, total)
    return total.astype(jnp.bfloat16)


def attend_open(p, lengths, got_kv, qkv, keys, values):
    count, _, span = got_kv.shape
    frames = count * span
    for k in range(count):
        qkv[HEAD_DIM:, k * span : (k + 1) * span] = got_kv[k]
    position = lax.broadcasted_iota(jnp.int32, (1, frames), 1)
    hidden_key = jnp.where(position < lengths[p.x], 0.0, -1e30)
    keys[...] = jnp.concatenate([qkv[HEAD_DIM : 2 * HEAD_DIM, :], extra_rows([hidden_key], HEAD_DIM, frames)], 0).T
    values[...] = jnp.concatenate([qkv[2 * HEAD_DIM :, :], extra_rows([1.0], 16, frames)], 0)


def in_turn(p, i, blocks):
    return (p.b // 2 + blocks - i) % blocks


def attend(p, lengths, queries, qkv, keys, values, results, lse, plain, lo, hi):
    count, _, span = queries.dst.shape
    block = 2 * span
    length = lengths[p.x]
    ones = extra_rows([1.0], HEAD_DIM, block)
    scaling = HEAD_DIM ** (-0.5)

    @pl.loop(lo, hi)
    def _(i):
        j = in_turn(p, i, count // 2)
        here = pl.ds(pl.multiple_of(j * block, block), block)
        for k in range(2):
            queries.wait_from(2 * j + k)
        query = jnp.concatenate([queries.dst[2 * j], queries.dst[2 * j + 1]], 1)
        qkv[:HEAD_DIM, here] = query
        query = jnp.concatenate([query * jnp.bfloat16(scaling), ones], 0)
        score = jnp.dot(keys[...], query, preferred_element_type=jnp.float32)
        peak = jnp.max(score, 0, keepdims=True)
        weights = jnp.exp(score - peak).astype(jnp.bfloat16)
        out = jnp.dot(values[...], weights, preferred_element_type=jnp.float32)
        total = out[HEAD_DIM : HEAD_DIM + 1]
        out = out[:HEAD_DIM] / total
        plain[:, here] = out
        lse[:, here] = peak + jnp.log(total)
        column = lax.broadcasted_iota(jnp.int32, (HEAD_DIM, block), 1) + j * block
        kept = jnp.where(column < length, out, 0.0).astype(jnp.bfloat16)
        for k in range(2):
            results.src[2 * j + k] = kept[:, k * span : (k + 1) * span]
            results.send_to(2 * j + k)


def attend_back_open(p, lengths, qkv, keys, values, sums):
    frames = qkv.shape[1]
    length = lengths[p.x]
    position = lax.broadcasted_iota(jnp.int32, (1, frames), 1)
    hidden_key = jnp.where(position < length, 0.0, -1e30)
    keys[...] = jnp.concatenate(
        [qkv[HEAD_DIM : 2 * HEAD_DIM, :], extra_rows([hidden_key, 1.0, 1.0, 1.0], HEAD_DIM, frames)], 0
    ).T
    values[...] = jnp.concatenate(
        [qkv[2 * HEAD_DIM :, :], extra_rows([1.0, 1.0, 1.0], HEAD_DIM, frames)], 0
    ).T
    sums[...] = jnp.zeros_like(sums)


def attend_back(p, upstreams, qkv, lse, plain, keys, values, sums, results, lo, hi):
    count, _, span = upstreams.dst.shape
    block = 2 * span
    scaling = HEAD_DIM ** (-0.5)

    @pl.loop(lo, hi)
    def _(i):
        j = in_turn(p, i, count // 2)
        here = pl.ds(pl.multiple_of(j * block, block), block)
        for k in range(2):
            upstreams.wait_from(2 * j + k)
        query = qkv[:HEAD_DIM, here] * jnp.bfloat16(scaling)
        upstream = jnp.concatenate([upstreams.dst[2 * j], upstreams.dst[2 * j + 1]], 1)
        delta = jnp.sum(upstream.astype(jnp.float32) * plain[:, here], 0, keepdims=True)
        left = jnp.concatenate(
            [query, extra_rows([1.0, *[-t for t in three_terms(lse[:, here])]], HEAD_DIM, block)], 0
        )
        right = jnp.concatenate([upstream, extra_rows([-t for t in three_terms(delta)], HEAD_DIM, block)], 0)
        weights = jnp.exp(jnp.dot(keys[...], left, preferred_element_type=jnp.float32))
        slope = jnp.dot(values[...], right, preferred_element_type=jnp.float32)
        slope = (weights * slope).astype(jnp.bfloat16)
        query_grad = (
            jnp.dot(qkv[HEAD_DIM : 2 * HEAD_DIM, :], slope, preferred_element_type=jnp.float32) * scaling
        ).astype(jnp.bfloat16)
        for k in range(2):
            results.src[2 * j + k] = query_grad[:, k * span : (k + 1) * span]
            results.send_to(2 * j + k)
        sums[:, HEAD_DIM:] += lax.dot_general(
            weights.astype(jnp.bfloat16), upstream, (((1,), (1,)), ((), ())), preferred_element_type=jnp.float32
        )
        sums[:, :HEAD_DIM] += lax.dot_general(
            slope, query, (((1,), (1,)), ((), ())), preferred_element_type=jnp.float32
        )


def attend_back_close(sums, grads_out):
    count, _, span = grads_out.shape

    @pl.loop(0, count)
    def _(k):
        rows = pl.ds(pl.multiple_of(k * span, span), span)
        grads_out[k] = sums[rows, :].T.astype(jnp.bfloat16)


def others(p, count, k):
    number = (p.b * 2 + p.x + k) % (2 * count)
    return (number // 2, number % 2)


def nt(left, right):
    return lax.dot_general(left, right, (((1,), (1,)), ((), ())), preferred_element_type=jnp.float32)


def mean(v):
    return jnp.mean(v, -1, keepdims=True)


def normal(v):
    center = v - mean(v)
    rstd = lax.rsqrt(mean(center * center) + epsilon)
    return center * rstd, rstd


def normal_back(grad, hat, rstd, scale):
    gx = grad * (1.0 + scale)
    return rstd * (gx - mean(gx) - hat * mean(gx * hat))


def fold(v):
    width = v.shape[1] // 8
    return jnp.concatenate([v[:, k * width : (k + 1) * width] for k in range(8)], 0)


class Refs:
    def __init__(self, names, refs):
        for name, ref in zip(names, refs):
            setattr(self, name, ref)


def back_kernel(depth, shards, names, *refs):
    r = Refs(names, refs)
    rest = list(refs[len(names) :])
    p = Place(depth)
    count = 4 * depth
    devices = 2 * count
    frames, model = r.base.shape
    half = model // 2
    chunk = 512
    bf = jnp.bfloat16
    units = r.w_up.shape[1]

    barrier = pltpu.get_barrier_semaphore()
    for k in range(1, devices):
        pl.semaphore_signal(barrier, inc=1, device_id=others(p, count, k), device_id_type=MESH)

    def fetch(src, slot):
        return pltpu.make_async_copy(src, r.weights.at[slot], r.weight_sems.at[slot])

    def columns(ref, k):
        return ref.at[:, pl.ds(k * chunk, chunk)]

    def fetch_first(slot):
        return fetch(columns((r.w_out, r.w_up, r.w_down)[slot // 2], slot % 2), slot)

    def fetch_qkv(slot):
        return fetch(columns(r.w_qkv, slot), slot)

    def fetch_skip(slot):
        return fetch(r.w_skip.at[pl.ds((slot // 2) * model, model), pl.ds((slot % 2) * chunk, chunk)], slot)

    late_loads = [
        pltpu.make_async_copy(src, dst, r.load_sems.at[k])
        for k, (src, dst) in enumerate(
            ((r.cot_far, r.cot_all), (r.qkv_far, r.qkv), (r.plain_far, r.plain), (r.xnormed_far, r.xnormed),
             (r.xjoined_far, r.xjoined))
        )
    ]
    for slot in range(6):
        fetch_first(slot).start()
    for copy in late_loads:
        copy.start()
    pl.semaphore_wait(barrier, devices - 1)

    def to_sibling(src, dst, k):
        return remote(src, dst, r.pair_sems.at[0, k], r.pair_sems.at[1, k], p.to_core)

    pair_cot = to_sibling(r.cot_all, r.cot_sib, 0)
    pair_n2 = to_sibling(r.n2_all, r.n2_sib, 1)
    pair_act = to_sibling(r.act.at[1 - p.c], r.act_sib, 2)
    pair_gin = to_sibling(r.gin.at[1 - p.c], r.gin_sib, 3)
    plane_n2 = Plane(p, lambda q: r.n2_all.at[0], lambda q: r.n2_all.at[q], r.n2_sems.at[0], r.n2_sems.at[1])
    plane_back = Plane(
        p, lambda q: r.part_back.at[q - 1], lambda q: r.got_back.at[q - 1], r.back_sems.at[0], r.back_sems.at[1]
    )
    plane_total = Plane(
        p, lambda q: r.part_total.at[q - 1], lambda q: r.got_total.at[q - 1], r.total_sems.at[0], r.total_sems.at[1]
    )
    share_mixed = QuadRows(p, 0, r.mixed, r.xmix, r.row_sems.at[0])
    share_branch = Quad(p, 0, r.gbranch.at[0], lambda k: r.gbranch.at[k], lambda k: r.branch_sems.at[k])

    def share_late(c):
        return Quad(p, c // 6, r.glate.at[0, c], lambda k: r.glate.at[k, c], lambda k: r.late_sems.at[c, k])

    length = r.lengths[p.x]
    position = p.b * frames
    kept = (position + lax.broadcasted_iota(jnp.int32, (frames, 1), 0) < length).astype(jnp.float32)
    kept_row = (position + lax.broadcasted_iota(jnp.int32, (1, frames), 1) < length).astype(jnp.float32)
    a_scale = kept * r.mods[0:1, :]
    f_scale = kept * r.mods[2:3, :]
    f_shift = kept * r.mods[3:4, :]
    mixed = r.mixed[...].reshape(model, frames).T
    for k in range(2):
        fetch_first(k).wait()
        cols = pl.ds(k * chunk, chunk)
        r.middle[:, cols] = r.base[:, cols] + jnp.dot(mixed, r.weights[k], preferred_element_type=jnp.float32)
    hat, rstd = normal(r.middle[...])
    r.n2_all[0] = (hat * (1.0 + f_scale) + f_shift).astype(bf)
    plane_n2.start()
    r.bias[...] = jnp.zeros_like(r.bias)
    for slot in range(2, 6):
        fetch_first(slot).wait()
    for copy in late_loads:
        copy.wait()
    pair_cot.start()

    @pl.loop(0, 4)
    def _(q):
        pl.when(q > 0)(lambda: plane_n2.copy(q).wait_recv())
        acts, grads = [], []
        for u in range(2):
            cols = pl.ds(u * chunk, chunk)
            inner = jnp.dot(r.n2_all[q], r.weights[2 + u], preferred_element_type=jnp.float32) + r.b_up[:, cols]
            cdf = 0.5 * (1.0 + lax.erf(inner * (0.5**0.5)))
            act = (inner * cdf).astype(bf)
            slope = cdf + inner * (jnp.exp(-0.5 * inner * inner) * (1.0 / math.sqrt(2.0 * math.pi)))
            act_grad = nt(r.cot_all[q, :, :half], r.weights[4, cols, :]) + nt(
                r.cot_all[q, :, half:], r.weights[5, cols, :]
            )
            grad = (act_grad * slope).astype(bf)
            r.bias[:, cols] += jnp.sum(grad.astype(jnp.float32), 0, keepdims=True)
            for k in range(4):
                here = slice(k * 128, (k + 1) * 128)
                at = (2 * u + k // 2) * 128
                r.act[k % 2, q, :, at : at + 128] = act[:, here]
                r.gin[k % 2, q, :, at : at + 128] = grad[:, here]
            acts.append(act)
            grads.append(grad)
        back = nt(grads[0], r.weights[2]) + nt(grads[1], r.weights[3])

        @pl.when(q == 0)
        def _():
            r.back[...] = back

        @pl.when(q > 0)
        def _():
            r.part_back[q - 1] = back.astype(bf)
            plane_back.copy(q).start()

        for k in range(2):
            cols = slice(k * half, (k + 1) * half)
            total = jnp.dot(acts[0], r.weights[4 + k, :chunk, :], preferred_element_type=jnp.float32)
            total = total + jnp.dot(acts[1], r.weights[4 + k, chunk:, :], preferred_element_type=jnp.float32)

            @pl.when(q == 0)
            def _():
                r.own_total[:, cols] = total

            @pl.when(q > 0)
            def _():
                r.part_total[q - 1, :, cols] = total.astype(bf)

    def blocks_of(first):
        return lambda j: jnp.concatenate([r.glate[k, first + j] for k in range(4)], 0)

    def branch_columns(j):
        here = pl.ds(pl.multiple_of(j * chunk, chunk), chunk)
        return jnp.concatenate([r.gbranch[k, :, here] for k in range(4)], 0)

    def tn(left, right):
        return lax.dot_general(left, right, (((0,), (0,)), ((), ())), preferred_element_type=jnp.float32)

    def flat(v):
        return v.reshape(4 * frames, v.shape[2])

    def down_part(k):
        cols = slice(k * half, (k + 1) * half)

        def make(j):
            mine = tn(flat(r.act[p.c]), flat(r.cot_all[:, :, cols]))
            return mine + tn(flat(r.act_sib[...]), flat(r.cot_sib[:, :, cols]))

        return make

    def up_part(k):
        cols = slice(k * 256, (k + 1) * 256)

        def make(j):
            mine = tn(flat(r.n2_all[...]), flat(r.gin[p.c, :, :, cols]))
            return mine + tn(flat(r.n2_sib[...]), flat(r.gin_sib[:, :, cols]))

        return make

    down, up, out, qkv, skip = [], [], [], [], []
    group = model // depth
    for k in range(2):
        down.append(LineReduce(p, down_part(k), units // (2 * depth), half, *rest[:5]))
        rest = rest[5:]
    for k in range(2):
        up.append(LineReduce(p, up_part(k), group, 256, *rest[:5]))
        rest = rest[5:]
    for sums, axis, x, take, res, (rows, cols, parts) in (
        (out, 0, r.xmix, branch_columns, r.out_grad, shards[0]),
        (qkv, 0, r.xnormed, blocks_of(0), r.qkv_grad, shards[1]),
        (skip, 1, r.xjoined, blocks_of(6), r.skip_grad, shards[2]),
    ):
        width = cols // parts
        for k in range(parts):
            sums.append(Reduce(p, axis, x, take, rows, k * width, width, res, *rest[:5]))
            rest = rest[5:]

    pair_act.start()
    pair_n2.start()
    pair_gin.start()
    pair_cot.wait_recv()
    pair_act.wait_recv()
    down[0].begin()
    down[0].hop(0)
    plane_back.arrived()
    middle = r.middle[...]
    hat, rstd = normal(middle)
    grad = r.back[...]
    for k in range(3):
        grad = grad + r.got_back[k].astype(jnp.float32)
    cot = r.cot_all[0].astype(jnp.float32)
    middle_grad = cot + normal_back(grad, hat, rstd, f_scale)
    r.back[...] = middle_grad
    branch_grad = middle_grad.astype(bf)
    r.gbranch[0] = branch_grad
    there = Exchange(p, count, r.mixed_grad, r.got, r.s1, r.r1, r.o1)
    back = Exchange(p, count, r.grads_out, r.got_grads, r.s2, r.r2, r.o2)
    queries = Exchange(p, count, r.queries_out, r.got_queries, r.s3, r.r3, r.o3)
    mixed_grad = nt(r.weights[0], branch_grad[:, :half]) + nt(r.weights[1], branch_grad[:, half:])
    r.mixed_grad[...] = (mixed_grad.astype(bf) * kept_row.astype(bf)).reshape(r.mixed_grad.shape)
    there.start()
    plane_total.start()
    share_mixed.start()
    share_branch.start()
    for slot in range(6):
        fetch_qkv(slot).start()
    r.vectors[2:3, :] = jnp.sum(kept * grad * hat, 0, keepdims=True)
    r.vectors[3:4, :] = jnp.sum(kept * grad, 0, keepdims=True)

    def end_down(k):
        def write(here, total):
            r.down_grad[:, pl.ds(pl.multiple_of(k * half + here.start, 128), here.size)] = total

        down[k].end(write)

    def end_up(k):
        def write(here, total):
            r.up_out[:, :, k * 256 : (k + 1) * 256] = total.astype(bf).reshape(8, group // 8, 256)

        up[k].end(write)

    ups = Octet(p, lambda to: r.up_out.at[to], lambda slot: r.up_got.at[slot], r.up_sems.at[0], r.up_sems.at[1])

    def up_spread():
        ups.start()
        r.up_got[ups.slot] = r.up_out[ups.slot]

    def up_arrived():
        ups.arrived()
        for t in range(8):
            for z in range(depth):
                at = (z * 8 + t) * 128
                r.up_grad[:, at : at + 128] = r.up_got[t, :, z * 128 : (z + 1) * 128].astype(jnp.float32)

    def ready(shares):
        for share in shares:
            if isinstance(share, Quad):
                share.relay()
        for share in shares:
            share.arrived()

    blocks = r.qkv.shape[1] // 256
    attend_back_open(p, r.lengths, r.qkv, r.keys, r.values, r.kv_sums)
    attend = functools.partial(
        attend_back, p, there, r.qkv, r.lse, r.plain, r.keys, r.values, r.kv_sums, queries
    )
    down[1].begin()
    down[1].hop(0)
    attend(0, blocks // 2)
    down[0].hop(1)
    attend(blocks // 2, blocks)
    attend_back_close(r.kv_sums, r.grads_out)
    back.start()
    down[1].hop(1)

    cosine, sine = r.cosine[...][None], r.sine[...][None]

    def send_part(part, h):
        h = h.reshape(model, frames).T
        for k in range(2):
            r.glate[0, 2 * part + k] = h[:, k * chunk : (k + 1) * chunk]
            share_late(2 * part + k).start()

    queries.arrived()
    send_part(0, turn(r.got_queries[...].astype(jnp.float32), cosine, -sine).astype(bf))
    for k in range(2):
        fetch_qkv(k).wait()
        made = nt(r.glate[0, k], r.weights[k])
        if k == 0:
            r.total[...] = made
        else:
            r.total[...] += made
    down[0].hop(2)
    pair_n2.wait_recv()
    pair_gin.wait_recv()
    up[0].begin()
    up[0].hop(0)
    plane_total.arrived()
    total = r.middle[...] + r.own_total[...] + r.b_down[...]
    for k in range(3):
        total = total + r.got_total[k].astype(jnp.float32)
    r.output[...] = total.astype(bf)
    ready([share_mixed, share_branch])
    out[0].begin()
    up[1].begin()
    up[1].hop(0)
    ready([share_late(0), share_late(1)])
    qkv[0].begin()
    back.arrived()
    send_part(1, turn(r.got_grads[:, :HEAD_DIM, :].astype(jnp.float32), cosine, -sine).astype(bf))
    send_part(2, r.got_grads[:, HEAD_DIM:, :])
    for k in range(2, 6):
        fetch_qkv(k).wait()
        r.total[...] += nt(r.glate[0, k], r.weights[k])
    for k in range(4):
        fetch_skip(k).start()
    hat, rstd = normal(r.base[...])
    grad = r.total[...]
    base_grad = (r.back[...] + normal_back(grad, hat, rstd, a_scale)).astype(bf)
    for k in range(2):
        r.glate[0, 6 + k] = base_grad[:, k * chunk : (k + 1) * chunk]
        share_late(6 + k).start()
    r.vectors[0:1, :] = jnp.sum(kept * grad * hat, 0, keepdims=True)
    r.vectors[1:2, :] = jnp.sum(kept * grad, 0, keepdims=True)

    r.vectors[4:5, :] = jnp.sum(cot, 0, keepdims=True)
    r.vectors[5:6, :] = jnp.sum(base_grad.astype(jnp.float32), 0, keepdims=True)
    r.vectors[6:7, :] = r.bias[...]
    r.vectors[7:8, :] = jnp.zeros((1, model), jnp.float32)
    smalls = Octet(p, lambda to: r.vectors, lambda slot: r.plane_got.at[slot], r.small_sems.at[0], r.small_sems.at[1])
    small = Rounds(p, r.line_sems.at[0], r.line_sems.at[1])

    def small_line(d):
        return small.one(d, r.line_out, r.line_got.at[d], small.line(0, d))

    def after_plane():
        r.plane_got[smalls.slot] = r.vectors[...]
        smalls.arrived()
        halves = []
        for x in range(2):
            total = r.plane_got[x]
            for k in range(1, 4):
                total = total + r.plane_got[2 * k + x]
            halves.append(total)
            r.line_out[4 * x : 4 * x + 4, :] = total[0:4]
        r.line_out[8:10, :] = halves[0][4:6] + halves[1][4:6]
        chip = p.y * 4 + p.x
        r.line_out[10:11, :] = r.plane_got[chip, 6:7, :] + r.plane_got[chip + 2, 6:7, :]
        r.line_out[11:16, :] = jnp.zeros((5, model), jnp.float32)
        for d in range(1, depth):
            small_line(d).start()

    smalls.start()
    down[1].hop(2)
    end_down(0)
    out[0].hop(0)
    up[0].hop(1)

    number = p.b * 2 + p.x
    timers = Octet(
        p,
        lambda to: r.times_full.at[number],
        lambda slot: r.times_full.at[p.z * 8 + slot],
        r.small_sems.at[2],
        r.small_sems.at[3],
    )

    def times_line(d):
        block = r.times_full.at[pl.ds(p.z * 8, 8)]
        return small.one(3 + d, block, block, small.line(0, d))

    def times_came(d):
        z = (p.z + depth - d) % depth
        block = r.times_full.at[pl.ds(z * 8, 8)]
        return small.one(3 + d, block, block, small.line(0, d))

    for i in range(2):
        total = None
        for j in range(2):
            fetch_skip(2 * i + j).wait()
            made = nt(r.glate[0, 6 + j], r.weights[2 * i + j])
            total = made if total is None else total + made
        r.joined_grad[i] = total.astype(bf)

    qkv[0].hop(0)
    end_down(1)
    up[1].hop(1)
    after_plane()
    out[0].hop(1)
    ready([share_late(6), share_late(7)])
    skip[0].begin()
    skip[1].begin()
    ready([share_late(2), share_late(3)])
    qkv[1].begin()
    up[0].hop(2)
    ready([share_late(4), share_late(5)])
    qkv[2].begin()
    out[0].hop(2)
    qkv[0].hop(1)
    up[1].hop(2)

    total = r.line_out[...]
    for d in range(1, depth):
        small_line(d).wait_recv()
        total = total + r.line_got[d]
    first, second = total[0:4], total[4:8]
    r.line_sum[...] = total
    total = jnp.zeros((8, r.w_mod.shape[0]), jnp.float32)
    turned = r.times[...].T
    share = r.w_mod.shape[0]
    for part in range(4):
        values = [first[part : part + 1, :], second[part : part + 1, :]]
        here = pl.ds(part * model, model)
        left = extra_rows([*three_terms(values[0]), *three_terms(values[1])], 8, model)
        total = total + nt(left, r.w_mod[:, here])
        r.mod_grad[:, here] = turned[:share, 0:1] * values[0] + turned[:share, 4:5] * values[1]
    made = jnp.concatenate(
        [total[0:1] + total[1:2] + total[2:3], total[3:4] + total[4:5] + total[5:6], jnp.zeros((6, share), jnp.float32)]
    )
    r.times_full[number] = jnp.concatenate([made, jnp.zeros((8, 128 - share), jnp.float32)], 1)
    timers.start()
    skip[0].hop(0)
    qkv[1].hop(0)
    qkv[0].hop(2)
    end_up(0)
    skip[1].hop(0)
    skip[0].hop(1)
    qkv[1].hop(1)
    qkv[2].hop(0)
    end_up(1)
    up_spread()
    timers.arrived()
    for d in range(1, depth):
        times_line(d).start()
    r.sums_out[...] = jnp.zeros_like(r.sums_out)
    at = pl.multiple_of((p.z * 2 + p.c) * 128, 128)
    r.sums_out[0:1, :] = r.line_sum[10:11, pl.ds(at, 128)]
    at = pl.multiple_of(number // 4 * 128, 128)
    near = r.line_sum[8:10, pl.ds(at, 128)]
    each = model // devices
    own = near[:, :each]
    for k in range(1, 4):
        own = jnp.where(number % 4 == k, near[:, k * each : (k + 1) * each], own)
    r.sums_out[1:2, :each] = own[0:1]
    r.sums_out[1:2, each : 2 * each] = own[1:2]
    out[0].end()
    qkv[0].end()
    skip[0].hop(2)
    skip[1].hop(1)
    qkv[1].hop(2)
    qkv[2].hop(1)
    skip[0].end()
    skip[1].hop(2)
    qkv[1].end()
    qkv[2].hop(2)
    skip[1].end()
    up_arrived()
    qkv[2].end()
    for d in range(1, depth):
        times_came(d).wait_recv()
    for one in [*down, *up, *out, *qkv, *skip, share_mixed, share_branch, plane_n2, plane_back, plane_total]:
        one.finish()
    for c in range(8):
        share_late(c).finish()
    for one in (pair_cot, pair_n2, pair_act, pair_gin):
        one.wait_send()
    for one in (there, back, queries, ups, smalls, timers):
        one.finish()
    for d in range(1, depth):
        small_line(d).wait_send()
        times_line(d).wait_send()


def back_call(depth, devices, args):
    base, qkv = args["base"], args["qkv_far"]
    frames, model = base.shape
    count = devices // 2
    units = args["w_up"].shape[1]
    ff = units * 4
    bf, f32 = jnp.bfloat16, jnp.float32
    share = args["w_mod"].shape[0]
    dma = pltpu.SemaphoreType.DMA
    sum_scratch = []
    for rows, width in [(units // (2 * depth), model // 2)] * 2 + [(model // depth, 256)] * 2:
        sum_scratch.append(pltpu.VMEM((depth * rows, width), f32))
        sum_scratch += LineReduce.scratch(rows, width, depth)
    shards = [
        (model // devices, model, 1),
        (model // devices, 3 * model, 3),
        (2 * model // devices, model, 2),
    ]
    for rows, cols, parts in shards:
        for _ in range(parts):
            sum_scratch.append(pltpu.VMEM((depth * rows, cols // parts), f32))
            sum_scratch += Reduce.scratch(rows, cols // parts, depth)

    def tall(n, *shape, kind=bf):
        return pltpu.VMEM((n, *shape), kind)

    scratch = dict(
        cot_all=tall(4, frames, model),
        qkv=tall(*qkv.shape),
        plain=tall(HEAD_DIM, qkv.shape[1], kind=f32),
        xnormed=tall(4, depth, 2, model // devices, frames),
        xjoined=tall(4, depth, 2, 2 * model // devices, frames),
        load_sems=dma((5,)),
        weights=tall(6, model, 512),
        middle=tall(frames, model, kind=f32),
        total=tall(frames, model, kind=f32),
        own_total=tall(frames, model, kind=f32),
        back=tall(frames, model, kind=f32),
        bias=tall(1, units, kind=f32),
        vectors=tall(8, model, kind=f32),
        n2_all=tall(4, frames, model),
        n2_sib=tall(4, frames, model),
        cot_sib=tall(4, frames, model),
        act=tall(2, 4, frames, units // 2),
        gin=tall(2, 4, frames, units // 2),
        act_sib=tall(4, frames, units // 2),
        gin_sib=tall(4, frames, units // 2),
        part_back=tall(3, frames, model),
        got_back=tall(3, frames, model),
        part_total=tall(3, frames, model),
        got_total=tall(3, frames, model),
        up_out=tall(8, model // devices, units // 2),
        up_got=tall(8, model // devices, units // 2),
        gbranch=tall(4, frames, model),
        glate=tall(4, 8, frames, 512),
        xmix=tall(4, depth, 2, model // devices, frames),
        mixed_grad=tall(count, HEAD_DIM, frames),
        got=tall(count, HEAD_DIM, frames),
        keys=tall(qkv.shape[1], 2 * HEAD_DIM),
        values=tall(qkv.shape[1], 2 * HEAD_DIM),
        kv_sums=tall(qkv.shape[1], 2 * HEAD_DIM, kind=f32),
        grads_out=tall(count, 2 * HEAD_DIM, frames),
        got_grads=tall(count, 2 * HEAD_DIM, frames),
        queries_out=tall(count, HEAD_DIM, frames),
        got_queries=tall(count, HEAD_DIM, frames),
        plane_got=tall(8, 8, model, kind=f32),
        line_out=tall(16, model, kind=f32),
        line_got=tall(depth, 16, model, kind=f32),
        line_sum=tall(16, model, kind=f32),
        weight_sems=dma((6,)),
        pair_sems=dma((2, 4)),
        n2_sems=dma((2, 4)),
        back_sems=dma((2, 4)),
        total_sems=dma((2, 4)),
        up_sems=dma((2, 8)),
        row_sems=dma((1, 7)),
        branch_sems=dma((6,)),
        late_sems=dma((8, 6)),
        s1=dma((count,)),
        r1=dma((count,)),
        o1=dma,
        s2=dma((count,)),
        r2=dma((count,)),
        o2=dma,
        s3=dma((count,)),
        r3=dma((count,)),
        o3=dma,
        small_sems=dma((4, 8)),
        line_sems=dma((2, 8)),
    )
    shape = jax.ShapeDtypeStruct
    outs = dict(
        output=shape((frames, model), bf),
        joined_grad=shape((2, frames, model), bf),
        skip_grad=shape((2 * model // devices, model), f32),
        qkv_grad=shape((model // devices, 3 * model), f32),
        out_grad=shape((model // devices, model), f32),
        up_grad=shape((model // devices, ff), f32),
        down_grad=shape((ff // devices, model), f32),
        mod_grad=shape((share, 4 * model), f32),
        sums_out=shape((8, 128), f32),
        times_full=shape((devices, 8, 128), f32),
    )
    names = [*args, *outs, *scratch]
    vmem = pl.BlockSpec(memory_space=pltpu.VMEM)
    specs = dict.fromkeys(args, vmem)
    specs["lengths"] = pl.BlockSpec(memory_space=pltpu.SMEM)
    for name in args:
        if name.startswith("w_") and name != "w_mod" or name.endswith("_far"):
            specs[name] = pl.BlockSpec(memory_space=pl.ANY)
    made = pl.pallas_call(
        functools.partial(back_kernel, depth, shards, names),
        name="back",
        out_shape=list(outs.values()),
        in_specs=list(specs.values()),
        out_specs=[vmem] * len(outs),
        scratch_shapes=list(scratch.values()) + sum_scratch,
        compiler_params=kernel_params(3),
    )(*args.values())
    return dict(zip(outs, made))


def front_kernel(depth, cuts, names, *refs):
    r = Refs(names, refs)
    p = Place(depth)
    count = 4 * depth
    devices = 2 * count
    frames, model = r.hidden.shape
    bf = jnp.bfloat16
    share = r.w_mod.shape[0]
    tile = pl.ds(pl.multiple_of((p.b // 2) * 128, 128), 128)
    part = r.time_row[:, tile].astype(jnp.float32)
    mark = lax.broadcasted_iota(jnp.int32, (8, 128), 0) // 4 == p.x
    for ref, x in ((r.own_time, p.x), (r.other_time, 1 - p.x)):
        slot = p.c * 2 + x
        picked = part[:, 0:share]
        for k in range(1, 4):
            picked = jnp.where(slot == k, part[:, k * share : (k + 1) * share], picked)
        picked = jnp.concatenate([picked, jnp.zeros((1, 128 - share), jnp.float32)], 1)
        ref[...] = jnp.where(mark, picked, 0.0)
    half = HEAD_DIM // 2
    position = p.b * frames + lax.broadcasted_iota(jnp.int32, (half, frames), 1)
    length = r.lengths[p.x]
    offset = jnp.where(position < length, position, position - length).astype(jnp.float32)
    index = lax.broadcasted_iota(jnp.int32, (half, frames), 0).astype(jnp.float32)
    angle = offset * jnp.exp(index * (-math.log(10000.0) / half))
    r.cosine[...] = jnp.cos(angle)
    r.sine[...] = jnp.sin(angle)
    greet_plane(p, count, (p.to_across, p.to_far_x))
    ask = remote(r.other_time, r.got_time, r.time_sems.at[0], r.time_sems.at[1], p.to_x)
    ask.start()

    groups = {}
    number = 0
    owns = []
    for name, src, dst in (
        ("skip", r.w_skip, r.skip_here),
        ("qkv", r.w_qkv, r.qkv_here),
        ("out", r.w_out, r.out_full),
    ):
        groups[name] = []
        for lo, hi, first in ranges(src.shape[1], src.shape[1] // cuts[name] if cuts[name] else 0):
            groups[name].append(
                Gather(p, src, dst, src.shape[0], lo, hi, True, first, r.sends.at[number], r.recvs.at[number])
            )
            number += 1
        owns.append((src, dst, src.shape[0]))
    packs = Gather(
        p, r.pack, r.pack_full, 8, 0, r.pack.shape[1], False, False, r.sends.at[number], r.recvs.at[number]
    )
    number += 1
    units = 2 * depth * 128

    def spread_up():
        for q in range(4):
            y, x = (p.y + q // 2) % 2, (p.x + q % 2) % 2
            for z in range(depth):
                for c in range(2):
                    cols = pl.ds(pl.multiple_of(p.shard(z, y, c, x) * 128, 128), 128)
                    r.up_out[q, :, (z * 2 + c) * 128 : (z * 2 + c + 1) * 128] = r.w_up[:, cols]
        r.up_mid[p.y, pl.ds(pl.multiple_of(p.x * rows_up, rows_up), rows_up), :] = r.up_out[0]
        plane_up.start()

    rows_up = r.w_up.shape[0]
    plane_up = Plane(
        p,
        lambda q: r.up_out.at[q],
        lambda q: r.up_mid.at[p.y, pl.ds(pl.multiple_of(p.x * rows_up, rows_up), rows_up)],
        r.up_sems.at[0],
        r.up_sems.at[1],
    )
    plane_cot = Plane(p, lambda q: r.cot, lambda q: r.cot_all.at[q], r.cot_sems.at[0], r.cot_sems.at[1])
    line_up = LineGather(p, r.up_mid, lambda z, c: r.up_here.at[z, :, c], r.line_sems.at[0], r.line_sems.at[1])
    line_down = LineGather(p, r.w_down, lambda z, c: r.down_here.at[z, c], r.line_sems.at[2], r.line_sems.at[3])
    lines = (line_up, line_down)
    own_up = pltpu.make_async_copy(r.up_mid, r.up_here.at[p.z, :, p.c], r.own_sems.at[3])
    own_down = pltpu.make_async_copy(r.w_down, r.down_here.at[p.z, p.c], r.own_sems.at[4])
    own_cot = pltpu.make_async_copy(r.cot, r.cot_all.at[0], r.own_sems.at[5])
    share_joined = QuadRows(p, 1, r.joined, r.xjoined, r.row_sems.at[0])
    share_normed = QuadRows(p, 0, r.normed, r.xnormed, r.row_sems.at[1])

    def lines_own():
        plane_up.arrived()
        own_up.start()
        for line in lines:
            line.own()

    queries = Exchange(p, count, r.queries_in, r.got_queries, r.s1, r.r1, r.o1)
    there = Exchange(p, count, r.heads_in, r.got, r.s3, r.r3, r.o3)
    back = Exchange(p, count, r.mixed_out, r.mixed, r.s2, r.r2, r.o2)

    def products():
        ask.wait_recv()
        both = r.own_time[...] + r.got_time[...]
        r.times[...] = both
        left = both[:, : r.w_mod.shape[0]].astype(bf)
        row = lax.broadcasted_iota(jnp.int32, (8, model), 0) % 4
        total = jnp.zeros((8, model), jnp.float32)
        for part in range(4):
            made = jnp.dot(
                left, r.w_mod[:, part * model : (part + 1) * model], preferred_element_type=jnp.float32
            )
            total = jnp.where(row == part, made, total)
        r.mods_part[0] = total
        small.one(0, r.mods_part.at[0], r.mods_got.at[0], p.to_core).start()

    def bias_tile():
        each = r.b_skip.shape[1]
        r.pack[...] = jnp.zeros((8, 128), jnp.float32)
        r.pack[0:1, :] = r.b_up_part[...].astype(jnp.float32)
        r.pack[1:2, :each] = r.b_skip[...].astype(jnp.float32)
        r.pack[1:2, each : 2 * each] = r.b_down_part[...].astype(jnp.float32)

    small = Rounds(p, r.small_sems.at[0], r.small_sems.at[1])

    def small_line(d):
        return small.one(d, r.mods_part.at[1], r.mods_got.at[d], small.line(0, d))

    def after_core():
        small.one(0, r.mods_part.at[0], r.mods_got.at[0], p.to_core).wait_recv()
        r.mods_part[1] = r.mods_part[0] + r.mods_got[0]
        for d in range(1, depth):
            small_line(d).start()

    def after_line():
        total = r.mods_part[1]
        for d in range(1, depth):
            small_line(d).wait_recv()
            total = total + r.mods_got[d]
        r.mods_part[2] = total
        small.one(4, r.mods_part.at[2], r.mods_got.at[4], p.to_y).start()

    def after_y():
        small.one(4, r.mods_part.at[2], r.mods_got.at[4], p.to_y).wait_recv()
        r.mods_part[3] = r.mods_part[2] + r.mods_got[4]
        small.one(5, r.mods_part.at[3], r.mods_got.at[5], p.to_x).start()

    def turned_inputs():
        half = depth // 2
        for k, ref in enumerate((r.hidden, r.skip_in)):
            r.joined[k * half : (k + 1) * half] = ref[...].T.reshape(half, *r.joined.shape[1:])

    def keep_skip():
        return pltpu.make_async_copy(r.skip_here, r.skip_full, r.load_sems.at[0])

    def keep_qkv():
        return pltpu.make_async_copy(r.qkv_here, r.qkv_full, r.load_sems.at[1])

    own_copies = []

    def complete(name):
        for g in groups[name]:
            g.shared()

    def first_norm():
        own_copies[0].wait()
        complete("skip")
        at = pl.multiple_of(p.shard(p.z, p.y, p.c, p.x) * 8, 8)
        r.pack_full[pl.ds(at, 8), :] = r.pack[...]
        packs.shared()
        small.one(5, r.mods_part.at[3], r.mods_got.at[5], p.to_x).wait_recv()
        total = r.mods_part[3] + r.mods_got[5]
        mods = jnp.where(p.x == 0, total[0:4], total[4:8])
        r.mods[0:4, :] = mods
        r.mods[4:8, :] = mods
        each = model // devices
        tiles = [r.pack_full[k * 8 : k * 8 + 2, :] for k in range(devices)]
        for z in range(depth):
            for c in range(2):
                at = pl.multiple_of(p.shard(z, p.y, c, p.x) * 8, 8)
                here = (z * 2 + c) * 128
                r.b_up[:, here : here + 128] = r.pack_full[pl.ds(at, 8), :][0:1]
        b_skip = jnp.concatenate([t[1:2, :each] for t in tiles], 1)
        r.b_down[...] = jnp.concatenate([t[1:2, each : 2 * each] for t in tiles], 1)
        length = r.lengths[p.x]
        kept = (p.b * frames + lax.broadcasted_iota(jnp.int32, (frames, 1), 0) < length).astype(jnp.float32)
        base = jnp.dot(r.hidden[...], r.skip_here[:model, :], preferred_element_type=jnp.float32)
        base = base + jnp.dot(r.skip_in[...], r.skip_here[model:, :], preferred_element_type=jnp.float32) + b_skip
        r.base[...] = base
        hat, _ = normal(base)
        normed = (hat * (1.0 + kept * mods[0:1]) + kept * mods[1:2]).astype(bf)
        r.normed[...] = normed.T.reshape(r.normed.shape)
        r.normed_here[...] = normed

    def projections():
        own_copies[1].wait()
        complete("qkv")
        share_normed.start()
        normed = r.normed_here[...]
        cosine, sine = r.cosine[...][None], r.sine[...][None]
        for part in (1, 2, 0):
            made = jnp.dot(
                normed, r.qkv_here[:, part * model : (part + 1) * model], preferred_element_type=jnp.float32
            )
            made = made.T.reshape(HEADS, HEAD_DIM, frames)
            if part < 2:
                made = turn(made, cosine, sine)
            if part == 0:
                r.queries_in[...] = made.astype(bf)
                queries.start()
                keep_skip().start()
                keep_qkv().start()
            else:
                r.heads_in[:, (part - 1) * HEAD_DIM : part * HEAD_DIM, :] = made.astype(bf)
            if part == 2:
                there.start()

    def attention(lo, hi):
        attend(p, r.lengths, queries, r.qkv, r.keys, r.values, back, r.lse, r.plain, lo, hi)

    blocks = count // 2

    def first_half():
        there.arrived()
        attend_open(p, r.lengths, r.got, r.qkv, r.keys, r.values)
        attention(0, blocks // 2)

    def second_half():
        attention(blocks // 2, blocks)

    events = []
    for k, name in enumerate(("skip", "qkv")):
        events += [(t + 1.5 * k, k, f) for g in groups[name] for t, f in g.steps()]
    events.append((0.3, 0, products))
    events.append((0.31, 0, bias_tile))
    events.append((0.35, 0, turned_inputs))
    events.append((0.36, 0, spread_up))
    events.append((0.9, 0, after_core))
    events.append((2.05, 9, after_line))
    events.append((3.05, 9, after_y))
    events += [(t + 0.5, 9, f) for t, f in packs.steps()]
    events.append((3.2, 5, lines_own))
    for g in groups["out"]:
        times = {0: 3.25, 1: 5.56, 2: 7.0, 3: 7.16, 4: 8.73, 5: 9.45}
        events += [(times[t], 2, f) for t, f in g.steps()]
    for k, line in enumerate(lines):
        events.append((5.55, 5 + k, functools.partial(line.line, 1)))
        events.append((7.15, 5 + k, functools.partial(line.line, 2)))
        events.append((8.72, 5 + k, functools.partial(line.line, 3)))
    events.append((5.6, 0, first_norm))
    events.append((7.11, 0, plane_cot.start))
    events.append((7.12, 0, share_joined.start))
    events.append((7.1, 0, projections))
    events.append((8.4, 0, first_half))
    events.append((9.4, 0, second_half))
    events.sort(key=lambda e: (e[0], e[1]))
    own_down.start()
    own_cot.start()
    own_copies += keep_own(p, owns, r.own_sems)
    play([f for _, _, f in events])
    complete("out")
    for line in lines:
        line.shared()
        line.sent()
    for group in groups.values():
        for g in group:
            g.sent()
    packs.sent()
    for one in (plane_up, there, queries):
        one.finish()
    plane_cot.arrived()
    plane_cot.finish()
    for share in (share_joined, share_normed):
        share.arrived()
        share.finish()
    back.arrived()
    back.finish()
    for copy in (own_copies[2], own_up, own_down, own_cot, keep_skip(), keep_qkv()):
        copy.wait()
    ask.wait_send()
    small.one(0, r.mods_part.at[0], r.mods_got.at[0], p.to_core).wait_send()
    for d in range(1, depth):
        small_line(d).wait_send()
    small.one(4, r.mods_part.at[2], r.mods_got.at[4], p.to_y).wait_send()
    small.one(5, r.mods_part.at[3], r.mods_got.at[5], p.to_x).wait_send()


def front_call(depth, devices, args):
    cuts = dict(skip=8, qkv=8, out=0)
    frames, model = args["hidden"].shape
    bf, f32 = jnp.bfloat16, jnp.float32
    count = devices // 2
    total = count * frames
    shape = jax.ShapeDtypeStruct
    vmem = pl.BlockSpec(memory_space=pltpu.VMEM)
    away = pl.BlockSpec(memory_space=pl.ANY)

    def whole(name):
        rows, cols = args[name].shape
        return shape((devices * rows, cols), bf)

    def by_owner(n):
        return (depth, 2, 2, 2, n // devices, frames)

    def quarter(n):
        return (4, depth, 2, n // devices, frames)

    units = 2 * depth * 128
    rows_up = args["w_up"].shape[0]
    far = dict(
        skip_full=whole("w_skip"),
        qkv_full=whole("w_qkv"),
        out_full=whole("w_out"),
        up_here=shape((depth, 2, 2, 2 * rows_up, units), bf),
        down_here=shape((depth, 2, 128, model), bf),
        cot_all=shape((4, frames, model), bf),
        xjoined=shape(quarter(2 * model), bf),
        xnormed=shape(quarter(model), bf),
        mixed=shape((count, HEAD_DIM, frames), bf),
    )
    half = HEAD_DIM // 2
    near = dict(
        cosine=shape((half, frames), f32),
        sine=shape((half, frames), f32),
        times=shape((8, 128), f32),
        mods=shape((8, model), f32),
        b_up=shape((1, units), f32),
        b_down=shape((1, model), f32),
        base=shape((frames, model), f32),
        qkv=shape((3 * HEAD_DIM, total), bf),
        lse=shape((1, total), f32),
        plain=shape((HEAD_DIM, total), f32),
    )
    dma = pltpu.SemaphoreType.DMA
    gathers = 6
    scratch = dict(
        own_time=pltpu.VMEM((8, 128), f32),
        other_time=pltpu.VMEM((8, 128), f32),
        got_time=pltpu.VMEM((8, 128), f32),
        pack=pltpu.VMEM((8, 128), f32),
        pack_full=pltpu.VMEM((devices * 8, 128), f32),
        mods_part=pltpu.VMEM((4, 8, model), f32),
        mods_got=pltpu.VMEM((6, 8, model), f32),
        small_sems=dma((2, 6)),
        skip_here=pltpu.VMEM((2 * model, model), bf),
        qkv_here=pltpu.VMEM((model, 3 * model), bf),
        joined=pltpu.VMEM(by_owner(2 * model), bf),
        normed=pltpu.VMEM(by_owner(model), bf),
        normed_here=pltpu.VMEM((frames, model), bf),
        up_out=pltpu.VMEM((4, rows_up, units), bf),
        up_mid=pltpu.VMEM((2, 2 * rows_up, units), bf),
        queries_in=pltpu.VMEM((count, HEAD_DIM, frames), bf),
        got_queries=pltpu.VMEM((count, HEAD_DIM, frames), bf),
        heads_in=pltpu.VMEM((count, 2 * HEAD_DIM, frames), bf),
        got=pltpu.VMEM((count, 2 * HEAD_DIM, frames), bf),
        keys=pltpu.VMEM((total, 2 * HEAD_DIM), bf),
        values=pltpu.VMEM((HEAD_DIM + 16, total), bf),
        mixed_out=pltpu.VMEM((count, HEAD_DIM, frames), bf),
        time_sems=dma((2,)),
        load_sems=dma((2,)),
        own_sems=dma((6,)),
        up_sems=dma((2, 4)),
        cot_sems=dma((2, 4)),
        line_sems=dma((4, 16)),
        row_sems=dma((2, 7)),
        sends=dma((gathers, Gather.SENDS)),
        recvs=dma((gathers, Gather.RECVS)),
        s1=dma((count,)),
        r1=dma((count,)),
        o1=dma,
        s2=dma((count,)),
        r2=dma((count,)),
        o2=dma,
        s3=dma((count,)),
        r3=dma((count,)),
        o3=dma,
    )
    names = [*args, *far, *near, *scratch]
    made = pl.pallas_call(
        functools.partial(front_kernel, depth, cuts, names),
        name="front",
        out_shape=[*far.values(), *near.values()],
        in_specs=[pl.BlockSpec(memory_space=pltpu.SMEM)] + [vmem] * (len(args) - 1),
        out_specs=[away] * len(far) + [vmem] * len(near),
        scratch_shapes=list(scratch.values()),
        compiler_params=kernel_params(1),
    )(*args.values())
    return dict(zip([*far, *near], made))


def write_kernel(count, times, sums, joined, *refs):
    ins, outs = refs[:count], refs[count:]
    for src, dst in zip(ins, outs):
        dst[...] = src[...]
    hidden_grad, skip_grad, time_grad, b_up, b_skip, b_down = outs[count:]
    hidden_grad[...] = joined[0]
    skip_grad[...] = joined[1]
    each = b_skip.shape[1]
    part = jnp.where(lax.axis_index("uly") == 0, times[:, 0, :each], times[:, 1, :each])
    time_grad[...] = jnp.concatenate([part[k : k + 1] for k in range(times.shape[0])], 1)
    b_up[...] = sums[0:1, :]
    b_down[...] = sums[1:2, :each]
    b_skip[...] = sums[1:2, each : 2 * each]


def write_call(made, names, each):
    shape = jax.ShapeDtypeStruct
    joined = made["joined_grad"]
    frames, model = joined.shape[1:]
    plain = [shape(made[name].shape, made[name].dtype) for name in names]
    return pl.pallas_call(
        functools.partial(write_kernel, len(names)),
        name="write",
        out_shape=plain
        + [shape((frames, model), joined.dtype)] * 2
        + [shape((1, model), jnp.float32), shape((1, 128), jnp.float32)]
        + [shape((1, each), jnp.float32)] * 2,
        in_specs=in_vmem(3 + len(names)),
        out_specs=in_vmem(6 + len(names)),
        compiler_params=pltpu.CompilerParams(vmem_limit_bytes=VMEM_BYTES),
    )(made["times_full"], made["sums_out"], joined, *[made[name] for name in names])


def first_with_second(left, right, dims):
    return lax.dot_general(left, right, ((dims[:1], dims[1:]), ((), ())), preferred_element_type=jnp.float32)


def turn(values, cosine, sine):
    half = HEAD_DIM // 2
    first, second = values[..., :half, :], values[..., half:, :]
    return jnp.concatenate([first * cosine - second * sine, second * cosine + first * sine], -2)


def on_device(hidden, skip_in, time_embed, lengths, cotangent, w_skip, b_skip, w_mod, w_qkv, w_out, w_up, b_up,
              w_down, b_down):
    blocks, rows = lax.axis_size("blk"), lax.axis_size("uly")
    devices, depth = blocks * rows, blocks // 4
    _, frames, model = hidden.shape
    front = front_call(
        depth,
        devices,
        dict(
            lengths=lengths[:, 0],
            time_row=time_embed[0],
            b_skip=b_skip[None],
            b_up_part=b_up[None],
            b_down_part=b_down[None],
            cot=cotangent[0],
            w_mod=w_mod,
            hidden=hidden[0],
            skip_in=skip_in[0],
            w_skip=w_skip,
            w_qkv=w_qkv,
            w_out=w_out,
            w_up=w_up,
            w_down=w_down,
        ),
    )
    made = back_call(
        depth,
        devices,
        dict(
            lengths=lengths[:, 0],
            base=front["base"],
            mods=front["mods"],
            b_up=front["b_up"],
            b_down=front["b_down"],
            cosine=front["cosine"],
            sine=front["sine"],
            w_mod=w_mod,
            times=front["times"],
            qkv_far=front["qkv"],
            lse=front["lse"],
            plain_far=front["plain"],
            cot_far=front["cot_all"],
            mixed=front["mixed"].reshape(depth, 2, 2, 2, model // devices, frames),
            xjoined_far=front["xjoined"],
            xnormed_far=front["xnormed"],
            w_out=front["out_full"],
            w_up=front["up_here"].reshape(model, -1),
            w_down=front["down_here"].reshape(-1, model),
            w_qkv=front["qkv_full"],
            w_skip=front["skip_full"],
        ),
    )
    names = ["output", "skip_grad", "mod_grad", "qkv_grad", "out_grad", "up_grad", "down_grad"]
    output, skip_grad, mod_grad, qkv_grad, out_grad, up_grad, down_grad, *small = write_call(
        made, names, b_skip.shape[0]
    )
    hidden_grad, skip_in_grad, time_grad, b_up_grad, b_skip_grad, b_down_grad = small
    return (
        output[None],
        hidden_grad[None],
        skip_in_grad[None],
        time_grad[None],
        skip_grad,
        b_skip_grad[0],
        mod_grad,
        qkv_grad,
        out_grad,
        up_grad,
        b_up_grad[0],
        down_grad,
        b_down_grad[0],
    )


def solution(mesh):
    placed = (
        P("uly", "blk", None),
        P("uly", "blk", None),
        P("uly", None, None),
        P(),
        P("uly", "blk", None),
        P(("blk", "uly"), None),
        P(("blk", "uly")),
        P(("blk", "uly"), None),
        P(("blk", "uly"), None),
        P(("blk", "uly"), None),
        P(("blk", "uly"), None),
        P(("blk", "uly")),
        P(("blk", "uly"), None),
        P(("blk", "uly")),
    )
    blocks = mesh.shape["blk"]
    special = mesh.shape["uly"] == 2 and blocks == HEADS and blocks % 4 == 0 and blocks > 4
    return jax.shard_map(
        on_device if special else per_device,
        mesh=mesh,
        in_specs=placed,
        out_specs=(
            P("uly", "blk", None),
            P("uly", "blk", None),
            P("uly", "blk", None),
            P("uly", None, None),
            P(("blk", "uly"), None),
            P(("blk", "uly")),
            P(("blk", "uly"), None),
            P(("blk", "uly"), None),
            P(("blk", "uly"), None),
            P(("blk", "uly"), None),
            P(("blk", "uly")),
            P(("blk", "uly"), None),
            P(("blk", "uly")),
        ),
        check_vma=False,
    )
```
